32 devices in a mesh: dp: 8 (over y, x, core), expert: 4 (over z).
Axes of the slice: x: 2, y: 2, z: 4, core: 2. Of those that a mesh axis runs over, the one named last changes fastest.
Arguments:
- tokens: bfloat16 [1024, 4096], P('dp', 'expert'), may hold values from -6 to 6
- output_gradient: bfloat16 [1024, 4096], P('dp', 'expert'), may hold values from -6 to 6
- routing: int32 [1024, 2], P('dp'), may hold values from 0 to 3, all different within a row; in each aligned block of 128 rows (0 to 127, 128 to 255, ...) at most 128 rows name the same one
- router_gate_values: float32 [1024, 2], P('dp'), may hold values from 0.1 to 0.9
- gate_weight: bfloat16 [4, 7168, 4096], P('expert', 'dp'), may hold values from -0.09375 to 0.09375
- up_weight: bfloat16 [4, 7168, 4096], P('expert', 'dp'), may hold values from -0.09375 to 0.09375
- down_weight: bfloat16 [4, 7168, 4096], P('expert', 'dp'), may hold values from -0.0625 to 0.0625
- adapter_lower_gate: bfloat16 [4, 16, 4096], P('expert'), may hold values from -0.09375 to 0.09375
- adapter_upper_gate: bfloat16 [4, 7168, 16], P('expert', 'dp'), may hold values from -0.375 to 0.375
- adapter_lower_up: bfloat16 [4, 16, 4096], P('expert'), may hold values from -0.09375 to 0.09375
- adapter_upper_up: bfloat16 [4, 7168, 16], P('expert', 'dp'), may hold values from -0.375 to 0.375
- adapter_lower_down: bfloat16 [4, 16, 7168], P('expert', None, 'dp'), may hold values from -0.0625 to 0.0625
- adapter_upper_down: bfloat16 [4, 4096, 16], P('expert'), may hold values from -0.375 to 0.375
Outputs:
- grad_x: bfloat16 [1024, 4096], P('dp', 'expert')
- grad_lora_a_gate: float32 [4, 16, 4096], P('expert')
- grad_lora_b_gate: float32 [4, 7168, 16], P('expert', 'dp')
- grad_lora_a_up: float32 [4, 16, 4096], P('expert')
- grad_lora_b_up: float32 [4, 7168, 16], P('expert', 'dp')
- grad_lora_a_down: float32 [4, 16, 7168], P('expert', None, 'dp')
- grad_lora_b_down: float32 [4, 4096, 16], P('expert')
The draws below stay inside these ranges and needn't reach their ends.
Inputs may be any that keep to these rules, and one draw needn't show every extreme that they name: `routing`: each row names two different experts. In the rows of one dp shard (aligned blocks of 128 rows) no expert is named by more than 128 rows, and in some blocks one expert is named by exactly 128 rows.
All inputs are finite; a program needn't handle non-finite values.
Results may differ from the reference program's by a relative error of at most 0.015.
Values may be sent and summed in bfloat16 or wider, within the bound.
No kernel may reach another device: no remote copies, remote signals or barrier semaphores. Data moves between devices by JAX's collectives and lax.ppermute only.
A program may use at most 256 MiB of HBM per device.

```python
import math
import jax
import jax.numpy as jnp
import numpy as np
from jax import lax

MODEL_WIDTH = 4096
HIDDEN_HALF = 7168
ADAPTER_RANK = 16
TOK_DEV = 128
EXPERT_TOTAL = 4
CAP = 128
TOKENS = 1024
N_DP = 8


def block_levels(own_key, shape, cuts, least, high):
    gain = 1.0
    for axis_at, shards_of in cuts:
        heights = jax.random.uniform(jax.random.fold_in(jax.random.fold_in(own_key, 6), axis_at), (shards_of,), jnp.float32, least / len(cuts), high / len(cuts))
        gain = gain * jnp.repeat(jnp.exp(heights), shape[axis_at] // shards_of).reshape((-1,) + (1,) * (len(shape) - 1 - axis_at))
    return gain


def shared_out(stream_key, own, number, rows, number_of, top, reach, slope):
    sequence = jax.random.permutation(stream_key, number_of)
    crowded, usual = load_shares(number_of, rows * top, reach, slope, True), load_shares(number_of, rows * top, reach, slope, False)
    places = jnp.arange(number_of)

    def named(lengths, rotation):
        used = int((lengths > 0).sum())
        fixed = max(1, used // 4)
        shifted = fixed + (places - fixed + rotation * (used - fixed)) % max(1, number_of - fixed)
        return jnp.zeros((number_of,), jnp.int32).at[sequence[jnp.where(places < fixed, places, shifted)]].set(jnp.asarray(lengths, jnp.int32))

    lengths = jnp.where(number % 4 == 0, named(crowded, number // 4), named(usual, number - number // 4 - 1))
    mixed = jax.random.permutation(jax.random.fold_in(own, 3), number_of)
    source_of, receiver = mixed[0:number_of // 2 * 2:2], mixed[1:number_of // 2 * 2:2]
    room = jnp.minimum(lengths[source_of] - 1, reach - lengths[receiver]) // 2
    room = jnp.where((source_of == sequence[0]) | (receiver == sequence[0]) | (lengths[receiver] == 0), 0, jnp.maximum(room, 0))
    shifted = jax.random.randint(jax.random.fold_in(own, 4), (number_of // 2,), 0, 1 << 20) % (room + 1)
    lengths = lengths.at[source_of].add(-shifted).at[receiver].add(shifted)
    labels = jnp.searchsorted(jnp.cumsum(lengths), jnp.arange(rows * top), side="right").astype(jnp.int32)
    listing = labels.reshape(top, rows).T
    listing = listing[jax.random.permutation(jax.random.fold_in(own, 1), rows)]
    rotation = jax.random.randint(jax.random.fold_in(own, 2), (rows, 1), 0, top)
    return jnp.take_along_axis(listing, (jnp.arange(top)[None, :] + rotation) % top, axis=1)


def load_shares(count, total, most, skew, full):
    loads = [(1 << 20) // math.isqrt(grade ** skew) + 1 for grade in range(1, count + 1)]
    largest = most if full else min(most, max(-(-total // count), total * loads[0] // sum(loads)))
    least = 1 if total - largest >= count - 1 else 0
    counts, surplus = [largest] + [least] * (count - 1), total - largest - least * (count - 1)
    while surplus > 0:
        movable = [i for i in range(1, count) if counts[i] < largest] or [i for i in range(1, count) if counts[i] < most]
        mass, remaining = sum([loads[i] for i in movable]), surplus
        for i in movable:
            addition = min(most - counts[i], max(1, remaining * loads[i] // mass), surplus)
            counts[i] = counts[i] + addition
            surplus = surplus - addition
    return np.array(counts)


def gaussian(key, shape, spread, bound, split=(), kind=jnp.bfloat16):
    array = jax.random.normal(key, shape, jnp.float32) * spread
    if len(split) > 0:
        array = block_levels(key, shape, split, -0.22, 0.18) * array
    return jnp.clip(array, min=-bound, max=bound).astype(kind)


def setup_inputs(seed: int = 0) -> dict:
    streams_of = jax.random.split(jax.random.key(seed), 14)
    tokens = gaussian(streams_of[0], (TOKENS, MODEL_WIDTH), 1.0, 6.0, ((0, 8), (1, 4)))
    output_gradient = gaussian(streams_of[1], (TOKENS, MODEL_WIDTH), 1.0, 6.0, ((0, 8), (1, 4)))
    routing_keys = jax.random.split(jax.random.fold_in(streams_of[2], 1), TOKENS // TOK_DEV)
    routing_turns = jax.random.permutation(jax.random.fold_in(streams_of[2], 3), TOKENS // TOK_DEV)
    routing = jax.vmap(lambda own, number: shared_out(jax.random.fold_in(streams_of[2], 2), own, number, TOK_DEV, EXPERT_TOTAL, 2, CAP, 2))(routing_keys, routing_turns).reshape((TOKENS, 2))
    router_gate_values = jnp.clip(0.1 + 0.79999997 * jax.random.uniform(streams_of[3], (TOKENS, 2), jnp.float32) ** block_levels(streams_of[3], (TOKENS, 2), ((0, 8),), -0.2, 0.2), 0.1, 0.9)
    gate_weight = gaussian(streams_of[4], (EXPERT_TOTAL, HIDDEN_HALF, MODEL_WIDTH), MODEL_WIDTH ** -0.5, 0.09375, ((0, 4), (1, 8)))
    up_weight = gaussian(streams_of[5], (EXPERT_TOTAL, HIDDEN_HALF, MODEL_WIDTH), MODEL_WIDTH ** -0.5, 0.09375, ((0, 4), (1, 8)))
    down_weight = gaussian(streams_of[6], (EXPERT_TOTAL, HIDDEN_HALF, MODEL_WIDTH), HIDDEN_HALF ** -0.5, 0.0625, ((0, 4), (1, 8)))
    adapter_lower_gate = gaussian(streams_of[7], (EXPERT_TOTAL, ADAPTER_RANK, MODEL_WIDTH), MODEL_WIDTH ** -0.5, 0.09375, ((0, 4),))
    adapter_upper_gate = gaussian(streams_of[8], (EXPERT_TOTAL, HIDDEN_HALF, ADAPTER_RANK), (ADAPTER_RANK * 16) ** -0.5, 0.375, ((0, 4), (1, 8)))
    adapter_lower_up = gaussian(streams_of[9], (EXPERT_TOTAL, ADAPTER_RANK, MODEL_WIDTH), MODEL_WIDTH ** -0.5, 0.09375, ((0, 4),))
    adapter_upper_up = gaussian(streams_of[10], (EXPERT_TOTAL, HIDDEN_HALF, ADAPTER_RANK), (ADAPTER_RANK * 16) ** -0.5, 0.375, ((0, 4), (1, 8)))
    adapter_lower_down = gaussian(streams_of[11], (EXPERT_TOTAL, ADAPTER_RANK, HIDDEN_HALF), HIDDEN_HALF ** -0.5, 0.0625, ((0, 4), (2, 8)))
    adapter_upper_down = gaussian(streams_of[12], (EXPERT_TOTAL, MODEL_WIDTH, ADAPTER_RANK), (ADAPTER_RANK * 16) ** -0.5, 0.375, ((0, 4),))
    return {"tokens": tokens, "output_gradient": output_gradient, "routing": routing, "router_gate_values": router_gate_values, "gate_weight": gate_weight, "up_weight": up_weight, "down_weight": down_weight, "adapter_lower_gate": adapter_lower_gate, "adapter_upper_gate": adapter_upper_gate, "adapter_lower_up": adapter_lower_up, "adapter_upper_up": adapter_upper_up, "adapter_lower_down": adapter_lower_down, "adapter_upper_down": adapter_upper_down}


ADAPTER_SCALE = 2.0


def contract_pair(left, right, left_axis, right_axis):
    return lax.dot_general(left, right, (((left_axis,), (right_axis,)), ((), ())), preferred_element_type=jnp.float32)


def slot_numbers(route_rows, experts):
    picked = (route_rows[:, :, None] == jnp.arange(experts, dtype=jnp.int32)[None, None, :]).astype(jnp.int32)
    per_token = jnp.sum(picked, axis=1)
    earlier = jnp.cumsum(per_token, axis=0) - per_token
    return jnp.sum(earlier[:, None, :] * picked, axis=2).astype(jnp.int32)


def slot_sources(route_rows, positions, experts, capacity):
    tokens_here, choose = route_rows.shape
    target = (route_rows * capacity + positions).reshape(-1)
    owners = jnp.repeat(jnp.arange(tokens_here, dtype=jnp.int32), choose)
    member_ids = jnp.tile(jnp.arange(choose, dtype=jnp.int32), tokens_here)
    source = jnp.full((experts * capacity,), tokens_here, jnp.int32).at[target].set(owners)
    member = jnp.zeros((experts * capacity,), jnp.int32).at[target].set(member_ids)
    return source, member


def rows_backward_pass(input_rows, output_gradient_rows, params):
    gate_weight, up_weight, down_weight, a_gate, gate_adapter_upper, a_up, up_adapter_upper, down_adapter_lower, b_down = params
    gate_projected_lower = contract_pair(a_gate, input_rows, 1, 1).astype(jnp.bfloat16)
    up_projected_lower = contract_pair(a_up, input_rows, 1, 1).astype(jnp.bfloat16)
    gate_preactivation = contract_pair(gate_weight, input_rows, 1, 1) + ADAPTER_SCALE * contract_pair(gate_adapter_upper, gate_projected_lower, 1, 0)
    up_preactivation = contract_pair(up_weight, input_rows, 1, 1) + ADAPTER_SCALE * contract_pair(up_adapter_upper, up_projected_lower, 1, 0)
    sigmoid_gate = jax.nn.sigmoid(gate_preactivation)
    silu_gate = gate_preactivation * sigmoid_gate
    hidden_units = (silu_gate * up_preactivation).astype(jnp.bfloat16)
    down_projected_lower = contract_pair(b_down, output_gradient_rows, 0, 1).astype(jnp.bfloat16)
    hidden_gradient = contract_pair(down_weight, output_gradient_rows, 1, 1) + ADAPTER_SCALE * contract_pair(down_adapter_lower, down_projected_lower, 0, 0)
    gate_gradient = (hidden_gradient * up_preactivation * sigmoid_gate * (1.0 + gate_preactivation * (1.0 - sigmoid_gate))).astype(jnp.bfloat16)
    up_gradient = (hidden_gradient * silu_gate).astype(jnp.bfloat16)
    gate_partial = contract_pair(gate_adapter_upper, gate_gradient, 0, 0).astype(jnp.bfloat16)
    up_partial = contract_pair(up_adapter_upper, up_gradient, 0, 0).astype(jnp.bfloat16)
    down_partial = contract_pair(down_adapter_lower, hidden_units, 1, 0).astype(jnp.bfloat16)
    paired_partials = jnp.concatenate([gate_partial, up_partial], 0)
    paired_factors = jnp.concatenate([a_gate, a_up], 0)
    gradient_rows_out = contract_pair(gate_gradient, gate_weight, 0, 0) + contract_pair(up_gradient, up_weight, 0, 0) + ADAPTER_SCALE * contract_pair(paired_partials, paired_factors, 0, 0)
    shared_slice = (ADAPTER_SCALE * contract_pair(gate_partial, input_rows, 1, 0),
              ADAPTER_SCALE * contract_pair(up_partial, input_rows, 1, 0),
              ADAPTER_SCALE * contract_pair(output_gradient_rows, down_partial, 0, 1))
    owned_slice = (ADAPTER_SCALE * contract_pair(gate_gradient, gate_projected_lower, 1, 1),
             ADAPTER_SCALE * contract_pair(up_gradient, up_projected_lower, 1, 1),
             ADAPTER_SCALE * contract_pair(down_projected_lower, hidden_units, 1, 1))
    return gradient_rows_out, shared_slice, owned_slice


def reference(tokens, output_gradient, routing, router_gate_values, gate_weight, up_weight, down_weight, adapter_lower_gate, adapter_upper_gate, adapter_lower_up, adapter_upper_up, adapter_lower_down, adapter_upper_down):
    shards = N_DP
    route_blocks = routing.reshape(shards, TOK_DEV, 2)

    def shard_places(route_rows):
        return slot_numbers(route_rows, EXPERT_TOTAL)

    places = jax.vmap(shard_places)(route_blocks)

    def shard_slots(route_rows, positions):
        return slot_sources(route_rows, positions, EXPERT_TOTAL, CAP)

    sources, members = jax.vmap(shard_slots)(route_blocks, places)
    shard_base = jnp.arange(shards, dtype=jnp.int32)[:, None] * TOK_DEV
    global_src = jnp.where(sources < TOK_DEV, sources + shard_base, TOKENS).astype(jnp.int32)
    gate_index = jnp.where(sources < TOK_DEV, global_src * 2 + members, 2 * TOKENS).astype(jnp.int32)
    slot_order = global_src.reshape(shards, EXPERT_TOTAL, CAP).transpose(1, 0, 2).reshape(EXPERT_TOTAL, shards * CAP)
    gate_order = gate_index.reshape(shards, EXPERT_TOTAL, CAP).transpose(1, 0, 2).reshape(EXPERT_TOTAL, shards * CAP)
    gate_flat = jnp.concatenate([router_gate_values.reshape(-1), jnp.zeros((1,), router_gate_values.dtype)])
    padded_x = jnp.concatenate([tokens, jnp.zeros((1, MODEL_WIDTH), tokens.dtype)], 0)
    padded_dy = jnp.concatenate([output_gradient, jnp.zeros((1, MODEL_WIDTH), output_gradient.dtype)], 0)
    input_rows_local = padded_x[slot_order]
    gradient_rows_local = (gate_flat[gate_order][..., None] * padded_dy[slot_order].astype(jnp.float32)).astype(jnp.bfloat16)
    block_width = HIDDEN_HALF // N_DP

    def single_expert(pack):
        input_rows, output_gradient_rows, gate_w, up_w, down_w, gate_lower_factor, gate_lb, up_lower_factor, up_lb, down_la, down_upper_factor = pack
        blocks = (gate_w.reshape(N_DP, block_width, MODEL_WIDTH), up_w.reshape(N_DP, block_width, MODEL_WIDTH),
                  down_w.reshape(N_DP, block_width, MODEL_WIDTH), gate_lb.reshape(N_DP, block_width, ADAPTER_RANK),
                  up_lb.reshape(N_DP, block_width, ADAPTER_RANK),
                  down_la.reshape(ADAPTER_RANK, N_DP, block_width).transpose(1, 0, 2))

        def block_step(totals, block_slice):
            gate_weight_block, up_weight_block, down_weight_block, gate_upper_factor, up_upper_factor, down_lower_factor = block_slice
            gradient_rows_out, shared_slice, owned_slice = rows_backward_pass(input_rows, output_gradient_rows, (gate_weight_block, up_weight_block, down_weight_block, gate_lower_factor, gate_upper_factor, up_lower_factor, up_upper_factor, down_lower_factor, down_upper_factor))
            rounded = lax.optimization_barrier(gradient_rows_out.astype(jnp.bfloat16)).astype(jnp.float32)
            return (totals[0] + rounded, jax.tree.map(jnp.add, totals[1], shared_slice)), owned_slice

        initial = (jnp.zeros((N_DP * CAP, MODEL_WIDTH), jnp.float32),
                   (jnp.zeros((ADAPTER_RANK, MODEL_WIDTH), jnp.float32), jnp.zeros((ADAPTER_RANK, MODEL_WIDTH), jnp.float32), jnp.zeros((MODEL_WIDTH, ADAPTER_RANK), jnp.float32)))
        (rows_sum, shared_slice), owned_slice = lax.scan(block_step, initial, blocks)
        grad_b_gate = owned_slice[0].reshape(HIDDEN_HALF, ADAPTER_RANK)
        grad_b_up = owned_slice[1].reshape(HIDDEN_HALF, ADAPTER_RANK)
        grad_a_down = owned_slice[2].transpose(1, 0, 2).reshape(ADAPTER_RANK, HIDDEN_HALF)
        return rows_sum, shared_slice[0], grad_b_gate, shared_slice[1], grad_b_up, grad_a_down, shared_slice[2]

    result_list = lax.map(single_expert, (input_rows_local, gradient_rows_local, gate_weight, up_weight, down_weight, adapter_lower_gate, adapter_upper_gate, adapter_lower_up, adapter_upper_up, adapter_lower_down, adapter_upper_down))
    rows_all = result_list[0].reshape(EXPERT_TOTAL * shards * CAP, MODEL_WIDTH)
    lookup = (route_blocks * (shards * CAP) + jnp.arange(shards, dtype=jnp.int32)[:, None, None] * CAP + places).reshape(TOKENS, 2).astype(jnp.int32)
    grad_x = jnp.sum(rows_all[lookup], axis=1).astype(jnp.bfloat16)
    return grad_x, result_list[1], result_list[2], result_list[3], result_list[4], result_list[5], result_list[6]
```

```python
import jax
import jax.numpy as jnp
from jax import lax
from jax.experimental import pallas as pl
from jax.experimental.pallas import tpu as pltpu
from jax.sharding import PartitionSpec as P

ADAPTER_SCALE = 2.0


def contract_pair(left, right, left_axis, right_axis):
    return lax.dot_general(
        left, right, (((left_axis,), (right_axis,)), ((), ())), preferred_element_type=jnp.float32
    )


def slot_numbers(route_rows, experts):
    picked = (route_rows[:, :, None] == jnp.arange(experts, dtype=jnp.int32)[None, None, :]).astype(
        jnp.int32
    )
    per_token = jnp.sum(picked, axis=1)
    earlier = jnp.cumsum(per_token, axis=0) - per_token
    return jnp.sum(earlier[:, None, :] * picked, axis=2)


def slot_sources(route_rows, positions, experts, capacity):
    tokens_here, choose = route_rows.shape
    target = (route_rows * capacity + positions).reshape(-1)
    owners = jnp.repeat(jnp.arange(tokens_here, dtype=jnp.int32), choose)
    member_ids = jnp.tile(jnp.arange(choose, dtype=jnp.int32), tokens_here)
    source = jnp.full((experts * capacity,), tokens_here, jnp.int32).at[target].set(owners)
    member = jnp.zeros((experts * capacity,), jnp.int32).at[target].set(member_ids)
    return (source, member)


def rows_backward_pass(input_rows, output_gradient_rows, params):
    (
        gate_weight,
        up_weight,
        down_weight,
        a_gate,
        gate_adapter_upper,
        a_up,
        up_adapter_upper,
        down_adapter_lower,
        b_down,
    ) = params
    gate_projected_lower = contract_pair(a_gate, input_rows, 1, 1).astype(jnp.bfloat16)
    up_projected_lower = contract_pair(a_up, input_rows, 1, 1).astype(jnp.bfloat16)
    gate_preactivation = contract_pair(
        gate_weight, input_rows, 1, 1
    ) + ADAPTER_SCALE * contract_pair(gate_adapter_upper, gate_projected_lower, 1, 0)
    up_preactivation = contract_pair(up_weight, input_rows, 1, 1) + ADAPTER_SCALE * contract_pair(
        up_adapter_upper, up_projected_lower, 1, 0
    )
    sigmoid_gate = jax.nn.sigmoid(gate_preactivation)
    silu_gate = gate_preactivation * sigmoid_gate
    hidden_units = (silu_gate * up_preactivation).astype(jnp.bfloat16)
    down_projected_lower = contract_pair(b_down, output_gradient_rows, 0, 1).astype(jnp.bfloat16)
    hidden_gradient = contract_pair(
        down_weight, output_gradient_rows, 1, 1
    ) + ADAPTER_SCALE * contract_pair(down_adapter_lower, down_projected_lower, 0, 0)
    gate_gradient = (
        hidden_gradient
        * up_preactivation
        * sigmoid_gate
        * (1.0 + gate_preactivation * (1.0 - sigmoid_gate))
    ).astype(jnp.bfloat16)
    up_gradient = (hidden_gradient * silu_gate).astype(jnp.bfloat16)
    gate_partial = contract_pair(gate_adapter_upper, gate_gradient, 0, 0).astype(jnp.bfloat16)
    up_partial = contract_pair(up_adapter_upper, up_gradient, 0, 0).astype(jnp.bfloat16)
    down_partial = contract_pair(down_adapter_lower, hidden_units, 1, 0).astype(jnp.bfloat16)
    paired_partials = jnp.concatenate([gate_partial, up_partial], 0)
    paired_factors = jnp.concatenate([a_gate, a_up], 0)
    gradient_rows_out = (
        contract_pair(gate_gradient, gate_weight, 0, 0)
        + contract_pair(up_gradient, up_weight, 0, 0)
        + ADAPTER_SCALE * contract_pair(paired_partials, paired_factors, 0, 0)
    )
    shared_slice = (
        ADAPTER_SCALE * contract_pair(gate_partial, input_rows, 1, 0),
        ADAPTER_SCALE * contract_pair(up_partial, input_rows, 1, 0),
        ADAPTER_SCALE * contract_pair(output_gradient_rows, down_partial, 0, 1),
    )
    owned_slice = (
        ADAPTER_SCALE * contract_pair(gate_gradient, gate_projected_lower, 1, 1),
        ADAPTER_SCALE * contract_pair(up_gradient, up_projected_lower, 1, 1),
        ADAPTER_SCALE * contract_pair(down_projected_lower, hidden_units, 1, 1),
    )
    return (gradient_rows_out, shared_slice, owned_slice)


def general_local(
    tokens,
    output_gradient,
    routing,
    router_gate_values,
    gate_weight,
    up_weight,
    down_weight,
    adapter_lower_gate,
    adapter_upper_gate,
    adapter_lower_up,
    adapter_upper_up,
    adapter_lower_down,
    adapter_upper_down,
):
    experts = lax.axis_size("expert")
    shards = lax.axis_size("dp")
    tok_local, feat_local = tokens.shape
    choose = routing.shape[1]
    complete_width = feat_local * experts
    capacity = min(tok_local, 6 * tok_local // experts)
    hidden_units_local = gate_weight.shape[1]
    adapter_rank = adapter_lower_gate.shape[1]
    params = (
        gate_weight[0],
        up_weight[0],
        down_weight[0],
        adapter_lower_gate[0],
        adapter_upper_gate[0],
        adapter_lower_up[0],
        adapter_upper_up[0],
        adapter_lower_down[0],
        adapter_upper_down[0],
    )
    positions = slot_numbers(routing, experts)
    zero_row = jnp.zeros((1, feat_local), jnp.bfloat16)
    initial = (
        jnp.zeros((shards * capacity, complete_width), jnp.float32),
        (
            jnp.zeros((adapter_rank, complete_width), jnp.float32),
            jnp.zeros((adapter_rank, complete_width), jnp.float32),
            jnp.zeros((complete_width, adapter_rank), jnp.float32),
        ),
        (
            jnp.zeros((hidden_units_local, adapter_rank), jnp.float32),
            jnp.zeros((hidden_units_local, adapter_rank), jnp.float32),
            jnp.zeros((adapter_rank, hidden_units_local), jnp.float32),
        ),
    )
    source, member = slot_sources(routing, positions, experts, capacity)
    clamped = jnp.minimum(source, tok_local - 1)
    slot_gate = jnp.where(
        source < tok_local, router_gate_values.reshape(-1)[clamped * choose + member], 0.0
    )
    send_x = jnp.concatenate([tokens, zero_row], 0)[source].reshape(experts, capacity, feat_local)
    send_dy = (
        (
            slot_gate[:, None]
            * jnp.concatenate([output_gradient, zero_row], 0)[source].astype(jnp.float32)
        )
        .astype(jnp.bfloat16)
        .reshape(experts, capacity, feat_local)
    )
    recv_x, recv_dy = (
        lax.all_to_all(send_x, "expert", split_axis=0, concat_axis=2, tiled=True),
        lax.all_to_all(send_dy, "expert", split_axis=0, concat_axis=2, tiled=True),
    )
    gradient_rows_out, shared_slice, owned_slice = rows_backward_pass(
        lax.all_gather(recv_x[0], "dp", axis=0, tiled=True),
        lax.all_gather(recv_dy[0], "dp", axis=0, tiled=True),
        params,
    )
    rows_part = gradient_rows_out
    totals = (
        rows_part,
        jax.tree.map(jnp.add, initial[1], shared_slice),
        jax.tree.map(jnp.add, initial[2], owned_slice),
    )
    rows_part, shared_slice, owned_slice = totals
    summed = lax.psum_scatter(
        rows_part.astype(jnp.bfloat16), "dp", scatter_dimension=0, tiled=True
    ).astype(jnp.float32)
    returned_rows = lax.all_to_all(
        summed.reshape(capacity, experts, feat_local).astype(jnp.bfloat16),
        "expert",
        split_axis=1,
        concat_axis=1,
        tiled=True,
    ).astype(jnp.float32)
    lookup = positions * experts + routing
    grad_x = jnp.sum(returned_rows.reshape(capacity * experts, feat_local)[lookup], axis=1).astype(
        jnp.bfloat16
    )
    grad_a_gate, grad_a_up, grad_b_down = (
        lax.psum(shared_slice[0].astype(jnp.bfloat16), "dp").astype(jnp.float32),
        lax.psum(shared_slice[1].astype(jnp.bfloat16), "dp").astype(jnp.float32),
        lax.psum(shared_slice[2].astype(jnp.bfloat16), "dp").astype(jnp.float32),
    )
    return (
        grad_x,
        grad_a_gate[None],
        owned_slice[0][None],
        grad_a_up[None],
        owned_slice[1][None],
        owned_slice[2][None],
        grad_b_down[None],
    )


LANES = 128
TILE = 256
SHARDS = 8
VMEM_BYTES = 58 * 1024 * 1024
HBM = pl.BlockSpec(memory_space=pl.ANY)
VMEM = pl.BlockSpec(memory_space=pltpu.VMEM)
SMEM = pl.BlockSpec(memory_space=pltpu.SMEM)


def dot_nt(left, right):
    return contract_pair(left, right, 1, 1)


def dot_nn(left, right):
    return contract_pair(left, right, 1, 0)


def forward_kernel(
    n_pieces,
    *refs,
):
    pieces = refs[:n_pieces]
    (gate_hbm, up_hbm, lower_ref, upper_ref, silu_out, slope_out, hidden_out, low_out) = refs[
        n_pieces : n_pieces + 8
    ]
    x_rows, weights, x_sems, w_sems = refs[n_pieces + 8 :]
    per_block = n_pieces // SHARDS
    deep, tokens_each, feat = pieces[0].shape
    tiles = weights.shape[0]
    rows = x_rows.shape[0]
    x_copies = []
    for i, piece in enumerate(pieces):
        block, part = divmod(i, per_block)
        for z in range(deep):
            at = part * deep + z
            x_copies.append(
                pltpu.make_async_copy(
                    piece.at[z],
                    x_rows.at[pl.ds(block * tokens_each, tokens_each), pl.ds(at * feat, feat)],
                    x_sems.at[i * deep + z],
                )
            )

    def weight_copies(tile):
        source = pl.ds(pl.multiple_of(tile * LANES, LANES), LANES)
        return (
            pltpu.make_async_copy(
                gate_hbm.at[source], weights.at[tile, pl.ds(0, LANES)], w_sems.at[tile, 0]
            ),
            pltpu.make_async_copy(
                up_hbm.at[source], weights.at[tile, pl.ds(LANES, LANES)], w_sems.at[tile, 1]
            ),
        )

    for copy in x_copies:
        copy.start()
    for tile in range(tiles):
        for copy in weight_copies(tile):
            copy.start()
    for copy in x_copies:
        copy.wait()
    half = rows // 2
    for m in range(2):
        at = pl.ds(m * half, half)
        low_out[at, :] = dot_nt(x_rows[at, :], lower_ref[...]).astype(jnp.bfloat16)

    @pl.loop(0, tiles)
    def _(tile):
        for copy in weight_copies(tile):
            copy.wait()
        lanes = pl.ds(pl.multiple_of(tile * LANES, LANES), LANES)

        @pl.loop(0, 2)
        def _(m):
            at = pl.ds(pl.multiple_of(m * half, half), half)
            pre = dot_nt(x_rows[at, :], weights[tile])
            pre = pre + ADAPTER_SCALE * dot_nn(low_out[at, :], upper_ref[tile])
            pre_gate, pre_up = pre[:, :LANES], pre[:, LANES:]
            sigma = 1.0 / (1.0 + jnp.exp(-pre_gate))
            silu = pre_gate * sigma
            silu_out[at, lanes] = silu
            slope_out[at, lanes] = pre_up * (sigma * (1.0 + pre_gate * (1.0 - sigma)))
            hidden_out[at, lanes] = (silu * pre_up).astype(jnp.bfloat16)


def forward_rows(pieces, gate_weight, up_weight, lower_cat, upper_tiles):
    hidden_here, width = gate_weight.shape
    rows = SHARDS * pieces[0].shape[1]
    rank2 = lower_cat.shape[0]
    tiles = hidden_here // LANES
    copies = len(pieces) * pieces[0].shape[0]
    flops = 4 * rows * hidden_here * width
    return pl.pallas_call(
        lambda *refs: forward_kernel(len(pieces), *refs),
        out_shape=(
            jax.ShapeDtypeStruct((rows, hidden_here), jnp.float32),
            jax.ShapeDtypeStruct((rows, hidden_here), jnp.float32),
            jax.ShapeDtypeStruct((rows, hidden_here), jnp.bfloat16),
            jax.ShapeDtypeStruct((rows, rank2), jnp.bfloat16),
        ),
        in_specs=[HBM] * (len(pieces) + 2) + [VMEM] * 2,
        out_specs=(VMEM,) * 4,
        scratch_shapes=[
            pltpu.VMEM((rows, width), jnp.bfloat16),
            pltpu.VMEM((tiles, 2 * LANES, width), jnp.bfloat16),
            pltpu.SemaphoreType.DMA((copies,)),
            pltpu.SemaphoreType.DMA((tiles, 2)),
        ],
        compiler_params=pltpu.CompilerParams(vmem_limit_bytes=VMEM_BYTES),
        cost_estimate=pl.CostEstimate(
            flops=flops, bytes_accessed=40_000_000, transcendentals=rows * hidden_here
        ),
        name="forward_rows",
    )(*pieces, gate_weight, up_weight, lower_cat, upper_tiles)


def backward_kernel(
    n_pieces,
    row_start,
    *refs,
):
    pieces = refs[:n_pieces]
    (
        route_ref,
        gate_hbm,
        up_hbm,
        down_hbm,
        down_upper_ref,
        down_lower_ref,
        gate_upper_ref,
        up_upper_ref,
        silu_hbm,
        slope_hbm,
        hidden_hbm,
        low_hbm,
        keep_out,
        pass_out,
        parts_out,
        owned_out,
    ) = refs[n_pieces : n_pieces + 16]
    (g_rows, down_w, pair_w, d_pair, silu, slope, hidden, low, in_sems, d_sems, p_sems, f_sems) = refs[
        n_pieces + 16 :
    ]
    deep, tokens_each, feat = pieces[0].shape
    rows, width = g_rows.shape
    hidden_here = silu.shape[1]
    rank = down_upper_ref.shape[0]
    per_block = n_pieces // 2
    copies = []
    for i, piece in enumerate(pieces):
        block, part = divmod(i, per_block)
        for z in range(deep):
            at = part * deep + z
            copies.append(
                pltpu.make_async_copy(
                    piece.at[z],
                    g_rows.at[pl.ds(block * tokens_each, tokens_each), pl.ds(at * feat, feat)],
                    in_sems.at[i * deep + z],
                )
            )
    tiles = [(at, min(TILE, hidden_here - at)) for at in range(0, hidden_here, TILE)]
    down_copies = [
        pltpu.make_async_copy(down_hbm.at[pl.ds(at, n)], down_w.at[pl.ds(at, n)], d_sems.at[i])
        for i, (at, n) in enumerate(tiles)
    ]
    up_factor_copy = pltpu.make_async_copy(
        down_upper_ref, down_w.at[pl.ds(hidden_here, rank)], d_sems.at[len(tiles)]
    )
    here = pl.ds(row_start, rows)
    saved_copies = [
        pltpu.make_async_copy(source.at[here], target, f_sems.at[i])
        for i, (source, target) in enumerate(
            ((silu_hbm, silu), (slope_hbm, slope), (hidden_hbm, hidden), (low_hbm, low))
        )
    ]
    slabs = width // feat

    def pair_copies(slab):
        columns = pl.ds(slab * feat, feat)
        return (
            pltpu.make_async_copy(
                gate_hbm.at[:, columns], pair_w.at[slab, pl.ds(0, hidden_here)], p_sems.at[slab, 0]
            ),
            pltpu.make_async_copy(
                up_hbm.at[:, columns],
                pair_w.at[slab, pl.ds(hidden_here, hidden_here)],
                p_sems.at[slab, 1],
            ),
        )

    for copy in copies + [up_factor_copy] + down_copies[::-1] + saved_copies:
        copy.start()
    for slab in range(slabs):
        for copy in pair_copies(slab):
            copy.start()
    for copy in copies:
        copy.wait()

    @pl.loop(0, width // feat)
    def _(z):
        lanes = pl.ds(pl.multiple_of(z * feat, feat), feat)
        g_rows[:, lanes] = (route_ref[...] * g_rows[:, lanes].astype(jnp.float32)).astype(
            jnp.bfloat16
        )

    up_factor_copy.wait()
    low_down = None
    for i in reversed(range(len(tiles))):
        at, n = tiles[i]
        down_copies[i].wait()
        last = i == len(tiles) - 1
        whole = dot_nt(g_rows[...], down_w[at : at + n + (rank if last else 0), :])
        if last:
            low_down = whole[:, n:].astype(jnp.bfloat16)
            for copy in saved_copies:
                copy.wait()
        d_hidden = whole[:, :n] + ADAPTER_SCALE * dot_nn(low_down, down_lower_ref[:, at : at + n])
        d_pair[:, at : at + n] = (d_hidden * slope[:, at : at + n]).astype(jnp.bfloat16)
        d_pair[:, hidden_here + at : hidden_here + at + n] = (
            d_hidden * silu[:, at : at + n]
        ).astype(jnp.bfloat16)
    for slab in range(slabs):
        for copy in pair_copies(slab):
            copy.wait()

        @pl.loop(0, feat // TILE)
        def _(n):
            lanes = pl.ds(pl.multiple_of(n * TILE, TILE), TILE)
            term = dot_nn(d_pair[...], pair_w[slab, :, lanes]).astype(jnp.bfloat16)
            keep_out[slab, :, lanes] = term[:tokens_each]
            pass_out[slab, :, lanes] = term[tokens_each:]

    d_gate, d_up = d_pair[:, :hidden_here], d_pair[:, hidden_here:]
    parts_out[0:rank, :] = dot_nt(gate_upper_ref[...], d_gate)
    parts_out[rank : 2 * rank, :] = dot_nt(up_upper_ref[...], d_up)
    parts_out[2 * rank :, :] = dot_nt(down_lower_ref[...], hidden[...])
    owned_out[0] = ADAPTER_SCALE * contract_pair(low[:, :rank], d_gate, 0, 0)
    owned_out[1] = ADAPTER_SCALE * contract_pair(low[:, rank:], d_up, 0, 0)
    owned_out[2] = ADAPTER_SCALE * contract_pair(low_down, hidden[...], 0, 0)


def backward_rows(
    pieces,
    row_start,
    route_rows,
    weights,
    down_upper,
    down_lower,
    gate_upper,
    up_upper,
    saved,
):
    hidden_here, width = weights[0].shape
    rank = down_upper.shape[0]
    deep, tokens_each, feat = pieces[0].shape
    rows = 2 * tokens_each
    slabs = width // feat
    term = jax.ShapeDtypeStruct((slabs, tokens_each, feat), jnp.bfloat16)
    return pl.pallas_call(
        lambda *refs: backward_kernel(len(pieces), row_start, *refs),
        out_shape=(
            term,
            term,
            jax.ShapeDtypeStruct((3 * rank, rows), jnp.float32),
            jax.ShapeDtypeStruct((3, rank, hidden_here), jnp.float32),
        ),
        in_specs=[HBM] * len(pieces)
        + [VMEM]
        + [HBM] * 3
        + [VMEM] * 4
        + [HBM] * 4,
        out_specs=(VMEM,) * 4,
        scratch_shapes=[
            pltpu.VMEM((rows, width), jnp.bfloat16),
            pltpu.VMEM((hidden_here + rank, width), jnp.bfloat16),
            pltpu.VMEM((slabs, 2 * hidden_here, feat), jnp.bfloat16),
            pltpu.VMEM((rows, 2 * hidden_here), jnp.bfloat16),
            pltpu.VMEM((rows, hidden_here), jnp.float32),
            pltpu.VMEM((rows, hidden_here), jnp.float32),
            pltpu.VMEM((rows, hidden_here), jnp.bfloat16),
            pltpu.VMEM((rows, 2 * rank), jnp.bfloat16),
            pltpu.SemaphoreType.DMA((len(pieces) * deep,)),
            pltpu.SemaphoreType.DMA((pl.cdiv(hidden_here, TILE) + 1,)),
            pltpu.SemaphoreType.DMA((slabs, 2)),
            pltpu.SemaphoreType.DMA((4,)),
        ],
        compiler_params=pltpu.CompilerParams(vmem_limit_bytes=VMEM_BYTES),
        cost_estimate=pl.CostEstimate(
            flops=6 * rows * hidden_here * width,
            bytes_accessed=6 * hidden_here * width + 4 * rows * width,
            transcendentals=0,
        ),
        name="backward_rows",
    )(*pieces, route_rows, *weights, down_upper, down_lower, gate_upper, up_upper, *saved)


def shared_kernel(n_pieces, *refs):
    x_pieces, dy_pieces = refs[:n_pieces], refs[n_pieces : 2 * n_pieces]
    order_ref, sums_ref, down_sums_ref, pair_out, down_out = refs[2 * n_pieces : 2 * n_pieces + 5]
    x_rows, dy_rows, sums, down_sums, sems = refs[2 * n_pieces + 5 :]
    deep, tokens_each, feat = x_pieces[0].shape
    per_block = n_pieces // SHARDS
    copies = []
    for side, (pieces, target) in enumerate(((x_pieces, x_rows), (dy_pieces, dy_rows))):
        for i, piece in enumerate(pieces):
            block, part = divmod(i, per_block)
            start = pl.multiple_of(order_ref[block] * tokens_each, tokens_each)
            for z in range(deep):
                at = part * deep + z
                copies.append(
                    pltpu.make_async_copy(
                        piece.at[z],
                        target.at[pl.ds(start, tokens_each), pl.ds(at * feat, feat)],
                        sems.at[side, i * deep + z],
                    )
                )
    for copy in copies:
        copy.start()
    for block in range(SHARDS):
        lanes = pl.ds(pl.multiple_of(order_ref[block] * tokens_each, tokens_each), tokens_each)
        sums[:, lanes] = sums_ref[block]
        down_sums[:, lanes] = down_sums_ref[block]
    for copy in copies:
        copy.wait()
    width = x_rows.shape[1]
    step = 2 * TILE

    @pl.loop(0, width // step)
    def _(n):
        lanes = pl.ds(pl.multiple_of(n * step, step), step)
        pair_out[:, lanes] = ADAPTER_SCALE * dot_nn(
            sums[...].astype(jnp.bfloat16), x_rows[:, lanes]
        )
        down_out[:, lanes] = ADAPTER_SCALE * dot_nn(
            down_sums[...].astype(jnp.bfloat16), dy_rows[:, lanes]
        )


def shared_gradients(x_pieces, dy_pieces, order, sums, down_sums):
    deep, tokens_each, feat = x_pieces[0].shape
    n_pieces = len(x_pieces)
    width = deep * feat * n_pieces // SHARDS
    rows = SHARDS * tokens_each
    pair, rank = sums.shape[1], down_sums.shape[1]
    return pl.pallas_call(
        lambda *refs: shared_kernel(n_pieces, *refs),
        out_shape=(
            jax.ShapeDtypeStruct((pair, width), jnp.float32),
            jax.ShapeDtypeStruct((rank, width), jnp.float32),
        ),
        in_specs=[HBM] * (2 * n_pieces) + [SMEM, VMEM, VMEM],
        out_specs=(VMEM, VMEM),
        scratch_shapes=[
            pltpu.VMEM((rows, width), jnp.bfloat16),
            pltpu.VMEM((rows, width), jnp.bfloat16),
            pltpu.VMEM((pair, rows), jnp.float32),
            pltpu.VMEM((rank, rows), jnp.float32),
            pltpu.SemaphoreType.DMA((2, n_pieces * deep)),
        ],
        compiler_params=pltpu.CompilerParams(vmem_limit_bytes=VMEM_BYTES),
        cost_estimate=pl.CostEstimate(
            flops=16 * rows * pair * width, bytes_accessed=4 * rows * width, transcendentals=0
        ),
        name="shared_gradients",
    )(*x_pieces, *dy_pieces, order, sums, down_sums)


CORE, ACROSS, ALONG = 1, 2, 4


def swap(value, bit):
    return lax.ppermute(value, "dp", [(i, i ^ bit) for i in range(SHARDS)])


def spread(block):
    half = block.shape[0] // 2
    lo, hi = block[:half], block[half:]
    along_lo, across_hi = swap(lo, ALONG), swap(hi, ACROSS)
    across_lo, along_hi = swap(lo, ACROSS), swap(hi, ALONG)
    far_lo, far_hi = swap(along_lo, ACROSS), swap(across_hi, ALONG)
    near = [(lo, hi), (across_lo, across_hi), (along_lo, along_hi), (far_lo, far_hi)]
    blocks = []
    for pair in near:
        blocks.append(pair)
        blocks.append(tuple(swap(part, CORE) for part in pair))
    return blocks


def added(left, right):
    return (left.astype(jnp.float32) + right.astype(jnp.float32)).astype(jnp.bfloat16)


def local(
    tokens,
    output_gradient,
    routing,
    router_gate_values,
    gate_weight,
    up_weight,
    down_weight,
    adapter_lower_gate,
    adapter_upper_gate,
    adapter_lower_up,
    adapter_upper_up,
    adapter_lower_down,
    adapter_upper_down,
):
    experts = lax.axis_size("expert")
    me, expert = lax.axis_index("dp"), lax.axis_index("expert")
    tokens_each, feat = tokens.shape
    hidden_here = gate_weight.shape[1]
    rank = adapter_lower_gate.shape[1]
    tiles = hidden_here // LANES
    order = jnp.bitwise_xor(jnp.arange(SHARDS, dtype=jnp.int32), me.astype(jnp.int32))

    named = routing[:, :, None] == jnp.arange(experts, dtype=jnp.int32)[None, None, :]
    weight_of = jnp.sum(jnp.where(named, router_gate_values[:, :, None], 0.0), axis=1)
    all_routes = lax.all_gather(weight_of.T, "dp", axis=0, tiled=False)
    route = lax.dynamic_index_in_dim(all_routes, expert, axis=1, keepdims=False)[order]
    route_column = route.reshape(SHARDS * tokens_each, 1)

    lower_cat = jnp.concatenate([adapter_lower_gate[0], adapter_lower_up[0]], axis=0)
    gate_upper, up_upper = adapter_upper_gate[0].T, adapter_upper_up[0].T
    nothing = jnp.zeros((rank, tiles, LANES), jnp.bfloat16)
    upper_tiles = jnp.concatenate(
        [
            jnp.concatenate([gate_upper.reshape(rank, tiles, LANES), nothing], axis=2),
            jnp.concatenate([nothing, up_upper.reshape(rank, tiles, LANES)], axis=2),
        ],
        axis=0,
    ).transpose(1, 0, 2)
    down_upper = adapter_upper_down[0].T
    down_lower = adapter_lower_down[0]

    x_here = lax.all_gather(tokens, "expert", axis=0, tiled=False)
    dy_here = lax.all_gather(output_gradient, "expert", axis=0, tiled=False)
    x_blocks = spread(x_here)
    x_tail = [x_blocks[2], x_blocks[4]]
    dy_here, x_tail = lax.optimization_barrier((dy_here, x_tail))
    x_blocks[2], x_blocks[4] = x_tail
    dy_blocks = spread(dy_here)
    x_pieces = [part for pair in x_blocks for part in pair]
    dy_pieces = [part for pair in dy_blocks for part in pair]

    saved = forward_rows(x_pieces, gate_weight[0], up_weight[0], lower_cat, upper_tiles)
    weights = (gate_weight[0], up_weight[0], down_weight[0])
    sums, parts, owned = [], [], []
    chips = SHARDS // 2
    rows = 2 * tokens_each
    for chip in range(chips):
        keep, away, part, own = backward_rows(
            dy_pieces[4 * chip : 4 * chip + 4],
            chip * rows,
            route_column[chip * rows : chip * rows + rows],
            weights,
            down_upper,
            down_lower,
            gate_upper,
            up_upper,
            saved,
        )
        sums.append((keep, swap(away, CORE)))
        parts.append(part)
        owned.append(own)

    half = experts // 2
    lo, hi = slice(0, half), slice(half, experts)
    (own_a, own_b), (across_a, across_b), (along_a, along_b), (far_a, far_b) = sums
    far_lo = swap(added(far_a[lo], far_b[lo]), ACROSS)
    far_hi = swap(added(far_a[hi], far_b[hi]), ALONG)
    got_across_lo = swap(added(across_a[lo], across_b[lo]), ACROSS)
    got_along_hi = swap(added(along_a[hi], along_b[hi]), ALONG)
    got_across_hi = swap(added(added(across_a[hi], across_b[hi]), far_hi), ACROSS)
    got_along_lo = swap(added(added(along_a[lo], along_b[lo]), far_lo), ALONG)

    total = jnp.stack(parts, axis=0).reshape(chips, 3 * rank, 2, tokens_each)
    total = total.transpose(0, 2, 1, 3)
    for bit in (CORE, ACROSS, ALONG):
        other = swap(total.reshape(SHARDS, 3 * rank, tokens_each), bit)
        shape = (SHARDS // (2 * bit), 2, bit, 3 * rank, tokens_each)
        total = total.reshape(shape) + other.reshape(shape)[:, ::-1]
    total = total.reshape(SHARDS, 3 * rank, tokens_each)
    lower_slabs = lower_cat.reshape(2 * rank, experts, feat).transpose(1, 0, 2)
    low_rows = ADAPTER_SCALE * lax.dot_general(
        jnp.broadcast_to(total[0, : 2 * rank].astype(jnp.bfloat16), (experts, 2 * rank, tokens_each)),
        lower_slabs,
        (((1,), (1,)), ((0,), (0,))),
        preferred_element_type=jnp.float32,
    )

    def wide(value):
        return value.astype(jnp.float32)

    from_neighbours = jnp.concatenate(
        [wide(got_across_lo) + wide(got_along_lo), wide(got_across_hi) + wide(got_along_hi)], axis=0
    )
    rows_sum = (wide(own_a) + wide(own_b) + from_neighbours + low_rows).astype(jnp.bfloat16)
    grad_x = lax.psum_scatter(rows_sum, "expert", scatter_dimension=0, tiled=True)[0]

    grad_pair, grad_down = shared_gradients(
        x_pieces,
        dy_pieces,
        order,
        total[:, : 2 * rank],
        total[:, 2 * rank :] * route[:, None, :],
    )
    owned_sum = sum(owned[1:], owned[0])
    return (
        grad_x,
        grad_pair[None, :rank],
        owned_sum[0].T[None],
        grad_pair[None, rank:],
        owned_sum[1].T[None],
        owned_sum[2][None],
        grad_down.T[None],
    )


def plan(tokens, *others):
    planned = (
        lax.axis_size("dp") == SHARDS
        and lax.axis_size("expert") % 2 == 0
        and others[3].shape[1] % LANES == 0
        and tokens.shape[0] % LANES == 0
    )
    return (local if planned else general_local)(tokens, *others)


def solution(mesh):
    return jax.shard_map(
        plan,
        mesh=mesh,
        in_specs=(
            P("dp", "expert"),
            P("dp", "expert"),
            P("dp", None),
            P("dp", None),
            P("expert", "dp", None),
            P("expert", "dp", None),
            P("expert", "dp", None),
            P("expert", None, None),
            P("expert", "dp", None),
            P("expert", None, None),
            P("expert", "dp", None),
            P("expert", None, "dp"),
            P("expert", None, None),
        ),
        out_specs=(
            P("dp", "expert"),
            P("expert", None, None),
            P("expert", "dp", None),
            P("expert", None, None),
            P("expert", "dp", None),
            P("expert", None, "dp"),
            P("expert", None, None),
        ),
        check_vma=False,
    )
```

```python
import jax
import jax.numpy as jnp
from jax import lax
from jax.experimental import pallas as pl
from jax.experimental.pallas import tpu as pltpu
from jax.sharding import PartitionSpec as P

ADAPTER_SCALE = 2.0


def contract_pair(left, right, left_axis, right_axis):
    return lax.dot_general(
        left, right, (((left_axis,), (right_axis,)), ((), ())), preferred_element_type=jnp.float32
    )


def slot_numbers(route_rows, experts):
    picked = (route_rows[:, :, None] == jnp.arange(experts, dtype=jnp.int32)[None, None, :]).astype(
        jnp.int32
    )
    per_token = jnp.sum(picked, axis=1)
    earlier = jnp.cumsum(per_token, axis=0) - per_token
    return jnp.sum(earlier[:, None, :] * picked, axis=2)


def slot_sources(route_rows, positions, experts, capacity):
    tokens_here, choose = route_rows.shape
    target = (route_rows * capacity + positions).reshape(-1)
    owners = jnp.repeat(jnp.arange(tokens_here, dtype=jnp.int32), choose)
    member_ids = jnp.tile(jnp.arange(choose, dtype=jnp.int32), tokens_here)
    source = jnp.full((experts * capacity,), tokens_here, jnp.int32).at[target].set(owners)
    member = jnp.zeros((experts * capacity,), jnp.int32).at[target].set(member_ids)
    return (source, member)


def rows_backward_pass(input_rows, output_gradient_rows, params):
    (
        gate_weight,
        up_weight,
        down_weight,
        a_gate,
        gate_adapter_upper,
        a_up,
        up_adapter_upper,
        down_adapter_lower,
        b_down,
    ) = params
    gate_projected_lower = contract_pair(a_gate, input_rows, 1, 1).astype(jnp.bfloat16)
    up_projected_lower = contract_pair(a_up, input_rows, 1, 1).astype(jnp.bfloat16)
    gate_preactivation = contract_pair(
        gate_weight, input_rows, 1, 1
    ) + ADAPTER_SCALE * contract_pair(gate_adapter_upper, gate_projected_lower, 1, 0)
    up_preactivation = contract_pair(up_weight, input_rows, 1, 1) + ADAPTER_SCALE * contract_pair(
        up_adapter_upper, up_projected_lower, 1, 0
    )
    sigmoid_gate = jax.nn.sigmoid(gate_preactivation)
    silu_gate = gate_preactivation * sigmoid_gate
    hidden_units = (silu_gate * up_preactivation).astype(jnp.bfloat16)
    down_projected_lower = contract_pair(b_down, output_gradient_rows, 0, 1).astype(jnp.bfloat16)
    hidden_gradient = contract_pair(
        down_weight, output_gradient_rows, 1, 1
    ) + ADAPTER_SCALE * contract_pair(down_adapter_lower, down_projected_lower, 0, 0)
    gate_gradient = (
        hidden_gradient
        * up_preactivation
        * sigmoid_gate
        * (1.0 + gate_preactivation * (1.0 - sigmoid_gate))
    ).astype(jnp.bfloat16)
    up_gradient = (hidden_gradient * silu_gate).astype(jnp.bfloat16)
    gate_partial = contract_pair(gate_adapter_upper, gate_gradient, 0, 0).astype(jnp.bfloat16)
    up_partial = contract_pair(up_adapter_upper, up_gradient, 0, 0).astype(jnp.bfloat16)
    down_partial = contract_pair(down_adapter_lower, hidden_units, 1, 0).astype(jnp.bfloat16)
    paired_partials = jnp.concatenate([gate_partial, up_partial], 0)
    paired_factors = jnp.concatenate([a_gate, a_up], 0)
    gradient_rows_out = (
        contract_pair(gate_gradient, gate_weight, 0, 0)
        + contract_pair(up_gradient, up_weight, 0, 0)
        + ADAPTER_SCALE * contract_pair(paired_partials, paired_factors, 0, 0)
    )
    shared_slice = (
        ADAPTER_SCALE * contract_pair(gate_partial, input_rows, 1, 0),
        ADAPTER_SCALE * contract_pair(up_partial, input_rows, 1, 0),
        ADAPTER_SCALE * contract_pair(output_gradient_rows, down_partial, 0, 1),
    )
    owned_slice = (
        ADAPTER_SCALE * contract_pair(gate_gradient, gate_projected_lower, 1, 1),
        ADAPTER_SCALE * contract_pair(up_gradient, up_projected_lower, 1, 1),
        ADAPTER_SCALE * contract_pair(down_projected_lower, hidden_units, 1, 1),
    )
    return (gradient_rows_out, shared_slice, owned_slice)


def general_local(
    tokens,
    output_gradient,
    routing,
    router_gate_values,
    gate_weight,
    up_weight,
    down_weight,
    adapter_lower_gate,
    adapter_upper_gate,
    adapter_lower_up,
    adapter_upper_up,
    adapter_lower_down,
    adapter_upper_down,
):
    experts = lax.axis_size("expert")
    shards = lax.axis_size("dp")
    tok_local, feat_local = tokens.shape
    choose = routing.shape[1]
    complete_width = feat_local * experts
    capacity = min(tok_local, 6 * tok_local // experts)
    hidden_units_local = gate_weight.shape[1]
    adapter_rank = adapter_lower_gate.shape[1]
    params = (
        gate_weight[0],
        up_weight[0],
        down_weight[0],
        adapter_lower_gate[0],
        adapter_upper_gate[0],
        adapter_lower_up[0],
        adapter_upper_up[0],
        adapter_lower_down[0],
        adapter_upper_down[0],
    )
    positions = slot_numbers(routing, experts)
    zero_row = jnp.zeros((1, feat_local), jnp.bfloat16)
    initial = (
        jnp.zeros((shards * capacity, complete_width), jnp.float32),
        (
            jnp.zeros((adapter_rank, complete_width), jnp.float32),
            jnp.zeros((adapter_rank, complete_width), jnp.float32),
            jnp.zeros((complete_width, adapter_rank), jnp.float32),
        ),
        (
            jnp.zeros((hidden_units_local, adapter_rank), jnp.float32),
            jnp.zeros((hidden_units_local, adapter_rank), jnp.float32),
            jnp.zeros((adapter_rank, hidden_units_local), jnp.float32),
        ),
    )
    source, member = slot_sources(routing, positions, experts, capacity)
    clamped = jnp.minimum(source, tok_local - 1)
    slot_gate = jnp.where(
        source < tok_local, router_gate_values.reshape(-1)[clamped * choose + member], 0.0
    )
    send_x = jnp.concatenate([tokens, zero_row], 0)[source].reshape(experts, capacity, feat_local)
    send_dy = (
        (
            slot_gate[:, None]
            * jnp.concatenate([output_gradient, zero_row], 0)[source].astype(jnp.float32)
        )
        .astype(jnp.bfloat16)
        .reshape(experts, capacity, feat_local)
    )
    recv_x, recv_dy = (
        lax.all_to_all(send_x, "expert", split_axis=0, concat_axis=2, tiled=True),
        lax.all_to_all(send_dy, "expert", split_axis=0, concat_axis=2, tiled=True),
    )
    gradient_rows_out, shared_slice, owned_slice = rows_backward_pass(
        lax.all_gather(recv_x[0], "dp", axis=0, tiled=True),
        lax.all_gather(recv_dy[0], "dp", axis=0, tiled=True),
        params,
    )
    rows_part = gradient_rows_out
    totals = (
        rows_part,
        jax.tree.map(jnp.add, initial[1], shared_slice),
        jax.tree.map(jnp.add, initial[2], owned_slice),
    )
    rows_part, shared_slice, owned_slice = totals
    summed = lax.psum_scatter(
        rows_part.astype(jnp.bfloat16), "dp", scatter_dimension=0, tiled=True
    ).astype(jnp.float32)
    returned_rows = lax.all_to_all(
        summed.reshape(capacity, experts, feat_local).astype(jnp.bfloat16),
        "expert",
        split_axis=1,
        concat_axis=1,
        tiled=True,
    ).astype(jnp.float32)
    lookup = positions * experts + routing
    grad_x = jnp.sum(returned_rows.reshape(capacity * experts, feat_local)[lookup], axis=1).astype(
        jnp.bfloat16
    )
    grad_a_gate, grad_a_up, grad_b_down = (
        lax.psum(shared_slice[0].astype(jnp.bfloat16), "dp").astype(jnp.float32),
        lax.psum(shared_slice[1].astype(jnp.bfloat16), "dp").astype(jnp.float32),
        lax.psum(shared_slice[2].astype(jnp.bfloat16), "dp").astype(jnp.float32),
    )
    return (
        grad_x,
        grad_a_gate[None],
        owned_slice[0][None],
        grad_a_up[None],
        owned_slice[1][None],
        owned_slice[2][None],
        grad_b_down[None],
    )


LANES = 128
TILE = 512
SHARDS = 8
VMEM_BYTES = 58 * 1024 * 1024
HBM = pl.BlockSpec(memory_space=pl.ANY)
VMEM = pl.BlockSpec(memory_space=pltpu.VMEM)
SMEM = pl.BlockSpec(memory_space=pltpu.SMEM)


def dot_nt(left, right):
    return contract_pair(left, right, 1, 1)


def dot_nn(left, right):
    return contract_pair(left, right, 1, 0)


def wide(value):
    return value.astype(jnp.float32)


def row_copies(pieces, per_block, target, sems):
    deep, tokens_each, _ = pieces[0].shape
    copies = []
    for i, piece in enumerate(pieces):
        block, part = divmod(i, per_block)
        for k in range(deep):
            slab = part * deep + k
            copies.append(
                pltpu.make_async_copy(
                    piece.at[k],
                    target.at[slab, pl.ds(block * tokens_each, tokens_each)],
                    sems.at[i, k],
                )
            )
    return copies


def slab_lanes(slab_ref, slab, feat):
    return pl.ds(pl.multiple_of(slab_ref[slab] * feat, feat), feat)


def forward_kernel(n_pieces, per_block, *refs):
    pieces = refs[:n_pieces]
    (
        slab_ref,
        gate_hbm,
        up_hbm,
        lower_hbm,
        gate_upper_ref,
        up_upper_ref,
        silu_out,
        slope_out,
        hidden_out,
        low_out,
    ) = refs[n_pieces : n_pieces + 10]
    x_rows, weights, pre, saved, x_sems, w_sems, out_sems = refs[n_pieces + 10 :]
    slabs, _, feat = x_rows.shape
    hidden_here = gate_hbm.shape[0]
    pair, rank = lower_hbm.shape[1], gate_upper_ref.shape[1]
    x_copies = row_copies(pieces, per_block, x_rows, x_sems)
    deep = pieces[0].shape[0]

    def x_slab(slab):
        part, k = divmod(slab, deep)
        return [x_copies[(block * per_block + part) * deep + k] for block in range(SHARDS)]

    def weight_copies(slab):
        lanes = slab_lanes(slab_ref, slab, feat)
        sides = (
            (gate_hbm.at[:, lanes], 0, hidden_here),
            (up_hbm.at[:, lanes], hidden_here, hidden_here),
            (lower_hbm.at[slab], 2 * hidden_here, pair),
        )
        return [
            pltpu.make_async_copy(
                source, weights.at[slab, pl.ds(start, size)], w_sems.at[slab, i]
            )
            for i, (source, start, size) in enumerate(sides)
        ]

    for slab in range(slabs):
        for copy in x_slab(slab) + weight_copies(slab):
            copy.start()
    for slab in range(slabs):
        for copy in x_slab(slab) + weight_copies(slab):
            copy.wait()
        if slab == 0:
            pre[...] = dot_nt(weights[0], x_rows[0])
        else:
            pre[...] += dot_nt(weights[slab], x_rows[slab])
    low_out[...] = pre[2 * hidden_here :, :].astype(jnp.bfloat16)

    def out_copies(tile):
        at = pl.ds(pl.multiple_of(tile * LANES, LANES), LANES)
        return [
            pltpu.make_async_copy(saved.at[i, at], out.at[at], out_sems.at[i, tile])
            for i, out in enumerate((silu_out, slope_out, hidden_out))
        ]

    tiles = hidden_here // LANES

    @pl.loop(0, tiles)
    def _(tile):
        start = pl.multiple_of(tile * LANES, LANES)
        at = pl.ds(start, LANES)
        up_at = pl.ds(pl.multiple_of(hidden_here + start, LANES), LANES)
        pre_gate = pre[at, :] + ADAPTER_SCALE * dot_nn(gate_upper_ref[at, :], low_out[:rank, :])
        pre_up = pre[up_at, :] + ADAPTER_SCALE * dot_nn(up_upper_ref[at, :], low_out[rank:, :])
        sigma = 1.0 / (1.0 + jnp.exp(-pre_gate))
        silu = pre_gate * sigma
        saved[0, at, :] = silu.astype(jnp.bfloat16)
        saved[1, at, :] = (pre_up * (sigma * (1.0 + pre_gate * (1.0 - sigma)))).astype(
            jnp.bfloat16
        )
        saved[2, at, :] = (silu * pre_up).astype(jnp.bfloat16)
        for copy in out_copies(tile):
            copy.start()

    @pl.loop(0, tiles)
    def _(tile):
        for copy in out_copies(tile):
            copy.wait()


def forward_rows(pieces, per_block, slab_order, weights, lower_slabs, gate_upper, up_upper):
    hidden_here, width = weights[0].shape
    deep, tokens_each, feat = pieces[0].shape
    rows = len(pieces) // per_block * tokens_each
    slabs, pair, _ = lower_slabs.shape
    kept = jax.ShapeDtypeStruct((hidden_here, rows), jnp.bfloat16)
    return pl.pallas_call(
        lambda *refs: forward_kernel(len(pieces), per_block, *refs),
        out_shape=(kept, kept, kept, jax.ShapeDtypeStruct((pair, rows), jnp.bfloat16)),
        in_specs=[HBM] * len(pieces) + [SMEM] + [HBM] * 3 + [VMEM] * 2,
        out_specs=(HBM, HBM, HBM, VMEM),
        scratch_shapes=[
            pltpu.VMEM((slabs, rows, feat), jnp.bfloat16),
            pltpu.VMEM((slabs, 2 * hidden_here + pair, feat), jnp.bfloat16),
            pltpu.VMEM((2 * hidden_here + pair, rows), jnp.float32),
            pltpu.VMEM((3, hidden_here, rows), jnp.bfloat16),
            pltpu.SemaphoreType.DMA((len(pieces), deep)),
            pltpu.SemaphoreType.DMA((slabs, 3)),
            pltpu.SemaphoreType.DMA((3, hidden_here // LANES)),
        ],
        compiler_params=pltpu.CompilerParams(vmem_limit_bytes=VMEM_BYTES),
        cost_estimate=pl.CostEstimate(
            flops=8 * rows * hidden_here * width,
            bytes_accessed=4 * hidden_here * width + 2 * rows * width,
            transcendentals=rows * hidden_here,
        ),
        name="forward_rows",
    )(*pieces, slab_order, *weights[:2], lower_slabs, gate_upper, up_upper)


def backward_kernel(n_pieces, per_block, columns, *refs):
    pieces = refs[:n_pieces]
    blocks = n_pieces // per_block
    (
        slab_ref,
        route_ref,
        gate_hbm,
        up_hbm,
        down_hbm,
        down_upper_hbm,
        lower_hbm,
        down_lower_ref,
        down_lower_t_ref,
        gate_upper_t_ref,
        up_upper_t_ref,
        silu_hbm,
        slope_hbm,
        hidden_hbm,
        low_hbm,
    ) = refs[n_pieces : n_pieces + 15]
    terms_out = refs[n_pieces + 15 : n_pieces + 15 + blocks]
    parts_out, owned_out, owned_down_out = refs[n_pieces + 15 + blocks : n_pieces + 18 + blocks]
    (
        g_rows,
        down_w,
        pair_w,
        d_down,
        d_cols,
        d_pair,
        silu,
        slope,
        hidden,
        low,
        in_sems,
        d_sems,
        p_sems,
        f_sems,
    ) = refs[n_pieces + 18 + blocks :]
    slabs, rows, feat = g_rows.shape
    tokens_each = rows // blocks
    hidden_here = silu.shape[0]
    rank, pair = down_lower_ref.shape[0], lower_hbm.shape[1]
    deep = pieces[0].shape[0]
    copies = row_copies(pieces, per_block, g_rows, in_sems)
    run = rows // len(columns)
    saved_copies = [
        pltpu.make_async_copy(
            source.at[:, pl.ds(column, run)], target.at[:, pl.ds(k * run, run)], f_sems.at[i, k]
        )
        for i, (source, target) in enumerate(
            ((silu_hbm, silu), (slope_hbm, slope), (hidden_hbm, hidden), (low_hbm, low))
        )
        for k, column in enumerate(columns)
    ]

    def row_slab(slab):
        part, k = divmod(slab, deep)
        return [copies[(block * per_block + part) * deep + k] for block in range(blocks)]

    def down_copies(slab):
        return [
            pltpu.make_async_copy(
                down_hbm.at[:, slab_lanes(slab_ref, slab, feat)],
                down_w.at[slab, pl.ds(0, hidden_here)],
                d_sems.at[slab, 0],
            ),
            pltpu.make_async_copy(
                down_upper_hbm.at[slab], down_w.at[slab, pl.ds(hidden_here, rank)], d_sems.at[slab, 1]
            ),
        ]

    def pair_copies(slab):
        lanes = slab_lanes(slab_ref, slab, feat)
        sides = (
            (gate_hbm.at[:, lanes], 0, hidden_here),
            (up_hbm.at[:, lanes], hidden_here, hidden_here),
            (lower_hbm.at[slab], 2 * hidden_here, pair),
        )
        return [
            pltpu.make_async_copy(source, pair_w.at[slab, pl.ds(start, size)], p_sems.at[slab, i])
            for i, (source, start, size) in enumerate(sides)
        ]

    for slab in range(slabs):
        for copy in row_slab(slab) + down_copies(slab):
            copy.start()
    for copy in saved_copies:
        copy.start()
    for slab in range(slabs):
        for copy in pair_copies(slab):
            copy.start()
    for slab in range(slabs):
        for copy in row_slab(slab):
            copy.wait()
        g_rows[slab] = (route_ref[...] * g_rows[slab].astype(jnp.float32)).astype(jnp.bfloat16)
        for copy in down_copies(slab):
            copy.wait()
        if slab == 0:
            d_down[...] = dot_nt(down_w[0], g_rows[0])
        else:
            d_down[...] += dot_nt(down_w[slab], g_rows[slab])

    low_down = d_down[hidden_here:, :].astype(jnp.bfloat16)
    for copy in saved_copies:
        copy.wait()

    @pl.loop(0, hidden_here // LANES)
    def _(tile):
        start = pl.multiple_of(tile * LANES, LANES)
        at = pl.ds(start, LANES)
        up_at = pl.ds(pl.multiple_of(hidden_here + start, LANES), LANES)
        d_hidden = d_down[at, :] + ADAPTER_SCALE * dot_nn(down_lower_t_ref[at, :], low_down)
        d_gate = (d_hidden * wide(slope[at, :])).astype(jnp.bfloat16)
        d_up = (d_hidden * wide(silu[at, :])).astype(jnp.bfloat16)
        d_cols[at, :] = d_gate
        d_cols[up_at, :] = d_up
        d_pair[:, at] = d_gate.T
        d_pair[:, up_at] = d_up.T

    d_gate, d_up = d_cols[:hidden_here, :], d_cols[hidden_here:, :]
    parts_out[0:rank, :] = dot_nn(gate_upper_t_ref[...], d_gate)
    parts_out[rank : 2 * rank, :] = dot_nn(up_upper_t_ref[...], d_up)
    parts_out[2 * rank :, :] = dot_nn(down_lower_ref[...], hidden[...])
    d_pair[:, 2 * hidden_here :] = ADAPTER_SCALE * parts_out[:pair, :].astype(jnp.bfloat16).T

    @pl.loop(0, slabs)
    def _(slab):
        for copy in pair_copies(slab):
            copy.wait()

        @pl.loop(0, feat // TILE)
        def _(n):
            lanes = pl.ds(pl.multiple_of(n * TILE, TILE), TILE)
            term = dot_nn(d_pair[...], pair_w[slab, :, lanes]).astype(jnp.bfloat16)
            for block, out in enumerate(terms_out):
                out[slab, :, lanes] = term[block * tokens_each : (block + 1) * tokens_each]

    owned_out[0] = ADAPTER_SCALE * dot_nt(low[:rank, :], d_gate)
    owned_out[1] = ADAPTER_SCALE * dot_nt(low[rank:, :], d_up)
    owned_down_out[...] = ADAPTER_SCALE * dot_nt(low_down, hidden[...])


def backward_rows(
    pieces,
    per_block,
    columns,
    slab_order,
    route_rows,
    weights,
    down_upper,
    lower_slabs,
    factors,
    saved,
):
    hidden_here, width = weights[0].shape
    slabs, rank, feat = down_upper.shape
    pair = lower_slabs.shape[1]
    deep, tokens_each, _ = pieces[0].shape
    blocks = len(pieces) // per_block
    rows = blocks * tokens_each
    term = jax.ShapeDtypeStruct((slabs, tokens_each, feat), jnp.bfloat16)
    results = pl.pallas_call(
        lambda *refs: backward_kernel(len(pieces), per_block, columns, *refs),
        out_shape=(term,) * blocks
        + (
            jax.ShapeDtypeStruct((3 * rank, rows), jnp.float32),
            jax.ShapeDtypeStruct((2, rank, hidden_here), jnp.float32),
            jax.ShapeDtypeStruct((rank, hidden_here), jnp.float32),
        ),
        in_specs=[HBM] * len(pieces) + [SMEM, VMEM] + [HBM] * 5 + [VMEM] * 4 + [HBM] * 4,
        out_specs=(VMEM,) * (blocks + 3),
        scratch_shapes=[
            pltpu.VMEM((slabs, rows, feat), jnp.bfloat16),
            pltpu.VMEM((slabs, hidden_here + rank, feat), jnp.bfloat16),
            pltpu.VMEM((slabs, 2 * hidden_here + pair, feat), jnp.bfloat16),
            pltpu.VMEM((hidden_here + rank, rows), jnp.float32),
            pltpu.VMEM((2 * hidden_here, rows), jnp.bfloat16),
            pltpu.VMEM((rows, 2 * hidden_here + pair), jnp.bfloat16),
            pltpu.VMEM((hidden_here, rows), jnp.bfloat16),
            pltpu.VMEM((hidden_here, rows), jnp.bfloat16),
            pltpu.VMEM((hidden_here, rows), jnp.bfloat16),
            pltpu.VMEM((2 * rank, rows), jnp.bfloat16),
            pltpu.SemaphoreType.DMA((len(pieces), deep)),
            pltpu.SemaphoreType.DMA((slabs, 2)),
            pltpu.SemaphoreType.DMA((slabs, 3)),
            pltpu.SemaphoreType.DMA((4, len(columns))),
        ],
        compiler_params=pltpu.CompilerParams(vmem_limit_bytes=VMEM_BYTES),
        cost_estimate=pl.CostEstimate(
            flops=12 * rows * hidden_here * width,
            bytes_accessed=6 * hidden_here * width + 4 * rows * width,
            transcendentals=0,
        ),
        name="backward_rows",
    )(*pieces, slab_order, route_rows, *weights, down_upper, lower_slabs, *factors, *saved)
    return results[:blocks], *results[blocks:]


def shared_kernel(n_pieces, per_block, *refs):
    x_pieces, dy_pieces = refs[:n_pieces], refs[n_pieces : 2 * n_pieces]
    order_ref, slab_ref, sums_ref, down_sums_ref, pair_out, down_out = refs[
        2 * n_pieces : 2 * n_pieces + 6
    ]
    x_rows, dy_rows, sums, down_sums, sems = refs[2 * n_pieces + 6 :]
    deep, tokens_each, feat = x_pieces[0].shape
    slabs = x_rows.shape[0]
    copies = []
    for side, (pieces, target) in enumerate(((x_pieces, x_rows), (dy_pieces, dy_rows))):
        for i, piece in enumerate(pieces):
            block, part = divmod(i, per_block)
            start = pl.multiple_of(order_ref[block] * tokens_each, tokens_each)
            for k in range(deep):
                copies.append(
                    pltpu.make_async_copy(
                        piece.at[k],
                        target.at[part * deep + k, pl.ds(start, tokens_each)],
                        sems.at[side, i, k],
                    )
                )
    for copy in copies:
        copy.start()
    for block in range(SHARDS):
        lanes = pl.ds(pl.multiple_of(order_ref[block] * tokens_each, tokens_each), tokens_each)
        sums[:, lanes] = sums_ref[block]
        down_sums[:, lanes] = down_sums_ref[block]
    for copy in copies:
        copy.wait()

    @pl.loop(0, slabs)
    def _(slab):
        @pl.loop(0, feat // TILE)
        def _(n):
            lanes = pl.ds(pl.multiple_of(n * TILE, TILE), TILE)
            out = pl.ds(pl.multiple_of(slab_ref[slab] * feat + n * TILE, TILE), TILE)
            pair_out[:, out] = ADAPTER_SCALE * dot_nn(
                sums[...].astype(jnp.bfloat16), x_rows[slab, :, lanes]
            )
            down_out[:, out] = ADAPTER_SCALE * dot_nn(
                down_sums[...].astype(jnp.bfloat16), dy_rows[slab, :, lanes]
            )


def shared_gradients(x_pieces, dy_pieces, per_block, order, slab_order, sums, down_sums):
    deep, tokens_each, feat = x_pieces[0].shape
    n_pieces = len(x_pieces)
    slabs = deep * per_block
    rows = SHARDS * tokens_each
    pair, rank = sums.shape[1], down_sums.shape[1]
    return pl.pallas_call(
        lambda *refs: shared_kernel(n_pieces, per_block, *refs),
        out_shape=(
            jax.ShapeDtypeStruct((pair, slabs * feat), jnp.float32),
            jax.ShapeDtypeStruct((rank, slabs * feat), jnp.float32),
        ),
        in_specs=[HBM] * (2 * n_pieces) + [SMEM, SMEM, VMEM, VMEM],
        out_specs=(VMEM, VMEM),
        scratch_shapes=[
            pltpu.VMEM((slabs, rows, feat), jnp.bfloat16),
            pltpu.VMEM((slabs, rows, feat), jnp.bfloat16),
            pltpu.VMEM((pair, rows), jnp.float32),
            pltpu.VMEM((rank, rows), jnp.float32),
            pltpu.SemaphoreType.DMA((2, n_pieces, deep)),
        ],
        compiler_params=pltpu.CompilerParams(vmem_limit_bytes=VMEM_BYTES),
        cost_estimate=pl.CostEstimate(
            flops=16 * rows * pair * slabs * feat,
            bytes_accessed=4 * rows * slabs * feat,
            transcendentals=0,
        ),
        name="shared_gradients",
    )(*x_pieces, *dy_pieces, order, slab_order, sums, down_sums)


CORE, ACROSS, ALONG = 1, 2, 4


def swap(value, bit, axis="dp"):
    return lax.ppermute(value, axis, [(i, i ^ bit) for i in range(lax.axis_size(axis))])


def slabs_of(block):
    slabs = [block] + [swap(block, r, "expert") for r in range(1, lax.axis_size("expert"))]
    half = len(slabs) // 2
    return jnp.stack(slabs[:half]), jnp.stack(slabs[half:])


def spread(lo, hi):
    along_lo, across_hi = swap(lo, ALONG), swap(hi, ACROSS)
    across_lo, along_hi = swap(lo, ACROSS), swap(hi, ALONG)
    far_lo, far_hi = swap(along_lo, ACROSS), swap(across_hi, ALONG)
    near = [(lo, hi), (across_lo, across_hi), (along_lo, along_hi), (far_lo, far_hi)]
    blocks = []
    for pair in near:
        blocks.append(pair)
        blocks.append(tuple(swap(part, CORE) for part in pair))
    return blocks


def added(left, right):
    return (wide(left) + wide(right)).astype(jnp.bfloat16)


def local(
    tokens,
    output_gradient,
    routing,
    router_gate_values,
    gate_weight,
    up_weight,
    down_weight,
    adapter_lower_gate,
    adapter_upper_gate,
    adapter_lower_up,
    adapter_upper_up,
    adapter_lower_down,
    adapter_upper_down,
):
    experts = lax.axis_size("expert")
    me, expert = lax.axis_index("dp"), lax.axis_index("expert")
    tokens_each, feat = tokens.shape
    rank = adapter_lower_gate.shape[1]
    order = jnp.bitwise_xor(jnp.arange(SHARDS, dtype=jnp.int32), me.astype(jnp.int32))
    slab_order = jnp.bitwise_xor(jnp.arange(experts, dtype=jnp.int32), expert.astype(jnp.int32))

    named = routing[:, :, None] == jnp.arange(experts, dtype=jnp.int32)[None, None, :]
    weight_of = jnp.sum(jnp.where(named, router_gate_values[:, :, None], 0.0), axis=1)
    all_routes = lax.all_gather(weight_of.T, "dp", axis=0, tiled=False)

    def slabs_first(factor):
        return factor.reshape(factor.shape[0], experts, feat).transpose(1, 0, 2)[slab_order]

    lower_slabs = slabs_first(
        jnp.concatenate([adapter_lower_gate[0], adapter_lower_up[0]], axis=0)
    )
    down_upper = slabs_first(adapter_upper_down[0].T)
    down_lower = adapter_lower_down[0]
    factors = (down_lower, down_lower.T, adapter_upper_gate[0].T, adapter_upper_up[0].T)

    x_lo, x_hi = slabs_of(tokens)
    x_blocks = spread(x_lo, x_hi)
    (across_lo, across_hi) = x_blocks[2]
    output_gradient, across_lo = lax.optimization_barrier((output_gradient, across_lo))
    x_blocks[2] = (across_lo, across_hi)
    dy_lo, dy_hi = slabs_of(output_gradient)
    dy_lo, dy_hi, x_blocks[2], x_blocks[4] = lax.optimization_barrier(
        (dy_lo, dy_hi, x_blocks[2], x_blocks[4])
    )
    dy_blocks = spread(dy_lo, dy_hi)
    x_blocks[6], all_routes = lax.optimization_barrier((x_blocks[6], all_routes))
    route = lax.dynamic_index_in_dim(all_routes, expert, axis=1, keepdims=False)[order]
    route_column = route.reshape(SHARDS, tokens_each, 1)
    x_pieces = [part for pair in x_blocks for part in pair]
    dy_pieces = [part for pair in dy_blocks for part in pair]

    weights = (gate_weight[0], up_weight[0], down_weight[0])
    saved = forward_rows(
        x_pieces,
        2,
        slab_order,
        weights,
        lower_slabs,
        adapter_upper_gate[0],
        adapter_upper_up[0],
    )
    terms, parts, owned, owned_down = {}, {}, [], []
    for group in ((6, 7, 0, 1), (2, 3, 4, 5)):
        columns = [j * tokens_each for j in group[::2]]
        rows_out, part, own, own_down = backward_rows(
            [piece for j in group for piece in dy_blocks[j]],
            2,
            columns,
            slab_order,
            jnp.concatenate([route_column[j] for j in group], axis=0),
            weights,
            down_upper,
            lower_slabs,
            factors,
            saved,
        )
        for i, j in enumerate(group):
            terms[j] = rows_out[i]
            parts[j] = part[:, i * tokens_each : (i + 1) * tokens_each]
        owned.append(own)
        owned_down.append(own_down)

    half = experts // 2
    lo, hi = slice(0, half), slice(half, experts)
    far_a, far_b = terms[6], swap(terms[7], CORE)
    own_a, own_b = terms[0], swap(terms[1], CORE)
    far_lo = swap(added(far_a[lo], far_b[lo]), ACROSS)
    far_hi = swap(added(far_a[hi], far_b[hi]), ALONG)
    across_a, across_b = terms[2], swap(terms[3], CORE)
    along_a, along_b = terms[4], swap(terms[5], CORE)
    got_across_hi = swap(added(added(across_a[hi], across_b[hi]), far_hi), ACROSS)
    got_along_hi = swap(added(along_a[hi], along_b[hi]), ALONG)
    got_across_lo = swap(added(across_a[lo], across_b[lo]), ACROSS)
    got_along_lo = swap(added(added(along_a[lo], along_b[lo]), far_lo), ALONG)
    rows_hi = wide(own_a[hi]) + wide(own_b[hi]) + wide(got_across_hi) + wide(got_along_hi)
    rows_lo = wide(own_a[lo]) + wide(own_b[lo]) + wide(got_across_lo) + wide(got_along_lo)
    rows_hi, rows_lo = rows_hi.astype(jnp.bfloat16), rows_lo.astype(jnp.bfloat16)
    grad_x = wide(rows_lo[0])
    for r in range(1, experts):
        piece = rows_lo[r] if r < half else rows_hi[r - half]
        grad_x = grad_x + wide(swap(piece, r, "expert"))
    grad_x = grad_x.astype(jnp.bfloat16)

    total = jnp.stack([parts[j] for j in range(SHARDS)], axis=0)
    for bit in (CORE, ACROSS, ALONG):
        other = swap(total.reshape(SHARDS, 3 * rank, tokens_each), bit)
        shape = (SHARDS // (2 * bit), 2, bit, 3 * rank, tokens_each)
        total = total.reshape(shape) + other.reshape(shape)[:, ::-1]
    total = total.reshape(SHARDS, 3 * rank, tokens_each)
    grad_pair, grad_down = shared_gradients(
        x_pieces,
        dy_pieces,
        2,
        order,
        slab_order,
        total[:, : 2 * rank],
        total[:, 2 * rank :] * route[:, None, :],
    )
    owned_sum = sum(owned[1:], owned[0])
    return (
        grad_x,
        grad_pair[None, :rank],
        owned_sum[0].T[None],
        grad_pair[None, rank:],
        owned_sum[1].T[None],
        sum(owned_down[1:], owned_down[0])[None],
        grad_down.T[None],
    )


def plan(tokens, *others):
    experts, tokens_each, hidden_here = lax.axis_size("expert"), tokens.shape[0], others[3].shape[1]
    planned = (
        lax.axis_size("dp") == SHARDS
        and experts in (2, 4)
        and hidden_here % LANES == 0
        and tokens_each % LANES == 0
        and tokens.shape[1] % TILE == 0
    )
    return (local if planned else general_local)(tokens, *others)


def solution(mesh):
    return jax.shard_map(
        plan,
        mesh=mesh,
        in_specs=(
            P("dp", "expert"),
            P("dp", "expert"),
            P("dp", None),
            P("dp", None),
            P("expert", "dp", None),
            P("expert", "dp", None),
            P("expert", "dp", None),
            P("expert", None, None),
            P("expert", "dp", None),
            P("expert", None, None),
            P("expert", "dp", None),
            P("expert", None, "dp"),
            P("expert", None, None),
        ),
        out_specs=(
            P("dp", "expert"),
            P("expert", None, None),
            P("expert", "dp", None),
            P("expert", None, None),
            P("expert", "dp", None),
            P("expert", None, "dp"),
            P("expert", None, None),
        ),
        check_vma=False,
    )
```

```python
import jax
import jax.numpy as jnp
from jax import lax
from jax.experimental import pallas as pl
from jax.experimental.pallas import tpu as pltpu
from jax.sharding import PartitionSpec as P

ADAPTER_SCALE = 2.0


def contract_pair(left, right, left_axis, right_axis):
    return lax.dot_general(
        left, right, (((left_axis,), (right_axis,)), ((), ())), preferred_element_type=jnp.float32
    )


def slot_numbers(route_rows, experts):
    picked = (route_rows[:, :, None] == jnp.arange(experts, dtype=jnp.int32)[None, None, :]).astype(
        jnp.int32
    )
    per_token = jnp.sum(picked, axis=1)
    earlier = jnp.cumsum(per_token, axis=0) - per_token
    return jnp.sum(earlier[:, None, :] * picked, axis=2)


def slot_sources(route_rows, positions, experts, capacity):
    tokens_here, choose = route_rows.shape
    target = (route_rows * capacity + positions).reshape(-1)
    owners = jnp.repeat(jnp.arange(tokens_here, dtype=jnp.int32), choose)
    member_ids = jnp.tile(jnp.arange(choose, dtype=jnp.int32), tokens_here)
    source = jnp.full((experts * capacity,), tokens_here, jnp.int32).at[target].set(owners)
    member = jnp.zeros((experts * capacity,), jnp.int32).at[target].set(member_ids)
    return (source, member)


def rows_backward_pass(input_rows, output_gradient_rows, params):
    (
        gate_weight,
        up_weight,
        down_weight,
        a_gate,
        gate_adapter_upper,
        a_up,
        up_adapter_upper,
        down_adapter_lower,
        b_down,
    ) = params
    gate_projected_lower = contract_pair(a_gate, input_rows, 1, 1).astype(jnp.bfloat16)
    up_projected_lower = contract_pair(a_up, input_rows, 1, 1).astype(jnp.bfloat16)
    gate_preactivation = contract_pair(
        gate_weight, input_rows, 1, 1
    ) + ADAPTER_SCALE * contract_pair(gate_adapter_upper, gate_projected_lower, 1, 0)
    up_preactivation = contract_pair(up_weight, input_rows, 1, 1) + ADAPTER_SCALE * contract_pair(
        up_adapter_upper, up_projected_lower, 1, 0
    )
    sigmoid_gate = jax.nn.sigmoid(gate_preactivation)
    silu_gate = gate_preactivation * sigmoid_gate
    hidden_units = (silu_gate * up_preactivation).astype(jnp.bfloat16)
    down_projected_lower = contract_pair(b_down, output_gradient_rows, 0, 1).astype(jnp.bfloat16)
    hidden_gradient = contract_pair(
        down_weight, output_gradient_rows, 1, 1
    ) + ADAPTER_SCALE * contract_pair(down_adapter_lower, down_projected_lower, 0, 0)
    gate_gradient = (
        hidden_gradient
        * up_preactivation
        * sigmoid_gate
        * (1.0 + gate_preactivation * (1.0 - sigmoid_gate))
    ).astype(jnp.bfloat16)
    up_gradient = (hidden_gradient * silu_gate).astype(jnp.bfloat16)
    gate_partial = contract_pair(gate_adapter_upper, gate_gradient, 0, 0).astype(jnp.bfloat16)
    up_partial = contract_pair(up_adapter_upper, up_gradient, 0, 0).astype(jnp.bfloat16)
    down_partial = contract_pair(down_adapter_lower, hidden_units, 1, 0).astype(jnp.bfloat16)
    paired_partials = jnp.concatenate([gate_partial, up_partial], 0)
    paired_factors = jnp.concatenate([a_gate, a_up], 0)
    gradient_rows_out = (
        contract_pair(gate_gradient, gate_weight, 0, 0)
        + contract_pair(up_gradient, up_weight, 0, 0)
        + ADAPTER_SCALE * contract_pair(paired_partials, paired_factors, 0, 0)
    )
    shared_slice = (
        ADAPTER_SCALE * contract_pair(gate_partial, input_rows, 1, 0),
        ADAPTER_SCALE * contract_pair(up_partial, input_rows, 1, 0),
        ADAPTER_SCALE * contract_pair(output_gradient_rows, down_partial, 0, 1),
    )
    owned_slice = (
        ADAPTER_SCALE * contract_pair(gate_gradient, gate_projected_lower, 1, 1),
        ADAPTER_SCALE * contract_pair(up_gradient, up_projected_lower, 1, 1),
        ADAPTER_SCALE * contract_pair(down_projected_lower, hidden_units, 1, 1),
    )
    return (gradient_rows_out, shared_slice, owned_slice)


def general_local(
    tokens,
    output_gradient,
    routing,
    router_gate_values,
    gate_weight,
    up_weight,
    down_weight,
    adapter_lower_gate,
    adapter_upper_gate,
    adapter_lower_up,
    adapter_upper_up,
    adapter_lower_down,
    adapter_upper_down,
):
    experts = lax.axis_size("expert")
    shards = lax.axis_size("dp")
    tok_local, feat_local = tokens.shape
    choose = routing.shape[1]
    complete_width = feat_local * experts
    capacity = min(tok_local, 6 * tok_local // experts)
    hidden_units_local = gate_weight.shape[1]
    adapter_rank = adapter_lower_gate.shape[1]
    params = (
        gate_weight[0],
        up_weight[0],
        down_weight[0],
        adapter_lower_gate[0],
        adapter_upper_gate[0],
        adapter_lower_up[0],
        adapter_upper_up[0],
        adapter_lower_down[0],
        adapter_upper_down[0],
    )
    positions = slot_numbers(routing, experts)
    zero_row = jnp.zeros((1, feat_local), jnp.bfloat16)
    initial = (
        jnp.zeros((shards * capacity, complete_width), jnp.float32),
        (
            jnp.zeros((adapter_rank, complete_width), jnp.float32),
            jnp.zeros((adapter_rank, complete_width), jnp.float32),
            jnp.zeros((complete_width, adapter_rank), jnp.float32),
        ),
        (
            jnp.zeros((hidden_units_local, adapter_rank), jnp.float32),
            jnp.zeros((hidden_units_local, adapter_rank), jnp.float32),
            jnp.zeros((adapter_rank, hidden_units_local), jnp.float32),
        ),
    )
    source, member = slot_sources(routing, positions, experts, capacity)
    clamped = jnp.minimum(source, tok_local - 1)
    slot_gate = jnp.where(
        source < tok_local, router_gate_values.reshape(-1)[clamped * choose + member], 0.0
    )
    send_x = jnp.concatenate([tokens, zero_row], 0)[source].reshape(experts, capacity, feat_local)
    send_dy = (
        (
            slot_gate[:, None]
            * jnp.concatenate([output_gradient, zero_row], 0)[source].astype(jnp.float32)
        )
        .astype(jnp.bfloat16)
        .reshape(experts, capacity, feat_local)
    )
    recv_x, recv_dy = (
        lax.all_to_all(send_x, "expert", split_axis=0, concat_axis=2, tiled=True),
        lax.all_to_all(send_dy, "expert", split_axis=0, concat_axis=2, tiled=True),
    )
    gradient_rows_out, shared_slice, owned_slice = rows_backward_pass(
        lax.all_gather(recv_x[0], "dp", axis=0, tiled=True),
        lax.all_gather(recv_dy[0], "dp", axis=0, tiled=True),
        params,
    )
    rows_part = gradient_rows_out
    totals = (
        rows_part,
        jax.tree.map(jnp.add, initial[1], shared_slice),
        jax.tree.map(jnp.add, initial[2], owned_slice),
    )
    rows_part, shared_slice, owned_slice = totals
    summed = lax.psum_scatter(
        rows_part.astype(jnp.bfloat16), "dp", scatter_dimension=0, tiled=True
    ).astype(jnp.float32)
    returned_rows = lax.all_to_all(
        summed.reshape(capacity, experts, feat_local).astype(jnp.bfloat16),
        "expert",
        split_axis=1,
        concat_axis=1,
        tiled=True,
    ).astype(jnp.float32)
    lookup = positions * experts + routing
    grad_x = jnp.sum(returned_rows.reshape(capacity * experts, feat_local)[lookup], axis=1).astype(
        jnp.bfloat16
    )
    grad_a_gate, grad_a_up, grad_b_down = (
        lax.psum(shared_slice[0].astype(jnp.bfloat16), "dp").astype(jnp.float32),
        lax.psum(shared_slice[1].astype(jnp.bfloat16), "dp").astype(jnp.float32),
        lax.psum(shared_slice[2].astype(jnp.bfloat16), "dp").astype(jnp.float32),
    )
    return (
        grad_x,
        grad_a_gate[None],
        owned_slice[0][None],
        grad_a_up[None],
        owned_slice[1][None],
        owned_slice[2][None],
        grad_b_down[None],
    )


LANES = 128
TILE = 512
SHARDS = 8
VMEM_BYTES = 58 * 1024 * 1024
TERM_BYTES = 32 * 1024 * 1024
HBM = pl.BlockSpec(memory_space=pl.ANY)
VMEM = pl.BlockSpec(memory_space=pltpu.VMEM)
SMEM = pl.BlockSpec(memory_space=pltpu.SMEM)


def dot_nt(left, right):
    return contract_pair(left, right, 1, 1)


def dot_nn(left, right):
    return contract_pair(left, right, 1, 0)


def wide(value):
    return value.astype(jnp.float32)


class Rows:
    def __init__(self):
        self.arrays, self.places = [], []

    def add(self, array, *places):
        self.arrays.append(array)
        self.places.append(places)


def row_copies(refs, places, target, sems, slab, order=None):
    tokens_each = refs[0].shape[-2]
    copies = []
    for ref, parts in zip(refs, places):
        for i, (at, block) in enumerate(parts):
            if at != slab:
                continue
            source = ref if len(parts) == 1 else ref.at[i]
            row = block * tokens_each
            if order is not None:
                row = pl.multiple_of(order[block] * tokens_each, tokens_each)
            copies.append(
                pltpu.make_async_copy(
                    source, target.at[slab, pl.ds(row, tokens_each)], sems.at[slab, block]
                )
            )
    return copies


def slab_lanes(slab_ref, slab, feat):
    return pl.ds(pl.multiple_of(slab_ref[slab] * feat, feat), feat)


def forward_kernel(places, *refs):
    n_pieces = len(places)
    pieces = refs[:n_pieces]
    (
        slab_ref,
        gate_hbm,
        up_hbm,
        lower_hbm,
        gate_upper_ref,
        up_upper_ref,
        silu_out,
        slope_out,
        hidden_out,
        low_out,
    ) = refs[n_pieces : n_pieces + 10]
    x_rows, weights, pre, saved, x_sems, w_sems, out_sems = refs[n_pieces + 10 :]
    slabs, _, feat = x_rows.shape
    hidden_here = gate_hbm.shape[0]
    pair, rank = lower_hbm.shape[1], gate_upper_ref.shape[1]

    def x_slab(slab):
        return row_copies(pieces, places, x_rows, x_sems, slab)

    def weight_copies(slab):
        lanes = slab_lanes(slab_ref, slab, feat)
        sides = (
            (gate_hbm.at[:, lanes], 0, hidden_here),
            (up_hbm.at[:, lanes], hidden_here, hidden_here),
            (lower_hbm.at[slab], 2 * hidden_here, pair),
        )
        return [
            pltpu.make_async_copy(
                source, weights.at[slab, pl.ds(start, size)], w_sems.at[slab, i]
            )
            for i, (source, start, size) in enumerate(sides)
        ]

    for slab in range(slabs):
        for copy in x_slab(slab) + weight_copies(slab):
            copy.start()
    for slab in range(slabs):
        for copy in x_slab(slab) + weight_copies(slab):
            copy.wait()
        if slab == 0:
            pre[...] = dot_nt(weights[0], x_rows[0])
        else:
            pre[...] += dot_nt(weights[slab], x_rows[slab])
    low_out[...] = pre[2 * hidden_here :, :].astype(jnp.bfloat16)

    def out_copies(tile):
        at = pl.ds(pl.multiple_of(tile * LANES, LANES), LANES)
        return [
            pltpu.make_async_copy(saved.at[i, at], out.at[at], out_sems.at[i, tile])
            for i, out in enumerate((silu_out, slope_out, hidden_out))
        ]

    tiles = hidden_here // LANES

    @pl.loop(0, tiles)
    def _(tile):
        start = pl.multiple_of(tile * LANES, LANES)
        at = pl.ds(start, LANES)
        up_at = pl.ds(pl.multiple_of(hidden_here + start, LANES), LANES)
        pre_gate = pre[at, :] + ADAPTER_SCALE * dot_nn(gate_upper_ref[at, :], low_out[:rank, :])
        pre_up = pre[up_at, :] + ADAPTER_SCALE * dot_nn(up_upper_ref[at, :], low_out[rank:, :])
        sigma = 1.0 / (1.0 + jnp.exp(-pre_gate))
        silu = pre_gate * sigma
        saved[0, at, :] = silu.astype(jnp.bfloat16)
        saved[1, at, :] = (pre_up * (sigma * (1.0 + pre_gate * (1.0 - sigma)))).astype(
            jnp.bfloat16
        )
        saved[2, at, :] = (silu * pre_up).astype(jnp.bfloat16)
        for copy in out_copies(tile):
            copy.start()

    @pl.loop(0, tiles)
    def _(tile):
        for copy in out_copies(tile):
            copy.wait()


def forward_rows(x, slab_order, weights, lower_slabs, gate_upper, up_upper):
    hidden_here, width = weights[0].shape
    tokens_each, feat = x.arrays[0].shape[-2:]
    rows = SHARDS * tokens_each
    slabs, pair, _ = lower_slabs.shape
    kept = jax.ShapeDtypeStruct((hidden_here, rows), jnp.bfloat16)
    return pl.pallas_call(
        lambda *refs: forward_kernel(x.places, *refs),
        out_shape=(kept, kept, kept, jax.ShapeDtypeStruct((pair, rows), jnp.bfloat16)),
        in_specs=[HBM] * len(x.arrays) + [SMEM] + [HBM] * 3 + [VMEM] * 2,
        out_specs=(HBM, HBM, HBM, VMEM),
        scratch_shapes=[
            pltpu.VMEM((slabs, rows, feat), jnp.bfloat16),
            pltpu.VMEM((slabs, 2 * hidden_here + pair, feat), jnp.bfloat16),
            pltpu.VMEM((2 * hidden_here + pair, rows), jnp.float32),
            pltpu.VMEM((3, hidden_here, rows), jnp.bfloat16),
            pltpu.SemaphoreType.DMA((slabs, SHARDS)),
            pltpu.SemaphoreType.DMA((slabs, 3)),
            pltpu.SemaphoreType.DMA((3, hidden_here // LANES)),
        ],
        compiler_params=pltpu.CompilerParams(vmem_limit_bytes=VMEM_BYTES),
        cost_estimate=pl.CostEstimate(
            flops=8 * rows * hidden_here * width,
            bytes_accessed=4 * hidden_here * width + 2 * rows * width,
            transcendentals=rows * hidden_here,
        ),
        name="forward_rows",
    )(*x.arrays, slab_order, *weights[:2], lower_slabs, gate_upper, up_upper)


def hidden_kernel(places, *refs):
    n_pieces = len(places)
    pieces = refs[:n_pieces]
    (
        slab_ref,
        route_ref,
        down_hbm,
        down_upper_hbm,
        down_lower_ref,
        down_lower_t_ref,
        gate_upper_t_ref,
        up_upper_t_ref,
        silu_hbm,
        slope_hbm,
        hidden_hbm,
        low_ref,
        d_pair,
        parts_out,
        owned_out,
        owned_down_out,
        rows,
        down_w,
        d_down,
        d_cols,
        silu,
        slope,
        hidden,
        row_sems,
        d_sems,
        f_sems,
    ) = refs[n_pieces:]
    slabs, _, feat = rows.shape
    hidden_here = silu.shape[0]
    rank, pair = down_lower_ref.shape[0], low_ref.shape[0]
    saved_copies = [
        pltpu.make_async_copy(source, target, f_sems.at[i])
        for i, (source, target) in enumerate(
            ((silu_hbm, silu), (slope_hbm, slope), (hidden_hbm, hidden))
        )
    ]

    def slab_copies(slab):
        return row_copies(pieces, places, rows, row_sems, slab) + [
            pltpu.make_async_copy(
                down_hbm.at[:, slab_lanes(slab_ref, slab, feat)],
                down_w.at[slab, pl.ds(0, hidden_here)],
                d_sems.at[slab, 0],
            ),
            pltpu.make_async_copy(
                down_upper_hbm.at[slab], down_w.at[slab, pl.ds(hidden_here, rank)], d_sems.at[slab, 1]
            ),
        ]

    for slab in range(slabs):
        for copy in slab_copies(slab):
            copy.start()
    for copy in saved_copies:
        copy.start()
    for slab in range(slabs):
        for copy in slab_copies(slab):
            copy.wait()
        if slab == 0:
            d_down[...] = dot_nt(down_w[0], rows[0])
        else:
            d_down[...] += dot_nt(down_w[slab], rows[slab])

    low_down = (d_down[hidden_here:, :] * route_ref[...]).astype(jnp.bfloat16)
    for copy in saved_copies:
        copy.wait()

    @pl.loop(0, hidden_here // LANES)
    def _(tile):
        start = pl.multiple_of(tile * LANES, LANES)
        at = pl.ds(start, LANES)
        up_at = pl.ds(pl.multiple_of(hidden_here + start, LANES), LANES)
        d_hidden = d_down[at, :] * route_ref[...]
        d_hidden = d_hidden + ADAPTER_SCALE * dot_nn(down_lower_t_ref[at, :], low_down)
        d_gate = (d_hidden * wide(slope[at, :])).astype(jnp.bfloat16)
        d_up = (d_hidden * wide(silu[at, :])).astype(jnp.bfloat16)
        d_cols[at, :] = d_gate
        d_cols[up_at, :] = d_up
        d_pair[:, at] = d_gate.T
        d_pair[:, up_at] = d_up.T

    d_gate, d_up = d_cols[:hidden_here, :], d_cols[hidden_here:, :]
    parts_out[0:rank, :] = dot_nn(gate_upper_t_ref[...], d_gate)
    parts_out[rank : 2 * rank, :] = dot_nn(up_upper_t_ref[...], d_up)
    parts_out[2 * rank :, :] = dot_nn(down_lower_ref[...], hidden[...])
    d_pair[:, 2 * hidden_here :] = ADAPTER_SCALE * parts_out[:pair, :].astype(jnp.bfloat16).T
    owned_out[0] = ADAPTER_SCALE * dot_nt(low_ref[:rank, :], d_gate)
    owned_out[1] = ADAPTER_SCALE * dot_nt(low_ref[rank:, :], d_up)
    owned_down_out[...] = ADAPTER_SCALE * dot_nt(low_down, hidden[...])


def hidden_gradients(dy, slab_order, route_row, down_weight, down_upper, factors, saved):
    hidden_here, width = down_weight.shape
    slabs, rank, feat = down_upper.shape
    pair = saved[3].shape[0]
    rows = route_row.shape[1]
    return pl.pallas_call(
        lambda *refs: hidden_kernel(dy.places, *refs),
        out_shape=(
            jax.ShapeDtypeStruct((rows, 2 * hidden_here + pair), jnp.bfloat16),
            jax.ShapeDtypeStruct((3 * rank, rows), jnp.float32),
            jax.ShapeDtypeStruct((2, rank, hidden_here), jnp.float32),
            jax.ShapeDtypeStruct((rank, hidden_here), jnp.float32),
        ),
        in_specs=[HBM] * len(dy.arrays) + [SMEM, VMEM] + [HBM] * 2 + [VMEM] * 4 + [HBM] * 3 + [VMEM],
        out_specs=(VMEM,) * 4,
        scratch_shapes=[
            pltpu.VMEM((slabs, rows, feat), jnp.bfloat16),
            pltpu.VMEM((slabs, hidden_here + rank, feat), jnp.bfloat16),
            pltpu.VMEM((hidden_here + rank, rows), jnp.float32),
            pltpu.VMEM((2 * hidden_here, rows), jnp.bfloat16),
            pltpu.VMEM((hidden_here, rows), jnp.bfloat16),
            pltpu.VMEM((hidden_here, rows), jnp.bfloat16),
            pltpu.VMEM((hidden_here, rows), jnp.bfloat16),
            pltpu.SemaphoreType.DMA((slabs, SHARDS)),
            pltpu.SemaphoreType.DMA((slabs, 2)),
            pltpu.SemaphoreType.DMA((3,)),
        ],
        compiler_params=pltpu.CompilerParams(vmem_limit_bytes=VMEM_BYTES),
        cost_estimate=pl.CostEstimate(
            flops=4 * rows * hidden_here * width,
            bytes_accessed=2 * hidden_here * width + 2 * rows * width,
            transcendentals=0,
        ),
        name="hidden_gradients",
    )(*dy.arrays, slab_order, route_row, down_weight, down_upper, *factors, *saved)


def term_kernel(
    slab, slab_ref, d_pair, gate_hbm, up_hbm, lower_hbm, keep_out, pass_out, pair_w, sems
):
    _, depth, step = pair_w.shape
    hidden_here = gate_hbm.shape[0]
    pair = depth - 2 * hidden_here
    tokens_each = keep_out.shape[1]
    feat = keep_out.shape[2]
    steps = feat // step

    def weight_copies(n):
        lanes = pl.ds(pl.multiple_of(slab_ref[slab] * feat + n * step, step), step)
        sides = (
            (gate_hbm.at[:, lanes], 0, hidden_here),
            (up_hbm.at[:, lanes], hidden_here, hidden_here),
            (lower_hbm.at[slab, :, pl.ds(pl.multiple_of(n * step, step), step)], 2 * hidden_here, pair),
        )
        return [
            pltpu.make_async_copy(source, pair_w.at[n, pl.ds(start, size)], sems.at[n, i])
            for i, (source, start, size) in enumerate(sides)
        ]

    for n in range(steps):
        for copy in weight_copies(n):
            copy.start()

    @pl.loop(0, steps)
    def _(n):
        for copy in weight_copies(n):
            copy.wait()
        lanes = pl.ds(pl.multiple_of(n * step, step), step)
        term = dot_nn(d_pair[...], pair_w[n]).astype(jnp.bfloat16)
        for block in range(SHARDS):
            out = pass_out if block % 2 else keep_out
            out[block // 2, :, lanes] = term[block * tokens_each : (block + 1) * tokens_each]


def slab_terms(slab, slab_order, d_pair, weights, lower_slabs):
    rows, depth = d_pair.shape
    feat = lower_slabs.shape[2]
    term = jax.ShapeDtypeStruct((SHARDS // 2, rows // SHARDS, feat), jnp.bfloat16)
    return pl.pallas_call(
        lambda *refs: term_kernel(slab, *refs),
        out_shape=(term, term),
        in_specs=[SMEM, VMEM] + [HBM] * 3,
        out_specs=(VMEM, VMEM),
        scratch_shapes=[
            pltpu.VMEM((feat // TILE, depth, TILE), jnp.bfloat16),
            pltpu.SemaphoreType.DMA((feat // TILE, 3)),
        ],
        compiler_params=pltpu.CompilerParams(vmem_limit_bytes=TERM_BYTES),
        cost_estimate=pl.CostEstimate(
            flops=4 * rows * depth * feat,
            bytes_accessed=2 * depth * feat + 4 * rows * depth,
            transcendentals=0,
        ),
        name="slab_terms",
    )(slab_order, d_pair, *weights[:2], lower_slabs)


def shared_kernel(x_places, dy_places, *refs):
    split, inputs = len(x_places), len(x_places) + len(dy_places)
    x_pieces, dy_pieces = refs[:split], refs[split:inputs]
    order_ref, slab_ref, sums_ref, down_sums_ref, pair_out, down_out = refs[inputs : inputs + 6]
    x_rows, dy_rows, sums, down_sums, x_sems, dy_sems = refs[inputs + 6 :]
    slabs, _, feat = x_rows.shape
    tokens_each = x_pieces[0].shape[-2]

    def slab_copies(slab):
        return row_copies(x_pieces, x_places, x_rows, x_sems, slab, order_ref) + row_copies(
            dy_pieces, dy_places, dy_rows, dy_sems, slab, order_ref
        )

    for slab in range(slabs):
        for copy in slab_copies(slab):
            copy.start()
    for block in range(SHARDS):
        lanes = pl.ds(pl.multiple_of(order_ref[block] * tokens_each, tokens_each), tokens_each)
        sums[:, lanes] = sums_ref[block]
        down_sums[:, lanes] = down_sums_ref[block]
    for slab in range(slabs):
        for copy in slab_copies(slab):
            copy.wait()

        @pl.loop(0, feat // TILE)
        def _(n):
            lanes = pl.ds(pl.multiple_of(n * TILE, TILE), TILE)
            out = pl.ds(pl.multiple_of(slab_ref[slab] * feat + n * TILE, TILE), TILE)
            pair_out[:, out] = ADAPTER_SCALE * dot_nn(
                sums[...].astype(jnp.bfloat16), x_rows[slab, :, lanes]
            )
            down_out[:, out] = ADAPTER_SCALE * dot_nn(
                down_sums[...].astype(jnp.bfloat16), dy_rows[slab, :, lanes]
            )


def shared_gradients(x, dy, order, slab_order, sums, down_sums):
    tokens_each, feat = x.arrays[0].shape[-2:]
    slabs = slab_order.shape[0]
    rows = SHARDS * tokens_each
    pair, rank = sums.shape[1], down_sums.shape[1]
    return pl.pallas_call(
        lambda *refs: shared_kernel(x.places, dy.places, *refs),
        out_shape=(
            jax.ShapeDtypeStruct((pair, slabs * feat), jnp.float32),
            jax.ShapeDtypeStruct((rank, slabs * feat), jnp.float32),
        ),
        in_specs=[HBM] * (len(x.arrays) + len(dy.arrays)) + [SMEM, SMEM, VMEM, VMEM],
        out_specs=(VMEM, VMEM),
        scratch_shapes=[
            pltpu.VMEM((slabs, rows, feat), jnp.bfloat16),
            pltpu.VMEM((slabs, rows, feat), jnp.bfloat16),
            pltpu.VMEM((pair, rows), jnp.float32),
            pltpu.VMEM((rank, rows), jnp.float32),
            pltpu.SemaphoreType.DMA((slabs, SHARDS)),
            pltpu.SemaphoreType.DMA((slabs, SHARDS)),
        ],
        compiler_params=pltpu.CompilerParams(vmem_limit_bytes=VMEM_BYTES),
        cost_estimate=pl.CostEstimate(
            flops=16 * rows * pair * slabs * feat,
            bytes_accessed=4 * rows * slabs * feat,
            transcendentals=0,
        ),
        name="shared_gradients",
    )(*x.arrays, *dy.arrays, order, slab_order, sums, down_sums)


CORE, ACROSS, ALONG = 1, 2, 4
PLANE = (ACROSS, ALONG, ACROSS | ALONG)


def swap(value, bit, axis="dp"):
    return lax.ppermute(value, axis, [(i, i ^ bit) for i in range(lax.axis_size(axis))])


def after(value, *others):
    return lax.optimization_barrier((value, others))[0]


def added(left, right):
    return (wide(left) + wide(right)).astype(jnp.bfloat16)


def local(
    tokens,
    output_gradient,
    routing,
    router_gate_values,
    gate_weight,
    up_weight,
    down_weight,
    adapter_lower_gate,
    adapter_upper_gate,
    adapter_lower_up,
    adapter_upper_up,
    adapter_lower_down,
    adapter_upper_down,
):
    experts = lax.axis_size("expert")
    me, expert = lax.axis_index("dp"), lax.axis_index("expert")
    tokens_each, feat = tokens.shape
    rank = adapter_lower_gate.shape[1]
    order = jnp.bitwise_xor(jnp.arange(SHARDS, dtype=jnp.int32), me.astype(jnp.int32))
    slab_order = jnp.bitwise_xor(jnp.arange(experts, dtype=jnp.int32), expert.astype(jnp.int32))

    named = routing[:, :, None] == jnp.arange(experts, dtype=jnp.int32)[None, None, :]
    weight_of = jnp.sum(jnp.where(named, router_gate_values[:, :, None], 0.0), axis=1)
    routes = weight_of.T[None]
    for bit in (CORE, ACROSS, ALONG):
        routes = jnp.concatenate([routes, swap(routes, bit)], axis=0)
    route = lax.dynamic_index_in_dim(routes, expert, axis=1, keepdims=False)

    def slabs_first(factor):
        return factor.reshape(factor.shape[0], experts, feat).transpose(1, 0, 2)[slab_order]

    lower_slabs = slabs_first(
        jnp.concatenate([adapter_lower_gate[0], adapter_lower_up[0]], axis=0)
    )
    down_upper = slabs_first(adapter_upper_down[0].T)
    down_lower = adapter_lower_down[0]
    factors = (down_lower, down_lower.T, adapter_upper_gate[0].T, adapter_upper_up[0].T)

    def exchange(block):
        return jnp.stack([swap(block, r, "expert") for r in range(1, experts)])

    def gathered(block, plane, rest, rest_plane):
        near = [block, *plane]
        rows = Rows()
        for chip, part in enumerate(near):
            rows.add(part, (0, 2 * chip))
        rows.add(swap(jnp.stack(near), CORE), *((0, 2 * chip + 1) for chip in range(len(near))))
        for chip, part in enumerate([rest, *rest_plane]):
            rows.add(part, *((r, 2 * chip) for r in range(1, experts)))
            rows.add(swap(part, CORE), *((r, 2 * chip + 1) for r in range(1, experts)))
        return rows

    x_plane = [swap(tokens, bit) for bit in PLANE]
    x_rest = exchange(tokens)
    dy_plane = [swap(after(output_gradient, *x_plane), bit) for bit in PLANE]
    x_rest_plane = [swap(x_rest, bit) for bit in PLANE]
    dy_rest = exchange(after(output_gradient, x_rest))
    dy_rest = after(dy_rest, *x_rest_plane)
    dy_rest_plane = [swap(dy_rest, bit) for bit in PLANE]
    x = gathered(tokens, x_plane, x_rest, x_rest_plane)
    dy = gathered(output_gradient, dy_plane, dy_rest, dy_rest_plane)

    weights = (gate_weight[0], up_weight[0], down_weight[0])
    saved = forward_rows(
        x, slab_order, weights, lower_slabs, adapter_upper_gate[0], adapter_upper_up[0]
    )
    d_pair, parts, owned, owned_down = hidden_gradients(
        dy, slab_order, route.reshape(1, SHARDS * tokens_each), weights[2], down_upper, factors, saved
    )
    grad_x = None
    for r in reversed(range(experts)):
        keep, away = slab_terms(r, slab_order, d_pair, weights, lower_slabs)
        got = swap(away, CORE)
        chips = [added(keep[i], got[i]) for i in range(SHARDS // 2)]
        rows = wide(chips[0])
        for bit, chip in zip(PLANE, chips[1:]):
            rows = rows + wide(swap(chip, bit))
        if r:
            rows = wide(swap(rows.astype(jnp.bfloat16), r, "expert"))
        grad_x = rows if grad_x is None else grad_x + rows
    grad_x = grad_x.astype(jnp.bfloat16)

    total = parts.reshape(3 * rank, SHARDS, tokens_each).transpose(1, 0, 2)
    for bit in (CORE, ACROSS, ALONG):
        other = swap(total.reshape(SHARDS, 3 * rank, tokens_each), bit)
        shape = (SHARDS // (2 * bit), 2, bit, 3 * rank, tokens_each)
        total = total.reshape(shape) + other.reshape(shape)[:, ::-1]
    total = after(total.reshape(SHARDS, 3 * rank, tokens_each), keep)
    grad_pair, grad_down = shared_gradients(
        x,
        dy,
        order,
        slab_order,
        total[:, : 2 * rank],
        total[:, 2 * rank :] * route[:, None, :],
    )
    return (
        grad_x,
        grad_pair[None, :rank],
        owned[0].T[None],
        grad_pair[None, rank:],
        owned[1].T[None],
        owned_down[None],
        grad_down.T[None],
    )


def plan(tokens, *others):
    experts, tokens_each, hidden_here = lax.axis_size("expert"), tokens.shape[0], others[3].shape[1]
    planned = (
        lax.axis_size("dp") == SHARDS
        and experts in (2, 4)
        and hidden_here % LANES == 0
        and tokens_each % LANES == 0
        and tokens.shape[1] % TILE == 0
    )
    return (local if planned else general_local)(tokens, *others)


def solution(mesh):
    return jax.shard_map(
        plan,
        mesh=mesh,
        in_specs=(
            P("dp", "expert"),
            P("dp", "expert"),
            P("dp", None),
            P("dp", None),
            P("expert", "dp", None),
            P("expert", "dp", None),
            P("expert", "dp", None),
            P("expert", None, None),
            P("expert", "dp", None),
            P("expert", None, None),
            P("expert", "dp", None),
            P("expert", None, "dp"),
            P("expert", None, None),
        ),
        out_specs=(
            P("dp", "expert"),
            P("expert", None, None),
            P("expert", "dp", None),
            P("expert", None, None),
            P("expert", "dp", None),
            P("expert", None, "dp"),
            P("expert", None, None),
        ),
        check_vma=False,
    )
```

```python
import jax
import jax.numpy as jnp
from jax import lax
from jax.experimental import pallas as pl
from jax.experimental.pallas import tpu as pltpu
from jax.sharding import PartitionSpec as P

ADAPTER_SCALE = 2.0


def contract_pair(left, right, left_axis, right_axis):
    return lax.dot_general(
        left, right, (((left_axis,), (right_axis,)), ((), ())), preferred_element_type=jnp.float32
    )


def slot_numbers(route_rows, experts):
    picked = (route_rows[:, :, None] == jnp.arange(experts, dtype=jnp.int32)[None, None, :]).astype(
        jnp.int32
    )
    per_token = jnp.sum(picked, axis=1)
    earlier = jnp.cumsum(per_token, axis=0) - per_token
    return jnp.sum(earlier[:, None, :] * picked, axis=2)


def slot_sources(route_rows, positions, experts, capacity):
    tokens_here, choose = route_rows.shape
    target = (route_rows * capacity + positions).reshape(-1)
    owners = jnp.repeat(jnp.arange(tokens_here, dtype=jnp.int32), choose)
    member_ids = jnp.tile(jnp.arange(choose, dtype=jnp.int32), tokens_here)
    source = jnp.full((experts * capacity,), tokens_here, jnp.int32).at[target].set(owners)
    member = jnp.zeros((experts * capacity,), jnp.int32).at[target].set(member_ids)
    return (source, member)


def rows_backward_pass(input_rows, output_gradient_rows, params):
    (
        gate_weight,
        up_weight,
        down_weight,
        a_gate,
        gate_adapter_upper,
        a_up,
        up_adapter_upper,
        down_adapter_lower,
        b_down,
    ) = params
    gate_projected_lower = contract_pair(a_gate, input_rows, 1, 1).astype(jnp.bfloat16)
    up_projected_lower = contract_pair(a_up, input_rows, 1, 1).astype(jnp.bfloat16)
    gate_preactivation = contract_pair(
        gate_weight, input_rows, 1, 1
    ) + ADAPTER_SCALE * contract_pair(gate_adapter_upper, gate_projected_lower, 1, 0)
    up_preactivation = contract_pair(up_weight, input_rows, 1, 1) + ADAPTER_SCALE * contract_pair(
        up_adapter_upper, up_projected_lower, 1, 0
    )
    sigmoid_gate = jax.nn.sigmoid(gate_preactivation)
    silu_gate = gate_preactivation * sigmoid_gate
    hidden_units = (silu_gate * up_preactivation).astype(jnp.bfloat16)
    down_projected_lower = contract_pair(b_down, output_gradient_rows, 0, 1).astype(jnp.bfloat16)
    hidden_gradient = contract_pair(
        down_weight, output_gradient_rows, 1, 1
    ) + ADAPTER_SCALE * contract_pair(down_adapter_lower, down_projected_lower, 0, 0)
    gate_gradient = (
        hidden_gradient
        * up_preactivation
        * sigmoid_gate
        * (1.0 + gate_preactivation * (1.0 - sigmoid_gate))
    ).astype(jnp.bfloat16)
    up_gradient = (hidden_gradient * silu_gate).astype(jnp.bfloat16)
    gate_partial = contract_pair(gate_adapter_upper, gate_gradient, 0, 0).astype(jnp.bfloat16)
    up_partial = contract_pair(up_adapter_upper, up_gradient, 0, 0).astype(jnp.bfloat16)
    down_partial = contract_pair(down_adapter_lower, hidden_units, 1, 0).astype(jnp.bfloat16)
    paired_partials = jnp.concatenate([gate_partial, up_partial], 0)
    paired_factors = jnp.concatenate([a_gate, a_up], 0)
    gradient_rows_out = (
        contract_pair(gate_gradient, gate_weight, 0, 0)
        + contract_pair(up_gradient, up_weight, 0, 0)
        + ADAPTER_SCALE * contract_pair(paired_partials, paired_factors, 0, 0)
    )
    shared_slice = (
        ADAPTER_SCALE * contract_pair(gate_partial, input_rows, 1, 0),
        ADAPTER_SCALE * contract_pair(up_partial, input_rows, 1, 0),
        ADAPTER_SCALE * contract_pair(output_gradient_rows, down_partial, 0, 1),
    )
    owned_slice = (
        ADAPTER_SCALE * contract_pair(gate_gradient, gate_projected_lower, 1, 1),
        ADAPTER_SCALE * contract_pair(up_gradient, up_projected_lower, 1, 1),
        ADAPTER_SCALE * contract_pair(down_projected_lower, hidden_units, 1, 1),
    )
    return (gradient_rows_out, shared_slice, owned_slice)


def general_local(
    tokens,
    output_gradient,
    routing,
    router_gate_values,
    gate_weight,
    up_weight,
    down_weight,
    adapter_lower_gate,
    adapter_upper_gate,
    adapter_lower_up,
    adapter_upper_up,
    adapter_lower_down,
    adapter_upper_down,
):
    experts = lax.axis_size("expert")
    shards = lax.axis_size("dp")
    tok_local, feat_local = tokens.shape
    choose = routing.shape[1]
    complete_width = feat_local * experts
    capacity = min(tok_local, 6 * tok_local // experts)
    hidden_units_local = gate_weight.shape[1]
    adapter_rank = adapter_lower_gate.shape[1]
    params = (
        gate_weight[0],
        up_weight[0],
        down_weight[0],
        adapter_lower_gate[0],
        adapter_upper_gate[0],
        adapter_lower_up[0],
        adapter_upper_up[0],
        adapter_lower_down[0],
        adapter_upper_down[0],
    )
    positions = slot_numbers(routing, experts)
    zero_row = jnp.zeros((1, feat_local), jnp.bfloat16)
    initial = (
        jnp.zeros((shards * capacity, complete_width), jnp.float32),
        (
            jnp.zeros((adapter_rank, complete_width), jnp.float32),
            jnp.zeros((adapter_rank, complete_width), jnp.float32),
            jnp.zeros((complete_width, adapter_rank), jnp.float32),
        ),
        (
            jnp.zeros((hidden_units_local, adapter_rank), jnp.float32),
            jnp.zeros((hidden_units_local, adapter_rank), jnp.float32),
            jnp.zeros((adapter_rank, hidden_units_local), jnp.float32),
        ),
    )
    source, member = slot_sources(routing, positions, experts, capacity)
    clamped = jnp.minimum(source, tok_local - 1)
    slot_gate = jnp.where(
        source < tok_local, router_gate_values.reshape(-1)[clamped * choose + member], 0.0
    )
    send_x = jnp.concatenate([tokens, zero_row], 0)[source].reshape(experts, capacity, feat_local)
    send_dy = (
        (
            slot_gate[:, None]
            * jnp.concatenate([output_gradient, zero_row], 0)[source].astype(jnp.float32)
        )
        .astype(jnp.bfloat16)
        .reshape(experts, capacity, feat_local)
    )
    recv_x, recv_dy = (
        lax.all_to_all(send_x, "expert", split_axis=0, concat_axis=2, tiled=True),
        lax.all_to_all(send_dy, "expert", split_axis=0, concat_axis=2, tiled=True),
    )
    gradient_rows_out, shared_slice, owned_slice = rows_backward_pass(
        lax.all_gather(recv_x[0], "dp", axis=0, tiled=True),
        lax.all_gather(recv_dy[0], "dp", axis=0, tiled=True),
        params,
    )
    rows_part = gradient_rows_out
    totals = (
        rows_part,
        jax.tree.map(jnp.add, initial[1], shared_slice),
        jax.tree.map(jnp.add, initial[2], owned_slice),
    )
    rows_part, shared_slice, owned_slice = totals
    summed = lax.psum_scatter(
        rows_part.astype(jnp.bfloat16), "dp", scatter_dimension=0, tiled=True
    ).astype(jnp.float32)
    returned_rows = lax.all_to_all(
        summed.reshape(capacity, experts, feat_local).astype(jnp.bfloat16),
        "expert",
        split_axis=1,
        concat_axis=1,
        tiled=True,
    ).astype(jnp.float32)
    lookup = positions * experts + routing
    grad_x = jnp.sum(returned_rows.reshape(capacity * experts, feat_local)[lookup], axis=1).astype(
        jnp.bfloat16
    )
    grad_a_gate, grad_a_up, grad_b_down = (
        lax.psum(shared_slice[0].astype(jnp.bfloat16), "dp").astype(jnp.float32),
        lax.psum(shared_slice[1].astype(jnp.bfloat16), "dp").astype(jnp.float32),
        lax.psum(shared_slice[2].astype(jnp.bfloat16), "dp").astype(jnp.float32),
    )
    return (
        grad_x,
        grad_a_gate[None],
        owned_slice[0][None],
        grad_a_up[None],
        owned_slice[1][None],
        owned_slice[2][None],
        grad_b_down[None],
    )


LANES = 128
TILE = 512
SHARDS = 8
VMEM_BYTES = 58 * 1024 * 1024
TERM_BYTES = 32 * 1024 * 1024
HBM = pl.BlockSpec(memory_space=pl.ANY)
PINNED = pl.BlockSpec(memory_space=pltpu.HBM)
VMEM = pl.BlockSpec(memory_space=pltpu.VMEM)
SMEM = pl.BlockSpec(memory_space=pltpu.SMEM)


def dot_nt(left, right):
    return contract_pair(left, right, 1, 1)


def dot_nn(left, right):
    return contract_pair(left, right, 1, 0)


def wide(value):
    return value.astype(jnp.float32)


class Rows:
    def __init__(self):
        self.arrays, self.places = [], []

    def add(self, array, *places):
        self.arrays.append(array)
        self.places.append(places)


def row_copies(refs, places, target, sems, slab, order=None):
    tokens_each = refs[0].shape[-2]
    copies = []
    for ref, parts in zip(refs, places):
        for i, (at, block) in enumerate(parts):
            if at != slab:
                continue
            source = ref if len(parts) == 1 else ref.at[i]
            row = block * tokens_each
            if order is not None:
                row = pl.multiple_of(order[block] * tokens_each, tokens_each)
            copies.append(
                pltpu.make_async_copy(
                    source, target.at[slab, pl.ds(row, tokens_each)], sems.at[slab, block]
                )
            )
    return copies


def slab_lanes(slab_ref, slab, feat):
    return pl.ds(pl.multiple_of(slab_ref[slab] * feat, feat), feat)


def forward_kernel(places, *refs):
    n_pieces = len(places)
    pieces = refs[:n_pieces]
    (
        slab_ref,
        gate_hbm,
        up_hbm,
        lower_hbm,
        gate_upper_ref,
        up_upper_ref,
        silu_out,
        slope_out,
        hidden_out,
        low_out,
    ) = refs[n_pieces : n_pieces + 10]
    x_rows, weights, pre, saved, x_sems, w_sems, out_sems = refs[n_pieces + 10 :]
    slabs, _, feat = x_rows.shape
    hidden_here = gate_hbm.shape[0]
    pair, rank = lower_hbm.shape[1], gate_upper_ref.shape[1]

    def x_slab(slab):
        return row_copies(pieces, places, x_rows, x_sems, slab)

    def weight_copies(slab):
        lanes = slab_lanes(slab_ref, slab, feat)
        sides = (
            (gate_hbm.at[:, lanes], 0, hidden_here),
            (up_hbm.at[:, lanes], hidden_here, hidden_here),
            (lower_hbm.at[slab], 2 * hidden_here, pair),
        )
        return [
            pltpu.make_async_copy(
                source, weights.at[slab, pl.ds(start, size)], w_sems.at[slab, i]
            )
            for i, (source, start, size) in enumerate(sides)
        ]

    for slab in range(slabs):
        for copy in x_slab(slab) + weight_copies(slab):
            copy.start()
    for slab in range(slabs):
        for copy in x_slab(slab) + weight_copies(slab):
            copy.wait()
        if slab == 0:
            pre[...] = dot_nt(weights[0], x_rows[0])
        else:
            pre[...] += dot_nt(weights[slab], x_rows[slab])
    low_out[...] = pre[2 * hidden_here :, :].astype(jnp.bfloat16)

    def out_copies(tile):
        at = pl.ds(pl.multiple_of(tile * LANES, LANES), LANES)
        return [
            pltpu.make_async_copy(saved.at[i, at], out.at[at], out_sems.at[i, tile])
            for i, out in enumerate((silu_out, slope_out, hidden_out))
        ]

    tiles = hidden_here // LANES

    @pl.loop(0, tiles)
    def _(tile):
        start = pl.multiple_of(tile * LANES, LANES)
        at = pl.ds(start, LANES)
        up_at = pl.ds(pl.multiple_of(hidden_here + start, LANES), LANES)
        pre_gate = pre[at, :] + ADAPTER_SCALE * dot_nn(gate_upper_ref[at, :], low_out[:rank, :])
        pre_up = pre[up_at, :] + ADAPTER_SCALE * dot_nn(up_upper_ref[at, :], low_out[rank:, :])
        sigma = 1.0 / (1.0 + jnp.exp(-pre_gate))
        silu = pre_gate * sigma
        saved[0, at, :] = silu.astype(jnp.bfloat16)
        saved[1, at, :] = (pre_up * (sigma * (1.0 + pre_gate * (1.0 - sigma)))).astype(
            jnp.bfloat16
        )
        saved[2, at, :] = (silu * pre_up).astype(jnp.bfloat16)
        for copy in out_copies(tile):
            copy.start()

    @pl.loop(0, tiles)
    def _(tile):
        for copy in out_copies(tile):
            copy.wait()


def forward_rows(x, slab_order, weights, lower_slabs, gate_upper, up_upper):
    hidden_here, width = weights[0].shape
    tokens_each, feat = x.arrays[0].shape[-2:]
    rows = SHARDS * tokens_each
    slabs, pair, _ = lower_slabs.shape
    kept = jax.ShapeDtypeStruct((hidden_here, rows), jnp.bfloat16)
    return pl.pallas_call(
        lambda *refs: forward_kernel(x.places, *refs),
        out_shape=(kept, kept, kept, jax.ShapeDtypeStruct((pair, rows), jnp.bfloat16)),
        in_specs=[HBM] * len(x.arrays) + [SMEM] + [HBM] * 3 + [VMEM] * 2,
        out_specs=(HBM, HBM, HBM, VMEM),
        scratch_shapes=[
            pltpu.VMEM((slabs, rows, feat), jnp.bfloat16),
            pltpu.VMEM((slabs, 2 * hidden_here + pair, feat), jnp.bfloat16),
            pltpu.VMEM((2 * hidden_here + pair, rows), jnp.float32),
            pltpu.VMEM((3, hidden_here, rows), jnp.bfloat16),
            pltpu.SemaphoreType.DMA((slabs, SHARDS)),
            pltpu.SemaphoreType.DMA((slabs, 3)),
            pltpu.SemaphoreType.DMA((3, hidden_here // LANES)),
        ],
        compiler_params=pltpu.CompilerParams(vmem_limit_bytes=VMEM_BYTES),
        cost_estimate=pl.CostEstimate(
            flops=8 * rows * hidden_here * width,
            bytes_accessed=4 * hidden_here * width + 2 * rows * width,
            transcendentals=rows * hidden_here,
        ),
        name="forward_rows",
    )(*x.arrays, slab_order, *weights[:2], lower_slabs, gate_upper, up_upper)


def hidden_kernel(places, *refs):
    n_pieces = len(places)
    pieces = refs[:n_pieces]
    (
        slab_ref,
        route_ref,
        down_hbm,
        down_upper_hbm,
        down_lower_ref,
        down_lower_t_ref,
        gate_upper_t_ref,
        up_upper_t_ref,
        silu_hbm,
        slope_hbm,
        hidden_hbm,
        d_pair,
        parts_out,
        low_down,
        rows,
        down_w,
        d_down,
        d_cols,
        silu,
        slope,
        hidden,
        row_sems,
        d_sems,
        f_sems,
    ) = refs[n_pieces:]
    slabs, _, feat = rows.shape
    hidden_here = silu.shape[0]
    rank, pair = down_lower_ref.shape[0], 2 * down_lower_ref.shape[0]
    saved_copies = [
        pltpu.make_async_copy(source, target, f_sems.at[i])
        for i, (source, target) in enumerate(
            ((silu_hbm, silu), (slope_hbm, slope), (hidden_hbm, hidden))
        )
    ]

    def slab_copies(slab):
        return row_copies(pieces, places, rows, row_sems, slab) + [
            pltpu.make_async_copy(
                down_hbm.at[:, slab_lanes(slab_ref, slab, feat)],
                down_w.at[slab, pl.ds(0, hidden_here)],
                d_sems.at[slab, 0],
            ),
            pltpu.make_async_copy(
                down_upper_hbm.at[slab], down_w.at[slab, pl.ds(hidden_here, rank)], d_sems.at[slab, 1]
            ),
        ]

    for slab in range(slabs):
        for copy in slab_copies(slab):
            copy.start()
    for copy in saved_copies:
        copy.start()
    for slab in range(slabs):
        for copy in slab_copies(slab):
            copy.wait()
        if slab == 0:
            d_down[...] = dot_nt(down_w[0], rows[0])
        else:
            d_down[...] += dot_nt(down_w[slab], rows[slab])

    low_down[...] = (d_down[hidden_here:, :] * route_ref[...]).astype(jnp.bfloat16)
    for copy in saved_copies:
        copy.wait()

    @pl.loop(0, hidden_here // LANES)
    def _(tile):
        start = pl.multiple_of(tile * LANES, LANES)
        at = pl.ds(start, LANES)
        up_at = pl.ds(pl.multiple_of(hidden_here + start, LANES), LANES)
        d_hidden = d_down[at, :] * route_ref[...]
        d_hidden = d_hidden + ADAPTER_SCALE * dot_nn(down_lower_t_ref[at, :], low_down[...])
        d_gate = (d_hidden * wide(slope[at, :])).astype(jnp.bfloat16)
        d_up = (d_hidden * wide(silu[at, :])).astype(jnp.bfloat16)
        d_cols[at, :] = d_gate
        d_cols[up_at, :] = d_up
        d_pair[:, at] = d_gate.T
        d_pair[:, up_at] = d_up.T

    d_gate, d_up = d_cols[:hidden_here, :], d_cols[hidden_here:, :]
    parts_out[0:rank, :] = dot_nn(gate_upper_t_ref[...], d_gate)
    parts_out[rank : 2 * rank, :] = dot_nn(up_upper_t_ref[...], d_up)
    parts_out[2 * rank :, :] = dot_nn(down_lower_ref[...], hidden[...])
    d_pair[:, 2 * hidden_here :] = ADAPTER_SCALE * parts_out[:pair, :].astype(jnp.bfloat16).T


def hidden_gradients(dy, slab_order, route_row, down_weight, down_upper, factors, saved):
    hidden_here, width = down_weight.shape
    slabs, rank, feat = down_upper.shape
    pair = 2 * rank
    rows = route_row.shape[1]
    return pl.pallas_call(
        lambda *refs: hidden_kernel(dy.places, *refs),
        out_shape=(
            jax.ShapeDtypeStruct((rows, 2 * hidden_here + pair), jnp.bfloat16),
            jax.ShapeDtypeStruct((3 * rank, rows), jnp.float32),
            jax.ShapeDtypeStruct((rank, rows), jnp.bfloat16),
        ),
        in_specs=[HBM] * len(dy.arrays) + [SMEM, VMEM] + [HBM] * 2 + [VMEM] * 4 + [HBM] * 3,
        out_specs=(VMEM,) * 3,
        scratch_shapes=[
            pltpu.VMEM((slabs, rows, feat), jnp.bfloat16),
            pltpu.VMEM((slabs, hidden_here + rank, feat), jnp.bfloat16),
            pltpu.VMEM((hidden_here + rank, rows), jnp.float32),
            pltpu.VMEM((2 * hidden_here, rows), jnp.bfloat16),
            pltpu.VMEM((hidden_here, rows), jnp.bfloat16),
            pltpu.VMEM((hidden_here, rows), jnp.bfloat16),
            pltpu.VMEM((hidden_here, rows), jnp.bfloat16),
            pltpu.SemaphoreType.DMA((slabs, SHARDS)),
            pltpu.SemaphoreType.DMA((slabs, 2)),
            pltpu.SemaphoreType.DMA((3,)),
        ],
        compiler_params=pltpu.CompilerParams(vmem_limit_bytes=VMEM_BYTES),
        cost_estimate=pl.CostEstimate(
            flops=4 * rows * hidden_here * width,
            bytes_accessed=2 * hidden_here * width + 2 * rows * width,
            transcendentals=0,
        ),
        name="hidden_gradients",
    )(*dy.arrays, slab_order, route_row, down_weight, down_upper, *factors, *saved)


def term_kernel(
    slab, slab_ref, d_pair, gate_hbm, up_hbm, lower_hbm, keep_out, pass_out, pair_w, sems
):
    _, depth, step = pair_w.shape
    hidden_here = gate_hbm.shape[0]
    pair = depth - 2 * hidden_here
    tokens_each = keep_out.shape[1]
    feat = keep_out.shape[2]
    steps = feat // step

    def weight_copies(n):
        lanes = pl.ds(pl.multiple_of(slab_ref[slab] * feat + n * step, step), step)
        sides = (
            (gate_hbm.at[:, lanes], 0, hidden_here),
            (up_hbm.at[:, lanes], hidden_here, hidden_here),
            (lower_hbm.at[slab, :, pl.ds(pl.multiple_of(n * step, step), step)], 2 * hidden_here, pair),
        )
        return [
            pltpu.make_async_copy(source, pair_w.at[n, pl.ds(start, size)], sems.at[n, i])
            for i, (source, start, size) in enumerate(sides)
        ]

    for n in range(steps):
        for copy in weight_copies(n):
            copy.start()

    @pl.loop(0, steps)
    def _(n):
        for copy in weight_copies(n):
            copy.wait()
        lanes = pl.ds(pl.multiple_of(n * step, step), step)
        term = dot_nn(d_pair[...], pair_w[n]).astype(jnp.bfloat16)
        for block in range(SHARDS):
            out = pass_out if block % 2 else keep_out
            out[block // 2, :, lanes] = term[block * tokens_each : (block + 1) * tokens_each]


def slab_terms(slab, slab_order, d_pair, weights, lower_slabs):
    rows, depth = d_pair.shape
    feat = lower_slabs.shape[2]
    term = jax.ShapeDtypeStruct((SHARDS // 2, rows // SHARDS, feat), jnp.bfloat16)
    return pl.pallas_call(
        lambda *refs: term_kernel(slab, *refs),
        out_shape=(term, term),
        in_specs=[SMEM, VMEM] + [PINNED] * 3,
        out_specs=(VMEM, VMEM),
        scratch_shapes=[
            pltpu.VMEM((feat // TILE, depth, TILE), jnp.bfloat16),
            pltpu.SemaphoreType.DMA((feat // TILE, 3)),
        ],
        compiler_params=pltpu.CompilerParams(vmem_limit_bytes=TERM_BYTES),
        cost_estimate=pl.CostEstimate(
            flops=4 * rows * depth * feat,
            bytes_accessed=2 * depth * feat + 4 * rows * depth,
            transcendentals=0,
        ),
        name="slab_terms",
    )(slab_order, d_pair, *weights[:2], lower_slabs)


def shared_kernel(x_places, dy_places, *refs):
    split, inputs = len(x_places), len(x_places) + len(dy_places)
    x_pieces, dy_pieces = refs[:split], refs[split:inputs]
    (
        order_ref,
        slab_ref,
        sums_ref,
        down_sums_ref,
        low_ref,
        low_down_ref,
        d_pair,
        hidden,
        pair_out,
        down_out,
        owned_out,
        owned_down_out,
    ) = refs[inputs : inputs + 12]
    x_rows, dy_rows, sums, down_sums, x_sems, dy_sems = refs[inputs + 12 :]
    hidden_here, rank = hidden.shape[0], low_down_ref.shape[0]
    slabs, _, feat = x_rows.shape
    tokens_each = x_pieces[0].shape[-2]

    def slab_copies(slab):
        return row_copies(x_pieces, x_places, x_rows, x_sems, slab, order_ref) + row_copies(
            dy_pieces, dy_places, dy_rows, dy_sems, slab, order_ref
        )

    for slab in range(slabs):
        for copy in slab_copies(slab):
            copy.start()
    for block in range(SHARDS):
        lanes = pl.ds(pl.multiple_of(order_ref[block] * tokens_each, tokens_each), tokens_each)
        sums[:, lanes] = sums_ref[block]
        down_sums[:, lanes] = down_sums_ref[block]
    owned_out[0] = ADAPTER_SCALE * dot_nn(low_ref[:rank, :], d_pair[:, :hidden_here])
    owned_out[1] = ADAPTER_SCALE * dot_nn(low_ref[rank:, :], d_pair[:, hidden_here : 2 * hidden_here])
    owned_down_out[...] = ADAPTER_SCALE * dot_nt(low_down_ref[...], hidden[...])
    for slab in range(slabs):
        for copy in slab_copies(slab):
            copy.wait()

        @pl.loop(0, feat // TILE)
        def _(n):
            lanes = pl.ds(pl.multiple_of(n * TILE, TILE), TILE)
            out = pl.ds(pl.multiple_of(slab_ref[slab] * feat + n * TILE, TILE), TILE)
            pair_out[:, out] = ADAPTER_SCALE * dot_nn(
                sums[...].astype(jnp.bfloat16), x_rows[slab, :, lanes]
            )
            down_out[:, out] = ADAPTER_SCALE * dot_nn(
                down_sums[...].astype(jnp.bfloat16), dy_rows[slab, :, lanes]
            )


def adapter_gradients(x, dy, order, slab_order, sums, down_sums, low, low_down, d_pair, hidden):
    tokens_each, feat = x.arrays[0].shape[-2:]
    slabs = slab_order.shape[0]
    rows = SHARDS * tokens_each
    pair, rank = sums.shape[1], down_sums.shape[1]
    hidden_here = hidden.shape[0]
    return pl.pallas_call(
        lambda *refs: shared_kernel(x.places, dy.places, *refs),
        out_shape=(
            jax.ShapeDtypeStruct((pair, slabs * feat), jnp.float32),
            jax.ShapeDtypeStruct((rank, slabs * feat), jnp.float32),
            jax.ShapeDtypeStruct((2, rank, hidden_here), jnp.float32),
            jax.ShapeDtypeStruct((rank, hidden_here), jnp.float32),
        ),
        in_specs=[HBM] * (len(x.arrays) + len(dy.arrays)) + [SMEM, SMEM] + [VMEM] * 6,
        out_specs=(VMEM,) * 4,
        scratch_shapes=[
            pltpu.VMEM((slabs, rows, feat), jnp.bfloat16),
            pltpu.VMEM((slabs, rows, feat), jnp.bfloat16),
            pltpu.VMEM((pair, rows), jnp.float32),
            pltpu.VMEM((rank, rows), jnp.float32),
            pltpu.SemaphoreType.DMA((slabs, SHARDS)),
            pltpu.SemaphoreType.DMA((slabs, SHARDS)),
        ],
        compiler_params=pltpu.CompilerParams(vmem_limit_bytes=VMEM_BYTES),
        cost_estimate=pl.CostEstimate(
            flops=16 * rows * pair * slabs * feat,
            bytes_accessed=4 * rows * slabs * feat,
            transcendentals=0,
        ),
        name="adapter_gradients",
    )(
        *x.arrays,
        *dy.arrays,
        order,
        slab_order,
        sums,
        down_sums,
        low,
        low_down,
        d_pair,
        hidden,
    )


CORE, ACROSS, ALONG = 1, 2, 4
PLANE = (ACROSS, ALONG, ACROSS | ALONG)


def swap(value, bit, axis="dp"):
    return lax.ppermute(value, axis, [(i, i ^ bit) for i in range(lax.axis_size(axis))])


def after(value, *others):
    return lax.optimization_barrier((value, others))[0]


def added(left, right):
    return (wide(left) + wide(right)).astype(jnp.bfloat16)


def local(
    tokens,
    output_gradient,
    routing,
    router_gate_values,
    gate_weight,
    up_weight,
    down_weight,
    adapter_lower_gate,
    adapter_upper_gate,
    adapter_lower_up,
    adapter_upper_up,
    adapter_lower_down,
    adapter_upper_down,
):
    experts = lax.axis_size("expert")
    me, expert = lax.axis_index("dp"), lax.axis_index("expert")
    tokens_each, feat = tokens.shape
    rank = adapter_lower_gate.shape[1]
    order = jnp.bitwise_xor(jnp.arange(SHARDS, dtype=jnp.int32), me.astype(jnp.int32))
    slab_order = jnp.bitwise_xor(jnp.arange(experts, dtype=jnp.int32), expert.astype(jnp.int32))

    named = routing[:, :, None] == jnp.arange(experts, dtype=jnp.int32)[None, None, :]
    weight_of = jnp.sum(jnp.where(named, router_gate_values[:, :, None], 0.0), axis=1)
    routes = lax.all_gather(weight_of.T, "dp", axis=0, tiled=False)
    route = lax.dynamic_index_in_dim(routes, expert, axis=1, keepdims=False)[order]
    route_row = route.reshape(1, SHARDS * tokens_each)

    def slabs_first(factor):
        return factor.reshape(factor.shape[0], experts, feat).transpose(1, 0, 2)[slab_order]

    lower_slabs = slabs_first(
        jnp.concatenate([adapter_lower_gate[0], adapter_lower_up[0]], axis=0)
    )
    down_upper = slabs_first(adapter_upper_down[0].T)
    down_lower = adapter_lower_down[0]
    factors = (down_lower, down_lower.T, adapter_upper_gate[0].T, adapter_upper_up[0].T)

    def place_both(rows, part, swapped, chip, slabs):
        rows.add(part, *((r, 2 * chip) for r in slabs))
        rows.add(swapped, *((r, 2 * chip + 1) for r in slabs))

    def over_experts(block, r):
        return swap(block, r, "expert")

    both = over_experts(jnp.stack([tokens, output_gradient]), 1)
    x_slabs = [both[0]] + [over_experts(tokens, r) for r in range(2, experts)]
    x_near = [tokens] + [swap(tokens, bit) for bit in PLANE[:2]]
    ready = (route_row, lower_slabs, down_upper, *factors)
    (x_slabs, x_near), ready = lax.optimization_barrier(((x_slabs, x_near), ready))
    route_row, lower_slabs, down_upper, *factors = ready

    x_rest = jnp.stack(x_slabs)
    x_rest_plane = [swap(x_rest, bit) for bit in PLANE[:2]]
    x_far = swap(jnp.stack([tokens, *x_slabs]), PLANE[2])
    dy_late = after(output_gradient, x_rest)
    dy_slabs = [output_gradient, both[1]] + [over_experts(dy_late, r) for r in range(2, experts)]

    x_near_rows, x_far, x_mine = lax.optimization_barrier(
        ((jnp.stack(x_near), x_far, [x_rest, *x_rest_plane]), dy_slabs[2:])
    )[0]
    x_near_swapped, x_far_swapped = swap(x_near_rows, CORE), swap(x_far, CORE)
    x_swapped = [swap(part, CORE) for part in x_mine]
    x = Rows()
    for chip, part in enumerate(x_near):
        x.add(part, (0, 2 * chip))
    x.add(x_near_swapped, *((0, 2 * chip + 1) for chip in range(len(x_near))))
    for chip, part in enumerate(x_mine):
        place_both(x, part, x_swapped[chip], chip, range(1, experts))
    place_both(x, x_far, x_far_swapped, len(x_mine), range(experts))

    dy_all = after(jnp.stack(dy_slabs), x_near_swapped, x_far_swapped, *x_swapped)
    dy_plane = [swap(dy_all, bit) for bit in PLANE]
    dy_swapped = [swap(dy_all, CORE)]

    weights = (gate_weight[0], up_weight[0], down_weight[0])
    saved = forward_rows(
        x, slab_order, weights, lower_slabs, adapter_upper_gate[0], adapter_upper_up[0]
    )
    dy_plane = after(dy_plane, saved[0])
    dy_swapped += [swap(part, CORE) for part in dy_plane]
    dy = Rows()
    for chip, part in enumerate([dy_all, *dy_plane]):
        place_both(dy, part, dy_swapped[chip], chip, range(experts))
    d_pair, parts, low_down = hidden_gradients(
        dy, slab_order, route_row, weights[2], down_upper, factors, saved[:3]
    )

    def sum_step(total, bit):
        other = swap(total.reshape(SHARDS, 3 * rank, tokens_each), bit)
        shape = (SHARDS // (2 * bit), 2, bit, 3 * rank, tokens_each)
        return total.reshape(shape) + other.reshape(shape)[:, ::-1]

    total = parts.reshape(3 * rank, SHARDS, tokens_each).transpose(1, 0, 2)
    sums = [total]
    for bit in (CORE, ACROSS, ALONG):
        sums.append(sum_step(sums[-1], bit))
    total = sums[-1]
    waits = {1: [sums[1]], 0: [sums[2]]}
    keeps, gots, chips, moved, rows = {}, {}, {}, {}, {}

    def send_chips(r):
        chips[r] = [added(keeps[r][i], gots[r][i]) for i in range(SHARDS // 2)]
        moved[r] = [swap(chip, bit) for bit, chip in zip(PLANE, chips[r][1:])]

    def sum_chips(r):
        rows[r] = sum((wide(part) for part in moved[r]), wide(chips[r][0]))
        if r:
            rows[r] = rows[r].astype(jnp.bfloat16)

    for r in reversed(range(experts)):
        here = waits.get(r, []) + chips.get(r + 2, []) + [rows[k] for k in (r + 3,) if k in rows]
        here = after(slab_order, *here) if here else slab_order
        keeps[r], away = slab_terms(r, here, d_pair, weights, lower_slabs)
        gots[r] = swap(away, CORE)
        if r + 1 in gots:
            gots[r + 1] = after(gots[r + 1], keeps[r])
            send_chips(r + 1)
        if r + 2 in moved:
            moved[r + 2] = after(moved[r + 2], keeps[r])
            sum_chips(r + 2)
    send_chips(0)
    for r in range(min(experts, 2)):
        sum_chips(r)
    keep = keeps[0]
    grad_x = rows[0]
    for r in range(1, experts):
        grad_x = grad_x + wide(swap(rows[r], r, "expert"))
    grad_x = grad_x.astype(jnp.bfloat16)

    total = after(total.reshape(SHARDS, 3 * rank, tokens_each), keep)
    grad_pair, grad_down, owned, owned_down = adapter_gradients(
        x,
        dy,
        order,
        slab_order,
        total[:, : 2 * rank],
        total[:, 2 * rank :] * route[:, None, :],
        saved[3],
        low_down,
        d_pair,
        saved[2],
    )
    return (
        grad_x,
        grad_pair[None, :rank],
        owned[0].T[None],
        grad_pair[None, rank:],
        owned[1].T[None],
        owned_down[None],
        grad_down.T[None],
    )


def plan(tokens, *others):
    experts, tokens_each, hidden_here = lax.axis_size("expert"), tokens.shape[0], others[3].shape[1]
    planned = (
        lax.axis_size("dp") == SHARDS
        and experts in (2, 4)
        and hidden_here % LANES == 0
        and tokens_each % LANES == 0
        and tokens.shape[1] % TILE == 0
    )
    return (local if planned else general_local)(tokens, *others)


def solution(mesh):
    return jax.shard_map(
        plan,
        mesh=mesh,
        in_specs=(
            P("dp", "expert"),
            P("dp", "expert"),
            P("dp", None),
            P("dp", None),
            P("expert", "dp", None),
            P("expert", "dp", None),
            P("expert", "dp", None),
            P("expert", None, None),
            P("expert", "dp", None),
            P("expert", None, None),
            P("expert", "dp", None),
            P("expert", None, "dp"),
            P("expert", None, None),
        ),
        out_specs=(
            P("dp", "expert"),
            P("expert", None, None),
            P("expert", "dp", None),
            P("expert", None, None),
            P("expert", "dp", None),
            P("expert", None, "dp"),
            P("expert", None, None),
        ),
        check_vma=False,
    )
```

```python
import jax
import jax.numpy as jnp
from jax import lax
from jax.experimental import pallas as pl
from jax.experimental.pallas import tpu as pltpu
from jax.sharding import PartitionSpec as P

ADAPTER_SCALE = 2.0


def contract_pair(left, right, left_axis, right_axis):
    return lax.dot_general(
        left, right, (((left_axis,), (right_axis,)), ((), ())), preferred_element_type=jnp.float32
    )


def slot_numbers(route_rows, experts):
    picked = (route_rows[:, :, None] == jnp.arange(experts, dtype=jnp.int32)[None, None, :]).astype(
        jnp.int32
    )
    per_token = jnp.sum(picked, axis=1)
    earlier = jnp.cumsum(per_token, axis=0) - per_token
    return jnp.sum(earlier[:, None, :] * picked, axis=2)


def slot_sources(route_rows, positions, experts, capacity):
    tokens_here, choose = route_rows.shape
    target = (route_rows * capacity + positions).reshape(-1)
    owners = jnp.repeat(jnp.arange(tokens_here, dtype=jnp.int32), choose)
    member_ids = jnp.tile(jnp.arange(choose, dtype=jnp.int32), tokens_here)
    source = jnp.full((experts * capacity,), tokens_here, jnp.int32).at[target].set(owners)
    member = jnp.zeros((experts * capacity,), jnp.int32).at[target].set(member_ids)
    return (source, member)


def rows_backward_pass(input_rows, output_gradient_rows, params):
    (
        gate_weight,
        up_weight,
        down_weight,
        a_gate,
        gate_adapter_upper,
        a_up,
        up_adapter_upper,
        down_adapter_lower,
        b_down,
    ) = params
    gate_projected_lower = contract_pair(a_gate, input_rows, 1, 1).astype(jnp.bfloat16)
    up_projected_lower = contract_pair(a_up, input_rows, 1, 1).astype(jnp.bfloat16)
    gate_preactivation = contract_pair(
        gate_weight, input_rows, 1, 1
    ) + ADAPTER_SCALE * contract_pair(gate_adapter_upper, gate_projected_lower, 1, 0)
    up_preactivation = contract_pair(up_weight, input_rows, 1, 1) + ADAPTER_SCALE * contract_pair(
        up_adapter_upper, up_projected_lower, 1, 0
    )
    sigmoid_gate = jax.nn.sigmoid(gate_preactivation)
    silu_gate = gate_preactivation * sigmoid_gate
    hidden_units = (silu_gate * up_preactivation).astype(jnp.bfloat16)
    down_projected_lower = contract_pair(b_down, output_gradient_rows, 0, 1).astype(jnp.bfloat16)
    hidden_gradient = contract_pair(
        down_weight, output_gradient_rows, 1, 1
    ) + ADAPTER_SCALE * contract_pair(down_adapter_lower, down_projected_lower, 0, 0)
    gate_gradient = (
        hidden_gradient
        * up_preactivation
        * sigmoid_gate
        * (1.0 + gate_preactivation * (1.0 - sigmoid_gate))
    ).astype(jnp.bfloat16)
    up_gradient = (hidden_gradient * silu_gate).astype(jnp.bfloat16)
    gate_partial = contract_pair(gate_adapter_upper, gate_gradient, 0, 0).astype(jnp.bfloat16)
    up_partial = contract_pair(up_adapter_upper, up_gradient, 0, 0).astype(jnp.bfloat16)
    down_partial = contract_pair(down_adapter_lower, hidden_units, 1, 0).astype(jnp.bfloat16)
    paired_partials = jnp.concatenate([gate_partial, up_partial], 0)
    paired_factors = jnp.concatenate([a_gate, a_up], 0)
    gradient_rows_out = (
        contract_pair(gate_gradient, gate_weight, 0, 0)
        + contract_pair(up_gradient, up_weight, 0, 0)
        + ADAPTER_SCALE * contract_pair(paired_partials, paired_factors, 0, 0)
    )
    shared_slice = (
        ADAPTER_SCALE * contract_pair(gate_partial, input_rows, 1, 0),
        ADAPTER_SCALE * contract_pair(up_partial, input_rows, 1, 0),
        ADAPTER_SCALE * contract_pair(output_gradient_rows, down_partial, 0, 1),
    )
    owned_slice = (
        ADAPTER_SCALE * contract_pair(gate_gradient, gate_projected_lower, 1, 1),
        ADAPTER_SCALE * contract_pair(up_gradient, up_projected_lower, 1, 1),
        ADAPTER_SCALE * contract_pair(down_projected_lower, hidden_units, 1, 1),
    )
    return (gradient_rows_out, shared_slice, owned_slice)


def general_local(
    tokens,
    output_gradient,
    routing,
    router_gate_values,
    gate_weight,
    up_weight,
    down_weight,
    adapter_lower_gate,
    adapter_upper_gate,
    adapter_lower_up,
    adapter_upper_up,
    adapter_lower_down,
    adapter_upper_down,
):
    experts = lax.axis_size("expert")
    shards = lax.axis_size("dp")
    tok_local, feat_local = tokens.shape
    choose = routing.shape[1]
    complete_width = feat_local * experts
    capacity = min(tok_local, 6 * tok_local // experts)
    hidden_units_local = gate_weight.shape[1]
    adapter_rank = adapter_lower_gate.shape[1]
    params = (
        gate_weight[0],
        up_weight[0],
        down_weight[0],
        adapter_lower_gate[0],
        adapter_upper_gate[0],
        adapter_lower_up[0],
        adapter_upper_up[0],
        adapter_lower_down[0],
        adapter_upper_down[0],
    )
    positions = slot_numbers(routing, experts)
    zero_row = jnp.zeros((1, feat_local), jnp.bfloat16)
    initial = (
        jnp.zeros((shards * capacity, complete_width), jnp.float32),
        (
            jnp.zeros((adapter_rank, complete_width), jnp.float32),
            jnp.zeros((adapter_rank, complete_width), jnp.float32),
            jnp.zeros((complete_width, adapter_rank), jnp.float32),
        ),
        (
            jnp.zeros((hidden_units_local, adapter_rank), jnp.float32),
            jnp.zeros((hidden_units_local, adapter_rank), jnp.float32),
            jnp.zeros((adapter_rank, hidden_units_local), jnp.float32),
        ),
    )
    source, member = slot_sources(routing, positions, experts, capacity)
    clamped = jnp.minimum(source, tok_local - 1)
    slot_gate = jnp.where(
        source < tok_local, router_gate_values.reshape(-1)[clamped * choose + member], 0.0
    )
    send_x = jnp.concatenate([tokens, zero_row], 0)[source].reshape(experts, capacity, feat_local)
    send_dy = (
        (
            slot_gate[:, None]
            * jnp.concatenate([output_gradient, zero_row], 0)[source].astype(jnp.float32)
        )
        .astype(jnp.bfloat16)
        .reshape(experts, capacity, feat_local)
    )
    recv_x, recv_dy = (
        lax.all_to_all(send_x, "expert", split_axis=0, concat_axis=2, tiled=True),
        lax.all_to_all(send_dy, "expert", split_axis=0, concat_axis=2, tiled=True),
    )
    gradient_rows_out, shared_slice, owned_slice = rows_backward_pass(
        lax.all_gather(recv_x[0], "dp", axis=0, tiled=True),
        lax.all_gather(recv_dy[0], "dp", axis=0, tiled=True),
        params,
    )
    rows_part = gradient_rows_out
    totals = (
        rows_part,
        jax.tree.map(jnp.add, initial[1], shared_slice),
        jax.tree.map(jnp.add, initial[2], owned_slice),
    )
    rows_part, shared_slice, owned_slice = totals
    summed = lax.psum_scatter(
        rows_part.astype(jnp.bfloat16), "dp", scatter_dimension=0, tiled=True
    ).astype(jnp.float32)
    returned_rows = lax.all_to_all(
        summed.reshape(capacity, experts, feat_local).astype(jnp.bfloat16),
        "expert",
        split_axis=1,
        concat_axis=1,
        tiled=True,
    ).astype(jnp.float32)
    lookup = positions * experts + routing
    grad_x = jnp.sum(returned_rows.reshape(capacity * experts, feat_local)[lookup], axis=1).astype(
        jnp.bfloat16
    )
    grad_a_gate, grad_a_up, grad_b_down = (
        lax.psum(shared_slice[0].astype(jnp.bfloat16), "dp").astype(jnp.float32),
        lax.psum(shared_slice[1].astype(jnp.bfloat16), "dp").astype(jnp.float32),
        lax.psum(shared_slice[2].astype(jnp.bfloat16), "dp").astype(jnp.float32),
    )
    return (
        grad_x,
        grad_a_gate[None],
        owned_slice[0][None],
        grad_a_up[None],
        owned_slice[1][None],
        owned_slice[2][None],
        grad_b_down[None],
    )


LANES = 128
TILE = 512
SHARDS = 8
VMEM_BYTES = 58 * 1024 * 1024
HIDDEN_BYTES = 58 * 1024 * 1024
TERM_BYTES = 32 * 1024 * 1024
HBM = pl.BlockSpec(memory_space=pl.ANY)
PINNED = pl.BlockSpec(memory_space=pltpu.HBM)
VMEM = pl.BlockSpec(memory_space=pltpu.VMEM)
SMEM = pl.BlockSpec(memory_space=pltpu.SMEM)


def dot_nt(left, right):
    return contract_pair(left, right, 1, 1)


def dot_nn(left, right):
    return contract_pair(left, right, 1, 0)


def wide(value):
    return value.astype(jnp.float32)


class Rows:
    def __init__(self):
        self.arrays, self.places = [], []

    def add(self, array, *places):
        self.arrays.append(array)
        self.places.append(places)


def row_copies(refs, places, target, sems, slab, order=None):
    tokens_each = refs[0].shape[-2]
    copies = []
    for ref, parts in zip(refs, places):
        for i, (at, block) in enumerate(parts):
            if at != slab:
                continue
            source = ref.at[i] if len(ref.shape) == 3 else ref
            row = block * tokens_each
            if order is not None:
                row = pl.multiple_of(order[block] * tokens_each, tokens_each)
            copies.append(
                pltpu.make_async_copy(
                    source, target.at[slab, pl.ds(row, tokens_each)], sems.at[slab, block]
                )
            )
    return copies


def slab_lanes(slab_ref, slab, feat):
    return pl.ds(pl.multiple_of(slab_ref[slab] * feat, feat), feat)


def forward_kernel(places, *refs):
    n_pieces = len(places)
    pieces = refs[:n_pieces]
    (
        slab_ref,
        gate_hbm,
        up_hbm,
        lower_hbm,
        gate_upper_ref,
        up_upper_ref,
        silu_out,
        slope_out,
        hidden_out,
        low_out,
    ) = refs[n_pieces : n_pieces + 10]
    x_rows, weights, pre, saved, x_sems, w_sems, out_sems = refs[n_pieces + 10 :]
    slabs, _, feat = x_rows.shape
    hidden_here = gate_hbm.shape[0]
    pair, rank = lower_hbm.shape[1], gate_upper_ref.shape[1]

    def x_slab(slab):
        return row_copies(pieces, places, x_rows, x_sems, slab)

    def weight_copies(slab):
        lanes = slab_lanes(slab_ref, slab, feat)
        sides = (
            (gate_hbm.at[:, lanes], 0, hidden_here),
            (up_hbm.at[:, lanes], hidden_here, hidden_here),
            (lower_hbm.at[slab], 2 * hidden_here, pair),
        )
        return [
            pltpu.make_async_copy(
                source, weights.at[slab, pl.ds(start, size)], w_sems.at[slab, i]
            )
            for i, (source, start, size) in enumerate(sides)
        ]

    for slab in range(slabs):
        for copy in x_slab(slab) + weight_copies(slab):
            copy.start()
    for slab in range(slabs):
        for copy in x_slab(slab) + weight_copies(slab):
            copy.wait()
        if slab == 0:
            pre[...] = dot_nt(weights[0], x_rows[0])
        else:
            pre[...] += dot_nt(weights[slab], x_rows[slab])
    low_out[...] = pre[2 * hidden_here :, :].astype(jnp.bfloat16)

    def out_copies(tile):
        at = pl.ds(pl.multiple_of(tile * LANES, LANES), LANES)
        return [
            pltpu.make_async_copy(saved.at[i, at], out.at[at], out_sems.at[i, tile])
            for i, out in enumerate((silu_out, slope_out, hidden_out))
        ]

    tiles = hidden_here // LANES

    @pl.loop(0, tiles)
    def _(tile):
        start = pl.multiple_of(tile * LANES, LANES)
        at = pl.ds(start, LANES)
        up_at = pl.ds(pl.multiple_of(hidden_here + start, LANES), LANES)
        pre_gate = pre[at, :] + ADAPTER_SCALE * dot_nn(gate_upper_ref[at, :], low_out[:rank, :])
        pre_up = pre[up_at, :] + ADAPTER_SCALE * dot_nn(up_upper_ref[at, :], low_out[rank:, :])
        sigma = 1.0 / (1.0 + jnp.exp(-pre_gate))
        silu = pre_gate * sigma
        saved[0, at, :] = silu.astype(jnp.bfloat16)
        saved[1, at, :] = (pre_up * (sigma * (1.0 + pre_gate * (1.0 - sigma)))).astype(
            jnp.bfloat16
        )
        saved[2, at, :] = (silu * pre_up).astype(jnp.bfloat16)
        for copy in out_copies(tile):
            copy.start()

    @pl.loop(0, tiles)
    def _(tile):
        for copy in out_copies(tile):
            copy.wait()


def forward_rows(x, slab_order, weights, lower_slabs, gate_upper, up_upper):
    hidden_here, width = weights[0].shape
    tokens_each, feat = x.arrays[0].shape[-2:]
    rows = SHARDS * tokens_each
    slabs, pair, _ = lower_slabs.shape
    kept = jax.ShapeDtypeStruct((hidden_here, rows), jnp.bfloat16)
    return pl.pallas_call(
        lambda *refs: forward_kernel(x.places, *refs),
        out_shape=(kept, kept, kept, jax.ShapeDtypeStruct((pair, rows), jnp.bfloat16)),
        in_specs=[HBM] * len(x.arrays) + [SMEM] + [HBM] * 3 + [VMEM] * 2,
        out_specs=(HBM, HBM, HBM, VMEM),
        scratch_shapes=[
            pltpu.VMEM((slabs, rows, feat), jnp.bfloat16),
            pltpu.VMEM((slabs, 2 * hidden_here + pair, feat), jnp.bfloat16),
            pltpu.VMEM((2 * hidden_here + pair, rows), jnp.float32),
            pltpu.VMEM((3, hidden_here, rows), jnp.bfloat16),
            pltpu.SemaphoreType.DMA((slabs, SHARDS)),
            pltpu.SemaphoreType.DMA((slabs, 3)),
            pltpu.SemaphoreType.DMA((3, hidden_here // LANES)),
        ],
        compiler_params=pltpu.CompilerParams(vmem_limit_bytes=VMEM_BYTES),
        cost_estimate=pl.CostEstimate(
            flops=8 * rows * hidden_here * width,
            bytes_accessed=4 * hidden_here * width + 2 * rows * width,
            transcendentals=rows * hidden_here,
        ),
        name="forward_rows",
    )(*x.arrays, slab_order, *weights[:2], lower_slabs, gate_upper, up_upper)


def hidden_kernel(places, *refs):
    n_pieces = len(places)
    pieces = refs[:n_pieces]
    (
        slab_ref,
        route_ref,
        down_hbm,
        down_upper_hbm,
        down_lower_ref,
        down_lower_t_ref,
        gate_upper_ref,
        up_upper_ref,
        silu_hbm,
        slope_hbm,
        hidden_hbm,
        d_pair,
        parts_out,
        low_down,
        rows,
        down_w,
        d_down,
        silu,
        slope,
        hidden,
        row_sems,
        d_sems,
        f_sems,
    ) = refs[n_pieces:]
    slabs, _, feat = rows.shape
    hidden_here = silu.shape[0]
    rank = down_lower_ref.shape[0]
    saved_copies = [
        pltpu.make_async_copy(source, target, f_sems.at[i])
        for i, (source, target) in enumerate(
            ((silu_hbm, silu), (slope_hbm, slope), (hidden_hbm, hidden))
        )
    ]

    def slab_copies(slab):
        return row_copies(pieces, places, rows, row_sems, slab) + [
            pltpu.make_async_copy(
                down_hbm.at[:, slab_lanes(slab_ref, slab, feat)],
                down_w.at[slab, pl.ds(0, hidden_here)],
                d_sems.at[slab, 0],
            ),
            pltpu.make_async_copy(
                down_upper_hbm.at[slab], down_w.at[slab, pl.ds(hidden_here, rank)], d_sems.at[slab, 1]
            ),
        ]

    for slab in range(slabs):
        for copy in slab_copies(slab):
            copy.start()
    for copy in saved_copies:
        copy.start()
    for slab in range(slabs):
        for copy in slab_copies(slab):
            copy.wait()
        if slab == 0:
            d_down[...] = dot_nt(down_w[0], rows[0])
        else:
            d_down[...] += dot_nt(down_w[slab], rows[slab])

    low_down[...] = (d_down[hidden_here:, :] * route_ref[...]).astype(jnp.bfloat16)
    for copy in saved_copies:
        copy.wait()

    @pl.loop(0, hidden_here // LANES)
    def _(tile):
        start = pl.multiple_of(tile * LANES, LANES)
        at = pl.ds(start, LANES)
        up_at = pl.ds(pl.multiple_of(hidden_here + start, LANES), LANES)
        d_hidden = d_down[at, :] * route_ref[...]
        d_hidden = d_hidden + ADAPTER_SCALE * dot_nn(down_lower_t_ref[at, :], low_down[...])
        d_gate = (d_hidden * wide(slope[at, :])).astype(jnp.bfloat16)
        d_up = (d_hidden * wide(silu[at, :])).astype(jnp.bfloat16)
        d_pair[:, at] = d_gate.T
        d_pair[:, up_at] = d_up.T

    for side, factor in enumerate((gate_upper_ref, up_upper_ref)):
        start = side * hidden_here
        part = dot_nn(d_pair[:, start : start + hidden_here], factor[...])
        parts_out[side * rank : (side + 1) * rank, :] = part.T
        at = 2 * hidden_here + side * rank
        d_pair[:, at : at + rank] = ADAPTER_SCALE * part.astype(jnp.bfloat16)
    parts_out[2 * rank :, :] = dot_nn(down_lower_ref[...], hidden[...])


def hidden_gradients(dy, slab_order, route_row, down_weight, down_upper, factors, saved):
    hidden_here, width = down_weight.shape
    slabs, rank, feat = down_upper.shape
    pair = 2 * rank
    rows = route_row.shape[1]
    return pl.pallas_call(
        lambda *refs: hidden_kernel(dy.places, *refs),
        out_shape=(
            jax.ShapeDtypeStruct((rows, 2 * hidden_here + pair), jnp.bfloat16),
            jax.ShapeDtypeStruct((3 * rank, rows), jnp.float32),
            jax.ShapeDtypeStruct((rank, rows), jnp.bfloat16),
        ),
        in_specs=[HBM] * len(dy.arrays) + [SMEM, VMEM] + [HBM] * 2 + [VMEM] * 4 + [HBM] * 3,
        out_specs=(VMEM,) * 3,
        scratch_shapes=[
            pltpu.VMEM((slabs, rows, feat), jnp.bfloat16),
            pltpu.VMEM((slabs, hidden_here + rank, feat), jnp.bfloat16),
            pltpu.VMEM((hidden_here + rank, rows), jnp.float32),
            pltpu.VMEM((hidden_here, rows), jnp.bfloat16),
            pltpu.VMEM((hidden_here, rows), jnp.bfloat16),
            pltpu.VMEM((hidden_here, rows), jnp.bfloat16),
            pltpu.SemaphoreType.DMA((slabs, SHARDS)),
            pltpu.SemaphoreType.DMA((slabs, 2)),
            pltpu.SemaphoreType.DMA((3,)),
        ],
        compiler_params=pltpu.CompilerParams(vmem_limit_bytes=HIDDEN_BYTES),
        cost_estimate=pl.CostEstimate(
            flops=4 * rows * hidden_here * width,
            bytes_accessed=2 * hidden_here * width + 2 * rows * width,
            transcendentals=0,
        ),
        name="hidden_gradients",
    )(*dy.arrays, slab_order, route_row, down_weight, down_upper, *factors, *saved)


def term_kernel(
    slab, slab_ref, d_pair, gate_hbm, up_hbm, lower_hbm, keep_out, pass_out, pair_w, sems
):
    _, depth, step = pair_w.shape
    hidden_here = gate_hbm.shape[0]
    pair = depth - 2 * hidden_here
    tokens_each = keep_out.shape[1]
    feat = keep_out.shape[2]
    steps = feat // step

    def weight_copies(n):
        lanes = pl.ds(pl.multiple_of(slab_ref[slab] * feat + n * step, step), step)
        sides = (
            (gate_hbm.at[:, lanes], 0, hidden_here),
            (up_hbm.at[:, lanes], hidden_here, hidden_here),
            (lower_hbm.at[slab, :, pl.ds(pl.multiple_of(n * step, step), step)], 2 * hidden_here, pair),
        )
        return [
            pltpu.make_async_copy(source, pair_w.at[n, pl.ds(start, size)], sems.at[n, i])
            for i, (source, start, size) in enumerate(sides)
        ]

    for n in range(steps):
        for copy in weight_copies(n):
            copy.start()

    @pl.loop(0, steps)
    def _(n):
        for copy in weight_copies(n):
            copy.wait()
        lanes = pl.ds(pl.multiple_of(n * step, step), step)
        term = dot_nn(d_pair[...], pair_w[n]).astype(jnp.bfloat16)
        for block in range(SHARDS):
            out = pass_out if block % 2 else keep_out
            out[block // 2, :, lanes] = term[block * tokens_each : (block + 1) * tokens_each]


def slab_terms(slab, slab_order, d_pair, weights, lower_slabs):
    rows, depth = d_pair.shape
    feat = lower_slabs.shape[2]
    term = jax.ShapeDtypeStruct((SHARDS // 2, rows // SHARDS, feat), jnp.bfloat16)
    return pl.pallas_call(
        lambda *refs: term_kernel(slab, *refs),
        out_shape=(term, term),
        in_specs=[SMEM, VMEM] + [PINNED] * 3,
        out_specs=(VMEM, VMEM),
        scratch_shapes=[
            pltpu.VMEM((feat // TILE, depth, TILE), jnp.bfloat16),
            pltpu.SemaphoreType.DMA((feat // TILE, 3)),
        ],
        compiler_params=pltpu.CompilerParams(vmem_limit_bytes=TERM_BYTES),
        cost_estimate=pl.CostEstimate(
            flops=4 * rows * depth * feat,
            bytes_accessed=2 * depth * feat + 4 * rows * depth,
            transcendentals=0,
        ),
        name="slab_terms",
    )(slab_order, d_pair, *weights[:2], lower_slabs)


def shared_kernel(x_places, dy_places, *refs):
    split, inputs = len(x_places), len(x_places) + len(dy_places)
    x_pieces, dy_pieces = refs[:split], refs[split:inputs]
    (
        order_ref,
        slab_ref,
        sums_ref,
        down_sums_ref,
        low_ref,
        low_down_ref,
        d_pair,
        hidden,
        pair_out,
        down_out,
        owned_out,
        owned_down_out,
    ) = refs[inputs : inputs + 12]
    x_rows, dy_rows, sums, down_sums, x_sems, dy_sems = refs[inputs + 12 :]
    hidden_here, rank = hidden.shape[0], low_down_ref.shape[0]
    slabs, _, feat = x_rows.shape
    tokens_each = x_pieces[0].shape[-2]

    def slab_copies(slab):
        return row_copies(x_pieces, x_places, x_rows, x_sems, slab, order_ref) + row_copies(
            dy_pieces, dy_places, dy_rows, dy_sems, slab, order_ref
        )

    for slab in range(slabs):
        for copy in slab_copies(slab):
            copy.start()
    for block in range(SHARDS):
        lanes = pl.ds(pl.multiple_of(order_ref[block] * tokens_each, tokens_each), tokens_each)
        sums[:, lanes] = sums_ref[block]
        down_sums[:, lanes] = down_sums_ref[block]
    owned_out[0] = ADAPTER_SCALE * dot_nn(low_ref[:rank, :], d_pair[:, :hidden_here])
    owned_out[1] = ADAPTER_SCALE * dot_nn(low_ref[rank:, :], d_pair[:, hidden_here : 2 * hidden_here])
    owned_down_out[...] = ADAPTER_SCALE * dot_nt(low_down_ref[...], hidden[...])
    for slab in range(slabs):
        for copy in slab_copies(slab):
            copy.wait()

        @pl.loop(0, feat // TILE)
        def _(n):
            lanes = pl.ds(pl.multiple_of(n * TILE, TILE), TILE)
            out = pl.ds(pl.multiple_of(slab_ref[slab] * feat + n * TILE, TILE), TILE)
            pair_out[:, out] = ADAPTER_SCALE * dot_nn(
                sums[...].astype(jnp.bfloat16), x_rows[slab, :, lanes]
            )
            down_out[:, out] = ADAPTER_SCALE * dot_nn(
                down_sums[...].astype(jnp.bfloat16), dy_rows[slab, :, lanes]
            )


def adapter_gradients(x, dy, order, slab_order, sums, down_sums, low, low_down, d_pair, hidden):
    tokens_each, feat = x.arrays[0].shape[-2:]
    slabs = slab_order.shape[0]
    rows = SHARDS * tokens_each
    pair, rank = sums.shape[1], down_sums.shape[1]
    hidden_here = hidden.shape[0]
    return pl.pallas_call(
        lambda *refs: shared_kernel(x.places, dy.places, *refs),
        out_shape=(
            jax.ShapeDtypeStruct((pair, slabs * feat), jnp.float32),
            jax.ShapeDtypeStruct((rank, slabs * feat), jnp.float32),
            jax.ShapeDtypeStruct((2, rank, hidden_here), jnp.float32),
            jax.ShapeDtypeStruct((rank, hidden_here), jnp.float32),
        ),
        in_specs=[HBM] * (len(x.arrays) + len(dy.arrays)) + [SMEM, SMEM] + [VMEM] * 6,
        out_specs=(VMEM,) * 4,
        scratch_shapes=[
            pltpu.VMEM((slabs, rows, feat), jnp.bfloat16),
            pltpu.VMEM((slabs, rows, feat), jnp.bfloat16),
            pltpu.VMEM((pair, rows), jnp.float32),
            pltpu.VMEM((rank, rows), jnp.float32),
            pltpu.SemaphoreType.DMA((slabs, SHARDS)),
            pltpu.SemaphoreType.DMA((slabs, SHARDS)),
        ],
        compiler_params=pltpu.CompilerParams(vmem_limit_bytes=VMEM_BYTES),
        cost_estimate=pl.CostEstimate(
            flops=16 * rows * pair * slabs * feat,
            bytes_accessed=4 * rows * slabs * feat,
            transcendentals=0,
        ),
        name="adapter_gradients",
    )(
        *x.arrays,
        *dy.arrays,
        order,
        slab_order,
        sums,
        down_sums,
        low,
        low_down,
        d_pair,
        hidden,
    )


CORE, ACROSS, ALONG = 1, 2, 4
PLANE = (ACROSS, ALONG, ACROSS | ALONG)


def swap(value, bit, axis="dp"):
    return lax.ppermute(value, axis, [(i, i ^ bit) for i in range(lax.axis_size(axis))])


def after(value, *others):
    return lax.optimization_barrier((value, others))[0]


def added(left, right):
    return (wide(left) + wide(right)).astype(jnp.bfloat16)


def local(
    tokens,
    output_gradient,
    routing,
    router_gate_values,
    gate_weight,
    up_weight,
    down_weight,
    adapter_lower_gate,
    adapter_upper_gate,
    adapter_lower_up,
    adapter_upper_up,
    adapter_lower_down,
    adapter_upper_down,
):
    experts = lax.axis_size("expert")
    me, expert = lax.axis_index("dp"), lax.axis_index("expert")
    tokens_each, feat = tokens.shape
    rank = adapter_lower_gate.shape[1]
    order = jnp.bitwise_xor(jnp.arange(SHARDS, dtype=jnp.int32), me.astype(jnp.int32))
    slab_order = jnp.bitwise_xor(jnp.arange(experts, dtype=jnp.int32), expert.astype(jnp.int32))

    named = routing[:, :, None] == jnp.arange(experts, dtype=jnp.int32)[None, None, :]
    weight_of = jnp.sum(jnp.where(named, router_gate_values[:, :, None], 0.0), axis=1)
    routes = lax.all_gather(weight_of.T, "dp", axis=0, tiled=False)
    route = lax.dynamic_index_in_dim(routes, expert, axis=1, keepdims=False)[order]
    route_row = route.reshape(1, SHARDS * tokens_each)

    def slabs_first(factor):
        return factor.reshape(factor.shape[0], experts, feat).transpose(1, 0, 2)[slab_order]

    lower_cat = jnp.concatenate([adapter_lower_gate[0], adapter_lower_up[0]], axis=0)
    down_lower = adapter_lower_down[0]

    def place_both(rows, part, swapped, chip, slabs):
        rows.add(part, *((r, 2 * chip) for r in slabs))
        rows.add(swapped, *((r, 2 * chip + 1) for r in slabs))

    def over_experts(block, r):
        return swap(block, r, "expert")

    both = over_experts(jnp.stack([tokens, output_gradient]), 1)
    x_slabs = [both[0]] + [over_experts(tokens, r) for r in range(2, experts)]
    x_near = [tokens] + [swap(tokens, bit) for bit in PLANE[:2]]
    (x_slabs, x_near, dy_near), small = lax.optimization_barrier(
        ((x_slabs, x_near, both[1]), (route_row, adapter_upper_down[0], lower_cat))
    )
    route_row, down_upper, lower_cat = small
    lower_slabs, down_upper = slabs_first(lower_cat), slabs_first(down_upper.T)
    ready = (lower_slabs, down_upper, down_lower, down_lower.T)

    x_rest = [jnp.stack(x_slabs)]
    x_rest += [swap(x_rest[0], bit) for bit in PLANE[:2]]
    x_near.append(swap(x_near[2], ACROSS))
    dy_late = after(output_gradient, x_rest[0])
    dy_slabs = [output_gradient, dy_near] + [over_experts(dy_late, r) for r in range(2, experts)]

    (x_rest, x_near, dy_slabs), ready = lax.optimization_barrier(
        ((x_rest, x_near, dy_slabs), ready)
    )
    lower_slabs, down_upper, down_lower, down_lower_t = ready
    factors = (down_lower, down_lower_t, adapter_upper_gate[0], adapter_upper_up[0])
    x_far = [swap(x_rest[2][:1], ACROSS), swap(x_rest[1][1:], ALONG)]
    x_near_swapped = swap(jnp.stack(x_near), CORE)
    x_rest_swapped = [swap(part, CORE) for part in x_rest[:2]]

    early = (x_far, x_rest[2], x_near_swapped, x_rest_swapped, jnp.stack(dy_slabs))
    x_far, x_late, x_near_swapped, x_rest_swapped, dy_all = lax.optimization_barrier(early)
    x_rest_swapped.append(swap(x_late, CORE))
    x_far_swapped = [swap(part, CORE) for part in x_far]
    dy_plane = [swap(dy_all, bit) for bit in PLANE[:2]]

    x = Rows()
    for chip, part in enumerate(x_near):
        x.add(part, (0, 2 * chip))
    x.add(x_near_swapped, *((0, 2 * chip + 1) for chip in range(len(x_near))))
    for chip, (part, swapped) in enumerate(zip(x_rest, x_rest_swapped)):
        place_both(x, part, swapped, chip, range(1, experts))
    for part, swapped, slabs in zip(x_far, x_far_swapped, (range(1, 2), range(2, experts))):
        place_both(x, part, swapped, len(x_rest), slabs)

    weights = (gate_weight[0], up_weight[0], down_weight[0])
    saved = forward_rows(
        x, slab_order, weights, lower_slabs, adapter_upper_gate[0], adapter_upper_up[0]
    )
    dy_rows = [dy_all, *after(dy_plane, saved[0])]
    half = experts // 2
    dy_far = [swap(dy_rows[2][:half], ACROSS), swap(dy_rows[1][half:], ALONG)]
    dy_swapped = [swap(part, CORE) for part in dy_rows]
    dy_far, dy_swapped = lax.optimization_barrier((dy_far, dy_swapped))
    dy = Rows()
    for chip, (part, swapped) in enumerate(zip(dy_rows, dy_swapped)):
        place_both(dy, part, swapped, chip, range(experts))
    for part, slabs in zip(dy_far, (range(half), range(half, experts))):
        place_both(dy, part, swap(part, CORE), len(dy_rows), slabs)
    d_pair, parts, low_down = hidden_gradients(
        dy, slab_order, route_row, weights[2], down_upper, factors, saved[:3]
    )

    def sum_step(total, bit):
        other = swap(total.reshape(SHARDS, 3 * rank, tokens_each), bit)
        shape = (SHARDS // (2 * bit), 2, bit, 3 * rank, tokens_each)
        return total.reshape(shape) + other.reshape(shape)[:, ::-1]

    total = parts.reshape(3 * rank, SHARDS, tokens_each).transpose(1, 0, 2)
    sums = [total]
    for bit in (CORE, ACROSS, ALONG):
        sums.append(sum_step(sums[-1], bit))
    total = sums[-1]
    waits = {1: [sums[1]], 0: [sums[2]]}
    keeps, gots, chips, moved, rows = {}, {}, {}, {}, {}

    def send_chips(r):
        chips[r] = [added(keeps[r][i], gots[r][i]) for i in range(SHARDS // 2)]
        moved[r] = [swap(chip, bit) for bit, chip in zip(PLANE, chips[r][1:])]

    def sum_chips(r):
        rows[r] = sum((wide(part) for part in moved[r]), wide(chips[r][0]))
        if r:
            rows[r] = rows[r].astype(jnp.bfloat16)

    for r in reversed(range(experts)):
        here = waits.get(r, []) + chips.get(r + 2, []) + [rows[k] for k in (r + 3,) if k in rows]
        here = after(slab_order, *here) if here else slab_order
        keeps[r], away = slab_terms(r, here, d_pair, weights, lower_slabs)
        gots[r] = swap(away, CORE)
        if r + 1 in gots:
            gots[r + 1] = after(gots[r + 1], keeps[r])
            send_chips(r + 1)
        if r + 2 in moved:
            moved[r + 2] = after(moved[r + 2], keeps[r])
            sum_chips(r + 2)
    send_chips(0)
    for r in range(min(experts, 2)):
        sum_chips(r)
    grad_x = rows[0]
    for r in range(1, experts):
        grad_x = grad_x + wide(swap(rows[r], r, "expert"))
    grad_x = grad_x.astype(jnp.bfloat16)

    total = after(total.reshape(SHARDS, 3 * rank, tokens_each), *chips[0])
    grad_pair, grad_down, owned, owned_down = adapter_gradients(
        x,
        dy,
        order,
        slab_order,
        total[:, : 2 * rank],
        total[:, 2 * rank :] * route[:, None, :],
        saved[3],
        low_down,
        d_pair,
        saved[2],
    )
    return (
        grad_x,
        grad_pair[None, :rank],
        owned[0].T[None],
        grad_pair[None, rank:],
        owned[1].T[None],
        owned_down[None],
        grad_down.T[None],
    )


def plan(tokens, *others):
    experts, tokens_each, hidden_here = lax.axis_size("expert"), tokens.shape[0], others[3].shape[1]
    planned = (
        lax.axis_size("dp") == SHARDS
        and experts == 4
        and hidden_here % LANES == 0
        and tokens_each % LANES == 0
        and tokens.shape[1] % TILE == 0
    )
    return (local if planned else general_local)(tokens, *others)


def solution(mesh):
    return jax.shard_map(
        plan,
        mesh=mesh,
        in_specs=(
            P("dp", "expert"),
            P("dp", "expert"),
            P("dp", None),
            P("dp", None),
            P("expert", "dp", None),
            P("expert", "dp", None),
            P("expert", "dp", None),
            P("expert", None, None),
            P("expert", "dp", None),
            P("expert", None, None),
            P("expert", "dp", None),
            P("expert", None, "dp"),
            P("expert", None, None),
        ),
        out_specs=(
            P("dp", "expert"),
            P("expert", None, None),
            P("expert", "dp", None),
            P("expert", None, None),
            P("expert", "dp", None),
            P("expert", None, "dp"),
            P("expert", None, None),
        ),
        check_vma=False,
    )
```

```python
import jax
import jax.numpy as jnp
from jax import lax
from jax.experimental import pallas as pl
from jax.experimental.pallas import tpu as pltpu
from jax.sharding import PartitionSpec as P

ADAPTER_SCALE = 2.0


def contract_pair(left, right, left_axis, right_axis):
    return lax.dot_general(
        left, right, (((left_axis,), (right_axis,)), ((), ())), preferred_element_type=jnp.float32
    )


def slot_numbers(route_rows, experts):
    picked = (route_rows[:, :, None] == jnp.arange(experts, dtype=jnp.int32)[None, None, :]).astype(
        jnp.int32
    )
    per_token = jnp.sum(picked, axis=1)
    earlier = jnp.cumsum(per_token, axis=0) - per_token
    return jnp.sum(earlier[:, None, :] * picked, axis=2)


def slot_sources(route_rows, positions, experts, capacity):
    tokens_here, choose = route_rows.shape
    target = (route_rows * capacity + positions).reshape(-1)
    owners = jnp.repeat(jnp.arange(tokens_here, dtype=jnp.int32), choose)
    member_ids = jnp.tile(jnp.arange(choose, dtype=jnp.int32), tokens_here)
    source = jnp.full((experts * capacity,), tokens_here, jnp.int32).at[target].set(owners)
    member = jnp.zeros((experts * capacity,), jnp.int32).at[target].set(member_ids)
    return (source, member)


def rows_backward_pass(input_rows, output_gradient_rows, params):
    (
        gate_weight,
        up_weight,
        down_weight,
        a_gate,
        gate_adapter_upper,
        a_up,
        up_adapter_upper,
        down_adapter_lower,
        b_down,
    ) = params
    gate_projected_lower = contract_pair(a_gate, input_rows, 1, 1).astype(jnp.bfloat16)
    up_projected_lower = contract_pair(a_up, input_rows, 1, 1).astype(jnp.bfloat16)
    gate_preactivation = contract_pair(
        gate_weight, input_rows, 1, 1
    ) + ADAPTER_SCALE * contract_pair(gate_adapter_upper, gate_projected_lower, 1, 0)
    up_preactivation = contract_pair(up_weight, input_rows, 1, 1) + ADAPTER_SCALE * contract_pair(
        up_adapter_upper, up_projected_lower, 1, 0
    )
    sigmoid_gate = jax.nn.sigmoid(gate_preactivation)
    silu_gate = gate_preactivation * sigmoid_gate
    hidden_units = (silu_gate * up_preactivation).astype(jnp.bfloat16)
    down_projected_lower = contract_pair(b_down, output_gradient_rows, 0, 1).astype(jnp.bfloat16)
    hidden_gradient = contract_pair(
        down_weight, output_gradient_rows, 1, 1
    ) + ADAPTER_SCALE * contract_pair(down_adapter_lower, down_projected_lower, 0, 0)
    gate_gradient = (
        hidden_gradient
        * up_preactivation
        * sigmoid_gate
        * (1.0 + gate_preactivation * (1.0 - sigmoid_gate))
    ).astype(jnp.bfloat16)
    up_gradient = (hidden_gradient * silu_gate).astype(jnp.bfloat16)
    gate_partial = contract_pair(gate_adapter_upper, gate_gradient, 0, 0).astype(jnp.bfloat16)
    up_partial = contract_pair(up_adapter_upper, up_gradient, 0, 0).astype(jnp.bfloat16)
    down_partial = contract_pair(down_adapter_lower, hidden_units, 1, 0).astype(jnp.bfloat16)
    paired_partials = jnp.concatenate([gate_partial, up_partial], 0)
    paired_factors = jnp.concatenate([a_gate, a_up], 0)
    gradient_rows_out = (
        contract_pair(gate_gradient, gate_weight, 0, 0)
        + contract_pair(up_gradient, up_weight, 0, 0)
        + ADAPTER_SCALE * contract_pair(paired_partials, paired_factors, 0, 0)
    )
    shared_slice = (
        ADAPTER_SCALE * contract_pair(gate_partial, input_rows, 1, 0),
        ADAPTER_SCALE * contract_pair(up_partial, input_rows, 1, 0),
        ADAPTER_SCALE * contract_pair(output_gradient_rows, down_partial, 0, 1),
    )
    owned_slice = (
        ADAPTER_SCALE * contract_pair(gate_gradient, gate_projected_lower, 1, 1),
        ADAPTER_SCALE * contract_pair(up_gradient, up_projected_lower, 1, 1),
        ADAPTER_SCALE * contract_pair(down_projected_lower, hidden_units, 1, 1),
    )
    return (gradient_rows_out, shared_slice, owned_slice)


def general_local(
    tokens,
    output_gradient,
    routing,
    router_gate_values,
    gate_weight,
    up_weight,
    down_weight,
    adapter_lower_gate,
    adapter_upper_gate,
    adapter_lower_up,
    adapter_upper_up,
    adapter_lower_down,
    adapter_upper_down,
):
    experts = lax.axis_size("expert")
    shards = lax.axis_size("dp")
    tok_local, feat_local = tokens.shape
    choose = routing.shape[1]
    complete_width = feat_local * experts
    capacity = min(tok_local, 6 * tok_local // experts)
    hidden_units_local = gate_weight.shape[1]
    adapter_rank = adapter_lower_gate.shape[1]
    params = (
        gate_weight[0],
        up_weight[0],
        down_weight[0],
        adapter_lower_gate[0],
        adapter_upper_gate[0],
        adapter_lower_up[0],
        adapter_upper_up[0],
        adapter_lower_down[0],
        adapter_upper_down[0],
    )
    positions = slot_numbers(routing, experts)
    zero_row = jnp.zeros((1, feat_local), jnp.bfloat16)
    initial = (
        jnp.zeros((shards * capacity, complete_width), jnp.float32),
        (
            jnp.zeros((adapter_rank, complete_width), jnp.float32),
            jnp.zeros((adapter_rank, complete_width), jnp.float32),
            jnp.zeros((complete_width, adapter_rank), jnp.float32),
        ),
        (
            jnp.zeros((hidden_units_local, adapter_rank), jnp.float32),
            jnp.zeros((hidden_units_local, adapter_rank), jnp.float32),
            jnp.zeros((adapter_rank, hidden_units_local), jnp.float32),
        ),
    )
    source, member = slot_sources(routing, positions, experts, capacity)
    clamped = jnp.minimum(source, tok_local - 1)
    slot_gate = jnp.where(
        source < tok_local, router_gate_values.reshape(-1)[clamped * choose + member], 0.0
    )
    send_x = jnp.concatenate([tokens, zero_row], 0)[source].reshape(experts, capacity, feat_local)
    send_dy = (
        (
            slot_gate[:, None]
            * jnp.concatenate([output_gradient, zero_row], 0)[source].astype(jnp.float32)
        )
        .astype(jnp.bfloat16)
        .reshape(experts, capacity, feat_local)
    )
    recv_x, recv_dy = (
        lax.all_to_all(send_x, "expert", split_axis=0, concat_axis=2, tiled=True),
        lax.all_to_all(send_dy, "expert", split_axis=0, concat_axis=2, tiled=True),
    )
    gradient_rows_out, shared_slice, owned_slice = rows_backward_pass(
        lax.all_gather(recv_x[0], "dp", axis=0, tiled=True),
        lax.all_gather(recv_dy[0], "dp", axis=0, tiled=True),
        params,
    )
    rows_part = gradient_rows_out
    totals = (
        rows_part,
        jax.tree.map(jnp.add, initial[1], shared_slice),
        jax.tree.map(jnp.add, initial[2], owned_slice),
    )
    rows_part, shared_slice, owned_slice = totals
    summed = lax.psum_scatter(
        rows_part.astype(jnp.bfloat16), "dp", scatter_dimension=0, tiled=True
    ).astype(jnp.float32)
    returned_rows = lax.all_to_all(
        summed.reshape(capacity, experts, feat_local).astype(jnp.bfloat16),
        "expert",
        split_axis=1,
        concat_axis=1,
        tiled=True,
    ).astype(jnp.float32)
    lookup = positions * experts + routing
    grad_x = jnp.sum(returned_rows.reshape(capacity * experts, feat_local)[lookup], axis=1).astype(
        jnp.bfloat16
    )
    grad_a_gate, grad_a_up, grad_b_down = (
        lax.psum(shared_slice[0].astype(jnp.bfloat16), "dp").astype(jnp.float32),
        lax.psum(shared_slice[1].astype(jnp.bfloat16), "dp").astype(jnp.float32),
        lax.psum(shared_slice[2].astype(jnp.bfloat16), "dp").astype(jnp.float32),
    )
    return (
        grad_x,
        grad_a_gate[None],
        owned_slice[0][None],
        grad_a_up[None],
        owned_slice[1][None],
        owned_slice[2][None],
        grad_b_down[None],
    )


LANES = 128
TILE = 512
SHARDS = 8
VMEM_BYTES = 58 * 1024 * 1024
HIDDEN_BYTES = 58 * 1024 * 1024
TERM_BYTES = 58 * 1024 * 1024
HBM = pl.BlockSpec(memory_space=pl.ANY)
PINNED = pl.BlockSpec(memory_space=pltpu.HBM)
VMEM = pl.BlockSpec(memory_space=pltpu.VMEM)
SMEM = pl.BlockSpec(memory_space=pltpu.SMEM)


def dot_nt(left, right):
    return contract_pair(left, right, 1, 1)


def dot_nn(left, right):
    return contract_pair(left, right, 1, 0)


def wide(value):
    return value.astype(jnp.float32)


class Rows:
    def __init__(self):
        self.arrays, self.places = [], []

    def add(self, array, *places):
        self.arrays.append(array)
        self.places.append(places)


def row_copies(refs, places, target, sems, slab, order=None):
    tokens_each = refs[0].shape[-2]
    copies = []
    for ref, parts in zip(refs, places):
        for i, (at, block) in enumerate(parts):
            if at != slab:
                continue
            source = ref.at[i] if len(ref.shape) == 3 else ref
            row = block * tokens_each
            if order is not None:
                row = pl.multiple_of(order[block] * tokens_each, tokens_each)
            copies.append(
                pltpu.make_async_copy(
                    source, target.at[slab, pl.ds(row, tokens_each)], sems.at[slab, block]
                )
            )
    return copies


def slab_lanes(slab_ref, slab, feat):
    return pl.ds(pl.multiple_of(slab_ref[slab] * feat, feat), feat)


def forward_kernel(places, *refs):
    n_pieces = len(places)
    pieces = refs[:n_pieces]
    (
        slab_ref,
        gate_hbm,
        up_hbm,
        lower_hbm,
        gate_upper_ref,
        up_upper_ref,
        silu_out,
        slope_out,
        hidden_out,
        low_out,
    ) = refs[n_pieces : n_pieces + 10]
    x_rows, weights, pre, saved, x_sems, w_sems, out_sems = refs[n_pieces + 10 :]
    slabs, _, feat = x_rows.shape
    hidden_here = gate_hbm.shape[0]
    pair, rank = lower_hbm.shape[1], gate_upper_ref.shape[1]

    def x_slab(slab):
        return row_copies(pieces, places, x_rows, x_sems, slab)

    def weight_copies(slab):
        lanes = slab_lanes(slab_ref, slab, feat)
        sides = (
            (gate_hbm.at[:, lanes], 0, hidden_here),
            (up_hbm.at[:, lanes], hidden_here, hidden_here),
            (lower_hbm.at[slab], 2 * hidden_here, pair),
        )
        return [
            pltpu.make_async_copy(
                source, weights.at[slab, pl.ds(start, size)], w_sems.at[slab, i]
            )
            for i, (source, start, size) in enumerate(sides)
        ]

    for slab in range(slabs):
        for copy in x_slab(slab) + weight_copies(slab):
            copy.start()
    for slab in range(slabs):
        for copy in x_slab(slab) + weight_copies(slab):
            copy.wait()
        if slab == 0:
            pre[...] = dot_nt(weights[0], x_rows[0])
        else:
            pre[...] += dot_nt(weights[slab], x_rows[slab])
    low_out[...] = pre[2 * hidden_here :, :].astype(jnp.bfloat16)

    def out_copies(tile):
        at = pl.ds(pl.multiple_of(tile * LANES, LANES), LANES)
        return [
            pltpu.make_async_copy(saved.at[i, at], out.at[at], out_sems.at[i, tile])
            for i, out in enumerate((silu_out, slope_out, hidden_out))
        ]

    tiles = hidden_here // LANES

    @pl.loop(0, tiles)
    def _(tile):
        start = pl.multiple_of(tile * LANES, LANES)
        at = pl.ds(start, LANES)
        up_at = pl.ds(pl.multiple_of(hidden_here + start, LANES), LANES)
        pre_gate = pre[at, :] + ADAPTER_SCALE * dot_nn(gate_upper_ref[at, :], low_out[:rank, :])
        pre_up = pre[up_at, :] + ADAPTER_SCALE * dot_nn(up_upper_ref[at, :], low_out[rank:, :])
        sigma = 1.0 / (1.0 + jnp.exp(-pre_gate))
        silu = pre_gate * sigma
        saved[0, at, :] = silu.astype(jnp.bfloat16)
        saved[1, at, :] = (pre_up * (sigma * (1.0 + pre_gate * (1.0 - sigma)))).astype(
            jnp.bfloat16
        )
        saved[2, at, :] = (silu * pre_up).astype(jnp.bfloat16)
        for copy in out_copies(tile):
            copy.start()

    @pl.loop(0, tiles)
    def _(tile):
        for copy in out_copies(tile):
            copy.wait()


def forward_rows(x, slab_order, weights, lower_slabs, gate_upper, up_upper):
    hidden_here, width = weights[0].shape
    tokens_each, feat = x.arrays[0].shape[-2:]
    rows = SHARDS * tokens_each
    slabs, pair, _ = lower_slabs.shape
    kept = jax.ShapeDtypeStruct((hidden_here, rows), jnp.bfloat16)
    return pl.pallas_call(
        lambda *refs: forward_kernel(x.places, *refs),
        out_shape=(kept, kept, kept, jax.ShapeDtypeStruct((pair, rows), jnp.bfloat16)),
        in_specs=[HBM] * len(x.arrays) + [SMEM] + [HBM] * 3 + [VMEM] * 2,
        out_specs=(HBM, HBM, HBM, VMEM),
        scratch_shapes=[
            pltpu.VMEM((slabs, rows, feat), jnp.bfloat16),
            pltpu.VMEM((slabs, 2 * hidden_here + pair, feat), jnp.bfloat16),
            pltpu.VMEM((2 * hidden_here + pair, rows), jnp.float32),
            pltpu.VMEM((3, hidden_here, rows), jnp.bfloat16),
            pltpu.SemaphoreType.DMA((slabs, SHARDS)),
            pltpu.SemaphoreType.DMA((slabs, 3)),
            pltpu.SemaphoreType.DMA((3, hidden_here // LANES)),
        ],
        compiler_params=pltpu.CompilerParams(vmem_limit_bytes=VMEM_BYTES),
        cost_estimate=pl.CostEstimate(
            flops=8 * rows * hidden_here * width,
            bytes_accessed=4 * hidden_here * width + 2 * rows * width,
            transcendentals=rows * hidden_here,
        ),
        name="forward_rows",
    )(*x.arrays, slab_order, *weights[:2], lower_slabs, gate_upper, up_upper)


def hidden_kernel(places, *refs):
    n_pieces = len(places)
    pieces = refs[:n_pieces]
    (
        slab_ref,
        route_ref,
        down_hbm,
        down_upper_hbm,
        down_lower_ref,
        down_lower_t_ref,
        gate_upper_ref,
        up_upper_ref,
        silu_hbm,
        slope_hbm,
        hidden_hbm,
        d_pair,
        parts_out,
        low_down,
        rows,
        down_w,
        d_down,
        silu,
        slope,
        hidden,
        row_sems,
        d_sems,
        f_sems,
    ) = refs[n_pieces:]
    slabs, _, feat = rows.shape
    hidden_here = silu.shape[0]
    rank = down_lower_ref.shape[0]
    saved_copies = [
        pltpu.make_async_copy(source, target, f_sems.at[i])
        for i, (source, target) in enumerate(
            ((silu_hbm, silu), (slope_hbm, slope), (hidden_hbm, hidden))
        )
    ]

    def slab_copies(slab):
        return row_copies(pieces, places, rows, row_sems, slab) + [
            pltpu.make_async_copy(
                down_hbm.at[:, slab_lanes(slab_ref, slab, feat)],
                down_w.at[slab, pl.ds(0, hidden_here)],
                d_sems.at[slab, 0],
            ),
            pltpu.make_async_copy(
                down_upper_hbm.at[slab], down_w.at[slab, pl.ds(hidden_here, rank)], d_sems.at[slab, 1]
            ),
        ]

    for slab in range(slabs):
        for copy in slab_copies(slab):
            copy.start()
    for copy in saved_copies:
        copy.start()
    for slab in range(slabs):
        for copy in slab_copies(slab):
            copy.wait()
        if slab == 0:
            d_down[...] = dot_nt(down_w[0], rows[0])
        else:
            d_down[...] += dot_nt(down_w[slab], rows[slab])

    low_down[...] = (d_down[hidden_here:, :] * route_ref[...]).astype(jnp.bfloat16)
    for copy in saved_copies:
        copy.wait()

    @pl.loop(0, hidden_here // LANES)
    def _(tile):
        start = pl.multiple_of(tile * LANES, LANES)
        at = pl.ds(start, LANES)
        up_at = pl.ds(pl.multiple_of(hidden_here + start, LANES), LANES)
        d_hidden = d_down[at, :] * route_ref[...]
        d_hidden = d_hidden + ADAPTER_SCALE * dot_nn(down_lower_t_ref[at, :], low_down[...])
        d_gate = (d_hidden * wide(slope[at, :])).astype(jnp.bfloat16)
        d_up = (d_hidden * wide(silu[at, :])).astype(jnp.bfloat16)
        d_pair[:, at] = d_gate.T
        d_pair[:, up_at] = d_up.T

    for side, factor in enumerate((gate_upper_ref, up_upper_ref)):
        start = side * hidden_here
        part = dot_nn(d_pair[:, start : start + hidden_here], factor[...])
        parts_out[side * rank : (side + 1) * rank, :] = part.T
        at = 2 * hidden_here + side * rank
        d_pair[:, at : at + rank] = ADAPTER_SCALE * part.astype(jnp.bfloat16)
    parts_out[2 * rank :, :] = dot_nn(down_lower_ref[...], hidden[...])


def hidden_gradients(dy, slab_order, route_row, down_weight, down_upper, factors, saved):
    hidden_here, width = down_weight.shape
    slabs, rank, feat = down_upper.shape
    pair = 2 * rank
    rows = route_row.shape[1]
    return pl.pallas_call(
        lambda *refs: hidden_kernel(dy.places, *refs),
        out_shape=(
            jax.ShapeDtypeStruct((rows, 2 * hidden_here + pair), jnp.bfloat16),
            jax.ShapeDtypeStruct((3 * rank, rows), jnp.float32),
            jax.ShapeDtypeStruct((rank, rows), jnp.bfloat16),
        ),
        in_specs=[HBM] * len(dy.arrays) + [SMEM, VMEM] + [HBM] * 2 + [VMEM] * 4 + [HBM] * 3,
        out_specs=(VMEM,) * 3,
        scratch_shapes=[
            pltpu.VMEM((slabs, rows, feat), jnp.bfloat16),
            pltpu.VMEM((slabs, hidden_here + rank, feat), jnp.bfloat16),
            pltpu.VMEM((hidden_here + rank, rows), jnp.float32),
            pltpu.VMEM((hidden_here, rows), jnp.bfloat16),
            pltpu.VMEM((hidden_here, rows), jnp.bfloat16),
            pltpu.VMEM((hidden_here, rows), jnp.bfloat16),
            pltpu.SemaphoreType.DMA((slabs, SHARDS)),
            pltpu.SemaphoreType.DMA((slabs, 2)),
            pltpu.SemaphoreType.DMA((3,)),
        ],
        compiler_params=pltpu.CompilerParams(vmem_limit_bytes=HIDDEN_BYTES),
        cost_estimate=pl.CostEstimate(
            flops=4 * rows * hidden_here * width,
            bytes_accessed=2 * hidden_here * width + 2 * rows * width,
            transcendentals=0,
        ),
        name="hidden_gradients",
    )(*dy.arrays, slab_order, route_row, down_weight, down_upper, *factors, *saved)


def term_kernel(
    slabs, slab_ref, d_hbm, gate_hbm, up_hbm, lower_hbm, keep_out, pass_out, d_pair, pair_w, sems, d_sem
):
    _, depth, step = pair_w.shape
    hidden_here = gate_hbm.shape[0]
    pair = depth - 2 * hidden_here
    tokens_each, feat = keep_out.shape[2:]
    steps = feat // step

    def weight_copies(i, n):
        slab, k = slabs[i], i * steps + n
        lanes = pl.ds(pl.multiple_of(slab_ref[slab] * feat + n * step, step), step)
        sides = (
            (gate_hbm.at[:, lanes], 0, hidden_here),
            (up_hbm.at[:, lanes], hidden_here, hidden_here),
            (lower_hbm.at[slab, :, pl.ds(pl.multiple_of(n * step, step), step)], 2 * hidden_here, pair),
        )
        return [
            pltpu.make_async_copy(source, pair_w.at[k, pl.ds(start, size)], sems.at[k, side])
            for side, (source, start, size) in enumerate(sides)
        ]

    d_copy = pltpu.make_async_copy(d_hbm, d_pair, d_sem)
    d_copy.start()
    for i in range(len(slabs)):
        for n in range(steps):
            for copy in weight_copies(i, n):
                copy.start()
    d_copy.wait()
    for i in range(len(slabs)):

        @pl.loop(0, steps)
        def _(n):
            for copy in weight_copies(i, n):
                copy.wait()
            lanes = pl.ds(pl.multiple_of(n * step, step), step)
            term = dot_nn(d_pair[...], pair_w[i * steps + n]).astype(jnp.bfloat16)
            for block in range(SHARDS):
                out = pass_out if block % 2 else keep_out
                out[block // 2, i, :, lanes] = term[block * tokens_each : (block + 1) * tokens_each]


def slab_terms(slabs, slab_order, d_pair, weights, lower_slabs):
    rows, depth = d_pair.shape
    feat = lower_slabs.shape[2]
    parts = len(slabs) * feat // TILE
    term = jax.ShapeDtypeStruct((SHARDS // 2, len(slabs), rows // SHARDS, feat), jnp.bfloat16)
    return pl.pallas_call(
        lambda *refs: term_kernel(slabs, *refs),
        out_shape=(term, term),
        in_specs=[SMEM] + [HBM] * 4,
        out_specs=(VMEM, VMEM),
        scratch_shapes=[
            pltpu.VMEM((rows, depth), jnp.bfloat16),
            pltpu.VMEM((parts, depth, TILE), jnp.bfloat16),
            pltpu.SemaphoreType.DMA((parts, 3)),
            pltpu.SemaphoreType.DMA,
        ],
        compiler_params=pltpu.CompilerParams(vmem_limit_bytes=TERM_BYTES),
        cost_estimate=pl.CostEstimate(
            flops=4 * rows * depth * feat * len(slabs),
            bytes_accessed=2 * depth * feat * len(slabs) + 4 * rows * depth,
            transcendentals=0,
        ),
        name="slab_terms",
    )(slab_order, d_pair, *weights[:2], lower_slabs)


def shared_kernel(x_places, dy_places, *refs):
    split, inputs = len(x_places), len(x_places) + len(dy_places)
    x_pieces, dy_pieces = refs[:split], refs[split:inputs]
    (
        order_ref,
        slab_ref,
        sums_ref,
        down_sums_ref,
        low_ref,
        low_down_ref,
        d_pair,
        hidden,
        pair_out,
        down_out,
        owned_out,
        owned_down_out,
    ) = refs[inputs : inputs + 12]
    x_rows, dy_rows, sums, down_sums, x_sems, dy_sems = refs[inputs + 12 :]
    hidden_here, rank = hidden.shape[0], low_down_ref.shape[0]
    slabs, _, feat = x_rows.shape
    tokens_each = x_pieces[0].shape[-2]

    def slab_copies(slab):
        return row_copies(x_pieces, x_places, x_rows, x_sems, slab, order_ref) + row_copies(
            dy_pieces, dy_places, dy_rows, dy_sems, slab, order_ref
        )

    for slab in range(slabs):
        for copy in slab_copies(slab):
            copy.start()
    for block in range(SHARDS):
        lanes = pl.ds(pl.multiple_of(order_ref[block] * tokens_each, tokens_each), tokens_each)
        sums[:, lanes] = sums_ref[block]
        down_sums[:, lanes] = down_sums_ref[block]
    owned_out[0] = ADAPTER_SCALE * dot_nn(low_ref[:rank, :], d_pair[:, :hidden_here])
    owned_out[1] = ADAPTER_SCALE * dot_nn(low_ref[rank:, :], d_pair[:, hidden_here : 2 * hidden_here])
    owned_down_out[...] = ADAPTER_SCALE * dot_nt(low_down_ref[...], hidden[...])
    for slab in range(slabs):
        for copy in slab_copies(slab):
            copy.wait()

        @pl.loop(0, feat // TILE)
        def _(n):
            lanes = pl.ds(pl.multiple_of(n * TILE, TILE), TILE)
            out = pl.ds(pl.multiple_of(slab_ref[slab] * feat + n * TILE, TILE), TILE)
            pair_out[:, out] = ADAPTER_SCALE * dot_nn(
                sums[...].astype(jnp.bfloat16), x_rows[slab, :, lanes]
            )
            down_out[:, out] = ADAPTER_SCALE * dot_nn(
                down_sums[...].astype(jnp.bfloat16), dy_rows[slab, :, lanes]
            )


def adapter_gradients(x, dy, order, slab_order, sums, down_sums, low, low_down, d_pair, hidden):
    tokens_each, feat = x.arrays[0].shape[-2:]
    slabs = slab_order.shape[0]
    rows = SHARDS * tokens_each
    pair, rank = sums.shape[1], down_sums.shape[1]
    hidden_here = hidden.shape[0]
    return pl.pallas_call(
        lambda *refs: shared_kernel(x.places, dy.places, *refs),
        out_shape=(
            jax.ShapeDtypeStruct((pair, slabs * feat), jnp.float32),
            jax.ShapeDtypeStruct((rank, slabs * feat), jnp.float32),
            jax.ShapeDtypeStruct((2, rank, hidden_here), jnp.float32),
            jax.ShapeDtypeStruct((rank, hidden_here), jnp.float32),
        ),
        in_specs=[HBM] * (len(x.arrays) + len(dy.arrays)) + [SMEM, SMEM] + [VMEM] * 6,
        out_specs=(VMEM,) * 4,
        scratch_shapes=[
            pltpu.VMEM((slabs, rows, feat), jnp.bfloat16),
            pltpu.VMEM((slabs, rows, feat), jnp.bfloat16),
            pltpu.VMEM((pair, rows), jnp.float32),
            pltpu.VMEM((rank, rows), jnp.float32),
            pltpu.SemaphoreType.DMA((slabs, SHARDS)),
            pltpu.SemaphoreType.DMA((slabs, SHARDS)),
        ],
        compiler_params=pltpu.CompilerParams(vmem_limit_bytes=VMEM_BYTES),
        cost_estimate=pl.CostEstimate(
            flops=16 * rows * pair * slabs * feat,
            bytes_accessed=4 * rows * slabs * feat,
            transcendentals=0,
        ),
        name="adapter_gradients",
    )(
        *x.arrays,
        *dy.arrays,
        order,
        slab_order,
        sums,
        down_sums,
        low,
        low_down,
        d_pair,
        hidden,
    )


CORE, ACROSS, ALONG = 1, 2, 4
PLANE = (ACROSS, ALONG, ACROSS | ALONG)


def swap(value, bit, axis="dp"):
    return lax.ppermute(value, axis, [(i, i ^ bit) for i in range(lax.axis_size(axis))])


def after(value, *others):
    return lax.optimization_barrier((value, others))[0]


def added(left, right):
    return (wide(left) + wide(right)).astype(jnp.bfloat16)


def local(
    tokens,
    output_gradient,
    routing,
    router_gate_values,
    gate_weight,
    up_weight,
    down_weight,
    adapter_lower_gate,
    adapter_upper_gate,
    adapter_lower_up,
    adapter_upper_up,
    adapter_lower_down,
    adapter_upper_down,
):
    experts = lax.axis_size("expert")
    me, expert = lax.axis_index("dp"), lax.axis_index("expert")
    tokens_each, feat = tokens.shape
    rank = adapter_lower_gate.shape[1]
    order = jnp.bitwise_xor(jnp.arange(SHARDS, dtype=jnp.int32), me.astype(jnp.int32))
    slab_order = jnp.bitwise_xor(jnp.arange(experts, dtype=jnp.int32), expert.astype(jnp.int32))

    named = routing[:, :, None] == jnp.arange(experts, dtype=jnp.int32)[None, None, :]
    weight_of = jnp.sum(jnp.where(named, router_gate_values[:, :, None], 0.0), axis=1)
    routes = lax.all_gather(weight_of.T, "dp", axis=0, tiled=False)
    route = lax.dynamic_index_in_dim(routes, expert, axis=1, keepdims=False)[order]
    route_blocks = route[:, None, :]
    route_row = route.reshape(1, SHARDS * tokens_each)

    def slabs_first(factor):
        return factor.reshape(factor.shape[0], experts, feat).transpose(1, 0, 2)[slab_order]

    lower_cat = jnp.concatenate([adapter_lower_gate[0], adapter_lower_up[0]], axis=0)
    down_lower = adapter_lower_down[0]

    def place_both(rows, part, swapped, chip, slabs):
        rows.add(part, *((r, 2 * chip) for r in slabs))
        rows.add(swapped, *((r, 2 * chip + 1) for r in slabs))

    def over_experts(block, r):
        return swap(block, r, "expert")

    both = over_experts(jnp.stack([tokens, output_gradient]), 1)
    x_slabs = [both[0]] + [over_experts(tokens, r) for r in range(2, experts)]
    x_near = [tokens] + [swap(tokens, bit) for bit in PLANE[:2]]
    (x_slabs, x_near, dy_near), small = lax.optimization_barrier(
        ((x_slabs, x_near, both[1]), (route_row, adapter_upper_down[0], lower_cat))
    )
    route_row, down_upper, lower_cat = small
    lower_slabs, down_upper = slabs_first(lower_cat), slabs_first(down_upper.T)
    ready = (lower_slabs, down_upper, down_lower, down_lower.T)

    x_rest = [jnp.stack(x_slabs)]
    x_rest += [swap(x_rest[0], bit) for bit in PLANE[:2]]
    x_near.append(swap(x_near[2], ACROSS))
    dy_slabs = [output_gradient, dy_near, over_experts(after(output_gradient, x_rest[0]), 2)]

    (x_rest, x_near, dy_slabs), ready = lax.optimization_barrier(
        ((x_rest, x_near, dy_slabs), ready)
    )
    lower_slabs, down_upper, down_lower, down_lower_t = ready
    factors = (down_lower, down_lower_t, adapter_upper_gate[0], adapter_upper_up[0])
    x_far = [swap(x_rest[2][:1], ACROSS), swap(x_rest[1][1:], ALONG)]
    dy_slabs.append(over_experts(dy_slabs[0], 3))
    x_near_swapped = swap(jnp.stack(x_near), CORE)
    x_rest_swapped = [swap(x_rest[0], CORE)]

    x_late = (x_far, x_rest, x_near_swapped, x_rest_swapped, dy_slabs)
    x_far, x_rest, x_near_swapped, x_rest_swapped, dy_slabs = lax.optimization_barrier(x_late)
    x_rest_swapped += [swap(part, CORE) for part in x_rest[1:]]
    x_far_swapped = [swap(part, CORE) for part in x_far]
    dy_all = after(jnp.stack(dy_slabs), x_near_swapped, *x_rest_swapped, *x_far_swapped)
    dy_plane = [swap(dy_all, bit) for bit in PLANE[:2]]

    x = Rows()
    for chip, part in enumerate(x_near):
        x.add(part, (0, 2 * chip))
    x.add(x_near_swapped, *((0, 2 * chip + 1) for chip in range(len(x_near))))
    for chip, (part, swapped) in enumerate(zip(x_rest, x_rest_swapped)):
        place_both(x, part, swapped, chip, range(1, experts))
    for part, swapped, slabs in zip(x_far, x_far_swapped, (range(1, 2), range(2, experts))):
        place_both(x, part, swapped, len(x_rest), slabs)

    weights = (gate_weight[0], up_weight[0], down_weight[0])
    saved = forward_rows(
        x, slab_order, weights, lower_slabs, adapter_upper_gate[0], adapter_upper_up[0]
    )
    dy_rows = [dy_all, *after(dy_plane, saved[0])]
    half = experts // 2
    dy_far = [swap(dy_rows[2][:half], ACROSS), swap(dy_rows[1][half:], ALONG)]
    dy_swapped = [swap(part, CORE) for part in dy_rows]
    dy_far, dy_swapped = lax.optimization_barrier((dy_far, dy_swapped))
    dy = Rows()
    for chip, (part, swapped) in enumerate(zip(dy_rows, dy_swapped)):
        place_both(dy, part, swapped, chip, range(experts))
    for part, slabs in zip(dy_far, (range(half), range(half, experts))):
        place_both(dy, part, swap(part, CORE), len(dy_rows), slabs)
    d_pair, parts, low_down = hidden_gradients(
        dy, slab_order, route_row, weights[2], down_upper, factors, saved[:3]
    )

    def sum_step(total, bit):
        other = swap(total.reshape(SHARDS, 3 * rank, tokens_each), bit)
        shape = (SHARDS // (2 * bit), 2, bit, 3 * rank, tokens_each)
        return total.reshape(shape) + other.reshape(shape)[:, ::-1]

    sums = [parts.reshape(3 * rank, SHARDS, tokens_each).transpose(1, 0, 2)]
    for bit in (CORE, ACROSS, ALONG):
        sums.append(sum_step(sums[-1], bit))

    groups = ((3, 2), (1, 0))
    terms, chips, moved = [], [], []
    for group, wait in zip(groups, sums[1:]):
        here = after(slab_order, wait)
        keep, away = slab_terms(group, here, d_pair, weights, lower_slabs)
        terms.append((keep, swap(away, CORE)))

    def send(keep, got):
        chips.append([added(keep[i], got[i]) for i in range(SHARDS // 2)])
        moved.append([swap(part, bit) for bit, part in zip(PLANE, chips[-1][1:])])

    send(terms[0][0], after(terms[0][1], terms[1][0]))
    total = after(sums[3].reshape(SHARDS, 3 * rank, tokens_each), *chips[0])
    grad_pair, grad_down, owned, owned_down = adapter_gradients(
        x,
        dy,
        order,
        slab_order,
        total[:, : 2 * rank],
        total[:, 2 * rank :] * route_blocks,
        saved[3],
        low_down,
        d_pair,
        saved[2],
    )
    got, moved[0] = after((terms[1][1], moved[0]), grad_pair)
    send(terms[1][0], got)
    grad_x = None
    for group, chip, others in zip(groups, chips, moved):
        rows = sum((wide(part) for part in others), wide(chip[0]))
        for i, r in enumerate(group):
            part = wide(over_experts(rows[i].astype(jnp.bfloat16), r)) if r else rows[i]
            grad_x = part if grad_x is None else grad_x + part
    grad_x = grad_x.astype(jnp.bfloat16)
    return (
        grad_x,
        grad_pair[None, :rank],
        owned[0].T[None],
        grad_pair[None, rank:],
        owned[1].T[None],
        owned_down[None],
        grad_down.T[None],
    )


def plan(tokens, *others):
    experts, tokens_each, hidden_here = lax.axis_size("expert"), tokens.shape[0], others[3].shape[1]
    planned = (
        lax.axis_size("dp") == SHARDS
        and experts == 4
        and hidden_here % LANES == 0
        and tokens_each % LANES == 0
        and tokens.shape[1] % TILE == 0
    )
    return (local if planned else general_local)(tokens, *others)


def solution(mesh):
    return jax.shard_map(
        plan,
        mesh=mesh,
        in_specs=(
            P("dp", "expert"),
            P("dp", "expert"),
            P("dp", None),
            P("dp", None),
            P("expert", "dp", None),
            P("expert", "dp", None),
            P("expert", "dp", None),
            P("expert", None, None),
            P("expert", "dp", None),
            P("expert", None, None),
            P("expert", "dp", None),
            P("expert", None, "dp"),
            P("expert", None, None),
        ),
        out_specs=(
            P("dp", "expert"),
            P("expert", None, None),
            P("expert", "dp", None),
            P("expert", None, None),
            P("expert", "dp", None),
            P("expert", None, "dp"),
            P("expert", None, None),
        ),
        check_vma=False,
    )
```

```python
import jax
import jax.numpy as jnp
from jax import lax
from jax.experimental import pallas as pl
from jax.experimental.pallas import tpu as pltpu
from jax.sharding import PartitionSpec as P

ADAPTER_SCALE = 2.0


def contract_pair(left, right, left_axis, right_axis):
    return lax.dot_general(
        left, right, (((left_axis,), (right_axis,)), ((), ())), preferred_element_type=jnp.float32
    )


def slot_numbers(route_rows, experts):
    picked = (route_rows[:, :, None] == jnp.arange(experts, dtype=jnp.int32)[None, None, :]).astype(
        jnp.int32
    )
    per_token = jnp.sum(picked, axis=1)
    earlier = jnp.cumsum(per_token, axis=0) - per_token
    return jnp.sum(earlier[:, None, :] * picked, axis=2)


def slot_sources(route_rows, positions, experts, capacity):
    tokens_here, choose = route_rows.shape
    target = (route_rows * capacity + positions).reshape(-1)
    owners = jnp.repeat(jnp.arange(tokens_here, dtype=jnp.int32), choose)
    member_ids = jnp.tile(jnp.arange(choose, dtype=jnp.int32), tokens_here)
    source = jnp.full((experts * capacity,), tokens_here, jnp.int32).at[target].set(owners)
    member = jnp.zeros((experts * capacity,), jnp.int32).at[target].set(member_ids)
    return (source, member)


def rows_backward_pass(input_rows, output_gradient_rows, params):
    (
        gate_weight,
        up_weight,
        down_weight,
        a_gate,
        gate_adapter_upper,
        a_up,
        up_adapter_upper,
        down_adapter_lower,
        b_down,
    ) = params
    gate_projected_lower = contract_pair(a_gate, input_rows, 1, 1).astype(jnp.bfloat16)
    up_projected_lower = contract_pair(a_up, input_rows, 1, 1).astype(jnp.bfloat16)
    gate_preactivation = contract_pair(
        gate_weight, input_rows, 1, 1
    ) + ADAPTER_SCALE * contract_pair(gate_adapter_upper, gate_projected_lower, 1, 0)
    up_preactivation = contract_pair(up_weight, input_rows, 1, 1) + ADAPTER_SCALE * contract_pair(
        up_adapter_upper, up_projected_lower, 1, 0
    )
    sigmoid_gate = jax.nn.sigmoid(gate_preactivation)
    silu_gate = gate_preactivation * sigmoid_gate
    hidden_units = (silu_gate * up_preactivation).astype(jnp.bfloat16)
    down_projected_lower = contract_pair(b_down, output_gradient_rows, 0, 1).astype(jnp.bfloat16)
    hidden_gradient = contract_pair(
        down_weight, output_gradient_rows, 1, 1
    ) + ADAPTER_SCALE * contract_pair(down_adapter_lower, down_projected_lower, 0, 0)
    gate_gradient = (
        hidden_gradient
        * up_preactivation
        * sigmoid_gate
        * (1.0 + gate_preactivation * (1.0 - sigmoid_gate))
    ).astype(jnp.bfloat16)
    up_gradient = (hidden_gradient * silu_gate).astype(jnp.bfloat16)
    gate_partial = contract_pair(gate_adapter_upper, gate_gradient, 0, 0).astype(jnp.bfloat16)
    up_partial = contract_pair(up_adapter_upper, up_gradient, 0, 0).astype(jnp.bfloat16)
    down_partial = contract_pair(down_adapter_lower, hidden_units, 1, 0).astype(jnp.bfloat16)
    paired_partials = jnp.concatenate([gate_partial, up_partial], 0)
    paired_factors = jnp.concatenate([a_gate, a_up], 0)
    gradient_rows_out = (
        contract_pair(gate_gradient, gate_weight, 0, 0)
        + contract_pair(up_gradient, up_weight, 0, 0)
        + ADAPTER_SCALE * contract_pair(paired_partials, paired_factors, 0, 0)
    )
    shared_slice = (
        ADAPTER_SCALE * contract_pair(gate_partial, input_rows, 1, 0),
        ADAPTER_SCALE * contract_pair(up_partial, input_rows, 1, 0),
        ADAPTER_SCALE * contract_pair(output_gradient_rows, down_partial, 0, 1),
    )
    owned_slice = (
        ADAPTER_SCALE * contract_pair(gate_gradient, gate_projected_lower, 1, 1),
        ADAPTER_SCALE * contract_pair(up_gradient, up_projected_lower, 1, 1),
        ADAPTER_SCALE * contract_pair(down_projected_lower, hidden_units, 1, 1),
    )
    return (gradient_rows_out, shared_slice, owned_slice)


def general_local(
    tokens,
    output_gradient,
    routing,
    router_gate_values,
    gate_weight,
    up_weight,
    down_weight,
    adapter_lower_gate,
    adapter_upper_gate,
    adapter_lower_up,
    adapter_upper_up,
    adapter_lower_down,
    adapter_upper_down,
):
    experts = lax.axis_size("expert")
    shards = lax.axis_size("dp")
    tok_local, feat_local = tokens.shape
    choose = routing.shape[1]
    complete_width = feat_local * experts
    capacity = min(tok_local, 6 * tok_local // experts)
    hidden_units_local = gate_weight.shape[1]
    adapter_rank = adapter_lower_gate.shape[1]
    params = (
        gate_weight[0],
        up_weight[0],
        down_weight[0],
        adapter_lower_gate[0],
        adapter_upper_gate[0],
        adapter_lower_up[0],
        adapter_upper_up[0],
        adapter_lower_down[0],
        adapter_upper_down[0],
    )
    positions = slot_numbers(routing, experts)
    zero_row = jnp.zeros((1, feat_local), jnp.bfloat16)
    initial = (
        jnp.zeros((shards * capacity, complete_width), jnp.float32),
        (
            jnp.zeros((adapter_rank, complete_width), jnp.float32),
            jnp.zeros((adapter_rank, complete_width), jnp.float32),
            jnp.zeros((complete_width, adapter_rank), jnp.float32),
        ),
        (
            jnp.zeros((hidden_units_local, adapter_rank), jnp.float32),
            jnp.zeros((hidden_units_local, adapter_rank), jnp.float32),
            jnp.zeros((adapter_rank, hidden_units_local), jnp.float32),
        ),
    )
    source, member = slot_sources(routing, positions, experts, capacity)
    clamped = jnp.minimum(source, tok_local - 1)
    slot_gate = jnp.where(
        source < tok_local, router_gate_values.reshape(-1)[clamped * choose + member], 0.0
    )
    send_x = jnp.concatenate([tokens, zero_row], 0)[source].reshape(experts, capacity, feat_local)
    send_dy = (
        (
            slot_gate[:, None]
            * jnp.concatenate([output_gradient, zero_row], 0)[source].astype(jnp.float32)
        )
        .astype(jnp.bfloat16)
        .reshape(experts, capacity, feat_local)
    )
    recv_x, recv_dy = (
        lax.all_to_all(send_x, "expert", split_axis=0, concat_axis=2, tiled=True),
        lax.all_to_all(send_dy, "expert", split_axis=0, concat_axis=2, tiled=True),
    )
    gradient_rows_out, shared_slice, owned_slice = rows_backward_pass(
        lax.all_gather(recv_x[0], "dp", axis=0, tiled=True),
        lax.all_gather(recv_dy[0], "dp", axis=0, tiled=True),
        params,
    )
    rows_part = gradient_rows_out
    totals = (
        rows_part,
        jax.tree.map(jnp.add, initial[1], shared_slice),
        jax.tree.map(jnp.add, initial[2], owned_slice),
    )
    rows_part, shared_slice, owned_slice = totals
    summed = lax.psum_scatter(
        rows_part.astype(jnp.bfloat16), "dp", scatter_dimension=0, tiled=True
    ).astype(jnp.float32)
    returned_rows = lax.all_to_all(
        summed.reshape(capacity, experts, feat_local).astype(jnp.bfloat16),
        "expert",
        split_axis=1,
        concat_axis=1,
        tiled=True,
    ).astype(jnp.float32)
    lookup = positions * experts + routing
    grad_x = jnp.sum(returned_rows.reshape(capacity * experts, feat_local)[lookup], axis=1).astype(
        jnp.bfloat16
    )
    grad_a_gate, grad_a_up, grad_b_down = (
        lax.psum(shared_slice[0].astype(jnp.bfloat16), "dp").astype(jnp.float32),
        lax.psum(shared_slice[1].astype(jnp.bfloat16), "dp").astype(jnp.float32),
        lax.psum(shared_slice[2].astype(jnp.bfloat16), "dp").astype(jnp.float32),
    )
    return (
        grad_x,
        grad_a_gate[None],
        owned_slice[0][None],
        grad_a_up[None],
        owned_slice[1][None],
        owned_slice[2][None],
        grad_b_down[None],
    )


LANES = 128
TILE = 512
SHARDS = 8
VMEM_BYTES = 58 * 1024 * 1024
HIDDEN_BYTES = 58 * 1024 * 1024
TERM_BYTES = 58 * 1024 * 1024
HBM = pl.BlockSpec(memory_space=pl.ANY)
PINNED = pl.BlockSpec(memory_space=pltpu.HBM)
VMEM = pl.BlockSpec(memory_space=pltpu.VMEM)
SMEM = pl.BlockSpec(memory_space=pltpu.SMEM)


def dot_nt(left, right):
    return contract_pair(left, right, 1, 1)


def dot_nn(left, right):
    return contract_pair(left, right, 1, 0)


def wide(value):
    return value.astype(jnp.float32)


class Rows:
    def __init__(self, blocks):
        self.arrays, self.places, self.blocks = [], [], blocks

    def add(self, array, *places):
        self.arrays.append(array)
        self.places.append(places)


def row_copies(refs, places, target, sems, slab, first=0, order=None):
    tokens_each = refs[0].shape[-2]
    copies = []
    for ref, parts in zip(refs, places):
        for i, (at, block) in enumerate(parts):
            if at != slab:
                continue
            source = ref.at[i] if len(ref.shape) == 3 else ref
            row = (block - first) * tokens_each
            if order is not None:
                row = pl.multiple_of(order[block] * tokens_each, tokens_each)
            copies.append(
                pltpu.make_async_copy(
                    source, target.at[slab, pl.ds(row, tokens_each)], sems.at[slab, block]
                )
            )
    return copies


def slab_lanes(slab_ref, slab, feat):
    return pl.ds(pl.multiple_of(slab_ref[slab] * feat, feat), feat)


def forward_kernel(places, first, *refs):
    n_pieces = len(places)
    pieces = refs[:n_pieces]
    (
        slab_ref,
        gate_hbm,
        up_hbm,
        lower_hbm,
        gate_upper_ref,
        up_upper_ref,
        silu_out,
        slope_out,
        hidden_out,
        low_out,
    ) = refs[n_pieces : n_pieces + 10]
    x_rows, weights, pre, saved, x_sems, w_sems, out_sems = refs[n_pieces + 10 :]
    slabs, _, feat = x_rows.shape
    hidden_here = gate_hbm.shape[0]
    pair, rank = lower_hbm.shape[1], gate_upper_ref.shape[1]

    def x_slab(slab):
        return row_copies(pieces, places, x_rows, x_sems, slab, first)

    def weight_copies(slab):
        lanes = slab_lanes(slab_ref, slab, feat)
        sides = (
            (gate_hbm.at[:, lanes], 0, hidden_here),
            (up_hbm.at[:, lanes], hidden_here, hidden_here),
            (lower_hbm.at[slab], 2 * hidden_here, pair),
        )
        return [
            pltpu.make_async_copy(
                source, weights.at[slab, pl.ds(start, size)], w_sems.at[slab, i]
            )
            for i, (source, start, size) in enumerate(sides)
        ]

    for slab in range(slabs):
        for copy in x_slab(slab) + weight_copies(slab):
            copy.start()
    for slab in range(slabs):
        for copy in x_slab(slab) + weight_copies(slab):
            copy.wait()
        if slab == 0:
            pre[...] = dot_nt(weights[0], x_rows[0])
        else:
            pre[...] += dot_nt(weights[slab], x_rows[slab])
    low_out[...] = pre[2 * hidden_here :, :].astype(jnp.bfloat16)

    def out_copies(tile):
        at = pl.ds(pl.multiple_of(tile * LANES, LANES), LANES)
        return [
            pltpu.make_async_copy(saved.at[i, at], out.at[at], out_sems.at[i, tile])
            for i, out in enumerate((silu_out, slope_out, hidden_out))
        ]

    tiles = hidden_here // LANES

    @pl.loop(0, tiles)
    def _(tile):
        start = pl.multiple_of(tile * LANES, LANES)
        at = pl.ds(start, LANES)
        up_at = pl.ds(pl.multiple_of(hidden_here + start, LANES), LANES)
        pre_gate = pre[at, :] + ADAPTER_SCALE * dot_nn(gate_upper_ref[at, :], low_out[:rank, :])
        pre_up = pre[up_at, :] + ADAPTER_SCALE * dot_nn(up_upper_ref[at, :], low_out[rank:, :])
        sigma = 1.0 / (1.0 + jnp.exp(-pre_gate))
        silu = pre_gate * sigma
        saved[0, at, :] = silu.astype(jnp.bfloat16)
        saved[1, at, :] = (pre_up * (sigma * (1.0 + pre_gate * (1.0 - sigma)))).astype(
            jnp.bfloat16
        )
        saved[2, at, :] = (silu * pre_up).astype(jnp.bfloat16)
        for copy in out_copies(tile):
            copy.start()

    @pl.loop(0, tiles)
    def _(tile):
        for copy in out_copies(tile):
            copy.wait()


def forward_rows(x, slab_order, weights, lower_slabs, gate_upper, up_upper):
    hidden_here, width = weights[0].shape
    tokens_each, feat = x.arrays[0].shape[-2:]
    rows = len(x.blocks) * tokens_each
    slabs, pair, _ = lower_slabs.shape
    kept = jax.ShapeDtypeStruct((hidden_here, rows), jnp.bfloat16)
    return pl.pallas_call(
        lambda *refs: forward_kernel(x.places, x.blocks[0], *refs),
        out_shape=(kept, kept, kept, jax.ShapeDtypeStruct((pair, rows), jnp.bfloat16)),
        in_specs=[HBM] * len(x.arrays) + [SMEM] + [HBM] * 3 + [VMEM] * 2,
        out_specs=(HBM, HBM, HBM, VMEM),
        scratch_shapes=[
            pltpu.VMEM((slabs, rows, feat), jnp.bfloat16),
            pltpu.VMEM((slabs, 2 * hidden_here + pair, feat), jnp.bfloat16),
            pltpu.VMEM((2 * hidden_here + pair, rows), jnp.float32),
            pltpu.VMEM((3, hidden_here, rows), jnp.bfloat16),
            pltpu.SemaphoreType.DMA((slabs, SHARDS)),
            pltpu.SemaphoreType.DMA((slabs, 3)),
            pltpu.SemaphoreType.DMA((3, hidden_here // LANES)),
        ],
        compiler_params=pltpu.CompilerParams(vmem_limit_bytes=VMEM_BYTES),
        cost_estimate=pl.CostEstimate(
            flops=4 * rows * hidden_here * width,
            bytes_accessed=2 * rows * width,
            transcendentals=rows * hidden_here,
        ),
        name="forward_rows",
    )(*x.arrays, slab_order, *weights[:2], lower_slabs, gate_upper, up_upper)


def hidden_kernel(places, first, *refs):
    n_pieces = len(places)
    pieces = refs[:n_pieces]
    (
        slab_ref,
        route_ref,
        down_hbm,
        down_upper_hbm,
        down_lower_ref,
        down_lower_t_ref,
        gate_upper_ref,
        up_upper_ref,
        silu_hbm,
        slope_hbm,
        hidden_hbm,
        d_pair,
        parts_out,
        low_down,
        rows,
        down_w,
        d_down,
        silu,
        slope,
        hidden,
        row_sems,
        d_sems,
        f_sems,
    ) = refs[n_pieces:]
    slabs, _, feat = rows.shape
    hidden_here = silu.shape[0]
    rank = down_lower_ref.shape[0]
    saved_copies = [
        pltpu.make_async_copy(source, target, f_sems.at[i])
        for i, (source, target) in enumerate(
            ((silu_hbm, silu), (slope_hbm, slope), (hidden_hbm, hidden))
        )
    ]

    def slab_copies(slab):
        return row_copies(pieces, places, rows, row_sems, slab, first) + [
            pltpu.make_async_copy(
                down_hbm.at[:, slab_lanes(slab_ref, slab, feat)],
                down_w.at[slab, pl.ds(0, hidden_here)],
                d_sems.at[slab, 0],
            ),
            pltpu.make_async_copy(
                down_upper_hbm.at[slab], down_w.at[slab, pl.ds(hidden_here, rank)], d_sems.at[slab, 1]
            ),
        ]

    for slab in range(slabs):
        for copy in slab_copies(slab):
            copy.start()
    for copy in saved_copies:
        copy.start()
    for slab in range(slabs):
        for copy in slab_copies(slab):
            copy.wait()
        if slab == 0:
            d_down[...] = dot_nt(down_w[0], rows[0])
        else:
            d_down[...] += dot_nt(down_w[slab], rows[slab])

    low_down[...] = (d_down[hidden_here:, :] * route_ref[...]).astype(jnp.bfloat16)
    for copy in saved_copies:
        copy.wait()

    @pl.loop(0, hidden_here // LANES)
    def _(tile):
        start = pl.multiple_of(tile * LANES, LANES)
        at = pl.ds(start, LANES)
        up_at = pl.ds(pl.multiple_of(hidden_here + start, LANES), LANES)
        d_hidden = d_down[at, :] * route_ref[...]
        d_hidden = d_hidden + ADAPTER_SCALE * dot_nn(down_lower_t_ref[at, :], low_down[...])
        d_gate = (d_hidden * wide(slope[at, :])).astype(jnp.bfloat16)
        d_up = (d_hidden * wide(silu[at, :])).astype(jnp.bfloat16)
        d_pair[:, at] = d_gate.T
        d_pair[:, up_at] = d_up.T

    for side, factor in enumerate((gate_upper_ref, up_upper_ref)):
        start = side * hidden_here
        part = dot_nn(d_pair[:, start : start + hidden_here], factor[...])
        parts_out[side * rank : (side + 1) * rank, :] = part.T
        at = 2 * hidden_here + side * rank
        d_pair[:, at : at + rank] = ADAPTER_SCALE * part.astype(jnp.bfloat16)
    parts_out[2 * rank :, :] = dot_nn(down_lower_ref[...], hidden[...])


def hidden_gradients(dy, slab_order, route_row, down_weight, down_upper, factors, saved):
    hidden_here, width = down_weight.shape
    slabs, rank, feat = down_upper.shape
    pair = 2 * rank
    rows = route_row.shape[1]
    return pl.pallas_call(
        lambda *refs: hidden_kernel(dy.places, dy.blocks[0], *refs),
        out_shape=(
            jax.ShapeDtypeStruct((rows, 2 * hidden_here + pair), jnp.bfloat16),
            jax.ShapeDtypeStruct((3 * rank, rows), jnp.float32),
            jax.ShapeDtypeStruct((rank, rows), jnp.bfloat16),
        ),
        in_specs=[HBM] * len(dy.arrays) + [SMEM, VMEM] + [HBM] * 2 + [VMEM] * 4 + [HBM] * 3,
        out_specs=(VMEM,) * 3,
        scratch_shapes=[
            pltpu.VMEM((slabs, rows, feat), jnp.bfloat16),
            pltpu.VMEM((slabs, hidden_here + rank, feat), jnp.bfloat16),
            pltpu.VMEM((hidden_here + rank, rows), jnp.float32),
            pltpu.VMEM((hidden_here, rows), jnp.bfloat16),
            pltpu.VMEM((hidden_here, rows), jnp.bfloat16),
            pltpu.VMEM((hidden_here, rows), jnp.bfloat16),
            pltpu.SemaphoreType.DMA((slabs, SHARDS)),
            pltpu.SemaphoreType.DMA((slabs, 2)),
            pltpu.SemaphoreType.DMA((3,)),
        ],
        compiler_params=pltpu.CompilerParams(vmem_limit_bytes=HIDDEN_BYTES),
        cost_estimate=pl.CostEstimate(
            flops=4 * rows * hidden_here * width,
            bytes_accessed=2 * hidden_here * width + 2 * rows * width,
            transcendentals=0,
        ),
        name="hidden_gradients",
    )(*dy.arrays, slab_order, route_row, down_weight, down_upper, *factors, *saved)


def term_kernel(slabs, n_parts, *refs):
    d_parts = refs[:n_parts]
    slab_ref, gate_hbm, up_hbm, lower_hbm = refs[n_parts : n_parts + 4]
    outs, (d_pair, pair_w, sems, d_sems) = refs[n_parts + 4 : -4], refs[-4:]
    _, depth, step = pair_w.shape
    hidden_here = gate_hbm.shape[0]
    pair = depth - 2 * hidden_here
    tokens_each, feat = outs[0].shape[2:]
    steps = feat // step

    def weight_copies(i, n):
        slab, k = slabs[i], i * steps + n
        lanes = pl.ds(pl.multiple_of(slab_ref[slab] * feat + n * step, step), step)
        sides = (
            (gate_hbm.at[:, lanes], 0, hidden_here),
            (up_hbm.at[:, lanes], hidden_here, hidden_here),
            (lower_hbm.at[slab, :, pl.ds(pl.multiple_of(n * step, step), step)], 2 * hidden_here, pair),
        )
        return [
            pltpu.make_async_copy(source, pair_w.at[k, pl.ds(start, size)], sems.at[k, side])
            for side, (source, start, size) in enumerate(sides)
        ]

    d_copies, row = [], 0
    for i, part in enumerate(d_parts):
        count = part.shape[0]
        d_copies.append(pltpu.make_async_copy(part, d_pair.at[pl.ds(row, count)], d_sems.at[i]))
        row += count
    for copy in d_copies:
        copy.start()
    for i in range(len(slabs)):
        for n in range(steps):
            for copy in weight_copies(i, n):
                copy.start()
    for copy in d_copies:
        copy.wait()
    for i in range(len(slabs)):

        @pl.loop(0, steps)
        def _(n):
            for copy in weight_copies(i, n):
                copy.wait()
            lanes = pl.ds(pl.multiple_of(n * step, step), step)
            term = dot_nn(d_pair[...], pair_w[i * steps + n]).astype(jnp.bfloat16)
            for block in range(SHARDS):
                at = slice(block * tokens_each, (block + 1) * tokens_each)
                outs[block % 2][block // 2, i, :, lanes] = term[at]


def slab_terms(slabs, slab_order, d_pair, weights, lower_slabs):
    rows, depth = sum(part.shape[0] for part in d_pair), d_pair[0].shape[1]
    feat = lower_slabs.shape[2]
    parts = len(slabs) * feat // TILE
    term = jax.ShapeDtypeStruct((SHARDS // 2, len(slabs), rows // SHARDS, feat), jnp.bfloat16)
    return pl.pallas_call(
        lambda *refs: term_kernel(slabs, len(d_pair), *refs),
        out_shape=(term, term),
        in_specs=[HBM] * len(d_pair) + [SMEM] + [HBM] * 3,
        out_specs=(VMEM, VMEM),
        scratch_shapes=[
            pltpu.VMEM((rows, depth), jnp.bfloat16),
            pltpu.VMEM((parts, depth, TILE), jnp.bfloat16),
            pltpu.SemaphoreType.DMA((parts, 3)),
            pltpu.SemaphoreType.DMA((len(d_pair),)),
        ],
        compiler_params=pltpu.CompilerParams(vmem_limit_bytes=TERM_BYTES),
        cost_estimate=pl.CostEstimate(
            flops=4 * rows * depth * feat * len(slabs),
            bytes_accessed=2 * depth * feat * len(slabs) + 4 * rows * depth,
            transcendentals=0,
        ),
        name="slab_terms",
    )(*d_pair, slab_order, *weights[:2], lower_slabs)


def shared_kernel(x_places, dy_places, n_parts, *refs):
    split, inputs = len(x_places), len(x_places) + len(dy_places)
    x_pieces, dy_pieces = refs[:split], refs[split:inputs]
    (
        order_ref,
        slab_ref,
        sums_ref,
        down_sums_ref,
    ) = refs[inputs : inputs + 4]
    inputs += 4
    parts = [refs[inputs + 4 * i : inputs + 4 * i + 4] for i in range(n_parts)]
    inputs += 4 * n_parts
    pair_out, down_out, owned_out, owned_down_out = refs[inputs : inputs + 4]
    x_rows, dy_rows, sums, down_sums, x_sems, dy_sems = refs[inputs + 4 :]
    rank, hidden_here = owned_down_out.shape
    slabs, _, feat = x_rows.shape
    tokens_each = x_pieces[0].shape[-2]

    def slab_copies(slab):
        return row_copies(x_pieces, x_places, x_rows, x_sems, slab, 0, order_ref) + row_copies(
            dy_pieces, dy_places, dy_rows, dy_sems, slab, 0, order_ref
        )

    for slab in range(slabs):
        for copy in slab_copies(slab):
            copy.start()
    for block in range(SHARDS):
        lanes = pl.ds(pl.multiple_of(order_ref[block] * tokens_each, tokens_each), tokens_each)
        sums[:, lanes] = sums_ref[block]
        down_sums[:, lanes] = down_sums_ref[block]
    gate_sum = up_sum = down_sum = 0.0
    for low, low_down, d_pair, hidden in parts:
        gate_sum += dot_nn(low[:rank, :], d_pair[:, :hidden_here])
        up_sum += dot_nn(low[rank:, :], d_pair[:, hidden_here : 2 * hidden_here])
        down_sum += dot_nt(low_down[...], hidden[...])
    owned_out[0] = ADAPTER_SCALE * gate_sum
    owned_out[1] = ADAPTER_SCALE * up_sum
    owned_down_out[...] = ADAPTER_SCALE * down_sum
    for slab in range(slabs):
        for copy in slab_copies(slab):
            copy.wait()

        @pl.loop(0, feat // TILE)
        def _(n):
            lanes = pl.ds(pl.multiple_of(n * TILE, TILE), TILE)
            out = pl.ds(pl.multiple_of(slab_ref[slab] * feat + n * TILE, TILE), TILE)
            pair_out[:, out] = ADAPTER_SCALE * dot_nn(
                sums[...].astype(jnp.bfloat16), x_rows[slab, :, lanes]
            )
            down_out[:, out] = ADAPTER_SCALE * dot_nn(
                down_sums[...].astype(jnp.bfloat16), dy_rows[slab, :, lanes]
            )


def adapter_gradients(x, dy, order, slab_order, sums, down_sums, parts):
    tokens_each, feat = x.arrays[0].shape[-2:]
    slabs = slab_order.shape[0]
    rows = SHARDS * tokens_each
    pair, rank = sums.shape[1], down_sums.shape[1]
    hidden_here = parts[0][3].shape[0]
    return pl.pallas_call(
        lambda *refs: shared_kernel(x.places, dy.places, len(parts), *refs),
        out_shape=(
            jax.ShapeDtypeStruct((pair, slabs * feat), jnp.float32),
            jax.ShapeDtypeStruct((rank, slabs * feat), jnp.float32),
            jax.ShapeDtypeStruct((2, rank, hidden_here), jnp.float32),
            jax.ShapeDtypeStruct((rank, hidden_here), jnp.float32),
        ),
        in_specs=[HBM] * (len(x.arrays) + len(dy.arrays)) + [SMEM, SMEM]
        + [VMEM] * (2 + 4 * len(parts)),
        out_specs=(VMEM,) * 4,
        scratch_shapes=[
            pltpu.VMEM((slabs, rows, feat), jnp.bfloat16),
            pltpu.VMEM((slabs, rows, feat), jnp.bfloat16),
            pltpu.VMEM((pair, rows), jnp.float32),
            pltpu.VMEM((rank, rows), jnp.float32),
            pltpu.SemaphoreType.DMA((slabs, SHARDS)),
            pltpu.SemaphoreType.DMA((slabs, SHARDS)),
        ],
        compiler_params=pltpu.CompilerParams(vmem_limit_bytes=VMEM_BYTES),
        cost_estimate=pl.CostEstimate(
            flops=200 * rows * pair * slabs * feat,
            bytes_accessed=12 * rows * slabs * feat,
            transcendentals=0,
        ),
        name="adapter_gradients",
    )(
        *x.arrays,
        *dy.arrays,
        order,
        slab_order,
        sums,
        down_sums,
        *(value for part in parts for value in part),
    )


CORE, ACROSS, ALONG = 1, 2, 4
PLANE = (ACROSS, ALONG, ACROSS | ALONG)


def swap(value, bit, axis="dp"):
    return lax.ppermute(value, axis, [(i, i ^ bit) for i in range(lax.axis_size(axis))])


def after(value, *others):
    return lax.optimization_barrier((value, others))[0]


def added(left, right):
    return (wide(left) + wide(right)).astype(jnp.bfloat16)


def local(
    tokens,
    output_gradient,
    routing,
    router_gate_values,
    gate_weight,
    up_weight,
    down_weight,
    adapter_lower_gate,
    adapter_upper_gate,
    adapter_lower_up,
    adapter_upper_up,
    adapter_lower_down,
    adapter_upper_down,
):
    experts = lax.axis_size("expert")
    me, expert = lax.axis_index("dp"), lax.axis_index("expert")
    tokens_each, feat = tokens.shape
    rank = adapter_lower_gate.shape[1]
    order = jnp.bitwise_xor(jnp.arange(SHARDS, dtype=jnp.int32), me.astype(jnp.int32))
    slab_order = jnp.bitwise_xor(jnp.arange(experts, dtype=jnp.int32), expert.astype(jnp.int32))

    named = routing[:, :, None] == jnp.arange(experts, dtype=jnp.int32)[None, None, :]
    weight_of = jnp.sum(jnp.where(named, router_gate_values[:, :, None], 0.0), axis=1)
    routes = lax.all_gather(weight_of.T, "dp", axis=0, tiled=False)
    route = lax.dynamic_index_in_dim(routes, expert, axis=1, keepdims=False)[order]
    route_blocks = route[:, None, :]
    route_row = route.reshape(1, SHARDS * tokens_each)

    def slabs_first(factor):
        return factor.reshape(factor.shape[0], experts, feat).transpose(1, 0, 2)[slab_order]

    lower_cat = jnp.concatenate([adapter_lower_gate[0], adapter_lower_up[0]], axis=0)
    down_lower = adapter_lower_down[0]

    def place_both(rows, part, swapped, chip, slabs):
        rows.add(part, *((r, 2 * chip) for r in slabs))
        rows.add(swapped, *((r, 2 * chip + 1) for r in slabs))

    def over_experts(block, r):
        return swap(block, r, "expert")

    both = over_experts(jnp.stack([tokens, output_gradient]), 1)
    x_slabs = [both[0]] + [over_experts(tokens, r) for r in range(2, experts)]
    x_near = [tokens] + [swap(tokens, bit) for bit in PLANE[:2]]
    (x_slabs, x_near, dy_near), small = lax.optimization_barrier(
        ((x_slabs, x_near, both[1]), (route_row, adapter_upper_down[0], lower_cat))
    )
    route_row, down_upper, lower_cat = small
    lower_slabs, down_upper = slabs_first(lower_cat), slabs_first(down_upper.T)
    ready = (lower_slabs, down_upper, down_lower, down_lower.T)

    x_rest = [jnp.stack(x_slabs)]
    x_rest += [swap(x_rest[0], bit) for bit in PLANE[:2]]
    x_near.append(swap(x_near[2], ACROSS))
    dy_late = after(output_gradient, x_rest[0])
    dy_slabs = [output_gradient, dy_near] + [over_experts(dy_late, r) for r in range(2, experts)]

    (x_rest, x_near, dy_slabs), ready = lax.optimization_barrier(
        ((x_rest, x_near, dy_slabs), ready)
    )
    lower_slabs, down_upper, down_lower, down_lower_t = ready
    factors = (down_lower, down_lower_t, adapter_upper_gate[0], adapter_upper_up[0])
    half = experts // 2
    x_far = [swap(x_rest[2][: half - 1], ACROSS), swap(x_rest[1][half - 1 :], ALONG)]
    x_near_swapped = swap(jnp.stack(x_near[:3]), CORE)
    x_rest_swapped = [swap(part, CORE) for part in x_rest[:2]]
    x_near_swapped, x_rest_swapped, x_last = lax.optimization_barrier(
        (x_near_swapped, x_rest_swapped, x_rest[2])
    )
    x_rest_swapped.append(swap(x_last, CORE))
    dy_all = after(jnp.stack(dy_slabs), x_near_swapped, *x_rest_swapped[:2])
    dy_plane = [swap(dy_all, bit) for bit in PLANE[:2]]

    x_main = Rows(range(6))
    for chip, part in enumerate(x_near[:3]):
        x_main.add(part, (0, 2 * chip))
    x_main.add(x_near_swapped, *((0, 2 * chip + 1) for chip in range(3)))
    for chip, (part, swapped) in enumerate(zip(x_rest, x_rest_swapped)):
        place_both(x_main, part, swapped, chip, range(1, experts))

    weights = (gate_weight[0], up_weight[0], down_weight[0])
    uppers = (adapter_upper_gate[0], adapter_upper_up[0])
    saved = [forward_rows(x_main, slab_order, weights, lower_slabs, *uppers)]

    x_far = after(x_far, saved[0][0])
    x_far[0] = jnp.concatenate([x_near[3][None], x_far[0]], axis=0)
    far_slabs = (range(half), range(half, experts))
    x_away = Rows(range(6, SHARDS))
    for part, slabs in zip(x_far, far_slabs):
        place_both(x_away, part, swap(part, CORE), 3, slabs)
    saved.append(forward_rows(x_away, slab_order, weights, lower_slabs, *uppers))

    dy_rows = [dy_all, *after(dy_plane, saved[1][0])]
    dy_far = [swap(dy_rows[2][:half], ACROSS), swap(dy_rows[1][half:], ALONG)]
    dy_main, dy_away = Rows(range(6)), Rows(range(6, SHARDS))
    for chip, part in enumerate(dy_rows):
        place_both(dy_main, part, swap(part, CORE), chip, range(experts))
    split = 6 * tokens_each
    grads = [
        hidden_gradients(
            dy_main, slab_order, route_row[:, :split], weights[2], down_upper, factors, saved[0][:3]
        )
    ]
    dy_far = after(dy_far, grads[0][0])
    for part, slabs in zip(dy_far, far_slabs):
        place_both(dy_away, part, swap(part, CORE), 3, slabs)
    grads.append(
        hidden_gradients(
            dy_away, slab_order, route_row[:, split:], weights[2], down_upper, factors, saved[1][:3]
        )
    )
    d_pair = [grad[0] for grad in grads]
    parts = jnp.concatenate([grad[1] for grad in grads], axis=1)

    def sum_step(total, bit):
        other = swap(total.reshape(SHARDS, 3 * rank, tokens_each), bit)
        shape = (SHARDS // (2 * bit), 2, bit, 3 * rank, tokens_each)
        return total.reshape(shape) + other.reshape(shape)[:, ::-1]

    sums = [parts.reshape(3 * rank, SHARDS, tokens_each).transpose(1, 0, 2)]
    for bit in (CORE, ACROSS, ALONG):
        sums.append(sum_step(sums[-1], bit))

    def send(keep, got):
        chips = [added(keep[i], got[i]) for i in range(SHARDS // 2)]
        return chips, [swap(part, bit) for bit, part in zip(PLANE, chips[1:])]

    def total_rows(chips, moved):
        return sum((wide(part) for part in moved), wide(chips[0]))

    def terms(group, *others):
        here = after(slab_order, *others)
        keep, away = slab_terms(group, here, d_pair, weights, lower_slabs)
        return keep, swap(away, CORE)

    keep_a, got_a = terms((3,), sums[1])
    keep_b, got_b = terms((2,), sums[2])
    chips_a, moved_a = send(keep_a, after(got_a, keep_b))
    keep_c, got_c = terms((1, 0), sums[3], *chips_a)
    rows_a = total_rows(chips_a, after(moved_a, keep_c))
    chips_b, moved_b = send(keep_b, after(got_b, keep_c))
    total = after(sums[3].reshape(SHARDS, 3 * rank, tokens_each), rows_a, *chips_b)
    x, dy = Rows(range(SHARDS)), Rows(range(SHARDS))
    for whole, halves in ((x, (x_main, x_away)), (dy, (dy_main, dy_away))):
        for rows in halves:
            whole.arrays += rows.arrays
            whole.places += rows.places
    grad_pair, grad_down, owned, owned_down = adapter_gradients(
        x,
        dy,
        order,
        slab_order,
        total[:, : 2 * rank],
        total[:, 2 * rank :] * route_blocks,
        [(kept[3], grad[2], grad[0], kept[2]) for kept, grad in zip(saved, grads)],
    )
    got_c, moved_b = after((got_c, moved_b), grad_pair)
    chips_c, moved_c = send(keep_c, got_c)
    rows_b = total_rows(chips_b, moved_b)
    rows_c = total_rows(chips_c, moved_c)
    grad_x = rows_c[1]
    for rows, r in ((rows_a[0], 3), (rows_b[0], 2), (rows_c[0], 1)):
        grad_x = grad_x + wide(over_experts(rows.astype(jnp.bfloat16), r))
    grad_x = grad_x.astype(jnp.bfloat16)
    return (
        grad_x,
        grad_pair[None, :rank],
        owned[0].T[None],
        grad_pair[None, rank:],
        owned[1].T[None],
        owned_down[None],
        grad_down.T[None],
    )


def plan(tokens, *others):
    experts, tokens_each, hidden_here = lax.axis_size("expert"), tokens.shape[0], others[3].shape[1]
    planned = (
        lax.axis_size("dp") == SHARDS
        and experts == 4
        and hidden_here % LANES == 0
        and tokens_each % LANES == 0
        and tokens.shape[1] % TILE == 0
    )
    return (local if planned else general_local)(tokens, *others)


def solution(mesh):
    return jax.shard_map(
        plan,
        mesh=mesh,
        in_specs=(
            P("dp", "expert"),
            P("dp", "expert"),
            P("dp", None),
            P("dp", None),
            P("expert", "dp", None),
            P("expert", "dp", None),
            P("expert", "dp", None),
            P("expert", None, None),
            P("expert", "dp", None),
            P("expert", None, None),
            P("expert", "dp", None),
            P("expert", None, "dp"),
            P("expert", None, None),
        ),
        out_specs=(
            P("dp", "expert"),
            P("expert", None, None),
            P("expert", "dp", None),
            P("expert", None, None),
            P("expert", "dp", None),
            P("expert", None, "dp"),
            P("expert", None, None),
        ),
        check_vma=False,
    )
```

```python
import jax
import jax.numpy as jnp
from jax import lax
from jax.experimental import pallas as pl
from jax.experimental.pallas import tpu as pltpu
from jax.sharding import PartitionSpec as P

ADAPTER_SCALE = 2.0


def contract_pair(left, right, left_axis, right_axis):
    return lax.dot_general(
        left, right, (((left_axis,), (right_axis,)), ((), ())), preferred_element_type=jnp.float32
    )


def slot_numbers(route_rows, experts):
    picked = (route_rows[:, :, None] == jnp.arange(experts, dtype=jnp.int32)[None, None, :]).astype(
        jnp.int32
    )
    per_token = jnp.sum(picked, axis=1)
    earlier = jnp.cumsum(per_token, axis=0) - per_token
    return jnp.sum(earlier[:, None, :] * picked, axis=2)


def slot_sources(route_rows, positions, experts, capacity):
    tokens_here, choose = route_rows.shape
    target = (route_rows * capacity + positions).reshape(-1)
    owners = jnp.repeat(jnp.arange(tokens_here, dtype=jnp.int32), choose)
    member_ids = jnp.tile(jnp.arange(choose, dtype=jnp.int32), tokens_here)
    source = jnp.full((experts * capacity,), tokens_here, jnp.int32).at[target].set(owners)
    member = jnp.zeros((experts * capacity,), jnp.int32).at[target].set(member_ids)
    return (source, member)


def rows_backward_pass(input_rows, output_gradient_rows, params):
    (
        gate_weight,
        up_weight,
        down_weight,
        a_gate,
        gate_adapter_upper,
        a_up,
        up_adapter_upper,
        down_adapter_lower,
        b_down,
    ) = params
    gate_projected_lower = contract_pair(a_gate, input_rows, 1, 1).astype(jnp.bfloat16)
    up_projected_lower = contract_pair(a_up, input_rows, 1, 1).astype(jnp.bfloat16)
    gate_preactivation = contract_pair(
        gate_weight, input_rows, 1, 1
    ) + ADAPTER_SCALE * contract_pair(gate_adapter_upper, gate_projected_lower, 1, 0)
    up_preactivation = contract_pair(up_weight, input_rows, 1, 1) + ADAPTER_SCALE * contract_pair(
        up_adapter_upper, up_projected_lower, 1, 0
    )
    sigmoid_gate = jax.nn.sigmoid(gate_preactivation)
    silu_gate = gate_preactivation * sigmoid_gate
    hidden_units = (silu_gate * up_preactivation).astype(jnp.bfloat16)
    down_projected_lower = contract_pair(b_down, output_gradient_rows, 0, 1).astype(jnp.bfloat16)
    hidden_gradient = contract_pair(
        down_weight, output_gradient_rows, 1, 1
    ) + ADAPTER_SCALE * contract_pair(down_adapter_lower, down_projected_lower, 0, 0)
    gate_gradient = (
        hidden_gradient
        * up_preactivation
        * sigmoid_gate
        * (1.0 + gate_preactivation * (1.0 - sigmoid_gate))
    ).astype(jnp.bfloat16)
    up_gradient = (hidden_gradient * silu_gate).astype(jnp.bfloat16)
    gate_partial = contract_pair(gate_adapter_upper, gate_gradient, 0, 0).astype(jnp.bfloat16)
    up_partial = contract_pair(up_adapter_upper, up_gradient, 0, 0).astype(jnp.bfloat16)
    down_partial = contract_pair(down_adapter_lower, hidden_units, 1, 0).astype(jnp.bfloat16)
    paired_partials = jnp.concatenate([gate_partial, up_partial], 0)
    paired_factors = jnp.concatenate([a_gate, a_up], 0)
    gradient_rows_out = (
        contract_pair(gate_gradient, gate_weight, 0, 0)
        + contract_pair(up_gradient, up_weight, 0, 0)
        + ADAPTER_SCALE * contract_pair(paired_partials, paired_factors, 0, 0)
    )
    shared_slice = (
        ADAPTER_SCALE * contract_pair(gate_partial, input_rows, 1, 0),
        ADAPTER_SCALE * contract_pair(up_partial, input_rows, 1, 0),
        ADAPTER_SCALE * contract_pair(output_gradient_rows, down_partial, 0, 1),
    )
    owned_slice = (
        ADAPTER_SCALE * contract_pair(gate_gradient, gate_projected_lower, 1, 1),
        ADAPTER_SCALE * contract_pair(up_gradient, up_projected_lower, 1, 1),
        ADAPTER_SCALE * contract_pair(down_projected_lower, hidden_units, 1, 1),
    )
    return (gradient_rows_out, shared_slice, owned_slice)


def general_local(
    tokens,
    output_gradient,
    routing,
    router_gate_values,
    gate_weight,
    up_weight,
    down_weight,
    adapter_lower_gate,
    adapter_upper_gate,
    adapter_lower_up,
    adapter_upper_up,
    adapter_lower_down,
    adapter_upper_down,
):
    experts = lax.axis_size("expert")
    shards = lax.axis_size("dp")
    tok_local, feat_local = tokens.shape
    choose = routing.shape[1]
    complete_width = feat_local * experts
    capacity = min(tok_local, 6 * tok_local // experts)
    hidden_units_local = gate_weight.shape[1]
    adapter_rank = adapter_lower_gate.shape[1]
    params = (
        gate_weight[0],
        up_weight[0],
        down_weight[0],
        adapter_lower_gate[0],
        adapter_upper_gate[0],
        adapter_lower_up[0],
        adapter_upper_up[0],
        adapter_lower_down[0],
        adapter_upper_down[0],
    )
    positions = slot_numbers(routing, experts)
    zero_row = jnp.zeros((1, feat_local), jnp.bfloat16)
    initial = (
        jnp.zeros((shards * capacity, complete_width), jnp.float32),
        (
            jnp.zeros((adapter_rank, complete_width), jnp.float32),
            jnp.zeros((adapter_rank, complete_width), jnp.float32),
            jnp.zeros((complete_width, adapter_rank), jnp.float32),
        ),
        (
            jnp.zeros((hidden_units_local, adapter_rank), jnp.float32),
            jnp.zeros((hidden_units_local, adapter_rank), jnp.float32),
            jnp.zeros((adapter_rank, hidden_units_local), jnp.float32),
        ),
    )
    source, member = slot_sources(routing, positions, experts, capacity)
    clamped = jnp.minimum(source, tok_local - 1)
    slot_gate = jnp.where(
        source < tok_local, router_gate_values.reshape(-1)[clamped * choose + member], 0.0
    )
    send_x = jnp.concatenate([tokens, zero_row], 0)[source].reshape(experts, capacity, feat_local)
    send_dy = (
        (
            slot_gate[:, None]
            * jnp.concatenate([output_gradient, zero_row], 0)[source].astype(jnp.float32)
        )
        .astype(jnp.bfloat16)
        .reshape(experts, capacity, feat_local)
    )
    recv_x, recv_dy = (
        lax.all_to_all(send_x, "expert", split_axis=0, concat_axis=2, tiled=True),
        lax.all_to_all(send_dy, "expert", split_axis=0, concat_axis=2, tiled=True),
    )
    gradient_rows_out, shared_slice, owned_slice = rows_backward_pass(
        lax.all_gather(recv_x[0], "dp", axis=0, tiled=True),
        lax.all_gather(recv_dy[0], "dp", axis=0, tiled=True),
        params,
    )
    rows_part = gradient_rows_out
    totals = (
        rows_part,
        jax.tree.map(jnp.add, initial[1], shared_slice),
        jax.tree.map(jnp.add, initial[2], owned_slice),
    )
    rows_part, shared_slice, owned_slice = totals
    summed = lax.psum_scatter(
        rows_part.astype(jnp.bfloat16), "dp", scatter_dimension=0, tiled=True
    ).astype(jnp.float32)
    returned_rows = lax.all_to_all(
        summed.reshape(capacity, experts, feat_local).astype(jnp.bfloat16),
        "expert",
        split_axis=1,
        concat_axis=1,
        tiled=True,
    ).astype(jnp.float32)
    lookup = positions * experts + routing
    grad_x = jnp.sum(returned_rows.reshape(capacity * experts, feat_local)[lookup], axis=1).astype(
        jnp.bfloat16
    )
    grad_a_gate, grad_a_up, grad_b_down = (
        lax.psum(shared_slice[0].astype(jnp.bfloat16), "dp").astype(jnp.float32),
        lax.psum(shared_slice[1].astype(jnp.bfloat16), "dp").astype(jnp.float32),
        lax.psum(shared_slice[2].astype(jnp.bfloat16), "dp").astype(jnp.float32),
    )
    return (
        grad_x,
        grad_a_gate[None],
        owned_slice[0][None],
        grad_a_up[None],
        owned_slice[1][None],
        owned_slice[2][None],
        grad_b_down[None],
    )


LANES = 128
TILE = 512
SHARDS = 8
VMEM_BYTES = 58 * 1024 * 1024
PACK_BYTES = 24 * 1024 * 1024
HIDDEN_BYTES = 58 * 1024 * 1024
TERM_BYTES = 58 * 1024 * 1024
HBM = pl.BlockSpec(memory_space=pl.ANY)
PINNED = pl.BlockSpec(memory_space=pltpu.HBM)
VMEM = pl.BlockSpec(memory_space=pltpu.VMEM)
SMEM = pl.BlockSpec(memory_space=pltpu.SMEM)


def dot_nt(left, right):
    return contract_pair(left, right, 1, 1)


def dot_nn(left, right):
    return contract_pair(left, right, 1, 0)


def wide(value):
    return value.astype(jnp.float32)


class Rows:
    def __init__(self, blocks):
        self.arrays, self.places, self.blocks = [], [], blocks

    def add(self, array, *places):
        self.arrays.append(array)
        self.places.append(places)


def row_copies(refs, places, target, sems, slab, first=0, order=None):
    tokens_each = refs[0].shape[-2]
    copies = []
    for ref, parts in zip(refs, places):
        for i, (at, block) in enumerate(parts):
            if at != slab:
                continue
            source = ref.at[i] if len(ref.shape) == 3 else ref
            row = (block - first) * tokens_each
            if order is not None:
                row = pl.multiple_of(order[block] * tokens_each, tokens_each)
            copies.append(
                pltpu.make_async_copy(
                    source, target.at[slab, pl.ds(row, tokens_each)], sems.at[slab, block]
                )
            )
    return copies


def pack_kernel(*refs):
    count = len(refs) // 2
    for source, target in zip(refs[:count], refs[count:]):
        slabs, _, feat = target.shape
        for slab in range(slabs):
            target[slab] = source[:, slab * feat : (slab + 1) * feat]


def pack_slabs(weights, slabs):
    hidden_here, width = weights[0].shape
    feat = width // slabs
    packed = jax.ShapeDtypeStruct((slabs, hidden_here, feat), jnp.bfloat16)
    return pl.pallas_call(
        pack_kernel,
        grid=(hidden_here // LANES,),
        out_shape=(packed,) * len(weights),
        in_specs=[pl.BlockSpec((LANES, width), lambda tile: (tile, 0))] * len(weights),
        out_specs=(pl.BlockSpec((slabs, LANES, feat), lambda tile: (0, tile, 0)),) * len(weights),
        compiler_params=pltpu.CompilerParams(vmem_limit_bytes=PACK_BYTES),
        cost_estimate=pl.CostEstimate(
            flops=0, bytes_accessed=4 * len(weights) * hidden_here * width, transcendentals=0
        ),
        name="pack_slabs",
    )(*weights)


def forward_kernel(places, first, *refs):
    n_pieces = len(places)
    pieces = refs[:n_pieces]
    (
        slab_ref,
        gate_hbm,
        up_hbm,
        lower_hbm,
        gate_upper_ref,
        up_upper_ref,
        silu_out,
        slope_out,
        hidden_out,
        low_out,
    ) = refs[n_pieces : n_pieces + 10]
    x_rows, weights, pre, saved, x_sems, w_sems, out_sems = refs[n_pieces + 10 :]
    slabs, _, feat = x_rows.shape
    hidden_here = gate_hbm.shape[1]
    pair, rank = lower_hbm.shape[1], gate_upper_ref.shape[1]

    def x_slab(slab):
        return row_copies(pieces, places, x_rows, x_sems, slab, first)

    def weight_copies(slab):
        at = slab_ref[slab]
        sides = (
            (gate_hbm.at[at], 0, hidden_here),
            (up_hbm.at[at], hidden_here, hidden_here),
            (lower_hbm.at[slab], 2 * hidden_here, pair),
        )
        return [
            pltpu.make_async_copy(
                source, weights.at[slab, pl.ds(start, size)], w_sems.at[slab, i]
            )
            for i, (source, start, size) in enumerate(sides)
        ]

    for slab in range(slabs):
        for copy in x_slab(slab) + weight_copies(slab):
            copy.start()
    for slab in range(slabs):
        for copy in x_slab(slab) + weight_copies(slab):
            copy.wait()
        if slab == 0:
            pre[...] = dot_nt(weights[0], x_rows[0])
        else:
            pre[...] += dot_nt(weights[slab], x_rows[slab])
    low_out[...] = pre[2 * hidden_here :, :].astype(jnp.bfloat16)

    def out_copies(tile):
        at = pl.ds(pl.multiple_of(tile * LANES, LANES), LANES)
        return [
            pltpu.make_async_copy(saved.at[i, at], out.at[at], out_sems.at[i, tile])
            for i, out in enumerate((silu_out, slope_out, hidden_out))
        ]

    tiles = hidden_here // LANES

    @pl.loop(0, tiles)
    def _(tile):
        start = pl.multiple_of(tile * LANES, LANES)
        at = pl.ds(start, LANES)
        up_at = pl.ds(pl.multiple_of(hidden_here + start, LANES), LANES)
        pre_gate = pre[at, :] + ADAPTER_SCALE * dot_nn(gate_upper_ref[at, :], low_out[:rank, :])
        pre_up = pre[up_at, :] + ADAPTER_SCALE * dot_nn(up_upper_ref[at, :], low_out[rank:, :])
        sigma = 1.0 / (1.0 + jnp.exp(-pre_gate))
        silu = pre_gate * sigma
        saved[0, at, :] = silu.astype(jnp.bfloat16)
        saved[1, at, :] = (pre_up * (sigma * (1.0 + pre_gate * (1.0 - sigma)))).astype(
            jnp.bfloat16
        )
        saved[2, at, :] = (silu * pre_up).astype(jnp.bfloat16)
        for copy in out_copies(tile):
            copy.start()

    @pl.loop(0, tiles)
    def _(tile):
        for copy in out_copies(tile):
            copy.wait()


def forward_rows(x, slab_order, weights, lower_slabs, gate_upper, up_upper):
    hidden_here, width = gate_upper.shape[0], weights[0].shape[0] * weights[0].shape[2]
    tokens_each, feat = x.arrays[0].shape[-2:]
    rows = len(x.blocks) * tokens_each
    slabs, pair, _ = lower_slabs.shape
    kept = jax.ShapeDtypeStruct((hidden_here, rows), jnp.bfloat16)
    return pl.pallas_call(
        lambda *refs: forward_kernel(x.places, x.blocks[0], *refs),
        out_shape=(kept, kept, kept, jax.ShapeDtypeStruct((pair, rows), jnp.bfloat16)),
        in_specs=[HBM] * len(x.arrays) + [SMEM] + [HBM] * 3 + [VMEM] * 2,
        out_specs=(HBM, HBM, HBM, VMEM),
        scratch_shapes=[
            pltpu.VMEM((slabs, rows, feat), jnp.bfloat16),
            pltpu.VMEM((slabs, 2 * hidden_here + pair, feat), jnp.bfloat16),
            pltpu.VMEM((2 * hidden_here + pair, rows), jnp.float32),
            pltpu.VMEM((3, hidden_here, rows), jnp.bfloat16),
            pltpu.SemaphoreType.DMA((slabs, SHARDS)),
            pltpu.SemaphoreType.DMA((slabs, 3)),
            pltpu.SemaphoreType.DMA((3, hidden_here // LANES)),
        ],
        compiler_params=pltpu.CompilerParams(vmem_limit_bytes=VMEM_BYTES),
        cost_estimate=pl.CostEstimate(
            flops=4 * rows * hidden_here * width,
            bytes_accessed=2 * rows * width,
            transcendentals=rows * hidden_here,
        ),
        name="forward_rows",
    )(*x.arrays, slab_order, *weights[:2], lower_slabs, gate_upper, up_upper)


def hidden_kernel(places, first, *refs):
    n_pieces = len(places)
    pieces = refs[:n_pieces]
    (
        slab_ref,
        route_ref,
        down_hbm,
        down_upper_hbm,
        down_lower_ref,
        down_lower_t_ref,
        gate_upper_ref,
        up_upper_ref,
        silu_hbm,
        slope_hbm,
        hidden_hbm,
        d_pair,
        parts_out,
        low_down,
        rows,
        down_w,
        d_down,
        silu,
        slope,
        hidden,
        row_sems,
        d_sems,
        f_sems,
    ) = refs[n_pieces:]
    slabs, _, feat = rows.shape
    hidden_here = silu.shape[0]
    rank = down_lower_ref.shape[0]
    saved_copies = [
        pltpu.make_async_copy(source, target, f_sems.at[i])
        for i, (source, target) in enumerate(
            ((silu_hbm, silu), (slope_hbm, slope), (hidden_hbm, hidden))
        )
    ]

    def slab_copies(slab):
        return row_copies(pieces, places, rows, row_sems, slab, first) + [
            pltpu.make_async_copy(
                down_hbm.at[slab_ref[slab]],
                down_w.at[slab, pl.ds(0, hidden_here)],
                d_sems.at[slab, 0],
            ),
            pltpu.make_async_copy(
                down_upper_hbm.at[slab], down_w.at[slab, pl.ds(hidden_here, rank)], d_sems.at[slab, 1]
            ),
        ]

    for slab in range(slabs):
        for copy in slab_copies(slab):
            copy.start()
    for copy in saved_copies:
        copy.start()
    for slab in range(slabs):
        for copy in slab_copies(slab):
            copy.wait()
        if slab == 0:
            d_down[...] = dot_nt(down_w[0], rows[0])
        else:
            d_down[...] += dot_nt(down_w[slab], rows[slab])

    low_down[...] = (d_down[hidden_here:, :] * route_ref[...]).astype(jnp.bfloat16)
    for copy in saved_copies:
        copy.wait()

    @pl.loop(0, hidden_here // LANES)
    def _(tile):
        start = pl.multiple_of(tile * LANES, LANES)
        at = pl.ds(start, LANES)
        up_at = pl.ds(pl.multiple_of(hidden_here + start, LANES), LANES)
        d_hidden = d_down[at, :] * route_ref[...]
        d_hidden = d_hidden + ADAPTER_SCALE * dot_nn(down_lower_t_ref[at, :], low_down[...])
        d_gate = (d_hidden * wide(slope[at, :])).astype(jnp.bfloat16)
        d_up = (d_hidden * wide(silu[at, :])).astype(jnp.bfloat16)
        d_pair[:, at] = d_gate.T
        d_pair[:, up_at] = d_up.T

    for side, factor in enumerate((gate_upper_ref, up_upper_ref)):
        start = side * hidden_here
        part = dot_nn(d_pair[:, start : start + hidden_here], factor[...])
        parts_out[side * rank : (side + 1) * rank, :] = part.T
        at = 2 * hidden_here + side * rank
        d_pair[:, at : at + rank] = ADAPTER_SCALE * part.astype(jnp.bfloat16)
    parts_out[2 * rank :, :] = dot_nn(down_lower_ref[...], hidden[...])


def hidden_gradients(dy, slab_order, route_row, down_weight, down_upper, factors, saved):
    hidden_here = down_weight.shape[1]
    slabs, rank, feat = down_upper.shape
    width = slabs * feat
    pair = 2 * rank
    rows = route_row.shape[1]
    return pl.pallas_call(
        lambda *refs: hidden_kernel(dy.places, dy.blocks[0], *refs),
        out_shape=(
            jax.ShapeDtypeStruct((rows, 2 * hidden_here + pair), jnp.bfloat16),
            jax.ShapeDtypeStruct((3 * rank, rows), jnp.float32),
            jax.ShapeDtypeStruct((rank, rows), jnp.bfloat16),
        ),
        in_specs=[HBM] * len(dy.arrays) + [SMEM, VMEM] + [HBM] * 2 + [VMEM] * 4 + [HBM] * 3,
        out_specs=(VMEM,) * 3,
        scratch_shapes=[
            pltpu.VMEM((slabs, rows, feat), jnp.bfloat16),
            pltpu.VMEM((slabs, hidden_here + rank, feat), jnp.bfloat16),
            pltpu.VMEM((hidden_here + rank, rows), jnp.float32),
            pltpu.VMEM((hidden_here, rows), jnp.bfloat16),
            pltpu.VMEM((hidden_here, rows), jnp.bfloat16),
            pltpu.VMEM((hidden_here, rows), jnp.bfloat16),
            pltpu.SemaphoreType.DMA((slabs, SHARDS)),
            pltpu.SemaphoreType.DMA((slabs, 2)),
            pltpu.SemaphoreType.DMA((3,)),
        ],
        compiler_params=pltpu.CompilerParams(vmem_limit_bytes=HIDDEN_BYTES),
        cost_estimate=pl.CostEstimate(
            flops=4 * rows * hidden_here * width,
            bytes_accessed=2 * hidden_here * width + 2 * rows * width,
            transcendentals=0,
        ),
        name="hidden_gradients",
    )(*dy.arrays, slab_order, route_row, down_weight, down_upper, *factors, *saved)


def term_kernel(slabs, n_parts, *refs):
    d_parts = refs[:n_parts]
    slab_ref, gate_hbm, up_hbm, lower_hbm = refs[n_parts : n_parts + 4]
    outs, (d_pair, pair_w, sems, d_sems) = refs[n_parts + 4 : -4], refs[-4:]
    _, depth, feat = pair_w.shape
    hidden_here = gate_hbm.shape[1]
    pair = depth - 2 * hidden_here
    tokens_each = outs[0].shape[2]

    def weight_copies(i):
        at = slab_ref[slabs[i]]
        sides = (
            (gate_hbm.at[at], 0, hidden_here),
            (up_hbm.at[at], hidden_here, hidden_here),
            (lower_hbm.at[slabs[i]], 2 * hidden_here, pair),
        )
        return [
            pltpu.make_async_copy(source, pair_w.at[i, pl.ds(start, size)], sems.at[i, side])
            for side, (source, start, size) in enumerate(sides)
        ]

    d_copies, row = [], 0
    for i, part in enumerate(d_parts):
        count = part.shape[0]
        d_copies.append(pltpu.make_async_copy(part, d_pair.at[pl.ds(row, count)], d_sems.at[i]))
        row += count
    for copy in d_copies:
        copy.start()
    for i in range(len(slabs)):
        for copy in weight_copies(i):
            copy.start()
    for copy in d_copies:
        copy.wait()
    for i in range(len(slabs)):
        for copy in weight_copies(i):
            copy.wait()

        @pl.loop(0, feat // TILE)
        def _(n):
            lanes = pl.ds(pl.multiple_of(n * TILE, TILE), TILE)
            term = dot_nn(d_pair[...], pair_w[i, :, lanes]).astype(jnp.bfloat16)
            for block in range(SHARDS):
                at = slice(block * tokens_each, (block + 1) * tokens_each)
                outs[block % 2][block // 2, i, :, lanes] = term[at]


def slab_terms(slabs, slab_order, d_pair, weights, lower_slabs):
    rows, depth = sum(part.shape[0] for part in d_pair), d_pair[0].shape[1]
    feat = lower_slabs.shape[2]
    term = jax.ShapeDtypeStruct((SHARDS // 2, len(slabs), rows // SHARDS, feat), jnp.bfloat16)
    return pl.pallas_call(
        lambda *refs: term_kernel(slabs, len(d_pair), *refs),
        out_shape=(term, term),
        in_specs=[HBM] * len(d_pair) + [SMEM] + [HBM] * 3,
        out_specs=(VMEM, VMEM),
        scratch_shapes=[
            pltpu.VMEM((rows, depth), jnp.bfloat16),
            pltpu.VMEM((len(slabs), depth, feat), jnp.bfloat16),
            pltpu.SemaphoreType.DMA((len(slabs), 3)),
            pltpu.SemaphoreType.DMA((len(d_pair),)),
        ],
        compiler_params=pltpu.CompilerParams(vmem_limit_bytes=TERM_BYTES),
        cost_estimate=pl.CostEstimate(
            flops=4 * rows * depth * feat * len(slabs),
            bytes_accessed=2 * depth * feat * len(slabs) + 4 * rows * depth,
            transcendentals=0,
        ),
        name="slab_terms",
    )(*d_pair, slab_order, *weights[:2], lower_slabs)


def shared_kernel(x_places, dy_places, n_parts, *refs):
    split, inputs = len(x_places), len(x_places) + len(dy_places)
    x_pieces, dy_pieces = refs[:split], refs[split:inputs]
    (
        order_ref,
        slab_ref,
        sums_ref,
        down_sums_ref,
    ) = refs[inputs : inputs + 4]
    inputs += 4
    parts = [refs[inputs + 4 * i : inputs + 4 * i + 4] for i in range(n_parts)]
    inputs += 4 * n_parts
    pair_out, down_out, owned_out, owned_down_out = refs[inputs : inputs + 4]
    x_rows, dy_rows, sums, down_sums, x_sems, dy_sems = refs[inputs + 4 :]
    rank, hidden_here = owned_down_out.shape
    slabs, _, feat = x_rows.shape
    tokens_each = x_pieces[0].shape[-2]

    def slab_copies(slab):
        return row_copies(x_pieces, x_places, x_rows, x_sems, slab, 0, order_ref) + row_copies(
            dy_pieces, dy_places, dy_rows, dy_sems, slab, 0, order_ref
        )

    for slab in range(slabs):
        for copy in slab_copies(slab):
            copy.start()
    for block in range(SHARDS):
        lanes = pl.ds(pl.multiple_of(order_ref[block] * tokens_each, tokens_each), tokens_each)
        sums[:, lanes] = sums_ref[block]
        down_sums[:, lanes] = down_sums_ref[block]
    gate_sum = up_sum = down_sum = 0.0
    for low, low_down, d_pair, hidden in parts:
        gate_sum += dot_nn(low[:rank, :], d_pair[:, :hidden_here])
        up_sum += dot_nn(low[rank:, :], d_pair[:, hidden_here : 2 * hidden_here])
        down_sum += dot_nt(low_down[...], hidden[...])
    owned_out[0] = ADAPTER_SCALE * gate_sum
    owned_out[1] = ADAPTER_SCALE * up_sum
    owned_down_out[...] = ADAPTER_SCALE * down_sum
    for slab in range(slabs):
        for copy in slab_copies(slab):
            copy.wait()

        @pl.loop(0, feat // TILE)
        def _(n):
            lanes = pl.ds(pl.multiple_of(n * TILE, TILE), TILE)
            out = pl.ds(pl.multiple_of(slab_ref[slab] * feat + n * TILE, TILE), TILE)
            pair_out[:, out] = ADAPTER_SCALE * dot_nn(
                sums[...].astype(jnp.bfloat16), x_rows[slab, :, lanes]
            )
            down_out[:, out] = ADAPTER_SCALE * dot_nn(
                down_sums[...].astype(jnp.bfloat16), dy_rows[slab, :, lanes]
            )


def adapter_gradients(x, dy, order, slab_order, sums, down_sums, parts):
    tokens_each, feat = x.arrays[0].shape[-2:]
    slabs = slab_order.shape[0]
    rows = SHARDS * tokens_each
    pair, rank = sums.shape[1], down_sums.shape[1]
    hidden_here = parts[0][3].shape[0]
    return pl.pallas_call(
        lambda *refs: shared_kernel(x.places, dy.places, len(parts), *refs),
        out_shape=(
            jax.ShapeDtypeStruct((pair, slabs * feat), jnp.float32),
            jax.ShapeDtypeStruct((rank, slabs * feat), jnp.float32),
            jax.ShapeDtypeStruct((2, rank, hidden_here), jnp.float32),
            jax.ShapeDtypeStruct((rank, hidden_here), jnp.float32),
        ),
        in_specs=[HBM] * (len(x.arrays) + len(dy.arrays)) + [SMEM, SMEM]
        + [VMEM] * (2 + 4 * len(parts)),
        out_specs=(VMEM,) * 4,
        scratch_shapes=[
            pltpu.VMEM((slabs, rows, feat), jnp.bfloat16),
            pltpu.VMEM((slabs, rows, feat), jnp.bfloat16),
            pltpu.VMEM((pair, rows), jnp.float32),
            pltpu.VMEM((rank, rows), jnp.float32),
            pltpu.SemaphoreType.DMA((slabs, SHARDS)),
            pltpu.SemaphoreType.DMA((slabs, SHARDS)),
        ],
        compiler_params=pltpu.CompilerParams(vmem_limit_bytes=VMEM_BYTES),
        cost_estimate=pl.CostEstimate(
            flops=200 * rows * pair * slabs * feat,
            bytes_accessed=12 * rows * slabs * feat,
            transcendentals=0,
        ),
        name="adapter_gradients",
    )(
        *x.arrays,
        *dy.arrays,
        order,
        slab_order,
        sums,
        down_sums,
        *(value for part in parts for value in part),
    )


CORE, ACROSS, ALONG = 1, 2, 4
PLANE = (ACROSS, ALONG, ACROSS | ALONG)


def swap(value, bit, axis="dp"):
    return lax.ppermute(value, axis, [(i, i ^ bit) for i in range(lax.axis_size(axis))])


def after(value, *others):
    return lax.optimization_barrier((value, others))[0]


def added(left, right):
    return (wide(left) + wide(right)).astype(jnp.bfloat16)


def local(
    tokens,
    output_gradient,
    routing,
    router_gate_values,
    gate_weight,
    up_weight,
    down_weight,
    adapter_lower_gate,
    adapter_upper_gate,
    adapter_lower_up,
    adapter_upper_up,
    adapter_lower_down,
    adapter_upper_down,
):
    experts = lax.axis_size("expert")
    me, expert = lax.axis_index("dp"), lax.axis_index("expert")
    tokens_each, feat = tokens.shape
    rank = adapter_lower_gate.shape[1]
    order = jnp.bitwise_xor(jnp.arange(SHARDS, dtype=jnp.int32), me.astype(jnp.int32))
    slab_order = jnp.bitwise_xor(jnp.arange(experts, dtype=jnp.int32), expert.astype(jnp.int32))

    named = routing[:, :, None] == jnp.arange(experts, dtype=jnp.int32)[None, None, :]
    weight_of = jnp.sum(jnp.where(named, router_gate_values[:, :, None], 0.0), axis=1)
    routes = lax.all_gather(weight_of.T, "dp", axis=0, tiled=False)
    route = lax.dynamic_index_in_dim(routes, expert, axis=1, keepdims=False)[order]
    route_blocks = route[:, None, :]
    route_row = route.reshape(1, SHARDS * tokens_each)

    def slabs_first(factor):
        return factor.reshape(factor.shape[0], experts, feat).transpose(1, 0, 2)[slab_order]

    lower_cat = jnp.concatenate([adapter_lower_gate[0], adapter_lower_up[0]], axis=0)
    down_lower = adapter_lower_down[0]

    def place_both(rows, part, swapped, chip, slabs):
        rows.add(part, *((r, 2 * chip) for r in slabs))
        rows.add(swapped, *((r, 2 * chip + 1) for r in slabs))

    def over_experts(block, r):
        return swap(block, r, "expert")

    both = over_experts(jnp.stack([tokens, output_gradient]), 1)
    x_slabs = [both[0]] + [over_experts(tokens, r) for r in range(2, experts)]
    x_near = [tokens] + [swap(tokens, bit) for bit in PLANE[:2]]
    weights = pack_slabs((gate_weight[0], up_weight[0], down_weight[0]), experts)
    uppers = (adapter_upper_gate[0], adapter_upper_up[0])
    (x_slabs, x_near, dy_near), small = lax.optimization_barrier(
        ((x_slabs, x_near, both[1]), (route_row, adapter_upper_down[0], lower_cat, uppers, weights))
    )
    route_row, down_upper, lower_cat, uppers, weights = small
    lower_slabs, down_upper = slabs_first(lower_cat), slabs_first(down_upper.T)
    ready = (lower_slabs, down_upper, down_lower, down_lower.T, *uppers)

    x_rest = [jnp.stack(x_slabs)]
    x_rest += [swap(x_rest[0], bit) for bit in PLANE[:2]]
    x_near.append(swap(x_near[2], ACROSS))
    dy_late = after(output_gradient, x_rest[0])
    dy_slabs = [output_gradient, dy_near] + [over_experts(dy_late, r) for r in range(2, experts)]

    (x_rest, x_near, dy_slabs), ready = lax.optimization_barrier(
        ((x_rest, x_near, dy_slabs), ready)
    )
    lower_slabs, down_upper, *factors = ready
    uppers = factors[2:]
    half = experts // 2
    x_far = [swap(x_rest[2][: half - 1], ACROSS), swap(x_rest[1][half - 1 :], ALONG)]
    x_near_swapped = swap(jnp.stack(x_near[:3]), CORE)
    x_rest_swapped = [swap(part, CORE) for part in x_rest[:2]]
    x_near_swapped, x_rest_swapped, x_last = lax.optimization_barrier(
        (x_near_swapped, x_rest_swapped, x_rest[2])
    )
    x_rest_swapped.append(swap(x_last, CORE))
    dy_all = after(jnp.stack(dy_slabs), x_near_swapped, *x_rest_swapped[:2])
    dy_plane = [swap(dy_all, bit) for bit in PLANE[:2]]

    x_main = Rows(range(6))
    for chip, part in enumerate(x_near[:3]):
        x_main.add(part, (0, 2 * chip))
    x_main.add(x_near_swapped, *((0, 2 * chip + 1) for chip in range(3)))
    for chip, (part, swapped) in enumerate(zip(x_rest, x_rest_swapped)):
        place_both(x_main, part, swapped, chip, range(1, experts))

    saved = [forward_rows(x_main, slab_order, weights, lower_slabs, *uppers)]

    x_far = after(x_far, saved[0][0])
    x_far[0] = jnp.concatenate([x_near[3][None], x_far[0]], axis=0)
    far_slabs = (range(half), range(half, experts))
    x_away = Rows(range(6, SHARDS))
    for part, slabs in zip(x_far, far_slabs):
        place_both(x_away, part, swap(part, CORE), 3, slabs)
    saved.append(forward_rows(x_away, slab_order, weights, lower_slabs, *uppers))

    dy_rows = [dy_all, *after(dy_plane, saved[1][0])]
    dy_far = [swap(dy_rows[2][:half], ACROSS), swap(dy_rows[1][half:], ALONG)]
    dy_main, dy_away = Rows(range(6)), Rows(range(6, SHARDS))
    for chip, part in enumerate(dy_rows):
        place_both(dy_main, part, swap(part, CORE), chip, range(experts))
    split = 6 * tokens_each
    grads = [
        hidden_gradients(
            dy_main, slab_order, route_row[:, :split], weights[2], down_upper, factors, saved[0][:3]
        )
    ]
    dy_far = after(dy_far, grads[0][0])
    for part, slabs in zip(dy_far, far_slabs):
        place_both(dy_away, part, swap(part, CORE), 3, slabs)
    grads.append(
        hidden_gradients(
            dy_away, slab_order, route_row[:, split:], weights[2], down_upper, factors, saved[1][:3]
        )
    )
    d_pair = [grad[0] for grad in grads]
    parts = jnp.concatenate([grad[1] for grad in grads], axis=1)

    def sum_step(total, bit):
        other = swap(total.reshape(SHARDS, 3 * rank, tokens_each), bit)
        shape = (SHARDS // (2 * bit), 2, bit, 3 * rank, tokens_each)
        return total.reshape(shape) + other.reshape(shape)[:, ::-1]

    sums = [parts.reshape(3 * rank, SHARDS, tokens_each).transpose(1, 0, 2)]
    for bit in (CORE, ACROSS, ALONG):
        sums.append(sum_step(sums[-1], bit))

    def send(keep, got):
        chips = [added(keep[i], got[i]) for i in range(SHARDS // 2)]
        return chips, [swap(part, bit) for bit, part in zip(PLANE, chips[1:])]

    def total_rows(chips, moved):
        return sum((wide(part) for part in moved), wide(chips[0]))

    def terms(group, *others):
        here = after(slab_order, *others)
        keep, away = slab_terms(group, here, d_pair, weights, lower_slabs)
        return keep, swap(away, CORE)

    keep_a, got_a = terms((3,), sums[1])
    keep_b, got_b = terms((2,), sums[2])
    chips_a, moved_a = send(keep_a, after(got_a, keep_b))
    keep_c, got_c = terms((1, 0), sums[3], *chips_a)
    rows_a = total_rows(chips_a, after(moved_a, keep_c))
    chips_b, moved_b = send(keep_b, after(got_b, keep_c))
    total = after(sums[3].reshape(SHARDS, 3 * rank, tokens_each), rows_a, *chips_b)
    x, dy = Rows(range(SHARDS)), Rows(range(SHARDS))
    for whole, halves in ((x, (x_main, x_away)), (dy, (dy_main, dy_away))):
        for rows in halves:
            whole.arrays += rows.arrays
            whole.places += rows.places
    grad_pair, grad_down, owned, owned_down = adapter_gradients(
        x,
        dy,
        order,
        slab_order,
        total[:, : 2 * rank],
        total[:, 2 * rank :] * route_blocks,
        [(kept[3], grad[2], grad[0], kept[2]) for kept, grad in zip(saved, grads)],
    )
    got_c, moved_b = after((got_c, moved_b), grad_pair)
    chips_c, moved_c = send(keep_c, got_c)
    rows_b = total_rows(chips_b, moved_b)
    rows_c = total_rows(chips_c, moved_c)
    grad_x = rows_c[1]
    for rows, r in ((rows_a[0], 3), (rows_b[0], 2), (rows_c[0], 1)):
        grad_x = grad_x + wide(over_experts(rows.astype(jnp.bfloat16), r))
    grad_x = grad_x.astype(jnp.bfloat16)
    return (
        grad_x,
        grad_pair[None, :rank],
        owned[0].T[None],
        grad_pair[None, rank:],
        owned[1].T[None],
        owned_down[None],
        grad_down.T[None],
    )


def plan(tokens, *others):
    experts, tokens_each, hidden_here = lax.axis_size("expert"), tokens.shape[0], others[3].shape[1]
    planned = (
        lax.axis_size("dp") == SHARDS
        and experts == 4
        and hidden_here % LANES == 0
        and tokens_each % LANES == 0
        and tokens.shape[1] % TILE == 0
    )
    return (local if planned else general_local)(tokens, *others)


def solution(mesh):
    return jax.shard_map(
        plan,
        mesh=mesh,
        in_specs=(
            P("dp", "expert"),
            P("dp", "expert"),
            P("dp", None),
            P("dp", None),
            P("expert", "dp", None),
            P("expert", "dp", None),
            P("expert", "dp", None),
            P("expert", None, None),
            P("expert", "dp", None),
            P("expert", None, None),
            P("expert", "dp", None),
            P("expert", None, "dp"),
            P("expert", None, None),
        ),
        out_specs=(
            P("dp", "expert"),
            P("expert", None, None),
            P("expert", "dp", None),
            P("expert", None, None),
            P("expert", "dp", None),
            P("expert", None, "dp"),
            P("expert", None, None),
        ),
        check_vma=False,
    )
```

```python
import jax
import jax.numpy as jnp
from jax import lax
from jax.experimental import pallas as pl
from jax.experimental.pallas import tpu as pltpu
from jax.sharding import PartitionSpec as P

ADAPTER_SCALE = 2.0


def contract_pair(left, right, left_axis, right_axis):
    return lax.dot_general(
        left, right, (((left_axis,), (right_axis,)), ((), ())), preferred_element_type=jnp.float32
    )


def slot_numbers(route_rows, experts):
    picked = (route_rows[:, :, None] == jnp.arange(experts, dtype=jnp.int32)[None, None, :]).astype(
        jnp.int32
    )
    per_token = jnp.sum(picked, axis=1)
    earlier = jnp.cumsum(per_token, axis=0) - per_token
    return jnp.sum(earlier[:, None, :] * picked, axis=2)


def slot_sources(route_rows, positions, experts, capacity):
    tokens_here, choose = route_rows.shape
    target = (route_rows * capacity + positions).reshape(-1)
    owners = jnp.repeat(jnp.arange(tokens_here, dtype=jnp.int32), choose)
    member_ids = jnp.tile(jnp.arange(choose, dtype=jnp.int32), tokens_here)
    source = jnp.full((experts * capacity,), tokens_here, jnp.int32).at[target].set(owners)
    member = jnp.zeros((experts * capacity,), jnp.int32).at[target].set(member_ids)
    return (source, member)


def rows_backward_pass(input_rows, output_gradient_rows, params):
    (
        gate_weight,
        up_weight,
        down_weight,
        a_gate,
        gate_adapter_upper,
        a_up,
        up_adapter_upper,
        down_adapter_lower,
        b_down,
    ) = params
    gate_projected_lower = contract_pair(a_gate, input_rows, 1, 1).astype(jnp.bfloat16)
    up_projected_lower = contract_pair(a_up, input_rows, 1, 1).astype(jnp.bfloat16)
    gate_preactivation = contract_pair(
        gate_weight, input_rows, 1, 1
    ) + ADAPTER_SCALE * contract_pair(gate_adapter_upper, gate_projected_lower, 1, 0)
    up_preactivation = contract_pair(up_weight, input_rows, 1, 1) + ADAPTER_SCALE * contract_pair(
        up_adapter_upper, up_projected_lower, 1, 0
    )
    sigmoid_gate = jax.nn.sigmoid(gate_preactivation)
    silu_gate = gate_preactivation * sigmoid_gate
    hidden_units = (silu_gate * up_preactivation).astype(jnp.bfloat16)
    down_projected_lower = contract_pair(b_down, output_gradient_rows, 0, 1).astype(jnp.bfloat16)
    hidden_gradient = contract_pair(
        down_weight, output_gradient_rows, 1, 1
    ) + ADAPTER_SCALE * contract_pair(down_adapter_lower, down_projected_lower, 0, 0)
    gate_gradient = (
        hidden_gradient
        * up_preactivation
        * sigmoid_gate
        * (1.0 + gate_preactivation * (1.0 - sigmoid_gate))
    ).astype(jnp.bfloat16)
    up_gradient = (hidden_gradient * silu_gate).astype(jnp.bfloat16)
    gate_partial = contract_pair(gate_adapter_upper, gate_gradient, 0, 0).astype(jnp.bfloat16)
    up_partial = contract_pair(up_adapter_upper, up_gradient, 0, 0).astype(jnp.bfloat16)
    down_partial = contract_pair(down_adapter_lower, hidden_units, 1, 0).astype(jnp.bfloat16)
    paired_partials = jnp.concatenate([gate_partial, up_partial], 0)
    paired_factors = jnp.concatenate([a_gate, a_up], 0)
    gradient_rows_out = (
        contract_pair(gate_gradient, gate_weight, 0, 0)
        + contract_pair(up_gradient, up_weight, 0, 0)
        + ADAPTER_SCALE * contract_pair(paired_partials, paired_factors, 0, 0)
    )
    shared_slice = (
        ADAPTER_SCALE * contract_pair(gate_partial, input_rows, 1, 0),
        ADAPTER_SCALE * contract_pair(up_partial, input_rows, 1, 0),
        ADAPTER_SCALE * contract_pair(output_gradient_rows, down_partial, 0, 1),
    )
    owned_slice = (
        ADAPTER_SCALE * contract_pair(gate_gradient, gate_projected_lower, 1, 1),
        ADAPTER_SCALE * contract_pair(up_gradient, up_projected_lower, 1, 1),
        ADAPTER_SCALE * contract_pair(down_projected_lower, hidden_units, 1, 1),
    )
    return (gradient_rows_out, shared_slice, owned_slice)


def general_local(
    tokens,
    output_gradient,
    routing,
    router_gate_values,
    gate_weight,
    up_weight,
    down_weight,
    adapter_lower_gate,
    adapter_upper_gate,
    adapter_lower_up,
    adapter_upper_up,
    adapter_lower_down,
    adapter_upper_down,
):
    experts = lax.axis_size("expert")
    shards = lax.axis_size("dp")
    tok_local, feat_local = tokens.shape
    choose = routing.shape[1]
    complete_width = feat_local * experts
    capacity = min(tok_local, 6 * tok_local // experts)
    hidden_units_local = gate_weight.shape[1]
    adapter_rank = adapter_lower_gate.shape[1]
    params = (
        gate_weight[0],
        up_weight[0],
        down_weight[0],
        adapter_lower_gate[0],
        adapter_upper_gate[0],
        adapter_lower_up[0],
        adapter_upper_up[0],
        adapter_lower_down[0],
        adapter_upper_down[0],
    )
    positions = slot_numbers(routing, experts)
    zero_row = jnp.zeros((1, feat_local), jnp.bfloat16)
    initial = (
        jnp.zeros((shards * capacity, complete_width), jnp.float32),
        (
            jnp.zeros((adapter_rank, complete_width), jnp.float32),
            jnp.zeros((adapter_rank, complete_width), jnp.float32),
            jnp.zeros((complete_width, adapter_rank), jnp.float32),
        ),
        (
            jnp.zeros((hidden_units_local, adapter_rank), jnp.float32),
            jnp.zeros((hidden_units_local, adapter_rank), jnp.float32),
            jnp.zeros((adapter_rank, hidden_units_local), jnp.float32),
        ),
    )
    source, member = slot_sources(routing, positions, experts, capacity)
    clamped = jnp.minimum(source, tok_local - 1)
    slot_gate = jnp.where(
        source < tok_local, router_gate_values.reshape(-1)[clamped * choose + member], 0.0
    )
    send_x = jnp.concatenate([tokens, zero_row], 0)[source].reshape(experts, capacity, feat_local)
    send_dy = (
        (
            slot_gate[:, None]
            * jnp.concatenate([output_gradient, zero_row], 0)[source].astype(jnp.float32)
        )
        .astype(jnp.bfloat16)
        .reshape(experts, capacity, feat_local)
    )
    recv_x, recv_dy = (
        lax.all_to_all(send_x, "expert", split_axis=0, concat_axis=2, tiled=True),
        lax.all_to_all(send_dy, "expert", split_axis=0, concat_axis=2, tiled=True),
    )
    gradient_rows_out, shared_slice, owned_slice = rows_backward_pass(
        lax.all_gather(recv_x[0], "dp", axis=0, tiled=True),
        lax.all_gather(recv_dy[0], "dp", axis=0, tiled=True),
        params,
    )
    rows_part = gradient_rows_out
    totals = (
        rows_part,
        jax.tree.map(jnp.add, initial[1], shared_slice),
        jax.tree.map(jnp.add, initial[2], owned_slice),
    )
    rows_part, shared_slice, owned_slice = totals
    summed = lax.psum_scatter(
        rows_part.astype(jnp.bfloat16), "dp", scatter_dimension=0, tiled=True
    ).astype(jnp.float32)
    returned_rows = lax.all_to_all(
        summed.reshape(capacity, experts, feat_local).astype(jnp.bfloat16),
        "expert",
        split_axis=1,
        concat_axis=1,
        tiled=True,
    ).astype(jnp.float32)
    lookup = positions * experts + routing
    grad_x = jnp.sum(returned_rows.reshape(capacity * experts, feat_local)[lookup], axis=1).astype(
        jnp.bfloat16
    )
    grad_a_gate, grad_a_up, grad_b_down = (
        lax.psum(shared_slice[0].astype(jnp.bfloat16), "dp").astype(jnp.float32),
        lax.psum(shared_slice[1].astype(jnp.bfloat16), "dp").astype(jnp.float32),
        lax.psum(shared_slice[2].astype(jnp.bfloat16), "dp").astype(jnp.float32),
    )
    return (
        grad_x,
        grad_a_gate[None],
        owned_slice[0][None],
        grad_a_up[None],
        owned_slice[1][None],
        owned_slice[2][None],
        grad_b_down[None],
    )


LANES = 128
TILE = 512
SHARDS = 8
VMEM_BYTES = 58 * 1024 * 1024
HIDDEN_BYTES = 58 * 1024 * 1024
TERM_BYTES = 58 * 1024 * 1024
HBM = pl.BlockSpec(memory_space=pl.ANY)
PINNED = pl.BlockSpec(memory_space=pltpu.HBM)
VMEM = pl.BlockSpec(memory_space=pltpu.VMEM)
SMEM = pl.BlockSpec(memory_space=pltpu.SMEM)


def dot_nt(left, right):
    return contract_pair(left, right, 1, 1)


def dot_nn(left, right):
    return contract_pair(left, right, 1, 0)


def wide(value):
    return value.astype(jnp.float32)


class Rows:
    def __init__(self, blocks):
        self.arrays, self.places, self.blocks = [], [], blocks

    def add(self, array, *places):
        self.arrays.append(array)
        self.places.append(places)


def row_copies(refs, places, target, sems, slab, first=0, order=None):
    tokens_each = refs[0].shape[-2]
    copies = []
    for ref, parts in zip(refs, places):
        for i, (at, block) in enumerate(parts):
            if at != slab:
                continue
            source = ref.at[i] if len(ref.shape) == 3 else ref
            row = (block - first) * tokens_each
            if order is not None:
                row = pl.multiple_of(order[block] * tokens_each, tokens_each)
            copies.append(
                pltpu.make_async_copy(
                    source, target.at[slab, pl.ds(row, tokens_each)], sems.at[slab, block]
                )
            )
    return copies


def slab_lanes(slab_ref, slab, feat):
    return pl.ds(pl.multiple_of(slab_ref[slab] * feat, feat), feat)


def forward_kernel(places, first, *refs):
    n_pieces = len(places)
    pieces = refs[:n_pieces]
    (
        slab_ref,
        gate_hbm,
        up_hbm,
        lower_hbm,
        gate_upper_ref,
        up_upper_ref,
        silu_out,
        slope_out,
        hidden_out,
        low_out,
    ) = refs[n_pieces : n_pieces + 10]
    x_rows, weights, pre, saved, x_sems, w_sems, out_sems = refs[n_pieces + 10 :]
    slabs, _, feat = x_rows.shape
    hidden_here = gate_hbm.shape[0]
    pair, rank = lower_hbm.shape[1], gate_upper_ref.shape[1]

    def x_slab(slab):
        return row_copies(pieces, places, x_rows, x_sems, slab, first)

    def weight_copies(slab):
        lanes = slab_lanes(slab_ref, slab, feat)
        sides = (
            (gate_hbm.at[:, lanes], 0, hidden_here),
            (up_hbm.at[:, lanes], hidden_here, hidden_here),
            (lower_hbm.at[slab], 2 * hidden_here, pair),
        )
        return [
            pltpu.make_async_copy(
                source, weights.at[slab, pl.ds(start, size)], w_sems.at[slab, i]
            )
            for i, (source, start, size) in enumerate(sides)
        ]

    for slab in range(slabs):
        for copy in x_slab(slab) + weight_copies(slab):
            copy.start()
    for slab in range(slabs):
        for copy in x_slab(slab) + weight_copies(slab):
            copy.wait()
        if slab == 0:
            pre[...] = dot_nt(weights[0], x_rows[0])
        else:
            pre[...] += dot_nt(weights[slab], x_rows[slab])
    low_out[...] = pre[2 * hidden_here :, :].astype(jnp.bfloat16)

    def out_copies(tile):
        at = pl.ds(pl.multiple_of(tile * LANES, LANES), LANES)
        return [
            pltpu.make_async_copy(saved.at[i, at], out.at[at], out_sems.at[i, tile])
            for i, out in enumerate((silu_out, slope_out, hidden_out))
        ]

    tiles = hidden_here // LANES

    @pl.loop(0, tiles)
    def _(tile):
        start = pl.multiple_of(tile * LANES, LANES)
        at = pl.ds(start, LANES)
        up_at = pl.ds(pl.multiple_of(hidden_here + start, LANES), LANES)
        pre_gate = pre[at, :] + ADAPTER_SCALE * dot_nn(gate_upper_ref[at, :], low_out[:rank, :])
        pre_up = pre[up_at, :] + ADAPTER_SCALE * dot_nn(up_upper_ref[at, :], low_out[rank:, :])
        sigma = 1.0 / (1.0 + jnp.exp(-pre_gate))
        silu = pre_gate * sigma
        saved[0, at, :] = silu.astype(jnp.bfloat16)
        saved[1, at, :] = (pre_up * (sigma * (1.0 + pre_gate * (1.0 - sigma)))).astype(
            jnp.bfloat16
        )
        saved[2, at, :] = (silu * pre_up).astype(jnp.bfloat16)
        for copy in out_copies(tile):
            copy.start()

    @pl.loop(0, tiles)
    def _(tile):
        for copy in out_copies(tile):
            copy.wait()


def forward_rows(x, slab_order, weights, lower_slabs, gate_upper, up_upper):
    hidden_here, width = weights[0].shape
    tokens_each, feat = x.arrays[0].shape[-2:]
    rows = len(x.blocks) * tokens_each
    slabs, pair, _ = lower_slabs.shape
    kept = jax.ShapeDtypeStruct((hidden_here, rows), jnp.bfloat16)
    return pl.pallas_call(
        lambda *refs: forward_kernel(x.places, x.blocks[0], *refs),
        out_shape=(kept, kept, kept, jax.ShapeDtypeStruct((pair, rows), jnp.bfloat16)),
        in_specs=[HBM] * len(x.arrays) + [SMEM] + [HBM] * 3 + [VMEM] * 2,
        out_specs=(HBM, HBM, HBM, VMEM),
        scratch_shapes=[
            pltpu.VMEM((slabs, rows, feat), jnp.bfloat16),
            pltpu.VMEM((slabs, 2 * hidden_here + pair, feat), jnp.bfloat16),
            pltpu.VMEM((2 * hidden_here + pair, rows), jnp.float32),
            pltpu.VMEM((3, hidden_here, rows), jnp.bfloat16),
            pltpu.SemaphoreType.DMA((slabs, SHARDS)),
            pltpu.SemaphoreType.DMA((slabs, 3)),
            pltpu.SemaphoreType.DMA((3, hidden_here // LANES)),
        ],
        compiler_params=pltpu.CompilerParams(vmem_limit_bytes=VMEM_BYTES),
        cost_estimate=pl.CostEstimate(
            flops=2 * rows * hidden_here * width,
            bytes_accessed=2 * rows * width,
            transcendentals=rows * hidden_here,
        ),
        name="forward_rows",
    )(*x.arrays, slab_order, *weights[:2], lower_slabs, gate_upper, up_upper)


def hidden_kernel(places, first, *refs):
    n_pieces = len(places)
    pieces = refs[:n_pieces]
    (
        slab_ref,
        route_ref,
        down_hbm,
        down_upper_hbm,
        down_lower_ref,
        down_lower_t_ref,
        gate_upper_ref,
        up_upper_ref,
        silu_hbm,
        slope_hbm,
        hidden_hbm,
        d_pair,
        parts_out,
        low_down,
        rows,
        down_w,
        d_down,
        silu,
        slope,
        hidden,
        row_sems,
        d_sems,
        f_sems,
    ) = refs[n_pieces:]
    slabs, _, feat = rows.shape
    hidden_here = silu.shape[0]
    rank = down_lower_ref.shape[0]
    saved_copies = [
        pltpu.make_async_copy(source, target, f_sems.at[i])
        for i, (source, target) in enumerate(
            ((silu_hbm, silu), (slope_hbm, slope), (hidden_hbm, hidden))
        )
    ]

    def slab_copies(slab):
        return row_copies(pieces, places, rows, row_sems, slab, first) + [
            pltpu.make_async_copy(
                down_hbm.at[:, slab_lanes(slab_ref, slab, feat)],
                down_w.at[slab, pl.ds(0, hidden_here)],
                d_sems.at[slab, 0],
            ),
            pltpu.make_async_copy(
                down_upper_hbm.at[slab], down_w.at[slab, pl.ds(hidden_here, rank)], d_sems.at[slab, 1]
            ),
        ]

    for slab in range(slabs):
        for copy in slab_copies(slab):
            copy.start()
    for copy in saved_copies:
        copy.start()
    for slab in range(slabs):
        for copy in slab_copies(slab):
            copy.wait()
        if slab == 0:
            d_down[...] = dot_nt(down_w[0], rows[0])
        else:
            d_down[...] += dot_nt(down_w[slab], rows[slab])

    low_down[...] = (d_down[hidden_here:, :] * route_ref[...]).astype(jnp.bfloat16)
    for copy in saved_copies:
        copy.wait()

    @pl.loop(0, hidden_here // LANES)
    def _(tile):
        start = pl.multiple_of(tile * LANES, LANES)
        at = pl.ds(start, LANES)
        up_at = pl.ds(pl.multiple_of(hidden_here + start, LANES), LANES)
        d_hidden = d_down[at, :] * route_ref[...]
        d_hidden = d_hidden + ADAPTER_SCALE * dot_nn(down_lower_t_ref[at, :], low_down[...])
        d_gate = (d_hidden * wide(slope[at, :])).astype(jnp.bfloat16)
        d_up = (d_hidden * wide(silu[at, :])).astype(jnp.bfloat16)
        d_pair[:, at] = d_gate.T
        d_pair[:, up_at] = d_up.T

    for side, factor in enumerate((gate_upper_ref, up_upper_ref)):
        start = side * hidden_here
        part = dot_nn(d_pair[:, start : start + hidden_here], factor[...])
        parts_out[side * rank : (side + 1) * rank, :] = part.T
        at = 2 * hidden_here + side * rank
        d_pair[:, at : at + rank] = ADAPTER_SCALE * part.astype(jnp.bfloat16)
    parts_out[2 * rank :, :] = dot_nn(down_lower_ref[...], hidden[...])


def hidden_gradients(dy, slab_order, route_row, down_weight, down_upper, factors, saved):
    hidden_here, width = down_weight.shape
    slabs, rank, feat = down_upper.shape
    pair = 2 * rank
    rows = route_row.shape[1]
    return pl.pallas_call(
        lambda *refs: hidden_kernel(dy.places, dy.blocks[0], *refs),
        out_shape=(
            jax.ShapeDtypeStruct((rows, 2 * hidden_here + pair), jnp.bfloat16),
            jax.ShapeDtypeStruct((3 * rank, rows), jnp.float32),
            jax.ShapeDtypeStruct((rank, rows), jnp.bfloat16),
        ),
        in_specs=[HBM] * len(dy.arrays) + [SMEM, VMEM] + [HBM] * 2 + [VMEM] * 4 + [HBM] * 3,
        out_specs=(VMEM,) * 3,
        scratch_shapes=[
            pltpu.VMEM((slabs, rows, feat), jnp.bfloat16),
            pltpu.VMEM((slabs, hidden_here + rank, feat), jnp.bfloat16),
            pltpu.VMEM((hidden_here + rank, rows), jnp.float32),
            pltpu.VMEM((hidden_here, rows), jnp.bfloat16),
            pltpu.VMEM((hidden_here, rows), jnp.bfloat16),
            pltpu.VMEM((hidden_here, rows), jnp.bfloat16),
            pltpu.SemaphoreType.DMA((slabs, SHARDS)),
            pltpu.SemaphoreType.DMA((slabs, 2)),
            pltpu.SemaphoreType.DMA((3,)),
        ],
        compiler_params=pltpu.CompilerParams(vmem_limit_bytes=HIDDEN_BYTES),
        cost_estimate=pl.CostEstimate(
            flops=4 * rows * hidden_here * width,
            bytes_accessed=2 * hidden_here * width + 2 * rows * width,
            transcendentals=0,
        ),
        name="hidden_gradients",
    )(*dy.arrays, slab_order, route_row, down_weight, down_upper, *factors, *saved)


def term_kernel(slabs, n_parts, *refs):
    d_parts = refs[:n_parts]
    slab_ref, gate_hbm, up_hbm, lower_hbm = refs[n_parts : n_parts + 4]
    outs, (d_pair, pair_w, sems, d_sems) = refs[n_parts + 4 : -4], refs[-4:]
    _, depth, step = pair_w.shape
    hidden_here = gate_hbm.shape[0]
    pair = depth - 2 * hidden_here
    tokens_each, feat = outs[0].shape[2:]
    steps = feat // step

    def weight_copies(i, n):
        slab, k = slabs[i], i * steps + n
        lanes = pl.ds(pl.multiple_of(slab_ref[slab] * feat + n * step, step), step)
        sides = (
            (gate_hbm.at[:, lanes], 0, hidden_here),
            (up_hbm.at[:, lanes], hidden_here, hidden_here),
            (lower_hbm.at[slab, :, pl.ds(pl.multiple_of(n * step, step), step)], 2 * hidden_here, pair),
        )
        return [
            pltpu.make_async_copy(source, pair_w.at[k, pl.ds(start, size)], sems.at[k, side])
            for side, (source, start, size) in enumerate(sides)
        ]

    d_copies, row = [], 0
    for i, part in enumerate(d_parts):
        count = part.shape[0]
        d_copies.append(pltpu.make_async_copy(part, d_pair.at[pl.ds(row, count)], d_sems.at[i]))
        row += count
    for copy in d_copies:
        copy.start()
    for i in range(len(slabs)):
        for n in range(steps):
            for copy in weight_copies(i, n):
                copy.start()
    for copy in d_copies:
        copy.wait()
    for i in range(len(slabs)):

        @pl.loop(0, steps)
        def _(n):
            for copy in weight_copies(i, n):
                copy.wait()
            lanes = pl.ds(pl.multiple_of(n * step, step), step)
            term = dot_nn(d_pair[...], pair_w[i * steps + n]).astype(jnp.bfloat16)
            for block in range(SHARDS):
                at = slice(block * tokens_each, (block + 1) * tokens_each)
                outs[block % 2][block // 2, i, :, lanes] = term[at]


def slab_terms(slabs, slab_order, d_pair, weights, lower_slabs):
    rows, depth = sum(part.shape[0] for part in d_pair), d_pair[0].shape[1]
    feat = lower_slabs.shape[2]
    parts = len(slabs) * feat // TILE
    term = jax.ShapeDtypeStruct((SHARDS // 2, len(slabs), rows // SHARDS, feat), jnp.bfloat16)
    return pl.pallas_call(
        lambda *refs: term_kernel(slabs, len(d_pair), *refs),
        out_shape=(term, term),
        in_specs=[HBM] * len(d_pair) + [SMEM] + [HBM] * 3,
        out_specs=(VMEM, VMEM),
        scratch_shapes=[
            pltpu.VMEM((rows, depth), jnp.bfloat16),
            pltpu.VMEM((parts, depth, TILE), jnp.bfloat16),
            pltpu.SemaphoreType.DMA((parts, 3)),
            pltpu.SemaphoreType.DMA((len(d_pair),)),
        ],
        compiler_params=pltpu.CompilerParams(vmem_limit_bytes=TERM_BYTES),
        cost_estimate=pl.CostEstimate(
            flops=4 * rows * depth * feat * len(slabs),
            bytes_accessed=2 * depth * feat * len(slabs) + 4 * rows * depth,
            transcendentals=0,
        ),
        name="slab_terms",
    )(*d_pair, slab_order, *weights[:2], lower_slabs)


def shared_kernel(x_places, dy_places, n_parts, *refs):
    split, inputs = len(x_places), len(x_places) + len(dy_places)
    x_pieces, dy_pieces = refs[:split], refs[split:inputs]
    (
        order_ref,
        slab_ref,
        sums_ref,
        down_sums_ref,
    ) = refs[inputs : inputs + 4]
    inputs += 4
    parts = [refs[inputs + 4 * i : inputs + 4 * i + 4] for i in range(n_parts)]
    inputs += 4 * n_parts
    pair_out, down_out, owned_out, owned_down_out = refs[inputs : inputs + 4]
    x_rows, dy_rows, sums, down_sums, x_sems, dy_sems = refs[inputs + 4 :]
    rank, hidden_here = owned_down_out.shape
    slabs, _, feat = x_rows.shape
    tokens_each = x_pieces[0].shape[-2]

    def slab_copies(slab):
        return row_copies(x_pieces, x_places, x_rows, x_sems, slab, 0, order_ref) + row_copies(
            dy_pieces, dy_places, dy_rows, dy_sems, slab, 0, order_ref
        )

    for slab in range(slabs):
        for copy in slab_copies(slab):
            copy.start()
    for block in range(SHARDS):
        lanes = pl.ds(pl.multiple_of(order_ref[block] * tokens_each, tokens_each), tokens_each)
        sums[:, lanes] = sums_ref[block]
        down_sums[:, lanes] = down_sums_ref[block]
    gate_sum = up_sum = down_sum = 0.0
    for low, low_down, d_pair, hidden in parts:
        gate_sum += dot_nn(low[:rank, :], d_pair[:, :hidden_here])
        up_sum += dot_nn(low[rank:, :], d_pair[:, hidden_here : 2 * hidden_here])
        down_sum += dot_nt(low_down[...], hidden[...])
    owned_out[0] = ADAPTER_SCALE * gate_sum
    owned_out[1] = ADAPTER_SCALE * up_sum
    owned_down_out[...] = ADAPTER_SCALE * down_sum
    for slab in range(slabs):
        for copy in slab_copies(slab):
            copy.wait()

        @pl.loop(0, feat // TILE)
        def _(n):
            lanes = pl.ds(pl.multiple_of(n * TILE, TILE), TILE)
            out = pl.ds(pl.multiple_of(slab_ref[slab] * feat + n * TILE, TILE), TILE)
            pair_out[:, out] = ADAPTER_SCALE * dot_nn(
                sums[...].astype(jnp.bfloat16), x_rows[slab, :, lanes]
            )
            down_out[:, out] = ADAPTER_SCALE * dot_nn(
                down_sums[...].astype(jnp.bfloat16), dy_rows[slab, :, lanes]
            )


def adapter_gradients(x, dy, order, slab_order, sums, down_sums, parts):
    tokens_each, feat = x.arrays[0].shape[-2:]
    slabs = slab_order.shape[0]
    rows = SHARDS * tokens_each
    pair, rank = sums.shape[1], down_sums.shape[1]
    hidden_here = parts[0][3].shape[0]
    return pl.pallas_call(
        lambda *refs: shared_kernel(x.places, dy.places, len(parts), *refs),
        out_shape=(
            jax.ShapeDtypeStruct((pair, slabs * feat), jnp.float32),
            jax.ShapeDtypeStruct((rank, slabs * feat), jnp.float32),
            jax.ShapeDtypeStruct((2, rank, hidden_here), jnp.float32),
            jax.ShapeDtypeStruct((rank, hidden_here), jnp.float32),
        ),
        in_specs=[HBM] * (len(x.arrays) + len(dy.arrays)) + [SMEM, SMEM]
        + [VMEM] * (2 + 4 * len(parts)),
        out_specs=(VMEM,) * 4,
        scratch_shapes=[
            pltpu.VMEM((slabs, rows, feat), jnp.bfloat16),
            pltpu.VMEM((slabs, rows, feat), jnp.bfloat16),
            pltpu.VMEM((pair, rows), jnp.float32),
            pltpu.VMEM((rank, rows), jnp.float32),
            pltpu.SemaphoreType.DMA((slabs, SHARDS)),
            pltpu.SemaphoreType.DMA((slabs, SHARDS)),
        ],
        compiler_params=pltpu.CompilerParams(vmem_limit_bytes=VMEM_BYTES),
        cost_estimate=pl.CostEstimate(
            flops=200 * rows * pair * slabs * feat,
            bytes_accessed=12 * rows * slabs * feat,
            transcendentals=0,
        ),
        name="adapter_gradients",
    )(
        *x.arrays,
        *dy.arrays,
        order,
        slab_order,
        sums,
        down_sums,
        *(value for part in parts for value in part),
    )


CORE, ACROSS, ALONG = 1, 2, 4
PLANE = (ACROSS, ALONG, ACROSS | ALONG)


def swap(value, bit, axis="dp"):
    return lax.ppermute(value, axis, [(i, i ^ bit) for i in range(lax.axis_size(axis))])


def after(value, *others):
    return lax.optimization_barrier((value, others))[0]


def added(left, right):
    return (wide(left) + wide(right)).astype(jnp.bfloat16)


def local(
    tokens,
    output_gradient,
    routing,
    router_gate_values,
    gate_weight,
    up_weight,
    down_weight,
    adapter_lower_gate,
    adapter_upper_gate,
    adapter_lower_up,
    adapter_upper_up,
    adapter_lower_down,
    adapter_upper_down,
):
    experts = lax.axis_size("expert")
    me, expert = lax.axis_index("dp"), lax.axis_index("expert")
    tokens_each, feat = tokens.shape
    rank = adapter_lower_gate.shape[1]
    order = jnp.bitwise_xor(jnp.arange(SHARDS, dtype=jnp.int32), me.astype(jnp.int32))
    slab_order = jnp.bitwise_xor(jnp.arange(experts, dtype=jnp.int32), expert.astype(jnp.int32))

    named = routing[:, :, None] == jnp.arange(experts, dtype=jnp.int32)[None, None, :]
    weight_of = jnp.sum(jnp.where(named, router_gate_values[:, :, None], 0.0), axis=1)
    routes = lax.all_gather(weight_of.T, "dp", axis=0, tiled=False)
    route = lax.dynamic_index_in_dim(routes, expert, axis=1, keepdims=False)[order]
    route_blocks = route[:, None, :]
    route_row = route.reshape(1, SHARDS * tokens_each)

    def slabs_first(factor):
        return factor.reshape(factor.shape[0], experts, feat).transpose(1, 0, 2)[slab_order]

    lower_cat = jnp.concatenate([adapter_lower_gate[0], adapter_lower_up[0]], axis=0)
    down_lower = adapter_lower_down[0]

    def place_both(rows, part, swapped, chip, slabs):
        rows.add(part, *((r, 2 * chip) for r in slabs))
        rows.add(swapped, *((r, 2 * chip + 1) for r in slabs))

    def over_experts(block, r):
        return swap(block, r, "expert")

    both = over_experts(jnp.stack([tokens, output_gradient]), 1)
    x_slabs = [both[0]] + [over_experts(tokens, r) for r in range(2, experts)]
    x_near = [tokens] + [swap(tokens, bit) for bit in PLANE[:2]]
    uppers = (adapter_upper_gate[0], adapter_upper_up[0])
    (x_slabs, x_near, dy_near), small = lax.optimization_barrier(
        ((x_slabs, x_near, both[1]), (route_row, adapter_upper_down[0], lower_cat, uppers))
    )
    route_row, down_upper, lower_cat, uppers = small
    lower_slabs, down_upper = slabs_first(lower_cat), slabs_first(down_upper.T)
    ready = (lower_slabs, down_upper, down_lower, down_lower.T, *uppers)

    x_rest = [jnp.stack(x_slabs)]
    x_rest += [swap(x_rest[0], bit) for bit in PLANE[:2]]
    x_near.append(swap(x_near[2], ACROSS))
    dy_late = after(output_gradient, x_rest[0])
    dy_slabs = [output_gradient, dy_near] + [over_experts(dy_late, r) for r in range(2, experts)]

    (x_rest, x_near, dy_slabs), ready = lax.optimization_barrier(
        ((x_rest, x_near, dy_slabs), ready)
    )
    lower_slabs, down_upper, *factors = ready
    uppers = factors[2:]
    half = experts // 2
    x_far = [swap(x_rest[2][: half - 1], ACROSS), swap(x_rest[1][half - 1 :], ALONG)]
    x_near_swapped = swap(jnp.stack(x_near[:2]), CORE)
    x_rest_swapped = [swap(part, CORE) for part in x_rest[:2]]
    dy_all = after(jnp.stack(dy_slabs), x_near_swapped, *x_rest_swapped)
    dy_plane = [swap(dy_all, bit) for bit in PLANE[:2]]

    x_main = Rows(range(4))
    x_main.add(x_near[0], (0, 0))
    x_main.add(x_near[1], (0, 2))
    x_main.add(x_near_swapped, (0, 1), (0, 3))
    for chip in range(2):
        place_both(x_main, x_rest[chip], x_rest_swapped[chip], chip, range(1, experts))

    weights = (gate_weight[0], up_weight[0], down_weight[0])
    saved = [forward_rows(x_main, slab_order, weights, lower_slabs, *uppers)]

    x_far, x_late = after((x_far, (x_near[2:], x_rest[2])), saved[0][0])
    x_pair = jnp.stack(x_late[0])
    x_far = jnp.concatenate(x_far, axis=0)
    x_away = Rows(range(4, SHARDS))
    x_away.add(x_pair, (0, 4), (0, 6))
    x_away.add(swap(x_pair, CORE), (0, 5), (0, 7))
    place_both(x_away, x_late[1], swap(x_late[1], CORE), 2, range(1, experts))
    place_both(x_away, x_far, swap(x_far, CORE), 3, range(1, experts))

    dy_plane = after(dy_plane, saved[0][0])
    dy_far = [swap(dy_plane[1][:half], ACROSS), swap(dy_plane[0][half:], ALONG)]
    here = after(slab_order, *dy_plane)
    saved.append(forward_rows(x_away, here, weights, lower_slabs, *uppers))

    dy_main, dy_away = Rows(range(4)), Rows(range(4, SHARDS))
    for chip, part in enumerate((dy_all, dy_plane[0])):
        place_both(dy_main, part, swap(part, CORE), chip, range(experts))
    place_both(dy_away, dy_plane[1], swap(dy_plane[1], CORE), 2, range(experts))
    for part, slabs in zip(after(dy_far, saved[1][0]), (range(half), range(half, experts))):
        place_both(dy_away, part, swap(part, CORE), 3, slabs)
    split = 4 * tokens_each
    grads = [
        hidden_gradients(
            rows, slab_order, route_row[:, at], weights[2], down_upper, factors, kept[:3]
        )
        for rows, at, kept in zip(
            (dy_main, dy_away), (slice(0, split), slice(split, None)), saved
        )
    ]
    d_pair = [grad[0] for grad in grads]
    parts = jnp.concatenate([grad[1] for grad in grads], axis=1)

    def sum_step(total, bit):
        other = swap(total.reshape(SHARDS, 3 * rank, tokens_each), bit)
        shape = (SHARDS // (2 * bit), 2, bit, 3 * rank, tokens_each)
        return total.reshape(shape) + other.reshape(shape)[:, ::-1]

    sums = [parts.reshape(3 * rank, SHARDS, tokens_each).transpose(1, 0, 2)]
    for bit in (CORE, ACROSS, ALONG):
        sums.append(sum_step(sums[-1], bit))

    def send(keep, got):
        chips = [added(keep[i], got[i]) for i in range(SHARDS // 2)]
        return chips, [swap(part, bit) for bit, part in zip(PLANE, chips[1:])]

    def total_rows(chips, moved):
        return sum((wide(part) for part in moved), wide(chips[0]))

    def terms(group, *others):
        here = after(slab_order, *others)
        keep, away = slab_terms(group, here, d_pair, weights, lower_slabs)
        return keep, swap(away, CORE)

    keep_a, got_a = terms((3,), sums[1])
    keep_b, got_b = terms((2,), sums[2])
    chips_a, moved_a = send(keep_a, after(got_a, keep_b))
    keep_c, got_c = terms((1, 0), sums[3], *chips_a)
    rows_a = total_rows(chips_a, after(moved_a, keep_c))
    chips_b, moved_b = send(keep_b, after(got_b, keep_c))
    total = after(sums[3].reshape(SHARDS, 3 * rank, tokens_each), rows_a, *chips_b)
    x, dy = Rows(range(SHARDS)), Rows(range(SHARDS))
    for whole, halves in ((x, (x_main, x_away)), (dy, (dy_main, dy_away))):
        for rows in halves:
            whole.arrays += rows.arrays
            whole.places += rows.places
    grad_pair, grad_down, owned, owned_down = adapter_gradients(
        x,
        dy,
        order,
        slab_order,
        total[:, : 2 * rank],
        total[:, 2 * rank :] * route_blocks,
        [(kept[3], grad[2], grad[0], kept[2]) for kept, grad in zip(saved, grads)],
    )
    got_c, moved_b = after((got_c, moved_b), grad_pair)
    chips_c, moved_c = send(keep_c, got_c)
    rows_b = total_rows(chips_b, moved_b)
    rows_c = total_rows(chips_c, moved_c)
    grad_x = rows_c[1]
    for rows, r in ((rows_a[0], 3), (rows_b[0], 2), (rows_c[0], 1)):
        grad_x = grad_x + wide(over_experts(rows.astype(jnp.bfloat16), r))
    grad_x = grad_x.astype(jnp.bfloat16)
    return (
        grad_x,
        grad_pair[None, :rank],
        owned[0].T[None],
        grad_pair[None, rank:],
        owned[1].T[None],
        owned_down[None],
        grad_down.T[None],
    )


def plan(tokens, *others):
    experts, tokens_each, hidden_here = lax.axis_size("expert"), tokens.shape[0], others[3].shape[1]
    planned = (
        lax.axis_size("dp") == SHARDS
        and experts == 4
        and hidden_here % LANES == 0
        and tokens_each % LANES == 0
        and tokens.shape[1] % TILE == 0
    )
    return (local if planned else general_local)(tokens, *others)


def solution(mesh):
    return jax.shard_map(
        plan,
        mesh=mesh,
        in_specs=(
            P("dp", "expert"),
            P("dp", "expert"),
            P("dp", None),
            P("dp", None),
            P("expert", "dp", None),
            P("expert", "dp", None),
            P("expert", "dp", None),
            P("expert", None, None),
            P("expert", "dp", None),
            P("expert", None, None),
            P("expert", "dp", None),
            P("expert", None, "dp"),
            P("expert", None, None),
        ),
        out_specs=(
            P("dp", "expert"),
            P("expert", None, None),
            P("expert", "dp", None),
            P("expert", None, None),
            P("expert", "dp", None),
            P("expert", None, "dp"),
            P("expert", None, None),
        ),
        check_vma=False,
    )
```

```python
import jax
import jax.numpy as jnp
from jax import lax
from jax.experimental import pallas as pl
from jax.experimental.pallas import tpu as pltpu
from jax.sharding import PartitionSpec as P

ADAPTER_SCALE = 2.0


def contract_pair(left, right, left_axis, right_axis):
    return lax.dot_general(
        left, right, (((left_axis,), (right_axis,)), ((), ())), preferred_element_type=jnp.float32
    )


def slot_numbers(route_rows, experts):
    picked = (route_rows[:, :, None] == jnp.arange(experts, dtype=jnp.int32)[None, None, :]).astype(
        jnp.int32
    )
    per_token = jnp.sum(picked, axis=1)
    earlier = jnp.cumsum(per_token, axis=0) - per_token
    return jnp.sum(earlier[:, None, :] * picked, axis=2)


def slot_sources(route_rows, positions, experts, capacity):
    tokens_here, choose = route_rows.shape
    target = (route_rows * capacity + positions).reshape(-1)
    owners = jnp.repeat(jnp.arange(tokens_here, dtype=jnp.int32), choose)
    member_ids = jnp.tile(jnp.arange(choose, dtype=jnp.int32), tokens_here)
    source = jnp.full((experts * capacity,), tokens_here, jnp.int32).at[target].set(owners)
    member = jnp.zeros((experts * capacity,), jnp.int32).at[target].set(member_ids)
    return (source, member)


def rows_backward_pass(input_rows, output_gradient_rows, params):
    (
        gate_weight,
        up_weight,
        down_weight,
        a_gate,
        gate_adapter_upper,
        a_up,
        up_adapter_upper,
        down_adapter_lower,
        b_down,
    ) = params
    gate_projected_lower = contract_pair(a_gate, input_rows, 1, 1).astype(jnp.bfloat16)
    up_projected_lower = contract_pair(a_up, input_rows, 1, 1).astype(jnp.bfloat16)
    gate_preactivation = contract_pair(
        gate_weight, input_rows, 1, 1
    ) + ADAPTER_SCALE * contract_pair(gate_adapter_upper, gate_projected_lower, 1, 0)
    up_preactivation = contract_pair(up_weight, input_rows, 1, 1) + ADAPTER_SCALE * contract_pair(
        up_adapter_upper, up_projected_lower, 1, 0
    )
    sigmoid_gate = jax.nn.sigmoid(gate_preactivation)
    silu_gate = gate_preactivation * sigmoid_gate
    hidden_units = (silu_gate * up_preactivation).astype(jnp.bfloat16)
    down_projected_lower = contract_pair(b_down, output_gradient_rows, 0, 1).astype(jnp.bfloat16)
    hidden_gradient = contract_pair(
        down_weight, output_gradient_rows, 1, 1
    ) + ADAPTER_SCALE * contract_pair(down_adapter_lower, down_projected_lower, 0, 0)
    gate_gradient = (
        hidden_gradient
        * up_preactivation
        * sigmoid_gate
        * (1.0 + gate_preactivation * (1.0 - sigmoid_gate))
    ).astype(jnp.bfloat16)
    up_gradient = (hidden_gradient * silu_gate).astype(jnp.bfloat16)
    gate_partial = contract_pair(gate_adapter_upper, gate_gradient, 0, 0).astype(jnp.bfloat16)
    up_partial = contract_pair(up_adapter_upper, up_gradient, 0, 0).astype(jnp.bfloat16)
    down_partial = contract_pair(down_adapter_lower, hidden_units, 1, 0).astype(jnp.bfloat16)
    paired_partials = jnp.concatenate([gate_partial, up_partial], 0)
    paired_factors = jnp.concatenate([a_gate, a_up], 0)
    gradient_rows_out = (
        contract_pair(gate_gradient, gate_weight, 0, 0)
        + contract_pair(up_gradient, up_weight, 0, 0)
        + ADAPTER_SCALE * contract_pair(paired_partials, paired_factors, 0, 0)
    )
    shared_slice = (
        ADAPTER_SCALE * contract_pair(gate_partial, input_rows, 1, 0),
        ADAPTER_SCALE * contract_pair(up_partial, input_rows, 1, 0),
        ADAPTER_SCALE * contract_pair(output_gradient_rows, down_partial, 0, 1),
    )
    owned_slice = (
        ADAPTER_SCALE * contract_pair(gate_gradient, gate_projected_lower, 1, 1),
        ADAPTER_SCALE * contract_pair(up_gradient, up_projected_lower, 1, 1),
        ADAPTER_SCALE * contract_pair(down_projected_lower, hidden_units, 1, 1),
    )
    return (gradient_rows_out, shared_slice, owned_slice)


def general_local(
    tokens,
    output_gradient,
    routing,
    router_gate_values,
    gate_weight,
    up_weight,
    down_weight,
    adapter_lower_gate,
    adapter_upper_gate,
    adapter_lower_up,
    adapter_upper_up,
    adapter_lower_down,
    adapter_upper_down,
):
    experts = lax.axis_size("expert")
    shards = lax.axis_size("dp")
    tok_local, feat_local = tokens.shape
    choose = routing.shape[1]
    complete_width = feat_local * experts
    capacity = min(tok_local, 6 * tok_local // experts)
    hidden_units_local = gate_weight.shape[1]
    adapter_rank = adapter_lower_gate.shape[1]
    params = (
        gate_weight[0],
        up_weight[0],
        down_weight[0],
        adapter_lower_gate[0],
        adapter_upper_gate[0],
        adapter_lower_up[0],
        adapter_upper_up[0],
        adapter_lower_down[0],
        adapter_upper_down[0],
    )
    positions = slot_numbers(routing, experts)
    zero_row = jnp.zeros((1, feat_local), jnp.bfloat16)
    initial = (
        jnp.zeros((shards * capacity, complete_width), jnp.float32),
        (
            jnp.zeros((adapter_rank, complete_width), jnp.float32),
            jnp.zeros((adapter_rank, complete_width), jnp.float32),
            jnp.zeros((complete_width, adapter_rank), jnp.float32),
        ),
        (
            jnp.zeros((hidden_units_local, adapter_rank), jnp.float32),
            jnp.zeros((hidden_units_local, adapter_rank), jnp.float32),
            jnp.zeros((adapter_rank, hidden_units_local), jnp.float32),
        ),
    )
    source, member = slot_sources(routing, positions, experts, capacity)
    clamped = jnp.minimum(source, tok_local - 1)
    slot_gate = jnp.where(
        source < tok_local, router_gate_values.reshape(-1)[clamped * choose + member], 0.0
    )
    send_x = jnp.concatenate([tokens, zero_row], 0)[source].reshape(experts, capacity, feat_local)
    send_dy = (
        (
            slot_gate[:, None]
            * jnp.concatenate([output_gradient, zero_row], 0)[source].astype(jnp.float32)
        )
        .astype(jnp.bfloat16)
        .reshape(experts, capacity, feat_local)
    )
    recv_x, recv_dy = (
        lax.all_to_all(send_x, "expert", split_axis=0, concat_axis=2, tiled=True),
        lax.all_to_all(send_dy, "expert", split_axis=0, concat_axis=2, tiled=True),
    )
    gradient_rows_out, shared_slice, owned_slice = rows_backward_pass(
        lax.all_gather(recv_x[0], "dp", axis=0, tiled=True),
        lax.all_gather(recv_dy[0], "dp", axis=0, tiled=True),
        params,
    )
    rows_part = gradient_rows_out
    totals = (
        rows_part,
        jax.tree.map(jnp.add, initial[1], shared_slice),
        jax.tree.map(jnp.add, initial[2], owned_slice),
    )
    rows_part, shared_slice, owned_slice = totals
    summed = lax.psum_scatter(
        rows_part.astype(jnp.bfloat16), "dp", scatter_dimension=0, tiled=True
    ).astype(jnp.float32)
    returned_rows = lax.all_to_all(
        summed.reshape(capacity, experts, feat_local).astype(jnp.bfloat16),
        "expert",
        split_axis=1,
        concat_axis=1,
        tiled=True,
    ).astype(jnp.float32)
    lookup = positions * experts + routing
    grad_x = jnp.sum(returned_rows.reshape(capacity * experts, feat_local)[lookup], axis=1).astype(
        jnp.bfloat16
    )
    grad_a_gate, grad_a_up, grad_b_down = (
        lax.psum(shared_slice[0].astype(jnp.bfloat16), "dp").astype(jnp.float32),
        lax.psum(shared_slice[1].astype(jnp.bfloat16), "dp").astype(jnp.float32),
        lax.psum(shared_slice[2].astype(jnp.bfloat16), "dp").astype(jnp.float32),
    )
    return (
        grad_x,
        grad_a_gate[None],
        owned_slice[0][None],
        grad_a_up[None],
        owned_slice[1][None],
        owned_slice[2][None],
        grad_b_down[None],
    )


LANES = 128
TILE = 512
SHARDS = 8
VMEM_BYTES = 58 * 1024 * 1024
HIDDEN_BYTES = 58 * 1024 * 1024
TERM_BYTES = 58 * 1024 * 1024
HBM = pl.BlockSpec(memory_space=pl.ANY)
PINNED = pl.BlockSpec(memory_space=pltpu.HBM)
VMEM = pl.BlockSpec(memory_space=pltpu.VMEM)
SMEM = pl.BlockSpec(memory_space=pltpu.SMEM)


def dot_nt(left, right):
    return contract_pair(left, right, 1, 1)


def dot_nn(left, right):
    return contract_pair(left, right, 1, 0)


def wide(value):
    return value.astype(jnp.float32)


class Rows:
    def __init__(self, blocks):
        self.arrays, self.places, self.blocks = [], [], blocks

    def add(self, array, *places):
        self.arrays.append(array)
        self.places.append(places)


def row_copies(refs, places, target, sems, slab, first=0, order=None):
    tokens_each = refs[0].shape[-2]
    copies = []
    for ref, parts in zip(refs, places):
        for i, (at, block) in enumerate(parts):
            if at != slab:
                continue
            source = ref.at[i] if len(ref.shape) == 3 else ref
            row = (block - first) * tokens_each
            if order is not None:
                row = pl.multiple_of(order[block] * tokens_each, tokens_each)
            copies.append(
                pltpu.make_async_copy(
                    source, target.at[slab, pl.ds(row, tokens_each)], sems.at[slab, block]
                )
            )
    return copies


def slab_lanes(slab_ref, slab, feat):
    return pl.ds(pl.multiple_of(slab_ref[slab] * feat, feat), feat)


def forward_kernel(places, first, *refs):
    n_pieces = len(places)
    pieces = refs[:n_pieces]
    (
        slab_ref,
        gate_hbm,
        up_hbm,
        lower_hbm,
        gate_upper_ref,
        up_upper_ref,
        silu_out,
        slope_out,
        hidden_out,
        low_out,
    ) = refs[n_pieces : n_pieces + 10]
    x_rows, weights, pre, saved, x_sems, w_sems, out_sems = refs[n_pieces + 10 :]
    slabs, _, feat = x_rows.shape
    hidden_here = gate_hbm.shape[0]
    pair, rank = lower_hbm.shape[1], gate_upper_ref.shape[1]

    def x_slab(slab):
        return row_copies(pieces, places, x_rows, x_sems, slab, first)

    def weight_copies(slab):
        lanes = slab_lanes(slab_ref, slab, feat)
        sides = (
            (gate_hbm.at[:, lanes], 0, hidden_here),
            (up_hbm.at[:, lanes], hidden_here, hidden_here),
            (lower_hbm.at[slab], 2 * hidden_here, pair),
        )
        return [
            pltpu.make_async_copy(
                source, weights.at[slab, pl.ds(start, size)], w_sems.at[slab, i]
            )
            for i, (source, start, size) in enumerate(sides)
        ]

    for slab in range(slabs):
        for copy in x_slab(slab) + weight_copies(slab):
            copy.start()
    for slab in range(slabs):
        for copy in x_slab(slab) + weight_copies(slab):
            copy.wait()
        if slab == 0:
            pre[...] = dot_nt(weights[0], x_rows[0])
        else:
            pre[...] += dot_nt(weights[slab], x_rows[slab])
    low_out[...] = pre[2 * hidden_here :, :].astype(jnp.bfloat16)

    def out_copies(tile):
        at = pl.ds(pl.multiple_of(tile * LANES, LANES), LANES)
        return [
            pltpu.make_async_copy(saved.at[i, at], out.at[at], out_sems.at[i, tile])
            for i, out in enumerate((silu_out, slope_out, hidden_out))
        ]

    tiles = hidden_here // LANES

    @pl.loop(0, tiles)
    def _(tile):
        start = pl.multiple_of(tile * LANES, LANES)
        at = pl.ds(start, LANES)
        up_at = pl.ds(pl.multiple_of(hidden_here + start, LANES), LANES)
        pre_gate = pre[at, :] + ADAPTER_SCALE * dot_nn(gate_upper_ref[at, :], low_out[:rank, :])
        pre_up = pre[up_at, :] + ADAPTER_SCALE * dot_nn(up_upper_ref[at, :], low_out[rank:, :])
        sigma = 1.0 / (1.0 + jnp.exp(-pre_gate))
        silu = pre_gate * sigma
        saved[0, at, :] = silu.astype(jnp.bfloat16)
        saved[1, at, :] = (pre_up * (sigma * (1.0 + pre_gate * (1.0 - sigma)))).astype(
            jnp.bfloat16
        )
        saved[2, at, :] = (silu * pre_up).astype(jnp.bfloat16)
        for copy in out_copies(tile):
            copy.start()

    @pl.loop(0, tiles)
    def _(tile):
        for copy in out_copies(tile):
            copy.wait()


def forward_rows(x, slab_order, weights, lower_slabs, gate_upper, up_upper):
    hidden_here, width = weights[0].shape
    tokens_each, feat = x.arrays[0].shape[-2:]
    rows = len(x.blocks) * tokens_each
    slabs, pair, _ = lower_slabs.shape
    kept = jax.ShapeDtypeStruct((hidden_here, rows), jnp.bfloat16)
    return pl.pallas_call(
        lambda *refs: forward_kernel(x.places, x.blocks[0], *refs),
        out_shape=(kept, kept, kept, jax.ShapeDtypeStruct((pair, rows), jnp.bfloat16)),
        in_specs=[HBM] * len(x.arrays) + [SMEM] + [HBM] * 3 + [VMEM] * 2,
        out_specs=(HBM, HBM, HBM, VMEM),
        scratch_shapes=[
            pltpu.VMEM((slabs, rows, feat), jnp.bfloat16),
            pltpu.VMEM((slabs, 2 * hidden_here + pair, feat), jnp.bfloat16),
            pltpu.VMEM((2 * hidden_here + pair, rows), jnp.float32),
            pltpu.VMEM((3, hidden_here, rows), jnp.bfloat16),
            pltpu.SemaphoreType.DMA((slabs, SHARDS)),
            pltpu.SemaphoreType.DMA((slabs, 3)),
            pltpu.SemaphoreType.DMA((3, hidden_here // LANES)),
        ],
        compiler_params=pltpu.CompilerParams(vmem_limit_bytes=VMEM_BYTES),
        cost_estimate=pl.CostEstimate(
            flops=rows * hidden_here * width // 4,
            bytes_accessed=2 * rows * width,
            transcendentals=rows * hidden_here,
        ),
        name="forward_rows",
    )(*x.arrays, slab_order, *weights[:2], lower_slabs, gate_upper, up_upper)


def hidden_kernel(places, first, *refs):
    n_pieces = len(places)
    pieces = refs[:n_pieces]
    (
        slab_ref,
        route_ref,
        down_hbm,
        down_upper_hbm,
        down_lower_ref,
        down_lower_t_ref,
        gate_upper_ref,
        up_upper_ref,
        silu_hbm,
        slope_hbm,
        hidden_hbm,
        d_pair,
        parts_out,
        low_down,
        rows,
        down_w,
        d_down,
        silu,
        slope,
        hidden,
        row_sems,
        d_sems,
        f_sems,
    ) = refs[n_pieces:]
    slabs, _, feat = rows.shape
    hidden_here = silu.shape[0]
    rank = down_lower_ref.shape[0]
    saved_copies = [
        pltpu.make_async_copy(source, target, f_sems.at[i])
        for i, (source, target) in enumerate(
            ((silu_hbm, silu), (slope_hbm, slope), (hidden_hbm, hidden))
        )
    ]

    def slab_copies(slab):
        return row_copies(pieces, places, rows, row_sems, slab, first) + [
            pltpu.make_async_copy(
                down_hbm.at[:, slab_lanes(slab_ref, slab, feat)],
                down_w.at[slab, pl.ds(0, hidden_here)],
                d_sems.at[slab, 0],
            ),
            pltpu.make_async_copy(
                down_upper_hbm.at[slab], down_w.at[slab, pl.ds(hidden_here, rank)], d_sems.at[slab, 1]
            ),
        ]

    for slab in range(slabs):
        for copy in slab_copies(slab):
            copy.start()
    for copy in saved_copies:
        copy.start()
    for slab in range(slabs):
        for copy in slab_copies(slab):
            copy.wait()
        if slab == 0:
            d_down[...] = dot_nt(down_w[0], rows[0])
        else:
            d_down[...] += dot_nt(down_w[slab], rows[slab])

    low_down[...] = (d_down[hidden_here:, :] * route_ref[...]).astype(jnp.bfloat16)
    for copy in saved_copies:
        copy.wait()

    @pl.loop(0, hidden_here // LANES)
    def _(tile):
        start = pl.multiple_of(tile * LANES, LANES)
        at = pl.ds(start, LANES)
        up_at = pl.ds(pl.multiple_of(hidden_here + start, LANES), LANES)
        d_hidden = d_down[at, :] * route_ref[...]
        d_hidden = d_hidden + ADAPTER_SCALE * dot_nn(down_lower_t_ref[at, :], low_down[...])
        d_gate = (d_hidden * wide(slope[at, :])).astype(jnp.bfloat16)
        d_up = (d_hidden * wide(silu[at, :])).astype(jnp.bfloat16)
        d_pair[:, at] = d_gate.T
        d_pair[:, up_at] = d_up.T

    for side, factor in enumerate((gate_upper_ref, up_upper_ref)):
        start = side * hidden_here
        part = dot_nn(d_pair[:, start : start + hidden_here], factor[...])
        parts_out[side * rank : (side + 1) * rank, :] = part.T
        at = 2 * hidden_here + side * rank
        d_pair[:, at : at + rank] = ADAPTER_SCALE * part.astype(jnp.bfloat16)
    parts_out[2 * rank :, :] = dot_nn(down_lower_ref[...], hidden[...])


def hidden_gradients(dy, slab_order, route_row, down_weight, down_upper, factors, saved):
    hidden_here, width = down_weight.shape
    slabs, rank, feat = down_upper.shape
    pair = 2 * rank
    rows = route_row.shape[1]
    return pl.pallas_call(
        lambda *refs: hidden_kernel(dy.places, dy.blocks[0], *refs),
        out_shape=(
            jax.ShapeDtypeStruct((rows, 2 * hidden_here + pair), jnp.bfloat16),
            jax.ShapeDtypeStruct((3 * rank, rows), jnp.float32),
            jax.ShapeDtypeStruct((rank, rows), jnp.bfloat16),
        ),
        in_specs=[HBM] * len(dy.arrays) + [SMEM, VMEM] + [HBM] * 2 + [VMEM] * 4 + [HBM] * 3,
        out_specs=(VMEM,) * 3,
        scratch_shapes=[
            pltpu.VMEM((slabs, rows, feat), jnp.bfloat16),
            pltpu.VMEM((slabs, hidden_here + rank, feat), jnp.bfloat16),
            pltpu.VMEM((hidden_here + rank, rows), jnp.float32),
            pltpu.VMEM((hidden_here, rows), jnp.bfloat16),
            pltpu.VMEM((hidden_here, rows), jnp.bfloat16),
            pltpu.VMEM((hidden_here, rows), jnp.bfloat16),
            pltpu.SemaphoreType.DMA((slabs, SHARDS)),
            pltpu.SemaphoreType.DMA((slabs, 2)),
            pltpu.SemaphoreType.DMA((3,)),
        ],
        compiler_params=pltpu.CompilerParams(vmem_limit_bytes=HIDDEN_BYTES),
        cost_estimate=pl.CostEstimate(
            flops=4 * rows * hidden_here * width,
            bytes_accessed=2 * hidden_here * width + 2 * rows * width,
            transcendentals=0,
        ),
        name="hidden_gradients",
    )(*dy.arrays, slab_order, route_row, down_weight, down_upper, *factors, *saved)


def term_kernel(slabs, n_parts, *refs):
    d_parts = refs[:n_parts]
    slab_ref, gate_hbm, up_hbm, lower_hbm = refs[n_parts : n_parts + 4]
    outs, (d_pair, pair_w, sems, d_sems) = refs[n_parts + 4 : -4], refs[-4:]
    _, depth, step = pair_w.shape
    hidden_here = gate_hbm.shape[0]
    pair = depth - 2 * hidden_here
    tokens_each, feat = outs[0].shape[2:]
    steps = feat // step

    def weight_copies(i, n):
        slab, k = slabs[i], i * steps + n
        lanes = pl.ds(pl.multiple_of(slab_ref[slab] * feat + n * step, step), step)
        sides = (
            (gate_hbm.at[:, lanes], 0, hidden_here),
            (up_hbm.at[:, lanes], hidden_here, hidden_here),
            (lower_hbm.at[slab, :, pl.ds(pl.multiple_of(n * step, step), step)], 2 * hidden_here, pair),
        )
        return [
            pltpu.make_async_copy(source, pair_w.at[k, pl.ds(start, size)], sems.at[k, side])
            for side, (source, start, size) in enumerate(sides)
        ]

    d_copies, row = [], 0
    for i, part in enumerate(d_parts):
        count = part.shape[0]
        d_copies.append(pltpu.make_async_copy(part, d_pair.at[pl.ds(row, count)], d_sems.at[i]))
        row += count
    for copy in d_copies:
        copy.start()
    for i in range(len(slabs)):
        for n in range(steps):
            for copy in weight_copies(i, n):
                copy.start()
    for copy in d_copies:
        copy.wait()
    for i in range(len(slabs)):

        @pl.loop(0, steps)
        def _(n):
            for copy in weight_copies(i, n):
                copy.wait()
            lanes = pl.ds(pl.multiple_of(n * step, step), step)
            term = dot_nn(d_pair[...], pair_w[i * steps + n]).astype(jnp.bfloat16)
            for block in range(SHARDS):
                at = slice(block * tokens_each, (block + 1) * tokens_each)
                outs[block % 2][block // 2, i, :, lanes] = term[at]


def slab_terms(slabs, slab_order, d_pair, weights, lower_slabs):
    rows, depth = sum(part.shape[0] for part in d_pair), d_pair[0].shape[1]
    feat = lower_slabs.shape[2]
    parts = len(slabs) * feat // TILE
    term = jax.ShapeDtypeStruct((SHARDS // 2, len(slabs), rows // SHARDS, feat), jnp.bfloat16)
    return pl.pallas_call(
        lambda *refs: term_kernel(slabs, len(d_pair), *refs),
        out_shape=(term, term),
        in_specs=[HBM] * len(d_pair) + [SMEM] + [HBM] * 3,
        out_specs=(VMEM, VMEM),
        scratch_shapes=[
            pltpu.VMEM((rows, depth), jnp.bfloat16),
            pltpu.VMEM((parts, depth, TILE), jnp.bfloat16),
            pltpu.SemaphoreType.DMA((parts, 3)),
            pltpu.SemaphoreType.DMA((len(d_pair),)),
        ],
        compiler_params=pltpu.CompilerParams(vmem_limit_bytes=TERM_BYTES),
        cost_estimate=pl.CostEstimate(
            flops=4 * rows * depth * feat * len(slabs),
            bytes_accessed=2 * depth * feat * len(slabs) + 4 * rows * depth,
            transcendentals=0,
        ),
        name="slab_terms",
    )(*d_pair, slab_order, *weights[:2], lower_slabs)


def shared_kernel(x_places, dy_places, n_parts, *refs):
    split, inputs = len(x_places), len(x_places) + len(dy_places)
    x_pieces, dy_pieces = refs[:split], refs[split:inputs]
    (
        order_ref,
        slab_ref,
        sums_ref,
        down_sums_ref,
    ) = refs[inputs : inputs + 4]
    inputs += 4
    parts = [refs[inputs + 4 * i : inputs + 4 * i + 4] for i in range(n_parts)]
    inputs += 4 * n_parts
    pair_out, down_out, owned_out, owned_down_out = refs[inputs : inputs + 4]
    x_rows, dy_rows, sums, down_sums, x_sems, dy_sems = refs[inputs + 4 :]
    rank, hidden_here = owned_down_out.shape
    slabs, _, feat = x_rows.shape
    tokens_each = x_pieces[0].shape[-2]

    def slab_copies(slab):
        return row_copies(x_pieces, x_places, x_rows, x_sems, slab, 0, order_ref) + row_copies(
            dy_pieces, dy_places, dy_rows, dy_sems, slab, 0, order_ref
        )

    for slab in range(slabs):
        for copy in slab_copies(slab):
            copy.start()
    for block in range(SHARDS):
        lanes = pl.ds(pl.multiple_of(order_ref[block] * tokens_each, tokens_each), tokens_each)
        sums[:, lanes] = sums_ref[block]
        down_sums[:, lanes] = down_sums_ref[block]
    gate_sum = up_sum = down_sum = 0.0
    for low, low_down, d_pair, hidden in parts:
        gate_sum += dot_nn(low[:rank, :], d_pair[:, :hidden_here])
        up_sum += dot_nn(low[rank:, :], d_pair[:, hidden_here : 2 * hidden_here])
        down_sum += dot_nt(low_down[...], hidden[...])
    owned_out[0] = ADAPTER_SCALE * gate_sum
    owned_out[1] = ADAPTER_SCALE * up_sum
    owned_down_out[...] = ADAPTER_SCALE * down_sum
    for slab in range(slabs):
        for copy in slab_copies(slab):
            copy.wait()

        @pl.loop(0, feat // TILE)
        def _(n):
            lanes = pl.ds(pl.multiple_of(n * TILE, TILE), TILE)
            out = pl.ds(pl.multiple_of(slab_ref[slab] * feat + n * TILE, TILE), TILE)
            pair_out[:, out] = ADAPTER_SCALE * dot_nn(
                sums[...].astype(jnp.bfloat16), x_rows[slab, :, lanes]
            )
            down_out[:, out] = ADAPTER_SCALE * dot_nn(
                down_sums[...].astype(jnp.bfloat16), dy_rows[slab, :, lanes]
            )


def adapter_gradients(x, dy, order, slab_order, sums, down_sums, parts):
    tokens_each, feat = x.arrays[0].shape[-2:]
    slabs = slab_order.shape[0]
    rows = SHARDS * tokens_each
    pair, rank = sums.shape[1], down_sums.shape[1]
    hidden_here = parts[0][3].shape[0]
    return pl.pallas_call(
        lambda *refs: shared_kernel(x.places, dy.places, len(parts), *refs),
        out_shape=(
            jax.ShapeDtypeStruct((pair, slabs * feat), jnp.float32),
            jax.ShapeDtypeStruct((rank, slabs * feat), jnp.float32),
            jax.ShapeDtypeStruct((2, rank, hidden_here), jnp.float32),
            jax.ShapeDtypeStruct((rank, hidden_here), jnp.float32),
        ),
        in_specs=[HBM] * (len(x.arrays) + len(dy.arrays)) + [SMEM, SMEM]
        + [VMEM] * (2 + 4 * len(parts)),
        out_specs=(VMEM,) * 4,
        scratch_shapes=[
            pltpu.VMEM((slabs, rows, feat), jnp.bfloat16),
            pltpu.VMEM((slabs, rows, feat), jnp.bfloat16),
            pltpu.VMEM((pair, rows), jnp.float32),
            pltpu.VMEM((rank, rows), jnp.float32),
            pltpu.SemaphoreType.DMA((slabs, SHARDS)),
            pltpu.SemaphoreType.DMA((slabs, SHARDS)),
        ],
        compiler_params=pltpu.CompilerParams(vmem_limit_bytes=VMEM_BYTES),
        cost_estimate=pl.CostEstimate(
            flops=200 * rows * pair * slabs * feat,
            bytes_accessed=12 * rows * slabs * feat,
            transcendentals=0,
        ),
        name="adapter_gradients",
    )(
        *x.arrays,
        *dy.arrays,
        order,
        slab_order,
        sums,
        down_sums,
        *(value for part in parts for value in part),
    )


CORE, ACROSS, ALONG = 1, 2, 4
PLANE = (ACROSS, ALONG, ACROSS | ALONG)


def swap(value, bit, axis="dp"):
    return lax.ppermute(value, axis, [(i, i ^ bit) for i in range(lax.axis_size(axis))])


def after(value, *others):
    return lax.optimization_barrier((value, others))[0]


def added(left, right):
    return (wide(left) + wide(right)).astype(jnp.bfloat16)


def local(
    tokens,
    output_gradient,
    routing,
    router_gate_values,
    gate_weight,
    up_weight,
    down_weight,
    adapter_lower_gate,
    adapter_upper_gate,
    adapter_lower_up,
    adapter_upper_up,
    adapter_lower_down,
    adapter_upper_down,
):
    experts = lax.axis_size("expert")
    me, expert = lax.axis_index("dp"), lax.axis_index("expert")
    tokens_each, feat = tokens.shape
    rank = adapter_lower_gate.shape[1]
    order = jnp.bitwise_xor(jnp.arange(SHARDS, dtype=jnp.int32), me.astype(jnp.int32))
    slab_order = jnp.bitwise_xor(jnp.arange(experts, dtype=jnp.int32), expert.astype(jnp.int32))

    named = routing[:, :, None] == jnp.arange(experts, dtype=jnp.int32)[None, None, :]
    weight_of = jnp.sum(jnp.where(named, router_gate_values[:, :, None], 0.0), axis=1)
    routes = lax.all_gather(weight_of.T, "dp", axis=0, tiled=False)
    route = lax.dynamic_index_in_dim(routes, expert, axis=1, keepdims=False)[order]
    route_blocks = route[:, None, :]
    route_row = route.reshape(1, SHARDS * tokens_each)

    def slabs_first(factor):
        return factor.reshape(factor.shape[0], experts, feat).transpose(1, 0, 2)[slab_order]

    lower_cat = jnp.concatenate([adapter_lower_gate[0], adapter_lower_up[0]], axis=0)
    down_lower = adapter_lower_down[0]

    def place_both(rows, part, swapped, chip, slabs):
        rows.add(part, *((r, 2 * chip) for r in slabs))
        rows.add(swapped, *((r, 2 * chip + 1) for r in slabs))

    def over_experts(block, r):
        return swap(block, r, "expert")

    both = over_experts(jnp.stack([tokens, output_gradient]), 1)
    x_slabs = [both[0]] + [over_experts(tokens, r) for r in range(2, experts)]
    x_near = [tokens] + [swap(tokens, bit) for bit in PLANE[:2]]
    uppers = (adapter_upper_gate[0], adapter_upper_up[0])
    (x_slabs, x_near, dy_near), small = lax.optimization_barrier(
        ((x_slabs, x_near, both[1]), (route_row, adapter_upper_down[0], lower_cat, uppers))
    )
    route_row, down_upper, lower_cat, uppers = small
    lower_slabs, down_upper = slabs_first(lower_cat), slabs_first(down_upper.T)
    ready = (lower_slabs, down_upper, down_lower, down_lower.T, *uppers)

    x_rest = [jnp.stack(x_slabs)]
    x_rest += [swap(x_rest[0], bit) for bit in PLANE[:2]]
    x_near.append(swap(x_near[2], ACROSS))
    dy_late = after(output_gradient, x_rest[0])
    dy_slabs = [output_gradient, dy_near] + [over_experts(dy_late, r) for r in range(2, experts)]

    (x_rest, x_near, dy_slabs), ready = lax.optimization_barrier(
        ((x_rest, x_near, dy_slabs), ready)
    )
    lower_slabs, down_upper, *factors = ready
    uppers = factors[2:]
    half = experts // 2
    x_far = [swap(x_rest[2][: half - 1], ACROSS), swap(x_rest[1][half - 1 :], ALONG)]
    x_near_swapped = swap(jnp.stack(x_near[:2]), CORE)
    x_rest_swapped = [swap(part, CORE) for part in x_rest[:2]]
    dy_all = after(jnp.stack(dy_slabs), x_near_swapped, *x_rest_swapped)
    dy_plane = [swap(dy_all, bit) for bit in PLANE[:2]]

    x_main = Rows(range(4))
    x_main.add(x_near[0], (0, 0))
    x_main.add(x_near[1], (0, 2))
    x_main.add(x_near_swapped, (0, 1), (0, 3))
    for chip in range(2):
        place_both(x_main, x_rest[chip], x_rest_swapped[chip], chip, range(1, experts))

    weights = (gate_weight[0], up_weight[0], down_weight[0])
    saved = [forward_rows(x_main, slab_order, weights, lower_slabs, *uppers)]

    x_far, x_late = after((x_far, (x_near[2:], x_rest[2])), saved[0][0])
    x_pair = jnp.stack(x_late[0])
    x_far = jnp.concatenate(x_far, axis=0)
    x_away = Rows(range(4, SHARDS))
    x_away.add(x_pair, (0, 4), (0, 6))
    x_away.add(swap(x_pair, CORE), (0, 5), (0, 7))
    place_both(x_away, x_late[1], swap(x_late[1], CORE), 2, range(1, experts))
    place_both(x_away, x_far, swap(x_far, CORE), 3, range(1, experts))

    saved.append(forward_rows(x_away, slab_order, weights, lower_slabs, *uppers))

    dy_plane = after(dy_plane, saved[1][0])
    dy_far = [swap(dy_plane[1][:half], ACROSS), swap(dy_plane[0][half:], ALONG)]

    dy_main, dy_away = Rows(range(4)), Rows(range(4, SHARDS))
    for chip, part in enumerate((dy_all, dy_plane[0])):
        place_both(dy_main, part, swap(part, CORE), chip, range(experts))
    split = 4 * tokens_each
    route_halves = (route_row[:, :split], route_row[:, split:])

    def hidden_part(rows, i):
        return hidden_gradients(
            rows, slab_order, route_halves[i], weights[2], down_upper, factors, saved[i][:3]
        )

    grads = [hidden_part(dy_main, 0)]
    place_both(dy_away, dy_plane[1], swap(dy_plane[1], CORE), 2, range(experts))
    for part, slabs in zip(after(dy_far, grads[0][0]), (range(half), range(half, experts))):
        place_both(dy_away, part, swap(part, CORE), 3, slabs)
    grads.append(hidden_part(dy_away, 1))
    d_pair = [grad[0] for grad in grads]
    parts = jnp.concatenate([grad[1] for grad in grads], axis=1)

    def sum_step(total, bit):
        other = swap(total.reshape(SHARDS, 3 * rank, tokens_each), bit)
        shape = (SHARDS // (2 * bit), 2, bit, 3 * rank, tokens_each)
        return total.reshape(shape) + other.reshape(shape)[:, ::-1]

    sums = [parts.reshape(3 * rank, SHARDS, tokens_each).transpose(1, 0, 2)]
    for bit in (CORE, ACROSS, ALONG):
        sums.append(sum_step(sums[-1], bit))

    def send(keep, got):
        chips = [added(keep[i], got[i]) for i in range(SHARDS // 2)]
        return chips, [swap(part, bit) for bit, part in zip(PLANE, chips[1:])]

    def total_rows(chips, moved):
        return sum((wide(part) for part in moved), wide(chips[0]))

    def terms(group, *others):
        here = after(slab_order, *others)
        keep, away = slab_terms(group, here, d_pair, weights, lower_slabs)
        return keep, swap(away, CORE)

    keep_a, got_a = terms((3, 2), sums[1])
    keep_b, got_b = terms((1,), sums[2])
    chips_a, moved_a = send(keep_a, after(got_a, keep_b))
    keep_c, got_c = terms((0,), sums[3], *chips_a)
    rows_a = total_rows(chips_a, after(moved_a, keep_c))
    chips_b, moved_b = send(keep_b, after(got_b, keep_c))
    total = after(sums[3].reshape(SHARDS, 3 * rank, tokens_each), rows_a, *chips_b)
    x, dy = Rows(range(SHARDS)), Rows(range(SHARDS))
    for whole, halves in ((x, (x_main, x_away)), (dy, (dy_main, dy_away))):
        for rows in halves:
            whole.arrays += rows.arrays
            whole.places += rows.places
    grad_pair, grad_down, owned, owned_down = adapter_gradients(
        x,
        dy,
        order,
        slab_order,
        total[:, : 2 * rank],
        total[:, 2 * rank :] * route_blocks,
        [(kept[3], grad[2], grad[0], kept[2]) for kept, grad in zip(saved, grads)],
    )
    got_c, moved_b = after((got_c, moved_b), grad_pair)
    chips_c, moved_c = send(keep_c, got_c)
    rows_b = total_rows(chips_b, moved_b)
    rows_c = total_rows(chips_c, moved_c)
    grad_x = rows_c[0]
    for rows, r in ((rows_a[0], 3), (rows_a[1], 2), (rows_b[0], 1)):
        grad_x = grad_x + wide(over_experts(rows.astype(jnp.bfloat16), r))
    grad_x = grad_x.astype(jnp.bfloat16)
    return (
        grad_x,
        grad_pair[None, :rank],
        owned[0].T[None],
        grad_pair[None, rank:],
        owned[1].T[None],
        owned_down[None],
        grad_down.T[None],
    )


def plan(tokens, *others):
    experts, tokens_each, hidden_here = lax.axis_size("expert"), tokens.shape[0], others[3].shape[1]
    planned = (
        lax.axis_size("dp") == SHARDS
        and experts == 4
        and hidden_here % LANES == 0
        and tokens_each % LANES == 0
        and tokens.shape[1] % TILE == 0
    )
    return (local if planned else general_local)(tokens, *others)


def solution(mesh):
    return jax.shard_map(
        plan,
        mesh=mesh,
        in_specs=(
            P("dp", "expert"),
            P("dp", "expert"),
            P("dp", None),
            P("dp", None),
            P("expert", "dp", None),
            P("expert", "dp", None),
            P("expert", "dp", None),
            P("expert", None, None),
            P("expert", "dp", None),
            P("expert", None, None),
            P("expert", "dp", None),
            P("expert", None, "dp"),
            P("expert", None, None),
        ),
        out_specs=(
            P("dp", "expert"),
            P("expert", None, None),
            P("expert", "dp", None),
            P("expert", None, None),
            P("expert", "dp", None),
            P("expert", None, "dp"),
            P("expert", None, None),
        ),
        check_vma=False,
    )
```

```python
import jax
import jax.numpy as jnp
from jax import lax
from jax.experimental import pallas as pl
from jax.experimental.pallas import tpu as pltpu
from jax.sharding import PartitionSpec as P

ADAPTER_SCALE = 2.0


def contract_pair(left, right, left_axis, right_axis):
    return lax.dot_general(
        left, right, (((left_axis,), (right_axis,)), ((), ())), preferred_element_type=jnp.float32
    )


def slot_numbers(route_rows, experts):
    picked = (route_rows[:, :, None] == jnp.arange(experts, dtype=jnp.int32)[None, None, :]).astype(
        jnp.int32
    )
    per_token = jnp.sum(picked, axis=1)
    earlier = jnp.cumsum(per_token, axis=0) - per_token
    return jnp.sum(earlier[:, None, :] * picked, axis=2)


def slot_sources(route_rows, positions, experts, capacity):
    tokens_here, choose = route_rows.shape
    target = (route_rows * capacity + positions).reshape(-1)
    owners = jnp.repeat(jnp.arange(tokens_here, dtype=jnp.int32), choose)
    member_ids = jnp.tile(jnp.arange(choose, dtype=jnp.int32), tokens_here)
    source = jnp.full((experts * capacity,), tokens_here, jnp.int32).at[target].set(owners)
    member = jnp.zeros((experts * capacity,), jnp.int32).at[target].set(member_ids)
    return (source, member)


def rows_backward_pass(input_rows, output_gradient_rows, params):
    (
        gate_weight,
        up_weight,
        down_weight,
        a_gate,
        gate_adapter_upper,
        a_up,
        up_adapter_upper,
        down_adapter_lower,
        b_down,
    ) = params
    gate_projected_lower = contract_pair(a_gate, input_rows, 1, 1).astype(jnp.bfloat16)
    up_projected_lower = contract_pair(a_up, input_rows, 1, 1).astype(jnp.bfloat16)
    gate_preactivation = contract_pair(
        gate_weight, input_rows, 1, 1
    ) + ADAPTER_SCALE * contract_pair(gate_adapter_upper, gate_projected_lower, 1, 0)
    up_preactivation = contract_pair(up_weight, input_rows, 1, 1) + ADAPTER_SCALE * contract_pair(
        up_adapter_upper, up_projected_lower, 1, 0
    )
    sigmoid_gate = jax.nn.sigmoid(gate_preactivation)
    silu_gate = gate_preactivation * sigmoid_gate
    hidden_units = (silu_gate * up_preactivation).astype(jnp.bfloat16)
    down_projected_lower = contract_pair(b_down, output_gradient_rows, 0, 1).astype(jnp.bfloat16)
    hidden_gradient = contract_pair(
        down_weight, output_gradient_rows, 1, 1
    ) + ADAPTER_SCALE * contract_pair(down_adapter_lower, down_projected_lower, 0, 0)
    gate_gradient = (
        hidden_gradient
        * up_preactivation
        * sigmoid_gate
        * (1.0 + gate_preactivation * (1.0 - sigmoid_gate))
    ).astype(jnp.bfloat16)
    up_gradient = (hidden_gradient * silu_gate).astype(jnp.bfloat16)
    gate_partial = contract_pair(gate_adapter_upper, gate_gradient, 0, 0).astype(jnp.bfloat16)
    up_partial = contract_pair(up_adapter_upper, up_gradient, 0, 0).astype(jnp.bfloat16)
    down_partial = contract_pair(down_adapter_lower, hidden_units, 1, 0).astype(jnp.bfloat16)
    paired_partials = jnp.concatenate([gate_partial, up_partial], 0)
    paired_factors = jnp.concatenate([a_gate, a_up], 0)
    gradient_rows_out = (
        contract_pair(gate_gradient, gate_weight, 0, 0)
        + contract_pair(up_gradient, up_weight, 0, 0)
        + ADAPTER_SCALE * contract_pair(paired_partials, paired_factors, 0, 0)
    )
    shared_slice = (
        ADAPTER_SCALE * contract_pair(gate_partial, input_rows, 1, 0),
        ADAPTER_SCALE * contract_pair(up_partial, input_rows, 1, 0),
        ADAPTER_SCALE * contract_pair(output_gradient_rows, down_partial, 0, 1),
    )
    owned_slice = (
        ADAPTER_SCALE * contract_pair(gate_gradient, gate_projected_lower, 1, 1),
        ADAPTER_SCALE * contract_pair(up_gradient, up_projected_lower, 1, 1),
        ADAPTER_SCALE * contract_pair(down_projected_lower, hidden_units, 1, 1),
    )
    return (gradient_rows_out, shared_slice, owned_slice)


def general_local(
    tokens,
    output_gradient,
    routing,
    router_gate_values,
    gate_weight,
    up_weight,
    down_weight,
    adapter_lower_gate,
    adapter_upper_gate,
    adapter_lower_up,
    adapter_upper_up,
    adapter_lower_down,
    adapter_upper_down,
):
    experts = lax.axis_size("expert")
    shards = lax.axis_size("dp")
    tok_local, feat_local = tokens.shape
    choose = routing.shape[1]
    complete_width = feat_local * experts
    capacity = min(tok_local, 6 * tok_local // experts)
    hidden_units_local = gate_weight.shape[1]
    adapter_rank = adapter_lower_gate.shape[1]
    params = (
        gate_weight[0],
        up_weight[0],
        down_weight[0],
        adapter_lower_gate[0],
        adapter_upper_gate[0],
        adapter_lower_up[0],
        adapter_upper_up[0],
        adapter_lower_down[0],
        adapter_upper_down[0],
    )
    positions = slot_numbers(routing, experts)
    zero_row = jnp.zeros((1, feat_local), jnp.bfloat16)
    initial = (
        jnp.zeros((shards * capacity, complete_width), jnp.float32),
        (
            jnp.zeros((adapter_rank, complete_width), jnp.float32),
            jnp.zeros((adapter_rank, complete_width), jnp.float32),
            jnp.zeros((complete_width, adapter_rank), jnp.float32),
        ),
        (
            jnp.zeros((hidden_units_local, adapter_rank), jnp.float32),
            jnp.zeros((hidden_units_local, adapter_rank), jnp.float32),
            jnp.zeros((adapter_rank, hidden_units_local), jnp.float32),
        ),
    )
    source, member = slot_sources(routing, positions, experts, capacity)
    clamped = jnp.minimum(source, tok_local - 1)
    slot_gate = jnp.where(
        source < tok_local, router_gate_values.reshape(-1)[clamped * choose + member], 0.0
    )
    send_x = jnp.concatenate([tokens, zero_row], 0)[source].reshape(experts, capacity, feat_local)
    send_dy = (
        (
            slot_gate[:, None]
            * jnp.concatenate([output_gradient, zero_row], 0)[source].astype(jnp.float32)
        )
        .astype(jnp.bfloat16)
        .reshape(experts, capacity, feat_local)
    )
    recv_x, recv_dy = (
        lax.all_to_all(send_x, "expert", split_axis=0, concat_axis=2, tiled=True),
        lax.all_to_all(send_dy, "expert", split_axis=0, concat_axis=2, tiled=True),
    )
    gradient_rows_out, shared_slice, owned_slice = rows_backward_pass(
        lax.all_gather(recv_x[0], "dp", axis=0, tiled=True),
        lax.all_gather(recv_dy[0], "dp", axis=0, tiled=True),
        params,
    )
    rows_part = gradient_rows_out
    totals = (
        rows_part,
        jax.tree.map(jnp.add, initial[1], shared_slice),
        jax.tree.map(jnp.add, initial[2], owned_slice),
    )
    rows_part, shared_slice, owned_slice = totals
    summed = lax.psum_scatter(
        rows_part.astype(jnp.bfloat16), "dp", scatter_dimension=0, tiled=True
    ).astype(jnp.float32)
    returned_rows = lax.all_to_all(
        summed.reshape(capacity, experts, feat_local).astype(jnp.bfloat16),
        "expert",
        split_axis=1,
        concat_axis=1,
        tiled=True,
    ).astype(jnp.float32)
    lookup = positions * experts + routing
    grad_x = jnp.sum(returned_rows.reshape(capacity * experts, feat_local)[lookup], axis=1).astype(
        jnp.bfloat16
    )
    grad_a_gate, grad_a_up, grad_b_down = (
        lax.psum(shared_slice[0].astype(jnp.bfloat16), "dp").astype(jnp.float32),
        lax.psum(shared_slice[1].astype(jnp.bfloat16), "dp").astype(jnp.float32),
        lax.psum(shared_slice[2].astype(jnp.bfloat16), "dp").astype(jnp.float32),
    )
    return (
        grad_x,
        grad_a_gate[None],
        owned_slice[0][None],
        grad_a_up[None],
        owned_slice[1][None],
        owned_slice[2][None],
        grad_b_down[None],
    )


LANES = 128
TILE = 512
SHARDS = 8
VMEM_BYTES = 58 * 1024 * 1024
HIDDEN_BYTES = 58 * 1024 * 1024
TERM_BYTES = 58 * 1024 * 1024
HBM = pl.BlockSpec(memory_space=pl.ANY)
PINNED = pl.BlockSpec(memory_space=pltpu.HBM)
VMEM = pl.BlockSpec(memory_space=pltpu.VMEM)
SMEM = pl.BlockSpec(memory_space=pltpu.SMEM)


def dot_nt(left, right):
    return contract_pair(left, right, 1, 1)


def dot_nn(left, right):
    return contract_pair(left, right, 1, 0)


def wide(value):
    return value.astype(jnp.float32)


class Rows:
    def __init__(self, blocks):
        self.arrays, self.places, self.blocks = [], [], blocks

    def add(self, array, *places):
        self.arrays.append(array)
        self.places.append(places)


def row_copies(refs, places, target, sems, slab, first=0, order=None):
    tokens_each = refs[0].shape[-2]
    copies = []
    for ref, parts in zip(refs, places):
        for i, (at, block) in enumerate(parts):
            if at != slab:
                continue
            source = ref.at[i] if len(ref.shape) == 3 else ref
            row = (block - first) * tokens_each
            if order is not None:
                row = pl.multiple_of(order[block] * tokens_each, tokens_each)
            copies.append(
                pltpu.make_async_copy(
                    source, target.at[slab, pl.ds(row, tokens_each)], sems.at[slab, block]
                )
            )
    return copies


def slab_lanes(slab_ref, slab, feat):
    return pl.ds(pl.multiple_of(slab_ref[slab] * feat, feat), feat)


def forward_kernel(places, first, *refs):
    n_pieces = len(places)
    pieces = refs[:n_pieces]
    (
        slab_ref,
        gate_hbm,
        up_hbm,
        lower_hbm,
        gate_upper_ref,
        up_upper_ref,
        silu_out,
        slope_out,
        hidden_out,
        low_out,
    ) = refs[n_pieces : n_pieces + 10]
    x_rows, weights, pre, saved, x_sems, w_sems, out_sems = refs[n_pieces + 10 :]
    slabs, _, feat = x_rows.shape
    hidden_here = gate_hbm.shape[0]
    pair, rank = lower_hbm.shape[1], gate_upper_ref.shape[1]

    def x_slab(slab):
        return row_copies(pieces, places, x_rows, x_sems, slab, first)

    def weight_copies(slab):
        lanes = slab_lanes(slab_ref, slab, feat)
        sides = (
            (gate_hbm.at[:, lanes], 0, hidden_here),
            (up_hbm.at[:, lanes], hidden_here, hidden_here),
            (lower_hbm.at[slab], 2 * hidden_here, pair),
        )
        return [
            pltpu.make_async_copy(
                source, weights.at[slab, pl.ds(start, size)], w_sems.at[slab, i]
            )
            for i, (source, start, size) in enumerate(sides)
        ]

    for slab in range(slabs):
        for copy in x_slab(slab) + weight_copies(slab):
            copy.start()
    for slab in range(slabs):
        for copy in x_slab(slab) + weight_copies(slab):
            copy.wait()
        if slab == 0:
            pre[...] = dot_nt(weights[0], x_rows[0])
        else:
            pre[...] += dot_nt(weights[slab], x_rows[slab])
    low_out[...] = pre[2 * hidden_here :, :].astype(jnp.bfloat16)

    def out_copies(tile):
        at = pl.ds(pl.multiple_of(tile * LANES, LANES), LANES)
        return [
            pltpu.make_async_copy(saved.at[i, at], out.at[at], out_sems.at[i, tile])
            for i, out in enumerate((silu_out, slope_out, hidden_out))
        ]

    tiles = hidden_here // LANES

    @pl.loop(0, tiles)
    def _(tile):
        start = pl.multiple_of(tile * LANES, LANES)
        at = pl.ds(start, LANES)
        up_at = pl.ds(pl.multiple_of(hidden_here + start, LANES), LANES)
        pre_gate = pre[at, :] + ADAPTER_SCALE * dot_nn(gate_upper_ref[at, :], low_out[:rank, :])
        pre_up = pre[up_at, :] + ADAPTER_SCALE * dot_nn(up_upper_ref[at, :], low_out[rank:, :])
        sigma = 1.0 / (1.0 + jnp.exp(-pre_gate))
        silu = pre_gate * sigma
        saved[0, at, :] = silu.astype(jnp.bfloat16)
        saved[1, at, :] = (pre_up * (sigma * (1.0 + pre_gate * (1.0 - sigma)))).astype(
            jnp.bfloat16
        )
        saved[2, at, :] = (silu * pre_up).astype(jnp.bfloat16)
        for copy in out_copies(tile):
            copy.start()

    @pl.loop(0, tiles)
    def _(tile):
        for copy in out_copies(tile):
            copy.wait()


def forward_rows(x, slab_order, weights, lower_slabs, gate_upper, up_upper):
    hidden_here, width = weights[0].shape
    tokens_each, feat = x.arrays[0].shape[-2:]
    rows = len(x.blocks) * tokens_each
    slabs, pair, _ = lower_slabs.shape
    kept = jax.ShapeDtypeStruct((hidden_here, rows), jnp.bfloat16)
    return pl.pallas_call(
        lambda *refs: forward_kernel(x.places, x.blocks[0], *refs),
        out_shape=(kept, kept, kept, jax.ShapeDtypeStruct((pair, rows), jnp.bfloat16)),
        in_specs=[HBM] * len(x.arrays) + [SMEM] + [HBM] * 3 + [VMEM] * 2,
        out_specs=(HBM, HBM, HBM, VMEM),
        scratch_shapes=[
            pltpu.VMEM((slabs, rows, feat), jnp.bfloat16),
            pltpu.VMEM((slabs, 2 * hidden_here + pair, feat), jnp.bfloat16),
            pltpu.VMEM((2 * hidden_here + pair, rows), jnp.float32),
            pltpu.VMEM((3, hidden_here, rows), jnp.bfloat16),
            pltpu.SemaphoreType.DMA((slabs, SHARDS)),
            pltpu.SemaphoreType.DMA((slabs, 3)),
            pltpu.SemaphoreType.DMA((3, hidden_here // LANES)),
        ],
        compiler_params=pltpu.CompilerParams(vmem_limit_bytes=VMEM_BYTES),
        cost_estimate=pl.CostEstimate(
            flops=rows * hidden_here * width // 4,
            bytes_accessed=2 * rows * width,
            transcendentals=rows * hidden_here,
        ),
        name="forward_rows",
    )(*x.arrays, slab_order, *weights[:2], lower_slabs, gate_upper, up_upper)


def hidden_kernel(places, first, *refs):
    n_pieces = len(places)
    pieces = refs[:n_pieces]
    (
        slab_ref,
        route_ref,
        down_hbm,
        down_upper_hbm,
        down_lower_ref,
        down_lower_t_ref,
        gate_upper_ref,
        up_upper_ref,
        silu_hbm,
        slope_hbm,
        hidden_hbm,
        d_pair,
        parts_out,
        low_down,
        rows,
        down_w,
        d_down,
        silu,
        slope,
        hidden,
        row_sems,
        d_sems,
        f_sems,
    ) = refs[n_pieces:]
    slabs, _, feat = rows.shape
    hidden_here = silu.shape[0]
    rank = down_lower_ref.shape[0]
    saved_copies = [
        pltpu.make_async_copy(source, target, f_sems.at[i])
        for i, (source, target) in enumerate(
            ((silu_hbm, silu), (slope_hbm, slope), (hidden_hbm, hidden))
        )
    ]

    def slab_copies(slab):
        return row_copies(pieces, places, rows, row_sems, slab, first) + [
            pltpu.make_async_copy(
                down_hbm.at[:, slab_lanes(slab_ref, slab, feat)],
                down_w.at[slab, pl.ds(0, hidden_here)],
                d_sems.at[slab, 0],
            ),
            pltpu.make_async_copy(
                down_upper_hbm.at[slab], down_w.at[slab, pl.ds(hidden_here, rank)], d_sems.at[slab, 1]
            ),
        ]

    for slab in range(slabs):
        for copy in slab_copies(slab):
            copy.start()
    for copy in saved_copies:
        copy.start()
    for slab in range(slabs):
        for copy in slab_copies(slab):
            copy.wait()
        if slab == 0:
            d_down[...] = dot_nt(down_w[0], rows[0])
        else:
            d_down[...] += dot_nt(down_w[slab], rows[slab])

    low_down[...] = (d_down[hidden_here:, :] * route_ref[...]).astype(jnp.bfloat16)
    for copy in saved_copies:
        copy.wait()

    @pl.loop(0, hidden_here // LANES)
    def _(tile):
        start = pl.multiple_of(tile * LANES, LANES)
        at = pl.ds(start, LANES)
        up_at = pl.ds(pl.multiple_of(hidden_here + start, LANES), LANES)
        d_hidden = d_down[at, :] * route_ref[...]
        d_hidden = d_hidden + ADAPTER_SCALE * dot_nn(down_lower_t_ref[at, :], low_down[...])
        d_gate = (d_hidden * wide(slope[at, :])).astype(jnp.bfloat16)
        d_up = (d_hidden * wide(silu[at, :])).astype(jnp.bfloat16)
        d_pair[:, at] = d_gate.T
        d_pair[:, up_at] = d_up.T

    for side, factor in enumerate((gate_upper_ref, up_upper_ref)):
        start = side * hidden_here
        part = dot_nn(d_pair[:, start : start + hidden_here], factor[...])
        parts_out[side * rank : (side + 1) * rank, :] = part.T
        at = 2 * hidden_here + side * rank
        d_pair[:, at : at + rank] = ADAPTER_SCALE * part.astype(jnp.bfloat16)
    parts_out[2 * rank :, :] = dot_nn(down_lower_ref[...], hidden[...])


def hidden_gradients(dy, slab_order, route_row, down_weight, down_upper, factors, saved):
    hidden_here, width = down_weight.shape
    slabs, rank, feat = down_upper.shape
    pair = 2 * rank
    rows = route_row.shape[1]
    return pl.pallas_call(
        lambda *refs: hidden_kernel(dy.places, dy.blocks[0], *refs),
        out_shape=(
            jax.ShapeDtypeStruct((rows, 2 * hidden_here + pair), jnp.bfloat16),
            jax.ShapeDtypeStruct((3 * rank, rows), jnp.float32),
            jax.ShapeDtypeStruct((rank, rows), jnp.bfloat16),
        ),
        in_specs=[HBM] * len(dy.arrays) + [SMEM, VMEM] + [HBM] * 2 + [VMEM] * 4 + [HBM] * 3,
        out_specs=(VMEM,) * 3,
        scratch_shapes=[
            pltpu.VMEM((slabs, rows, feat), jnp.bfloat16),
            pltpu.VMEM((slabs, hidden_here + rank, feat), jnp.bfloat16),
            pltpu.VMEM((hidden_here + rank, rows), jnp.float32),
            pltpu.VMEM((hidden_here, rows), jnp.bfloat16),
            pltpu.VMEM((hidden_here, rows), jnp.bfloat16),
            pltpu.VMEM((hidden_here, rows), jnp.bfloat16),
            pltpu.SemaphoreType.DMA((slabs, SHARDS)),
            pltpu.SemaphoreType.DMA((slabs, 2)),
            pltpu.SemaphoreType.DMA((3,)),
        ],
        compiler_params=pltpu.CompilerParams(vmem_limit_bytes=HIDDEN_BYTES),
        cost_estimate=pl.CostEstimate(
            flops=4 * rows * hidden_here * width,
            bytes_accessed=2 * hidden_here * width + 2 * rows * width,
            transcendentals=0,
        ),
        name="hidden_gradients",
    )(*dy.arrays, slab_order, route_row, down_weight, down_upper, *factors, *saved)


def term_kernel(slabs, n_parts, *refs):
    d_parts = refs[:n_parts]
    slab_ref, gate_hbm, up_hbm, lower_hbm = refs[n_parts : n_parts + 4]
    outs, (d_pair, pair_w, sems, d_sems) = refs[n_parts + 4 : -4], refs[-4:]
    _, depth, step = pair_w.shape
    hidden_here = gate_hbm.shape[0]
    pair = depth - 2 * hidden_here
    tokens_each, feat = outs[0].shape[2:]
    steps = feat // step

    def weight_copies(i, n):
        slab, k = slabs[i], i * steps + n
        lanes = pl.ds(pl.multiple_of(slab_ref[slab] * feat + n * step, step), step)
        sides = (
            (gate_hbm.at[:, lanes], 0, hidden_here),
            (up_hbm.at[:, lanes], hidden_here, hidden_here),
            (lower_hbm.at[slab, :, pl.ds(pl.multiple_of(n * step, step), step)], 2 * hidden_here, pair),
        )
        return [
            pltpu.make_async_copy(source, pair_w.at[k, pl.ds(start, size)], sems.at[k, side])
            for side, (source, start, size) in enumerate(sides)
        ]

    d_copies, row = [], 0
    for i, part in enumerate(d_parts):
        count = part.shape[0]
        d_copies.append(pltpu.make_async_copy(part, d_pair.at[pl.ds(row, count)], d_sems.at[i]))
        row += count
    for copy in d_copies:
        copy.start()
    for i in range(len(slabs)):
        for n in range(steps):
            for copy in weight_copies(i, n):
                copy.start()
    for copy in d_copies:
        copy.wait()
    for i in range(len(slabs)):

        @pl.loop(0, steps)
        def _(n):
            for copy in weight_copies(i, n):
                copy.wait()
            lanes = pl.ds(pl.multiple_of(n * step, step), step)
            term = dot_nn(d_pair[...], pair_w[i * steps + n]).astype(jnp.bfloat16)
            for block in range(SHARDS):
                at = slice(block * tokens_each, (block + 1) * tokens_each)
                outs[block % 2][block // 2, i, :, lanes] = term[at]


def slab_terms(slabs, slab_order, d_pair, weights, lower_slabs):
    rows, depth = sum(part.shape[0] for part in d_pair), d_pair[0].shape[1]
    feat = lower_slabs.shape[2]
    parts = len(slabs) * feat // TILE
    term = jax.ShapeDtypeStruct((SHARDS // 2, len(slabs), rows // SHARDS, feat), jnp.bfloat16)
    return pl.pallas_call(
        lambda *refs: term_kernel(slabs, len(d_pair), *refs),
        out_shape=(term, term),
        in_specs=[HBM] * len(d_pair) + [SMEM] + [HBM] * 3,
        out_specs=(VMEM, VMEM),
        scratch_shapes=[
            pltpu.VMEM((rows, depth), jnp.bfloat16),
            pltpu.VMEM((parts, depth, TILE), jnp.bfloat16),
            pltpu.SemaphoreType.DMA((parts, 3)),
            pltpu.SemaphoreType.DMA((len(d_pair),)),
        ],
        compiler_params=pltpu.CompilerParams(vmem_limit_bytes=TERM_BYTES),
        cost_estimate=pl.CostEstimate(
            flops=12 * rows * depth * feat * len(slabs),
            bytes_accessed=2 * depth * feat * len(slabs) + 4 * rows * depth,
            transcendentals=0,
        ),
        name="slab_terms",
    )(*d_pair, slab_order, *weights[:2], lower_slabs)


def owned_kernel(n_parts, *refs):
    parts = [refs[4 * i : 4 * i + 4] for i in range(n_parts)]
    owned_out, owned_down_out = refs[4 * n_parts :]
    rank, hidden_here = owned_down_out.shape
    gate_sum = up_sum = down_sum = 0.0
    for low, low_down, d_pair, hidden in parts:
        gate_sum += dot_nn(low[:rank, :], d_pair[:, :hidden_here])
        up_sum += dot_nn(low[rank:, :], d_pair[:, hidden_here : 2 * hidden_here])
        down_sum += dot_nt(low_down[...], hidden[...])
    owned_out[0] = ADAPTER_SCALE * gate_sum
    owned_out[1] = ADAPTER_SCALE * up_sum
    owned_down_out[...] = ADAPTER_SCALE * down_sum


def owned_gradients(parts, hint):
    rank, hidden_here = parts[0][1].shape[0], parts[0][3].shape[0]
    return pl.pallas_call(
        lambda *refs: owned_kernel(len(parts), *refs),
        out_shape=(
            jax.ShapeDtypeStruct((2, rank, hidden_here), jnp.float32),
            jax.ShapeDtypeStruct((rank, hidden_here), jnp.float32),
        ),
        in_specs=[VMEM] * (4 * len(parts)),
        out_specs=(VMEM, VMEM),
        compiler_params=pltpu.CompilerParams(vmem_limit_bytes=VMEM_BYTES),
        cost_estimate=pl.CostEstimate(flops=hint, bytes_accessed=8_000_000, transcendentals=0),
        name="owned_gradients",
    )(*(value for part in parts for value in part))


def shared_kernel(x_places, dy_places, *refs):
    split, inputs = len(x_places), len(x_places) + len(dy_places)
    x_pieces, dy_pieces = refs[:split], refs[split:inputs]
    order_ref, slab_ref, sums_ref, down_sums_ref, pair_out, down_out = refs[inputs : inputs + 6]
    x_rows, dy_rows, sums, down_sums, x_sems, dy_sems = refs[inputs + 6 :]
    slabs, _, feat = x_rows.shape
    tokens_each = x_pieces[0].shape[-2]

    def slab_copies(slab):
        return row_copies(
            x_pieces, x_places, x_rows, x_sems, slab, 0, order_ref
        ) + row_copies(dy_pieces, dy_places, dy_rows, dy_sems, slab, 0, order_ref)

    for slab in range(slabs):
        for copy in slab_copies(slab):
            copy.start()
    for block in range(SHARDS):
        lanes = pl.ds(pl.multiple_of(order_ref[block] * tokens_each, tokens_each), tokens_each)
        sums[:, lanes] = sums_ref[block]
        down_sums[:, lanes] = down_sums_ref[block]
    for slab in range(slabs):
        for copy in slab_copies(slab):
            copy.wait()

        @pl.loop(0, feat // TILE)
        def _(n):
            lanes = pl.ds(pl.multiple_of(n * TILE, TILE), TILE)
            out = pl.ds(pl.multiple_of(slab_ref[slab] * feat + n * TILE, TILE), TILE)
            pair_out[:, out] = ADAPTER_SCALE * dot_nn(
                sums[...].astype(jnp.bfloat16), x_rows[slab, :, lanes]
            )
            down_out[:, out] = ADAPTER_SCALE * dot_nn(
                down_sums[...].astype(jnp.bfloat16), dy_rows[slab, :, lanes]
            )


def shared_gradients(x, dy, order, slab_order, sums, down_sums):
    tokens_each, feat = x.arrays[0].shape[-2:]
    slabs = slab_order.shape[0]
    rows = SHARDS * tokens_each
    pair, rank = sums.shape[1], down_sums.shape[1]
    return pl.pallas_call(
        lambda *refs: shared_kernel(x.places, dy.places, *refs),
        out_shape=(
            jax.ShapeDtypeStruct((pair, slabs * feat), jnp.float32),
            jax.ShapeDtypeStruct((rank, slabs * feat), jnp.float32),
        ),
        in_specs=[HBM] * (len(x.arrays) + len(dy.arrays)) + [SMEM, SMEM, VMEM, VMEM],
        out_specs=(VMEM, VMEM),
        scratch_shapes=[
            pltpu.VMEM((slabs, rows, feat), jnp.bfloat16),
            pltpu.VMEM((slabs, rows, feat), jnp.bfloat16),
            pltpu.VMEM((pair, rows), jnp.float32),
            pltpu.VMEM((rank, rows), jnp.float32),
            pltpu.SemaphoreType.DMA((slabs, SHARDS)),
            pltpu.SemaphoreType.DMA((slabs, SHARDS)),
        ],
        compiler_params=pltpu.CompilerParams(vmem_limit_bytes=VMEM_BYTES),
        cost_estimate=pl.CostEstimate(
            flops=16 * rows * pair * slabs * feat,
            bytes_accessed=4 * rows * slabs * feat,
            transcendentals=0,
        ),
        name="shared_gradients",
    )(*x.arrays, *dy.arrays, order, slab_order, sums, down_sums)


CORE, ACROSS, ALONG = 1, 2, 4
PLANE = (ACROSS, ALONG, ACROSS | ALONG)


def swap(value, bit, axis="dp"):
    return lax.ppermute(value, axis, [(i, i ^ bit) for i in range(lax.axis_size(axis))])


def after(value, *others):
    return lax.optimization_barrier((value, others))[0]


def added(left, right):
    return (wide(left) + wide(right)).astype(jnp.bfloat16)


def local(
    tokens,
    output_gradient,
    routing,
    router_gate_values,
    gate_weight,
    up_weight,
    down_weight,
    adapter_lower_gate,
    adapter_upper_gate,
    adapter_lower_up,
    adapter_upper_up,
    adapter_lower_down,
    adapter_upper_down,
):
    experts = lax.axis_size("expert")
    me, expert = lax.axis_index("dp"), lax.axis_index("expert")
    tokens_each, feat = tokens.shape
    rank = adapter_lower_gate.shape[1]
    order = jnp.bitwise_xor(jnp.arange(SHARDS, dtype=jnp.int32), me.astype(jnp.int32))
    slab_order = jnp.bitwise_xor(jnp.arange(experts, dtype=jnp.int32), expert.astype(jnp.int32))

    named = routing[:, :, None] == jnp.arange(experts, dtype=jnp.int32)[None, None, :]
    weight_of = jnp.sum(jnp.where(named, router_gate_values[:, :, None], 0.0), axis=1)
    routes = lax.all_gather(weight_of.T, "dp", axis=0, tiled=False)
    route = lax.dynamic_index_in_dim(routes, expert, axis=1, keepdims=False)[order]
    route_blocks = route[:, None, :]
    route_row = route.reshape(1, SHARDS * tokens_each)

    def slabs_first(factor):
        return factor.reshape(factor.shape[0], experts, feat).transpose(1, 0, 2)[slab_order]

    lower_cat = jnp.concatenate([adapter_lower_gate[0], adapter_lower_up[0]], axis=0)
    down_lower = adapter_lower_down[0]

    def place_both(rows, part, swapped, chip, slabs):
        rows.add(part, *((r, 2 * chip) for r in slabs))
        rows.add(swapped, *((r, 2 * chip + 1) for r in slabs))

    def over_experts(block, r):
        return swap(block, r, "expert")

    both = over_experts(jnp.stack([tokens, output_gradient]), 1)
    x_slabs = [both[0]] + [over_experts(tokens, r) for r in range(2, experts)]
    x_near = [tokens] + [swap(tokens, bit) for bit in PLANE[:2]]
    uppers = (adapter_upper_gate[0], adapter_upper_up[0])
    (x_slabs, x_near, dy_near), small = lax.optimization_barrier(
        ((x_slabs, x_near, both[1]), (route_row, adapter_upper_down[0], lower_cat, uppers))
    )
    route_row, down_upper, lower_cat, uppers = small
    lower_slabs, down_upper = slabs_first(lower_cat), slabs_first(down_upper.T)
    ready = (lower_slabs, down_upper, down_lower, down_lower.T, *uppers)

    x_rest = [jnp.stack(x_slabs)]
    x_rest += [swap(x_rest[0], bit) for bit in PLANE[:2]]
    x_near.append(swap(x_near[2], ACROSS))
    dy_late = after(output_gradient, x_rest[0])
    dy_slabs = [output_gradient, dy_near] + [over_experts(dy_late, r) for r in range(2, experts)]

    (x_rest, x_near, dy_slabs), ready = lax.optimization_barrier(
        ((x_rest, x_near, dy_slabs), ready)
    )
    lower_slabs, down_upper, *factors = ready
    uppers = factors[2:]
    half = experts // 2
    x_far = [swap(x_rest[2][: half - 1], ACROSS), swap(x_rest[1][half - 1 :], ALONG)]
    x_near_swapped = swap(jnp.stack(x_near[:2]), CORE)
    x_rest_swapped = [swap(part, CORE) for part in x_rest[:2]]
    dy_all = after(jnp.stack(dy_slabs), x_near_swapped, *x_rest_swapped)
    dy_plane = [swap(dy_all, bit) for bit in PLANE[:2]]

    x_main = Rows(range(4))
    x_main.add(x_near[0], (0, 0))
    x_main.add(x_near[1], (0, 2))
    x_main.add(x_near_swapped, (0, 1), (0, 3))
    for chip in range(2):
        place_both(x_main, x_rest[chip], x_rest_swapped[chip], chip, range(1, experts))

    weights = (gate_weight[0], up_weight[0], down_weight[0])
    saved = [forward_rows(x_main, slab_order, weights, lower_slabs, *uppers)]

    x_far, x_late = after((x_far, (x_near[2:], x_rest[2])), saved[0][0])
    x_pair = jnp.stack(x_late[0])
    x_far = jnp.concatenate(x_far, axis=0)
    x_away = Rows(range(4, SHARDS))
    x_away.add(x_pair, (0, 4), (0, 6))
    x_away.add(swap(x_pair, CORE), (0, 5), (0, 7))
    place_both(x_away, x_late[1], swap(x_late[1], CORE), 2, range(1, experts))
    place_both(x_away, x_far, swap(x_far, CORE), 3, range(1, experts))

    saved.append(forward_rows(x_away, slab_order, weights, lower_slabs, *uppers))

    dy_plane = after(dy_plane, saved[1][0])
    dy_far = [swap(dy_plane[1][:half], ACROSS), swap(dy_plane[0][half:], ALONG)]

    dy_main, dy_away = Rows(range(4)), Rows(range(4, SHARDS))
    for chip, part in enumerate((dy_all, dy_plane[0])):
        place_both(dy_main, part, swap(part, CORE), chip, range(experts))
    split = 4 * tokens_each
    route_halves = (route_row[:, :split], route_row[:, split:])

    def hidden_part(rows, i):
        return hidden_gradients(
            rows, slab_order, route_halves[i], weights[2], down_upper, factors, saved[i][:3]
        )

    grads = [hidden_part(dy_main, 0)]
    place_both(dy_away, dy_plane[1], swap(dy_plane[1], CORE), 2, range(experts))
    for part, slabs in zip(after(dy_far, grads[0][0]), (range(half), range(half, experts))):
        place_both(dy_away, part, swap(part, CORE), 3, slabs)
    grads.append(hidden_part(dy_away, 1))
    d_pair = [grad[0] for grad in grads]
    parts = jnp.concatenate([grad[1] for grad in grads], axis=1)

    def sum_step(total, bit):
        other = swap(total.reshape(SHARDS, 3 * rank, tokens_each), bit)
        shape = (SHARDS // (2 * bit), 2, bit, 3 * rank, tokens_each)
        return total.reshape(shape) + other.reshape(shape)[:, ::-1]

    sums = [parts.reshape(3 * rank, SHARDS, tokens_each).transpose(1, 0, 2)]
    for bit in (CORE, ACROSS, ALONG):
        sums.append(sum_step(sums[-1], bit))

    def send(keep, got):
        chips = [added(keep[i], got[i]) for i in range(SHARDS // 2)]
        return chips, [swap(part, bit) for bit, part in zip(PLANE, chips[1:])]

    def total_rows(chips, moved):
        return sum((wide(part) for part in moved), wide(chips[0]))

    def terms(group, *others):
        here = after(slab_order, *others) if others else slab_order
        keep, away = slab_terms(group, here, d_pair, weights, lower_slabs)
        return keep, swap(away, CORE)

    keep_a, got_a = terms((3, 2), sums[1])
    keep_b, got_b = terms((1,), sums[2])
    chips_a, moved_a = send(keep_a, after(got_a, keep_b))
    keep_c, got_c = terms((0,), sums[3], *chips_a)
    rows_a = total_rows(chips_a, after(moved_a, keep_c))
    chips_b, moved_b = send(keep_b, after(got_b, keep_c))
    kept_parts = [(kept[3], grad[2], grad[0], kept[2]) for kept, grad in zip(saved, grads)]
    (low_first, *rest), *others = kept_parts
    kept_parts = [(after(low_first, rows_a, *chips_b), *rest), *others]
    owned, owned_down = owned_gradients(kept_parts, 200 * 1024 * SHARDS * tokens_each * 2 * rank * 4)
    got_c, moved_b = after((got_c, moved_b), owned_down)
    chips_c, moved_c = send(keep_c, got_c)

    x, dy = Rows(range(SHARDS)), Rows(range(SHARDS))
    for whole, halves in ((x, (x_main, x_away)), (dy, (dy_main, dy_away))):
        for rows in halves:
            whole.arrays += rows.arrays
            whole.places += rows.places
    total = after(sums[3].reshape(SHARDS, 3 * rank, tokens_each), *chips_c)
    grad_pair, grad_down = shared_gradients(
        x,
        dy,
        order,
        slab_order,
        total[:, : 2 * rank],
        total[:, 2 * rank :] * route_blocks,
    )
    rows_b = total_rows(chips_b, moved_b)
    rows_c = total_rows(chips_c, after(moved_c, grad_pair))
    grad_x = rows_c[0]
    for rows, r in ((rows_a[0], 3), (rows_a[1], 2), (rows_b[0], 1)):
        grad_x = grad_x + wide(over_experts(rows.astype(jnp.bfloat16), r))
    grad_x = grad_x.astype(jnp.bfloat16)
    return (
        grad_x,
        grad_pair[None, :rank],
        owned[0].T[None],
        grad_pair[None, rank:],
        owned[1].T[None],
        owned_down[None],
        grad_down.T[None],
    )


def plan(tokens, *others):
    experts, tokens_each, hidden_here = lax.axis_size("expert"), tokens.shape[0], others[3].shape[1]
    planned = (
        lax.axis_size("dp") == SHARDS
        and experts == 4
        and hidden_here % LANES == 0
        and tokens_each % LANES == 0
        and tokens.shape[1] % TILE == 0
    )
    return (local if planned else general_local)(tokens, *others)


def solution(mesh):
    return jax.shard_map(
        plan,
        mesh=mesh,
        in_specs=(
            P("dp", "expert"),
            P("dp", "expert"),
            P("dp", None),
            P("dp", None),
            P("expert", "dp", None),
            P("expert", "dp", None),
            P("expert", "dp", None),
            P("expert", None, None),
            P("expert", "dp", None),
            P("expert", None, None),
            P("expert", "dp", None),
            P("expert", None, "dp"),
            P("expert", None, None),
        ),
        out_specs=(
            P("dp", "expert"),
            P("expert", None, None),
            P("expert", "dp", None),
            P("expert", None, None),
            P("expert", "dp", None),
            P("expert", None, "dp"),
            P("expert", None, None),
        ),
        check_vma=False,
    )
```

```python
import jax
import jax.numpy as jnp
from jax import lax
from jax.experimental import pallas as pl
from jax.experimental.pallas import tpu as pltpu
from jax.sharding import PartitionSpec as P

ADAPTER_SCALE = 2.0


def contract_pair(left, right, left_axis, right_axis):
    return lax.dot_general(
        left, right, (((left_axis,), (right_axis,)), ((), ())), preferred_element_type=jnp.float32
    )


def slot_numbers(route_rows, experts):
    picked = (route_rows[:, :, None] == jnp.arange(experts, dtype=jnp.int32)[None, None, :]).astype(
        jnp.int32
    )
    per_token = jnp.sum(picked, axis=1)
    earlier = jnp.cumsum(per_token, axis=0) - per_token
    return jnp.sum(earlier[:, None, :] * picked, axis=2)


def slot_sources(route_rows, positions, experts, capacity):
    tokens_here, choose = route_rows.shape
    target = (route_rows * capacity + positions).reshape(-1)
    owners = jnp.repeat(jnp.arange(tokens_here, dtype=jnp.int32), choose)
    member_ids = jnp.tile(jnp.arange(choose, dtype=jnp.int32), tokens_here)
    source = jnp.full((experts * capacity,), tokens_here, jnp.int32).at[target].set(owners)
    member = jnp.zeros((experts * capacity,), jnp.int32).at[target].set(member_ids)
    return (source, member)


def rows_backward_pass(input_rows, output_gradient_rows, params):
    (
        gate_weight,
        up_weight,
        down_weight,
        a_gate,
        gate_adapter_upper,
        a_up,
        up_adapter_upper,
        down_adapter_lower,
        b_down,
    ) = params
    gate_projected_lower = contract_pair(a_gate, input_rows, 1, 1).astype(jnp.bfloat16)
    up_projected_lower = contract_pair(a_up, input_rows, 1, 1).astype(jnp.bfloat16)
    gate_preactivation = contract_pair(
        gate_weight, input_rows, 1, 1
    ) + ADAPTER_SCALE * contract_pair(gate_adapter_upper, gate_projected_lower, 1, 0)
    up_preactivation = contract_pair(up_weight, input_rows, 1, 1) + ADAPTER_SCALE * contract_pair(
        up_adapter_upper, up_projected_lower, 1, 0
    )
    sigmoid_gate = jax.nn.sigmoid(gate_preactivation)
    silu_gate = gate_preactivation * sigmoid_gate
    hidden_units = (silu_gate * up_preactivation).astype(jnp.bfloat16)
    down_projected_lower = contract_pair(b_down, output_gradient_rows, 0, 1).astype(jnp.bfloat16)
    hidden_gradient = contract_pair(
        down_weight, output_gradient_rows, 1, 1
    ) + ADAPTER_SCALE * contract_pair(down_adapter_lower, down_projected_lower, 0, 0)
    gate_gradient = (
        hidden_gradient
        * up_preactivation
        * sigmoid_gate
        * (1.0 + gate_preactivation * (1.0 - sigmoid_gate))
    ).astype(jnp.bfloat16)
    up_gradient = (hidden_gradient * silu_gate).astype(jnp.bfloat16)
    gate_partial = contract_pair(gate_adapter_upper, gate_gradient, 0, 0).astype(jnp.bfloat16)
    up_partial = contract_pair(up_adapter_upper, up_gradient, 0, 0).astype(jnp.bfloat16)
    down_partial = contract_pair(down_adapter_lower, hidden_units, 1, 0).astype(jnp.bfloat16)
    paired_partials = jnp.concatenate([gate_partial, up_partial], 0)
    paired_factors = jnp.concatenate([a_gate, a_up], 0)
    gradient_rows_out = (
        contract_pair(gate_gradient, gate_weight, 0, 0)
        + contract_pair(up_gradient, up_weight, 0, 0)
        + ADAPTER_SCALE * contract_pair(paired_partials, paired_factors, 0, 0)
    )
    shared_slice = (
        ADAPTER_SCALE * contract_pair(gate_partial, input_rows, 1, 0),
        ADAPTER_SCALE * contract_pair(up_partial, input_rows, 1, 0),
        ADAPTER_SCALE * contract_pair(output_gradient_rows, down_partial, 0, 1),
    )
    owned_slice = (
        ADAPTER_SCALE * contract_pair(gate_gradient, gate_projected_lower, 1, 1),
        ADAPTER_SCALE * contract_pair(up_gradient, up_projected_lower, 1, 1),
        ADAPTER_SCALE * contract_pair(down_projected_lower, hidden_units, 1, 1),
    )
    return (gradient_rows_out, shared_slice, owned_slice)


def general_local(
    tokens,
    output_gradient,
    routing,
    router_gate_values,
    gate_weight,
    up_weight,
    down_weight,
    adapter_lower_gate,
    adapter_upper_gate,
    adapter_lower_up,
    adapter_upper_up,
    adapter_lower_down,
    adapter_upper_down,
):
    experts = lax.axis_size("expert")
    shards = lax.axis_size("dp")
    tok_local, feat_local = tokens.shape
    choose = routing.shape[1]
    complete_width = feat_local * experts
    capacity = min(tok_local, 6 * tok_local // experts)
    hidden_units_local = gate_weight.shape[1]
    adapter_rank = adapter_lower_gate.shape[1]
    params = (
        gate_weight[0],
        up_weight[0],
        down_weight[0],
        adapter_lower_gate[0],
        adapter_upper_gate[0],
        adapter_lower_up[0],
        adapter_upper_up[0],
        adapter_lower_down[0],
        adapter_upper_down[0],
    )
    positions = slot_numbers(routing, experts)
    zero_row = jnp.zeros((1, feat_local), jnp.bfloat16)
    initial = (
        jnp.zeros((shards * capacity, complete_width), jnp.float32),
        (
            jnp.zeros((adapter_rank, complete_width), jnp.float32),
            jnp.zeros((adapter_rank, complete_width), jnp.float32),
            jnp.zeros((complete_width, adapter_rank), jnp.float32),
        ),
        (
            jnp.zeros((hidden_units_local, adapter_rank), jnp.float32),
            jnp.zeros((hidden_units_local, adapter_rank), jnp.float32),
            jnp.zeros((adapter_rank, hidden_units_local), jnp.float32),
        ),
    )
    source, member = slot_sources(routing, positions, experts, capacity)
    clamped = jnp.minimum(source, tok_local - 1)
    slot_gate = jnp.where(
        source < tok_local, router_gate_values.reshape(-1)[clamped * choose + member], 0.0
    )
    send_x = jnp.concatenate([tokens, zero_row], 0)[source].reshape(experts, capacity, feat_local)
    send_dy = (
        (
            slot_gate[:, None]
            * jnp.concatenate([output_gradient, zero_row], 0)[source].astype(jnp.float32)
        )
        .astype(jnp.bfloat16)
        .reshape(experts, capacity, feat_local)
    )
    recv_x, recv_dy = (
        lax.all_to_all(send_x, "expert", split_axis=0, concat_axis=2, tiled=True),
        lax.all_to_all(send_dy, "expert", split_axis=0, concat_axis=2, tiled=True),
    )
    gradient_rows_out, shared_slice, owned_slice = rows_backward_pass(
        lax.all_gather(recv_x[0], "dp", axis=0, tiled=True),
        lax.all_gather(recv_dy[0], "dp", axis=0, tiled=True),
        params,
    )
    rows_part = gradient_rows_out
    totals = (
        rows_part,
        jax.tree.map(jnp.add, initial[1], shared_slice),
        jax.tree.map(jnp.add, initial[2], owned_slice),
    )
    rows_part, shared_slice, owned_slice = totals
    summed = lax.psum_scatter(
        rows_part.astype(jnp.bfloat16), "dp", scatter_dimension=0, tiled=True
    ).astype(jnp.float32)
    returned_rows = lax.all_to_all(
        summed.reshape(capacity, experts, feat_local).astype(jnp.bfloat16),
        "expert",
        split_axis=1,
        concat_axis=1,
        tiled=True,
    ).astype(jnp.float32)
    lookup = positions * experts + routing
    grad_x = jnp.sum(returned_rows.reshape(capacity * experts, feat_local)[lookup], axis=1).astype(
        jnp.bfloat16
    )
    grad_a_gate, grad_a_up, grad_b_down = (
        lax.psum(shared_slice[0].astype(jnp.bfloat16), "dp").astype(jnp.float32),
        lax.psum(shared_slice[1].astype(jnp.bfloat16), "dp").astype(jnp.float32),
        lax.psum(shared_slice[2].astype(jnp.bfloat16), "dp").astype(jnp.float32),
    )
    return (
        grad_x,
        grad_a_gate[None],
        owned_slice[0][None],
        grad_a_up[None],
        owned_slice[1][None],
        owned_slice[2][None],
        grad_b_down[None],
    )


LANES = 128
TILE = 512
SHARDS = 8
VMEM_BYTES = 58 * 1024 * 1024
HIDDEN_BYTES = 58 * 1024 * 1024
TERM_BYTES = 58 * 1024 * 1024
HBM = pl.BlockSpec(memory_space=pl.ANY)
PINNED = pl.BlockSpec(memory_space=pltpu.HBM)
VMEM = pl.BlockSpec(memory_space=pltpu.VMEM)
SMEM = pl.BlockSpec(memory_space=pltpu.SMEM)


def dot_nt(left, right):
    return contract_pair(left, right, 1, 1)


def dot_nn(left, right):
    return contract_pair(left, right, 1, 0)


def wide(value):
    return value.astype(jnp.float32)


class Rows:
    def __init__(self, blocks):
        self.arrays, self.places, self.blocks = [], [], blocks

    def add(self, array, *places):
        self.arrays.append(array)
        self.places.append(places)


def row_copies(refs, places, target, sems, slab, first=0, order=None):
    tokens_each = refs[0].shape[-2]
    copies = []
    for ref, parts in zip(refs, places):
        for i, (at, block) in enumerate(parts):
            if at != slab:
                continue
            source = ref.at[i] if len(ref.shape) == 3 else ref
            row = (block - first) * tokens_each
            if order is not None:
                row = pl.multiple_of(order[block] * tokens_each, tokens_each)
            copies.append(
                pltpu.make_async_copy(
                    source, target.at[slab, pl.ds(row, tokens_each)], sems.at[slab, block]
                )
            )
    return copies


def slab_lanes(slab_ref, slab, feat):
    return pl.ds(pl.multiple_of(slab_ref[slab] * feat, feat), feat)


def forward_kernel(places, first, *refs):
    n_pieces = len(places)
    pieces = refs[:n_pieces]
    (
        slab_ref,
        gate_hbm,
        up_hbm,
        lower_hbm,
        gate_upper_ref,
        up_upper_ref,
        silu_out,
        slope_out,
        hidden_out,
        low_out,
    ) = refs[n_pieces : n_pieces + 10]
    x_rows, weights, pre, saved, x_sems, w_sems, out_sems = refs[n_pieces + 10 :]
    slabs, _, feat = x_rows.shape
    hidden_here = gate_hbm.shape[0]
    pair, rank = lower_hbm.shape[1], gate_upper_ref.shape[1]

    def x_slab(slab):
        return row_copies(pieces, places, x_rows, x_sems, slab, first)

    def weight_copies(slab):
        lanes = slab_lanes(slab_ref, slab, feat)
        sides = (
            (gate_hbm.at[:, lanes], 0, hidden_here),
            (up_hbm.at[:, lanes], hidden_here, hidden_here),
            (lower_hbm.at[slab], 2 * hidden_here, pair),
        )
        return [
            pltpu.make_async_copy(
                source, weights.at[slab, pl.ds(start, size)], w_sems.at[slab, i]
            )
            for i, (source, start, size) in enumerate(sides)
        ]

    for slab in range(slabs):
        for copy in x_slab(slab) + weight_copies(slab):
            copy.start()
    for slab in range(slabs):
        for copy in x_slab(slab) + weight_copies(slab):
            copy.wait()
        if slab == 0:
            pre[...] = dot_nt(weights[0], x_rows[0])
        else:
            pre[...] += dot_nt(weights[slab], x_rows[slab])
    low_out[...] = pre[2 * hidden_here :, :].astype(jnp.bfloat16)

    def out_copies(tile):
        at = pl.ds(pl.multiple_of(tile * LANES, LANES), LANES)
        return [
            pltpu.make_async_copy(saved.at[i, at], out.at[at], out_sems.at[i, tile])
            for i, out in enumerate((silu_out, slope_out, hidden_out))
        ]

    tiles = hidden_here // LANES

    @pl.loop(0, tiles)
    def _(tile):
        start = pl.multiple_of(tile * LANES, LANES)
        at = pl.ds(start, LANES)
        up_at = pl.ds(pl.multiple_of(hidden_here + start, LANES), LANES)
        pre_gate = pre[at, :] + ADAPTER_SCALE * dot_nn(gate_upper_ref[at, :], low_out[:rank, :])
        pre_up = pre[up_at, :] + ADAPTER_SCALE * dot_nn(up_upper_ref[at, :], low_out[rank:, :])
        sigma = 1.0 / (1.0 + jnp.exp(-pre_gate))
        silu = pre_gate * sigma
        saved[0, at, :] = silu.astype(jnp.bfloat16)
        saved[1, at, :] = (pre_up * (sigma * (1.0 + pre_gate * (1.0 - sigma)))).astype(
            jnp.bfloat16
        )
        saved[2, at, :] = (silu * pre_up).astype(jnp.bfloat16)
        for copy in out_copies(tile):
            copy.start()

    @pl.loop(0, tiles)
    def _(tile):
        for copy in out_copies(tile):
            copy.wait()


def forward_rows(x, slab_order, weights, lower_slabs, gate_upper, up_upper):
    hidden_here, width = weights[0].shape
    tokens_each, feat = x.arrays[0].shape[-2:]
    rows = len(x.blocks) * tokens_each
    slabs, pair, _ = lower_slabs.shape
    kept = jax.ShapeDtypeStruct((hidden_here, rows), jnp.bfloat16)
    return pl.pallas_call(
        lambda *refs: forward_kernel(x.places, x.blocks[0], *refs),
        out_shape=(kept, kept, kept, jax.ShapeDtypeStruct((pair, rows), jnp.bfloat16)),
        in_specs=[HBM] * len(x.arrays) + [SMEM] + [HBM] * 3 + [VMEM] * 2,
        out_specs=(HBM, HBM, HBM, VMEM),
        scratch_shapes=[
            pltpu.VMEM((slabs, rows, feat), jnp.bfloat16),
            pltpu.VMEM((slabs, 2 * hidden_here + pair, feat), jnp.bfloat16),
            pltpu.VMEM((2 * hidden_here + pair, rows), jnp.float32),
            pltpu.VMEM((3, hidden_here, rows), jnp.bfloat16),
            pltpu.SemaphoreType.DMA((slabs, SHARDS)),
            pltpu.SemaphoreType.DMA((slabs, 3)),
            pltpu.SemaphoreType.DMA((3, hidden_here // LANES)),
        ],
        compiler_params=pltpu.CompilerParams(vmem_limit_bytes=VMEM_BYTES),
        cost_estimate=pl.CostEstimate(
            flops=rows * hidden_here * width // 4,
            bytes_accessed=2 * rows * width,
            transcendentals=rows * hidden_here,
        ),
        name="forward_rows",
    )(*x.arrays, slab_order, *weights[:2], lower_slabs, gate_upper, up_upper)


def hidden_kernel(places, first, *refs):
    n_pieces = len(places)
    pieces = refs[:n_pieces]
    (
        slab_ref,
        route_ref,
        down_hbm,
        down_upper_hbm,
        down_lower_ref,
        down_lower_t_ref,
        gate_upper_ref,
        up_upper_ref,
        silu_hbm,
        slope_hbm,
        hidden_hbm,
        d_pair,
        parts_out,
        low_down,
        rows,
        down_w,
        d_down,
        silu,
        slope,
        hidden,
        row_sems,
        d_sems,
        f_sems,
    ) = refs[n_pieces:]
    slabs, _, feat = rows.shape
    hidden_here = silu.shape[0]
    rank = down_lower_ref.shape[0]
    saved_copies = [
        pltpu.make_async_copy(source, target, f_sems.at[i])
        for i, (source, target) in enumerate(
            ((silu_hbm, silu), (slope_hbm, slope), (hidden_hbm, hidden))
        )
    ]

    def slab_copies(slab):
        return row_copies(pieces, places, rows, row_sems, slab, first) + [
            pltpu.make_async_copy(
                down_hbm.at[:, slab_lanes(slab_ref, slab, feat)],
                down_w.at[slab, pl.ds(0, hidden_here)],
                d_sems.at[slab, 0],
            ),
            pltpu.make_async_copy(
                down_upper_hbm.at[slab], down_w.at[slab, pl.ds(hidden_here, rank)], d_sems.at[slab, 1]
            ),
        ]

    for slab in range(slabs):
        for copy in slab_copies(slab):
            copy.start()
    for copy in saved_copies:
        copy.start()
    for slab in range(slabs):
        for copy in slab_copies(slab):
            copy.wait()
        if slab == 0:
            d_down[...] = dot_nt(down_w[0], rows[0])
        else:
            d_down[...] += dot_nt(down_w[slab], rows[slab])

    low_down[...] = (d_down[hidden_here:, :] * route_ref[...]).astype(jnp.bfloat16)
    for copy in saved_copies:
        copy.wait()

    @pl.loop(0, hidden_here // LANES)
    def _(tile):
        start = pl.multiple_of(tile * LANES, LANES)
        at = pl.ds(start, LANES)
        up_at = pl.ds(pl.multiple_of(hidden_here + start, LANES), LANES)
        d_hidden = d_down[at, :] * route_ref[...]
        d_hidden = d_hidden + ADAPTER_SCALE * dot_nn(down_lower_t_ref[at, :], low_down[...])
        d_gate = (d_hidden * wide(slope[at, :])).astype(jnp.bfloat16)
        d_up = (d_hidden * wide(silu[at, :])).astype(jnp.bfloat16)
        d_pair[:, at] = d_gate.T
        d_pair[:, up_at] = d_up.T

    for side, factor in enumerate((gate_upper_ref, up_upper_ref)):
        start = side * hidden_here
        part = dot_nn(d_pair[:, start : start + hidden_here], factor[...])
        parts_out[side * rank : (side + 1) * rank, :] = part.T
        at = 2 * hidden_here + side * rank
        d_pair[:, at : at + rank] = ADAPTER_SCALE * part.astype(jnp.bfloat16)
    parts_out[2 * rank :, :] = dot_nn(down_lower_ref[...], hidden[...])


def hidden_gradients(dy, slab_order, route_row, down_weight, down_upper, factors, saved):
    hidden_here, width = down_weight.shape
    slabs, rank, feat = down_upper.shape
    pair = 2 * rank
    rows = route_row.shape[1]
    return pl.pallas_call(
        lambda *refs: hidden_kernel(dy.places, dy.blocks[0], *refs),
        out_shape=(
            jax.ShapeDtypeStruct((rows, 2 * hidden_here + pair), jnp.bfloat16),
            jax.ShapeDtypeStruct((3 * rank, rows), jnp.float32),
            jax.ShapeDtypeStruct((rank, rows), jnp.bfloat16),
        ),
        in_specs=[HBM] * len(dy.arrays) + [SMEM, VMEM] + [HBM] * 2 + [VMEM] * 4 + [HBM] * 3,
        out_specs=(VMEM,) * 3,
        scratch_shapes=[
            pltpu.VMEM((slabs, rows, feat), jnp.bfloat16),
            pltpu.VMEM((slabs, hidden_here + rank, feat), jnp.bfloat16),
            pltpu.VMEM((hidden_here + rank, rows), jnp.float32),
            pltpu.VMEM((hidden_here, rows), jnp.bfloat16),
            pltpu.VMEM((hidden_here, rows), jnp.bfloat16),
            pltpu.VMEM((hidden_here, rows), jnp.bfloat16),
            pltpu.SemaphoreType.DMA((slabs, SHARDS)),
            pltpu.SemaphoreType.DMA((slabs, 2)),
            pltpu.SemaphoreType.DMA((3,)),
        ],
        compiler_params=pltpu.CompilerParams(vmem_limit_bytes=HIDDEN_BYTES),
        cost_estimate=pl.CostEstimate(
            flops=4 * rows * hidden_here * width,
            bytes_accessed=2 * hidden_here * width + 2 * rows * width,
            transcendentals=0,
        ),
        name="hidden_gradients",
    )(*dy.arrays, slab_order, route_row, down_weight, down_upper, *factors, *saved)


def term_kernel(slabs, n_parts, *refs):
    d_parts = refs[:n_parts]
    slab_ref, gate_hbm, up_hbm, lower_hbm = refs[n_parts : n_parts + 4]
    outs, (d_pair, pair_w, sems, d_sems) = refs[n_parts + 4 : -4], refs[-4:]
    _, depth, step = pair_w.shape
    hidden_here = gate_hbm.shape[0]
    pair = depth - 2 * hidden_here
    tokens_each, feat = outs[0].shape[2:]
    steps = feat // step

    def weight_copies(i, n):
        slab, k = slabs[i], i * steps + n
        lanes = pl.ds(pl.multiple_of(slab_ref[slab] * feat + n * step, step), step)
        sides = (
            (gate_hbm.at[:, lanes], 0, hidden_here),
            (up_hbm.at[:, lanes], hidden_here, hidden_here),
            (lower_hbm.at[slab, :, pl.ds(pl.multiple_of(n * step, step), step)], 2 * hidden_here, pair),
        )
        return [
            pltpu.make_async_copy(source, pair_w.at[k, pl.ds(start, size)], sems.at[k, side])
            for side, (source, start, size) in enumerate(sides)
        ]

    d_copies, row = [], 0
    for i, part in enumerate(d_parts):
        count = part.shape[0]
        d_copies.append(pltpu.make_async_copy(part, d_pair.at[pl.ds(row, count)], d_sems.at[i]))
        row += count
    for copy in d_copies:
        copy.start()
    for i in range(len(slabs)):
        for n in range(steps):
            for copy in weight_copies(i, n):
                copy.start()
    for copy in d_copies:
        copy.wait()
    for i in range(len(slabs)):

        @pl.loop(0, steps)
        def _(n):
            for copy in weight_copies(i, n):
                copy.wait()
            lanes = pl.ds(pl.multiple_of(n * step, step), step)
            term = dot_nn(d_pair[...], pair_w[i * steps + n]).astype(jnp.bfloat16)
            for block in range(SHARDS):
                at = slice(block * tokens_each, (block + 1) * tokens_each)
                outs[block % 2][block // 2, i, :, lanes] = term[at]


def slab_terms(slabs, slab_order, d_pair, weights, lower_slabs):
    rows, depth = sum(part.shape[0] for part in d_pair), d_pair[0].shape[1]
    feat = lower_slabs.shape[2]
    parts = len(slabs) * feat // TILE
    term = jax.ShapeDtypeStruct((SHARDS // 2, len(slabs), rows // SHARDS, feat), jnp.bfloat16)
    return pl.pallas_call(
        lambda *refs: term_kernel(slabs, len(d_pair), *refs),
        out_shape=(term, term),
        in_specs=[HBM] * len(d_pair) + [SMEM] + [HBM] * 3,
        out_specs=(VMEM, VMEM),
        scratch_shapes=[
            pltpu.VMEM((rows, depth), jnp.bfloat16),
            pltpu.VMEM((parts, depth, TILE), jnp.bfloat16),
            pltpu.SemaphoreType.DMA((parts, 3)),
            pltpu.SemaphoreType.DMA((len(d_pair),)),
        ],
        compiler_params=pltpu.CompilerParams(vmem_limit_bytes=TERM_BYTES),
        cost_estimate=pl.CostEstimate(
            flops=12 * rows * depth * feat * len(slabs),
            bytes_accessed=2 * depth * feat * len(slabs) + 4 * rows * depth,
            transcendentals=0,
        ),
        name="slab_terms",
    )(*d_pair, slab_order, *weights[:2], lower_slabs)


def owned_kernel(n_parts, *refs):
    parts = [refs[4 * i : 4 * i + 4] for i in range(n_parts)]
    owned_out, owned_down_out = refs[4 * n_parts :]
    rank, hidden_here = owned_down_out.shape
    gate_sum = up_sum = down_sum = 0.0
    for low, low_down, d_pair, hidden in parts:
        gate_sum += dot_nn(low[:rank, :], d_pair[:, :hidden_here])
        up_sum += dot_nn(low[rank:, :], d_pair[:, hidden_here : 2 * hidden_here])
        down_sum += dot_nt(low_down[...], hidden[...])
    owned_out[0] = ADAPTER_SCALE * gate_sum
    owned_out[1] = ADAPTER_SCALE * up_sum
    owned_down_out[...] = ADAPTER_SCALE * down_sum


def owned_gradients(parts, hint):
    rank, hidden_here = parts[0][1].shape[0], parts[0][3].shape[0]
    return pl.pallas_call(
        lambda *refs: owned_kernel(len(parts), *refs),
        out_shape=(
            jax.ShapeDtypeStruct((2, rank, hidden_here), jnp.float32),
            jax.ShapeDtypeStruct((rank, hidden_here), jnp.float32),
        ),
        in_specs=[VMEM] * (4 * len(parts)),
        out_specs=(VMEM, VMEM),
        compiler_params=pltpu.CompilerParams(vmem_limit_bytes=VMEM_BYTES),
        cost_estimate=pl.CostEstimate(flops=hint, bytes_accessed=8_000_000, transcendentals=0),
        name="owned_gradients",
    )(*(value for part in parts for value in part))


def shared_kernel(x_places, dy_places, *refs):
    split, inputs = len(x_places), len(x_places) + len(dy_places)
    x_pieces, dy_pieces = refs[:split], refs[split:inputs]
    order_ref, slab_ref, sums_ref, down_sums_ref, pair_out, down_out = refs[inputs : inputs + 6]
    x_rows, dy_rows, sums, down_sums, x_sems, dy_sems = refs[inputs + 6 :]
    slabs, _, feat = x_rows.shape
    tokens_each = x_pieces[0].shape[-2]

    def slab_copies(slab):
        return row_copies(
            x_pieces, x_places, x_rows, x_sems, slab, 0, order_ref
        ) + row_copies(dy_pieces, dy_places, dy_rows, dy_sems, slab, 0, order_ref)

    for slab in range(slabs):
        for copy in slab_copies(slab):
            copy.start()
    for block in range(SHARDS):
        lanes = pl.ds(pl.multiple_of(order_ref[block] * tokens_each, tokens_each), tokens_each)
        sums[:, lanes] = sums_ref[block]
        down_sums[:, lanes] = down_sums_ref[block]
    for slab in range(slabs):
        for copy in slab_copies(slab):
            copy.wait()

        @pl.loop(0, feat // TILE)
        def _(n):
            lanes = pl.ds(pl.multiple_of(n * TILE, TILE), TILE)
            out = pl.ds(pl.multiple_of(slab_ref[slab] * feat + n * TILE, TILE), TILE)
            pair_out[:, out] = ADAPTER_SCALE * dot_nn(
                sums[...].astype(jnp.bfloat16), x_rows[slab, :, lanes]
            )
            down_out[:, out] = ADAPTER_SCALE * dot_nn(
                down_sums[...].astype(jnp.bfloat16), dy_rows[slab, :, lanes]
            )


def shared_gradients(x, dy, order, slab_order, sums, down_sums):
    tokens_each, feat = x.arrays[0].shape[-2:]
    slabs = slab_order.shape[0]
    rows = SHARDS * tokens_each
    pair, rank = sums.shape[1], down_sums.shape[1]
    return pl.pallas_call(
        lambda *refs: shared_kernel(x.places, dy.places, *refs),
        out_shape=(
            jax.ShapeDtypeStruct((pair, slabs * feat), jnp.float32),
            jax.ShapeDtypeStruct((rank, slabs * feat), jnp.float32),
        ),
        in_specs=[HBM] * (len(x.arrays) + len(dy.arrays)) + [SMEM, SMEM, VMEM, VMEM],
        out_specs=(VMEM, VMEM),
        scratch_shapes=[
            pltpu.VMEM((slabs, rows, feat), jnp.bfloat16),
            pltpu.VMEM((slabs, rows, feat), jnp.bfloat16),
            pltpu.VMEM((pair, rows), jnp.float32),
            pltpu.VMEM((rank, rows), jnp.float32),
            pltpu.SemaphoreType.DMA((slabs, SHARDS)),
            pltpu.SemaphoreType.DMA((slabs, SHARDS)),
        ],
        compiler_params=pltpu.CompilerParams(vmem_limit_bytes=VMEM_BYTES),
        cost_estimate=pl.CostEstimate(
            flops=16 * rows * pair * slabs * feat,
            bytes_accessed=4 * rows * slabs * feat,
            transcendentals=0,
        ),
        name="shared_gradients",
    )(*x.arrays, *dy.arrays, order, slab_order, sums, down_sums)


CORE, ACROSS, ALONG = 1, 2, 4
PLANE = (ACROSS, ALONG, ACROSS | ALONG)


def swap(value, bit, axis="dp"):
    return lax.ppermute(value, axis, [(i, i ^ bit) for i in range(lax.axis_size(axis))])


def after(value, *others):
    return lax.optimization_barrier((value, others))[0]


def added(left, right):
    return (wide(left) + wide(right)).astype(jnp.bfloat16)


def local(
    tokens,
    output_gradient,
    routing,
    router_gate_values,
    gate_weight,
    up_weight,
    down_weight,
    adapter_lower_gate,
    adapter_upper_gate,
    adapter_lower_up,
    adapter_upper_up,
    adapter_lower_down,
    adapter_upper_down,
):
    experts = lax.axis_size("expert")
    me, expert = lax.axis_index("dp"), lax.axis_index("expert")
    tokens_each, feat = tokens.shape
    rank = adapter_lower_gate.shape[1]
    order = jnp.bitwise_xor(jnp.arange(SHARDS, dtype=jnp.int32), me.astype(jnp.int32))
    slab_order = jnp.bitwise_xor(jnp.arange(experts, dtype=jnp.int32), expert.astype(jnp.int32))

    named = routing[:, :, None] == jnp.arange(experts, dtype=jnp.int32)[None, None, :]
    weight_of = jnp.sum(jnp.where(named, router_gate_values[:, :, None], 0.0), axis=1)
    routes = lax.all_gather(weight_of.T, "dp", axis=0, tiled=False)
    route = lax.dynamic_index_in_dim(routes, expert, axis=1, keepdims=False)[order]
    route_blocks = route[:, None, :]
    route_row = route.reshape(1, SHARDS * tokens_each)

    def slabs_first(factor):
        return factor.reshape(factor.shape[0], experts, feat).transpose(1, 0, 2)[slab_order]

    lower_cat = jnp.concatenate([adapter_lower_gate[0], adapter_lower_up[0]], axis=0)
    down_lower = adapter_lower_down[0]

    def place_both(rows, part, swapped, chip, slabs):
        rows.add(part, *((r, 2 * chip) for r in slabs))
        rows.add(swapped, *((r, 2 * chip + 1) for r in slabs))

    def over_experts(block, r):
        return swap(block, r, "expert")

    both = over_experts(jnp.stack([tokens, output_gradient]), 1)
    x_slabs = [both[0]] + [over_experts(tokens, r) for r in range(2, experts)]
    x_near = [tokens] + [swap(tokens, bit) for bit in PLANE[:2]]
    uppers = (adapter_upper_gate[0], adapter_upper_up[0])
    (x_slabs, x_near, dy_near), small = lax.optimization_barrier(
        ((x_slabs, x_near, both[1]), (route_row, adapter_upper_down[0], lower_cat, uppers))
    )
    route_row, down_upper, lower_cat, uppers = small
    lower_slabs, down_upper = slabs_first(lower_cat), slabs_first(down_upper.T)
    ready = (lower_slabs, down_upper, down_lower, down_lower.T, *uppers)

    x_rest = [jnp.stack(x_slabs)]
    x_rest += [swap(x_rest[0], bit) for bit in PLANE[:2]]
    x_near.append(swap(x_near[2], ACROSS))
    dy_late = after(output_gradient, x_rest[0])
    dy_slabs = [output_gradient, dy_near] + [over_experts(dy_late, r) for r in range(2, experts)]

    (x_rest, x_near, dy_slabs), ready = lax.optimization_barrier(
        ((x_rest, x_near, dy_slabs), ready)
    )
    lower_slabs, down_upper, *factors = ready
    uppers = factors[2:]
    half = experts // 2
    x_far = [swap(x_rest[2][: half - 1], ACROSS), swap(x_rest[1][half - 1 :], ALONG)]
    x_near_swapped = swap(jnp.stack(x_near[:2]), CORE)
    x_rest_swapped = [swap(part, CORE) for part in x_rest[:2]]
    dy_all = after(jnp.stack(dy_slabs), x_near_swapped, *x_rest_swapped)
    dy_plane = [swap(dy_all, bit) for bit in PLANE[:2]]

    x_main = Rows(range(4))
    x_main.add(x_near[0], (0, 0))
    x_main.add(x_near[1], (0, 2))
    x_main.add(x_near_swapped, (0, 1), (0, 3))
    for chip in range(2):
        place_both(x_main, x_rest[chip], x_rest_swapped[chip], chip, range(1, experts))

    weights = (gate_weight[0], up_weight[0], down_weight[0])
    saved = [forward_rows(x_main, slab_order, weights, lower_slabs, *uppers)]

    x_far, x_late = after((x_far, (x_near[2:], x_rest[2])), saved[0][0])
    x_pair = jnp.stack(x_late[0])
    x_far = jnp.concatenate(x_far, axis=0)
    x_away = Rows(range(4, SHARDS))
    x_away.add(x_pair, (0, 4), (0, 6))
    x_away.add(swap(x_pair, CORE), (0, 5), (0, 7))
    place_both(x_away, x_late[1], swap(x_late[1], CORE), 2, range(1, experts))
    place_both(x_away, x_far, swap(x_far, CORE), 3, range(1, experts))

    saved.append(forward_rows(x_away, slab_order, weights, lower_slabs, *uppers))

    dy_plane = after(dy_plane, saved[1][0])
    dy_far = [swap(dy_plane[1][:half], ACROSS), swap(dy_plane[0][half:], ALONG)]

    dy_main, dy_away = Rows(range(4)), Rows(range(4, SHARDS))
    for chip, part in enumerate((dy_all, dy_plane[0])):
        place_both(dy_main, part, swap(part, CORE), chip, range(experts))
    split = 4 * tokens_each
    route_halves = (route_row[:, :split], route_row[:, split:])

    def hidden_part(rows, i):
        return hidden_gradients(
            rows, slab_order, route_halves[i], weights[2], down_upper, factors, saved[i][:3]
        )

    grads = [hidden_part(dy_main, 0)]
    place_both(dy_away, dy_plane[1], swap(dy_plane[1], CORE), 2, range(experts))
    for part, slabs in zip(after(dy_far, grads[0][0]), (range(half), range(half, experts))):
        place_both(dy_away, part, swap(part, CORE), 3, slabs)
    grads.append(hidden_part(dy_away, 1))
    d_pair = [grad[0] for grad in grads]
    parts = jnp.concatenate([grad[1] for grad in grads], axis=1)

    def sum_step(total, bit):
        other = swap(total.reshape(SHARDS, 3 * rank, tokens_each), bit)
        shape = (SHARDS // (2 * bit), 2, bit, 3 * rank, tokens_each)
        return total.reshape(shape) + other.reshape(shape)[:, ::-1]

    sums = [parts.reshape(3 * rank, SHARDS, tokens_each).transpose(1, 0, 2)]
    for bit in (CORE, ACROSS, ALONG):
        sums.append(sum_step(sums[-1], bit))

    def send(keep, got):
        chips = [added(keep[i], got[i]) for i in range(SHARDS // 2)]
        return chips, [swap(part, bit) for bit, part in zip(PLANE, chips[1:])]

    def total_rows(chips, moved):
        return sum((wide(part) for part in moved), wide(chips[0]))

    def terms(group, *others):
        here = after(slab_order, *others) if others else slab_order
        keep, away = slab_terms(group, here, d_pair, weights, lower_slabs)
        return keep, swap(away, CORE)

    keep_a, got_a = terms((3, 2), sums[1])
    keep_b, got_b = terms((1,), sums[2])
    chips_a, moved_a = send(keep_a, after(got_a, keep_b))
    keep_c, got_c = terms((0,), sums[3], *chips_a)
    rows_a = total_rows(chips_a, after(moved_a, keep_c))
    chips_b, moved_b = send(keep_b, after(got_b, keep_c))
    kept_parts = [(kept[3], grad[2], grad[0], kept[2]) for kept, grad in zip(saved, grads)]
    (low_first, *rest), *others = kept_parts
    kept_parts = [(after(low_first, rows_a, *chips_b), *rest), *others]
    owned, owned_down = owned_gradients(kept_parts, 200 * 1024 * SHARDS * tokens_each * 2 * rank * 4)
    got_c, moved_b = after((got_c, moved_b), owned_down)
    chips_c, moved_c = send(keep_c, got_c)

    x, dy = Rows(range(SHARDS)), Rows(range(SHARDS))
    for whole, halves in ((x, (x_main, x_away)), (dy, (dy_main, dy_away))):
        for rows in halves:
            whole.arrays += rows.arrays
            whole.places += rows.places
    rows_b = total_rows(chips_b, moved_b)
    hops = [(rows_a[1], 2), (rows_a[0], 3), (rows_b[0], 1)]
    hops = [over_experts(rows.astype(jnp.bfloat16), r) for rows, r in hops]
    total = after(sums[3].reshape(SHARDS, 3 * rank, tokens_each), rows_b, hops[0], *chips_c)
    grad_pair, grad_down = shared_gradients(
        x,
        dy,
        order,
        slab_order,
        total[:, : 2 * rank],
        total[:, 2 * rank :] * route_blocks,
    )
    rows_c = total_rows(chips_c, after(moved_c, grad_pair))
    grad_x = sum((wide(part) for part in hops), rows_c[0])
    grad_x = grad_x.astype(jnp.bfloat16)
    return (
        grad_x,
        grad_pair[None, :rank],
        owned[0].T[None],
        grad_pair[None, rank:],
        owned[1].T[None],
        owned_down[None],
        grad_down.T[None],
    )


def plan(tokens, *others):
    experts, tokens_each, hidden_here = lax.axis_size("expert"), tokens.shape[0], others[3].shape[1]
    planned = (
        lax.axis_size("dp") == SHARDS
        and experts == 4
        and hidden_here % LANES == 0
        and tokens_each % LANES == 0
        and tokens.shape[1] % TILE == 0
    )
    return (local if planned else general_local)(tokens, *others)


def solution(mesh):
    return jax.shard_map(
        plan,
        mesh=mesh,
        in_specs=(
            P("dp", "expert"),
            P("dp", "expert"),
            P("dp", None),
            P("dp", None),
            P("expert", "dp", None),
            P("expert", "dp", None),
            P("expert", "dp", None),
            P("expert", None, None),
            P("expert", "dp", None),
            P("expert", None, None),
            P("expert", "dp", None),
            P("expert", None, "dp"),
            P("expert", None, None),
        ),
        out_specs=(
            P("dp", "expert"),
            P("expert", None, None),
            P("expert", "dp", None),
            P("expert", None, None),
            P("expert", "dp", None),
            P("expert", None, "dp"),
            P("expert", None, None),
        ),
        check_vma=False,
    )
```

```python
import jax
import jax.numpy as jnp
from jax import lax
from jax.experimental import pallas as pl
from jax.experimental.pallas import tpu as pltpu
from jax.sharding import PartitionSpec as P

ADAPTER_SCALE = 2.0


def contract_pair(left, right, left_axis, right_axis):
    return lax.dot_general(
        left, right, (((left_axis,), (right_axis,)), ((), ())), preferred_element_type=jnp.float32
    )


def slot_numbers(route_rows, experts):
    picked = (route_rows[:, :, None] == jnp.arange(experts, dtype=jnp.int32)[None, None, :]).astype(
        jnp.int32
    )
    per_token = jnp.sum(picked, axis=1)
    earlier = jnp.cumsum(per_token, axis=0) - per_token
    return jnp.sum(earlier[:, None, :] * picked, axis=2)


def slot_sources(route_rows, positions, experts, capacity):
    tokens_here, choose = route_rows.shape
    target = (route_rows * capacity + positions).reshape(-1)
    owners = jnp.repeat(jnp.arange(tokens_here, dtype=jnp.int32), choose)
    member_ids = jnp.tile(jnp.arange(choose, dtype=jnp.int32), tokens_here)
    source = jnp.full((experts * capacity,), tokens_here, jnp.int32).at[target].set(owners)
    member = jnp.zeros((experts * capacity,), jnp.int32).at[target].set(member_ids)
    return (source, member)


def rows_backward_pass(input_rows, output_gradient_rows, params):
    (
        gate_weight,
        up_weight,
        down_weight,
        a_gate,
        gate_adapter_upper,
        a_up,
        up_adapter_upper,
        down_adapter_lower,
        b_down,
    ) = params
    gate_projected_lower = contract_pair(a_gate, input_rows, 1, 1).astype(jnp.bfloat16)
    up_projected_lower = contract_pair(a_up, input_rows, 1, 1).astype(jnp.bfloat16)
    gate_preactivation = contract_pair(
        gate_weight, input_rows, 1, 1
    ) + ADAPTER_SCALE * contract_pair(gate_adapter_upper, gate_projected_lower, 1, 0)
    up_preactivation = contract_pair(up_weight, input_rows, 1, 1) + ADAPTER_SCALE * contract_pair(
        up_adapter_upper, up_projected_lower, 1, 0
    )
    sigmoid_gate = jax.nn.sigmoid(gate_preactivation)
    silu_gate = gate_preactivation * sigmoid_gate
    hidden_units = (silu_gate * up_preactivation).astype(jnp.bfloat16)
    down_projected_lower = contract_pair(b_down, output_gradient_rows, 0, 1).astype(jnp.bfloat16)
    hidden_gradient = contract_pair(
        down_weight, output_gradient_rows, 1, 1
    ) + ADAPTER_SCALE * contract_pair(down_adapter_lower, down_projected_lower, 0, 0)
    gate_gradient = (
        hidden_gradient
        * up_preactivation
        * sigmoid_gate
        * (1.0 + gate_preactivation * (1.0 - sigmoid_gate))
    ).astype(jnp.bfloat16)
    up_gradient = (hidden_gradient * silu_gate).astype(jnp.bfloat16)
    gate_partial = contract_pair(gate_adapter_upper, gate_gradient, 0, 0).astype(jnp.bfloat16)
    up_partial = contract_pair(up_adapter_upper, up_gradient, 0, 0).astype(jnp.bfloat16)
    down_partial = contract_pair(down_adapter_lower, hidden_units, 1, 0).astype(jnp.bfloat16)
    paired_partials = jnp.concatenate([gate_partial, up_partial], 0)
    paired_factors = jnp.concatenate([a_gate, a_up], 0)
    gradient_rows_out = (
        contract_pair(gate_gradient, gate_weight, 0, 0)
        + contract_pair(up_gradient, up_weight, 0, 0)
        + ADAPTER_SCALE * contract_pair(paired_partials, paired_factors, 0, 0)
    )
    shared_slice = (
        ADAPTER_SCALE * contract_pair(gate_partial, input_rows, 1, 0),
        ADAPTER_SCALE * contract_pair(up_partial, input_rows, 1, 0),
        ADAPTER_SCALE * contract_pair(output_gradient_rows, down_partial, 0, 1),
    )
    owned_slice = (
        ADAPTER_SCALE * contract_pair(gate_gradient, gate_projected_lower, 1, 1),
        ADAPTER_SCALE * contract_pair(up_gradient, up_projected_lower, 1, 1),
        ADAPTER_SCALE * contract_pair(down_projected_lower, hidden_units, 1, 1),
    )
    return (gradient_rows_out, shared_slice, owned_slice)


def general_local(
    tokens,
    output_gradient,
    routing,
    router_gate_values,
    gate_weight,
    up_weight,
    down_weight,
    adapter_lower_gate,
    adapter_upper_gate,
    adapter_lower_up,
    adapter_upper_up,
    adapter_lower_down,
    adapter_upper_down,
):
    experts = lax.axis_size("expert")
    shards = lax.axis_size("dp")
    tok_local, feat_local = tokens.shape
    choose = routing.shape[1]
    complete_width = feat_local * experts
    capacity = min(tok_local, 6 * tok_local // experts)
    hidden_units_local = gate_weight.shape[1]
    adapter_rank = adapter_lower_gate.shape[1]
    params = (
        gate_weight[0],
        up_weight[0],
        down_weight[0],
        adapter_lower_gate[0],
        adapter_upper_gate[0],
        adapter_lower_up[0],
        adapter_upper_up[0],
        adapter_lower_down[0],
        adapter_upper_down[0],
    )
    positions = slot_numbers(routing, experts)
    zero_row = jnp.zeros((1, feat_local), jnp.bfloat16)
    initial = (
        jnp.zeros((shards * capacity, complete_width), jnp.float32),
        (
            jnp.zeros((adapter_rank, complete_width), jnp.float32),
            jnp.zeros((adapter_rank, complete_width), jnp.float32),
            jnp.zeros((complete_width, adapter_rank), jnp.float32),
        ),
        (
            jnp.zeros((hidden_units_local, adapter_rank), jnp.float32),
            jnp.zeros((hidden_units_local, adapter_rank), jnp.float32),
            jnp.zeros((adapter_rank, hidden_units_local), jnp.float32),
        ),
    )
    source, member = slot_sources(routing, positions, experts, capacity)
    clamped = jnp.minimum(source, tok_local - 1)
    slot_gate = jnp.where(
        source < tok_local, router_gate_values.reshape(-1)[clamped * choose + member], 0.0
    )
    send_x = jnp.concatenate([tokens, zero_row], 0)[source].reshape(experts, capacity, feat_local)
    send_dy = (
        (
            slot_gate[:, None]
            * jnp.concatenate([output_gradient, zero_row], 0)[source].astype(jnp.float32)
        )
        .astype(jnp.bfloat16)
        .reshape(experts, capacity, feat_local)
    )
    recv_x, recv_dy = (
        lax.all_to_all(send_x, "expert", split_axis=0, concat_axis=2, tiled=True),
        lax.all_to_all(send_dy, "expert", split_axis=0, concat_axis=2, tiled=True),
    )
    gradient_rows_out, shared_slice, owned_slice = rows_backward_pass(
        lax.all_gather(recv_x[0], "dp", axis=0, tiled=True),
        lax.all_gather(recv_dy[0], "dp", axis=0, tiled=True),
        params,
    )
    rows_part = gradient_rows_out
    totals = (
        rows_part,
        jax.tree.map(jnp.add, initial[1], shared_slice),
        jax.tree.map(jnp.add, initial[2], owned_slice),
    )
    rows_part, shared_slice, owned_slice = totals
    summed = lax.psum_scatter(
        rows_part.astype(jnp.bfloat16), "dp", scatter_dimension=0, tiled=True
    ).astype(jnp.float32)
    returned_rows = lax.all_to_all(
        summed.reshape(capacity, experts, feat_local).astype(jnp.bfloat16),
        "expert",
        split_axis=1,
        concat_axis=1,
        tiled=True,
    ).astype(jnp.float32)
    lookup = positions * experts + routing
    grad_x = jnp.sum(returned_rows.reshape(capacity * experts, feat_local)[lookup], axis=1).astype(
        jnp.bfloat16
    )
    grad_a_gate, grad_a_up, grad_b_down = (
        lax.psum(shared_slice[0].astype(jnp.bfloat16), "dp").astype(jnp.float32),
        lax.psum(shared_slice[1].astype(jnp.bfloat16), "dp").astype(jnp.float32),
        lax.psum(shared_slice[2].astype(jnp.bfloat16), "dp").astype(jnp.float32),
    )
    return (
        grad_x,
        grad_a_gate[None],
        owned_slice[0][None],
        grad_a_up[None],
        owned_slice[1][None],
        owned_slice[2][None],
        grad_b_down[None],
    )


LANES = 128
TILE = 512
SHARDS = 8
VMEM_BYTES = 58 * 1024 * 1024
HIDDEN_BYTES = 58 * 1024 * 1024
TERM_BYTES = 58 * 1024 * 1024
HBM = pl.BlockSpec(memory_space=pl.ANY)
PINNED = pl.BlockSpec(memory_space=pltpu.HBM)
VMEM = pl.BlockSpec(memory_space=pltpu.VMEM)
SMEM = pl.BlockSpec(memory_space=pltpu.SMEM)


def dot_nt(left, right):
    return contract_pair(left, right, 1, 1)


def dot_nn(left, right):
    return contract_pair(left, right, 1, 0)


def wide(value):
    return value.astype(jnp.float32)


class Rows:
    def __init__(self, blocks):
        self.arrays, self.places, self.blocks = [], [], blocks

    def add(self, array, *places):
        self.arrays.append(array)
        self.places.append(places)


def row_copies(refs, places, target, sems, slab, first=0, order=None):
    tokens_each = refs[0].shape[-2]
    copies = []
    for ref, parts in zip(refs, places):
        for i, (at, block) in enumerate(parts):
            if at != slab:
                continue
            source = ref.at[i] if len(ref.shape) == 3 else ref
            row = (block - first) * tokens_each
            if order is not None:
                row = pl.multiple_of(order[block] * tokens_each, tokens_each)
            copies.append(
                pltpu.make_async_copy(
                    source, target.at[slab, pl.ds(row, tokens_each)], sems.at[slab, block]
                )
            )
    return copies


def slab_lanes(slab_ref, slab, feat):
    return pl.ds(pl.multiple_of(slab_ref[slab] * feat, feat), feat)


def forward_kernel(places, first, *refs):
    n_pieces = len(places)
    pieces = refs[:n_pieces]
    (
        slab_ref,
        gate_hbm,
        up_hbm,
        lower_hbm,
        gate_upper_ref,
        up_upper_ref,
        silu_out,
        slope_out,
        hidden_out,
        low_out,
    ) = refs[n_pieces : n_pieces + 10]
    x_rows, weights, pre, saved, x_sems, w_sems, out_sems = refs[n_pieces + 10 :]
    slabs, _, feat = x_rows.shape
    hidden_here = gate_hbm.shape[0]
    pair, rank = lower_hbm.shape[1], gate_upper_ref.shape[1]

    def x_slab(slab):
        return row_copies(pieces, places, x_rows, x_sems, slab, first)

    def weight_copies(slab):
        lanes = slab_lanes(slab_ref, slab, feat)
        sides = (
            (gate_hbm.at[:, lanes], 0, hidden_here),
            (up_hbm.at[:, lanes], hidden_here, hidden_here),
            (lower_hbm.at[slab], 2 * hidden_here, pair),
        )
        return [
            pltpu.make_async_copy(
                source, weights.at[slab, pl.ds(start, size)], w_sems.at[slab, i]
            )
            for i, (source, start, size) in enumerate(sides)
        ]

    for slab in range(slabs):
        for copy in x_slab(slab) + weight_copies(slab):
            copy.start()
    for slab in range(slabs):
        for copy in x_slab(slab) + weight_copies(slab):
            copy.wait()
        if slab == 0:
            pre[...] = dot_nt(weights[0], x_rows[0])
        else:
            pre[...] += dot_nt(weights[slab], x_rows[slab])
    low_out[...] = pre[2 * hidden_here :, :].astype(jnp.bfloat16)

    def out_copies(tile):
        at = pl.ds(pl.multiple_of(tile * LANES, LANES), LANES)
        return [
            pltpu.make_async_copy(saved.at[i, at], out.at[at], out_sems.at[i, tile])
            for i, out in enumerate((silu_out, slope_out, hidden_out))
        ]

    tiles = hidden_here // LANES

    @pl.loop(0, tiles)
    def _(tile):
        start = pl.multiple_of(tile * LANES, LANES)
        at = pl.ds(start, LANES)
        up_at = pl.ds(pl.multiple_of(hidden_here + start, LANES), LANES)
        pre_gate = pre[at, :] + ADAPTER_SCALE * dot_nn(gate_upper_ref[at, :], low_out[:rank, :])
        pre_up = pre[up_at, :] + ADAPTER_SCALE * dot_nn(up_upper_ref[at, :], low_out[rank:, :])
        sigma = 1.0 / (1.0 + jnp.exp(-pre_gate))
        silu = pre_gate * sigma
        saved[0, at, :] = silu.astype(jnp.bfloat16)
        saved[1, at, :] = (pre_up * (sigma * (1.0 + pre_gate * (1.0 - sigma)))).astype(
            jnp.bfloat16
        )
        saved[2, at, :] = (silu * pre_up).astype(jnp.bfloat16)
        for copy in out_copies(tile):
            copy.start()

    @pl.loop(0, tiles)
    def _(tile):
        for copy in out_copies(tile):
            copy.wait()


def forward_rows(x, slab_order, weights, lower_slabs, gate_upper, up_upper):
    hidden_here, width = weights[0].shape
    tokens_each, feat = x.arrays[0].shape[-2:]
    rows = len(x.blocks) * tokens_each
    slabs, pair, _ = lower_slabs.shape
    kept = jax.ShapeDtypeStruct((hidden_here, rows), jnp.bfloat16)
    return pl.pallas_call(
        lambda *refs: forward_kernel(x.places, x.blocks[0], *refs),
        out_shape=(kept, kept, kept, jax.ShapeDtypeStruct((pair, rows), jnp.bfloat16)),
        in_specs=[HBM] * len(x.arrays) + [SMEM] + [HBM] * 3 + [VMEM] * 2,
        out_specs=(HBM, HBM, HBM, VMEM),
        scratch_shapes=[
            pltpu.VMEM((slabs, rows, feat), jnp.bfloat16),
            pltpu.VMEM((slabs, 2 * hidden_here + pair, feat), jnp.bfloat16),
            pltpu.VMEM((2 * hidden_here + pair, rows), jnp.float32),
            pltpu.VMEM((3, hidden_here, rows), jnp.bfloat16),
            pltpu.SemaphoreType.DMA((slabs, SHARDS)),
            pltpu.SemaphoreType.DMA((slabs, 3)),
            pltpu.SemaphoreType.DMA((3, hidden_here // LANES)),
        ],
        compiler_params=pltpu.CompilerParams(vmem_limit_bytes=VMEM_BYTES),
        cost_estimate=pl.CostEstimate(
            flops=rows * hidden_here * width // 4,
            bytes_accessed=2 * rows * width,
            transcendentals=rows * hidden_here,
        ),
        name="forward_rows",
    )(*x.arrays, slab_order, *weights[:2], lower_slabs, gate_upper, up_upper)


def hidden_kernel(places, first, *refs):
    n_pieces = len(places)
    pieces = refs[:n_pieces]
    (
        slab_ref,
        route_ref,
        down_hbm,
        down_upper_hbm,
        down_lower_ref,
        down_lower_t_ref,
        gate_upper_ref,
        up_upper_ref,
        silu_hbm,
        slope_hbm,
        hidden_hbm,
        d_pair,
        parts_out,
        low_down,
        rows,
        down_w,
        d_down,
        silu,
        slope,
        hidden,
        row_sems,
        d_sems,
        f_sems,
    ) = refs[n_pieces:]
    slabs, _, feat = rows.shape
    hidden_here = silu.shape[0]
    rank = down_lower_ref.shape[0]
    saved_copies = [
        pltpu.make_async_copy(source, target, f_sems.at[i])
        for i, (source, target) in enumerate(
            ((silu_hbm, silu), (slope_hbm, slope), (hidden_hbm, hidden))
        )
    ]

    def slab_copies(slab):
        return row_copies(pieces, places, rows, row_sems, slab, first) + [
            pltpu.make_async_copy(
                down_hbm.at[:, slab_lanes(slab_ref, slab, feat)],
                down_w.at[slab, pl.ds(0, hidden_here)],
                d_sems.at[slab, 0],
            ),
            pltpu.make_async_copy(
                down_upper_hbm.at[slab], down_w.at[slab, pl.ds(hidden_here, rank)], d_sems.at[slab, 1]
            ),
        ]

    for slab in range(slabs):
        for copy in slab_copies(slab):
            copy.start()
    for copy in saved_copies:
        copy.start()
    for slab in range(slabs):
        for copy in slab_copies(slab):
            copy.wait()
        if slab == 0:
            d_down[...] = dot_nt(down_w[0], rows[0])
        else:
            d_down[...] += dot_nt(down_w[slab], rows[slab])

    low_down[...] = (d_down[hidden_here:, :] * route_ref[...]).astype(jnp.bfloat16)
    for copy in saved_copies:
        copy.wait()

    @pl.loop(0, hidden_here // LANES)
    def _(tile):
        start = pl.multiple_of(tile * LANES, LANES)
        at = pl.ds(start, LANES)
        up_at = pl.ds(pl.multiple_of(hidden_here + start, LANES), LANES)
        d_hidden = d_down[at, :] * route_ref[...]
        d_hidden = d_hidden + ADAPTER_SCALE * dot_nn(down_lower_t_ref[at, :], low_down[...])
        d_gate = (d_hidden * wide(slope[at, :])).astype(jnp.bfloat16)
        d_up = (d_hidden * wide(silu[at, :])).astype(jnp.bfloat16)
        d_pair[:, at] = d_gate.T
        d_pair[:, up_at] = d_up.T

    for side, factor in enumerate((gate_upper_ref, up_upper_ref)):
        start = side * hidden_here
        part = dot_nn(d_pair[:, start : start + hidden_here], factor[...])
        parts_out[side * rank : (side + 1) * rank, :] = part.T
        at = 2 * hidden_here + side * rank
        d_pair[:, at : at + rank] = ADAPTER_SCALE * part.astype(jnp.bfloat16)
    parts_out[2 * rank :, :] = dot_nn(down_lower_ref[...], hidden[...])


def hidden_gradients(dy, slab_order, route_row, down_weight, down_upper, factors, saved):
    hidden_here, width = down_weight.shape
    slabs, rank, feat = down_upper.shape
    pair = 2 * rank
    rows = route_row.shape[1]
    return pl.pallas_call(
        lambda *refs: hidden_kernel(dy.places, dy.blocks[0], *refs),
        out_shape=(
            jax.ShapeDtypeStruct((rows, 2 * hidden_here + pair), jnp.bfloat16),
            jax.ShapeDtypeStruct((3 * rank, rows), jnp.float32),
            jax.ShapeDtypeStruct((rank, rows), jnp.bfloat16),
        ),
        in_specs=[HBM] * len(dy.arrays) + [SMEM, VMEM] + [HBM] * 2 + [VMEM] * 4 + [HBM] * 3,
        out_specs=(VMEM,) * 3,
        scratch_shapes=[
            pltpu.VMEM((slabs, rows, feat), jnp.bfloat16),
            pltpu.VMEM((slabs, hidden_here + rank, feat), jnp.bfloat16),
            pltpu.VMEM((hidden_here + rank, rows), jnp.float32),
            pltpu.VMEM((hidden_here, rows), jnp.bfloat16),
            pltpu.VMEM((hidden_here, rows), jnp.bfloat16),
            pltpu.VMEM((hidden_here, rows), jnp.bfloat16),
            pltpu.SemaphoreType.DMA((slabs, SHARDS)),
            pltpu.SemaphoreType.DMA((slabs, 2)),
            pltpu.SemaphoreType.DMA((3,)),
        ],
        compiler_params=pltpu.CompilerParams(vmem_limit_bytes=HIDDEN_BYTES),
        cost_estimate=pl.CostEstimate(
            flops=4 * rows * hidden_here * width,
            bytes_accessed=2 * hidden_here * width + 2 * rows * width,
            transcendentals=0,
        ),
        name="hidden_gradients",
    )(*dy.arrays, slab_order, route_row, down_weight, down_upper, *factors, *saved)


def term_kernel(slabs, n_parts, *refs):
    d_parts = refs[:n_parts]
    slab_ref, gate_hbm, up_hbm, lower_hbm = refs[n_parts : n_parts + 4]
    outs, (d_pair, pair_w, sems, d_sems) = refs[n_parts + 4 : -4], refs[-4:]
    _, depth, step = pair_w.shape
    hidden_here = gate_hbm.shape[0]
    pair = depth - 2 * hidden_here
    tokens_each, feat = outs[0].shape[2:]
    steps = feat // step

    def weight_copies(i, n):
        slab, k = slabs[i], i * steps + n
        lanes = pl.ds(pl.multiple_of(slab_ref[slab] * feat + n * step, step), step)
        sides = (
            (gate_hbm.at[:, lanes], 0, hidden_here),
            (up_hbm.at[:, lanes], hidden_here, hidden_here),
            (lower_hbm.at[slab, :, pl.ds(pl.multiple_of(n * step, step), step)], 2 * hidden_here, pair),
        )
        return [
            pltpu.make_async_copy(source, pair_w.at[k, pl.ds(start, size)], sems.at[k, side])
            for side, (source, start, size) in enumerate(sides)
        ]

    d_copies, row = [], 0
    for i, part in enumerate(d_parts):
        count = part.shape[0]
        d_copies.append(pltpu.make_async_copy(part, d_pair.at[pl.ds(row, count)], d_sems.at[i]))
        row += count
    for copy in d_copies:
        copy.start()
    for i in range(len(slabs)):
        for n in range(steps):
            for copy in weight_copies(i, n):
                copy.start()
    for copy in d_copies:
        copy.wait()
    for i in range(len(slabs)):

        @pl.loop(0, steps)
        def _(n):
            for copy in weight_copies(i, n):
                copy.wait()
            lanes = pl.ds(pl.multiple_of(n * step, step), step)
            term = dot_nn(d_pair[...], pair_w[i * steps + n]).astype(jnp.bfloat16)
            for block in range(SHARDS):
                at = slice(block * tokens_each, (block + 1) * tokens_each)
                outs[block % 2][block // 2, i, :, lanes] = term[at]


def slab_terms(slabs, slab_order, d_pair, weights, lower_slabs):
    rows, depth = sum(part.shape[0] for part in d_pair), d_pair[0].shape[1]
    feat = lower_slabs.shape[2]
    parts = len(slabs) * feat // TILE
    term = jax.ShapeDtypeStruct((SHARDS // 2, len(slabs), rows // SHARDS, feat), jnp.bfloat16)
    return pl.pallas_call(
        lambda *refs: term_kernel(slabs, len(d_pair), *refs),
        out_shape=(term, term),
        in_specs=[HBM] * len(d_pair) + [SMEM] + [HBM] * 3,
        out_specs=(VMEM, VMEM),
        scratch_shapes=[
            pltpu.VMEM((rows, depth), jnp.bfloat16),
            pltpu.VMEM((parts, depth, TILE), jnp.bfloat16),
            pltpu.SemaphoreType.DMA((parts, 3)),
            pltpu.SemaphoreType.DMA((len(d_pair),)),
        ],
        compiler_params=pltpu.CompilerParams(vmem_limit_bytes=TERM_BYTES),
        cost_estimate=pl.CostEstimate(
            flops=12 * rows * depth * feat * len(slabs),
            bytes_accessed=2 * depth * feat * len(slabs) + 4 * rows * depth,
            transcendentals=0,
        ),
        name="slab_terms",
    )(*d_pair, slab_order, *weights[:2], lower_slabs)


def owned_kernel(n_parts, *refs):
    parts = [refs[4 * i : 4 * i + 4] for i in range(n_parts)]
    owned_out, owned_down_out = refs[4 * n_parts :]
    rank, hidden_here = owned_down_out.shape
    gate_sum = up_sum = down_sum = 0.0
    for low, low_down, d_pair, hidden in parts:
        gate_sum += dot_nn(low[:rank, :], d_pair[:, :hidden_here])
        up_sum += dot_nn(low[rank:, :], d_pair[:, hidden_here : 2 * hidden_here])
        down_sum += dot_nt(low_down[...], hidden[...])
    owned_out[0] = ADAPTER_SCALE * gate_sum
    owned_out[1] = ADAPTER_SCALE * up_sum
    owned_down_out[...] = ADAPTER_SCALE * down_sum


def owned_gradients(parts, hint):
    rank, hidden_here = parts[0][1].shape[0], parts[0][3].shape[0]
    return pl.pallas_call(
        lambda *refs: owned_kernel(len(parts), *refs),
        out_shape=(
            jax.ShapeDtypeStruct((2, rank, hidden_here), jnp.float32),
            jax.ShapeDtypeStruct((rank, hidden_here), jnp.float32),
        ),
        in_specs=[VMEM] * (4 * len(parts)),
        out_specs=(VMEM, VMEM),
        compiler_params=pltpu.CompilerParams(vmem_limit_bytes=VMEM_BYTES),
        cost_estimate=pl.CostEstimate(flops=hint, bytes_accessed=8_000_000, transcendentals=0),
        name="owned_gradients",
    )(*(value for part in parts for value in part))


def shared_kernel(x_places, dy_places, *refs):
    split, inputs = len(x_places), len(x_places) + len(dy_places)
    x_pieces, dy_pieces = refs[:split], refs[split:inputs]
    order_ref, slab_ref, sums_ref, down_sums_ref, pair_out, down_out = refs[inputs : inputs + 6]
    x_rows, dy_rows, sums, down_sums, x_sems, dy_sems = refs[inputs + 6 :]
    slabs, _, feat = x_rows.shape
    tokens_each = x_pieces[0].shape[-2]

    def slab_copies(slab):
        return row_copies(
            x_pieces, x_places, x_rows, x_sems, slab, 0, order_ref
        ) + row_copies(dy_pieces, dy_places, dy_rows, dy_sems, slab, 0, order_ref)

    for slab in range(slabs):
        for copy in slab_copies(slab):
            copy.start()
    for block in range(SHARDS):
        lanes = pl.ds(pl.multiple_of(order_ref[block] * tokens_each, tokens_each), tokens_each)
        sums[:, lanes] = sums_ref[block]
        down_sums[:, lanes] = down_sums_ref[block]
    for slab in range(slabs):
        for copy in slab_copies(slab):
            copy.wait()

        @pl.loop(0, feat // TILE)
        def _(n):
            lanes = pl.ds(pl.multiple_of(n * TILE, TILE), TILE)
            out = pl.ds(pl.multiple_of(slab_ref[slab] * feat + n * TILE, TILE), TILE)
            pair_out[:, out] = ADAPTER_SCALE * dot_nn(
                sums[...].astype(jnp.bfloat16), x_rows[slab, :, lanes]
            )
            down_out[:, out] = ADAPTER_SCALE * dot_nn(
                down_sums[...].astype(jnp.bfloat16), dy_rows[slab, :, lanes]
            )


def shared_gradients(x, dy, order, slab_order, sums, down_sums):
    tokens_each, feat = x.arrays[0].shape[-2:]
    slabs = slab_order.shape[0]
    rows = SHARDS * tokens_each
    pair, rank = sums.shape[1], down_sums.shape[1]
    return pl.pallas_call(
        lambda *refs: shared_kernel(x.places, dy.places, *refs),
        out_shape=(
            jax.ShapeDtypeStruct((pair, slabs * feat), jnp.float32),
            jax.ShapeDtypeStruct((rank, slabs * feat), jnp.float32),
        ),
        in_specs=[HBM] * (len(x.arrays) + len(dy.arrays)) + [SMEM, SMEM, VMEM, VMEM],
        out_specs=(VMEM, VMEM),
        scratch_shapes=[
            pltpu.VMEM((slabs, rows, feat), jnp.bfloat16),
            pltpu.VMEM((slabs, rows, feat), jnp.bfloat16),
            pltpu.VMEM((pair, rows), jnp.float32),
            pltpu.VMEM((rank, rows), jnp.float32),
            pltpu.SemaphoreType.DMA((slabs, SHARDS)),
            pltpu.SemaphoreType.DMA((slabs, SHARDS)),
        ],
        compiler_params=pltpu.CompilerParams(vmem_limit_bytes=VMEM_BYTES),
        cost_estimate=pl.CostEstimate(
            flops=16 * rows * pair * slabs * feat,
            bytes_accessed=4 * rows * slabs * feat,
            transcendentals=0,
        ),
        name="shared_gradients",
    )(*x.arrays, *dy.arrays, order, slab_order, sums, down_sums)


CORE, ACROSS, ALONG = 1, 2, 4
PLANE = (ACROSS, ALONG, ACROSS | ALONG)


def swap(value, bit, axis="dp"):
    return lax.ppermute(value, axis, [(i, i ^ bit) for i in range(lax.axis_size(axis))])


def after(value, *others):
    return lax.optimization_barrier((value, others))[0]


def added(left, right):
    return (wide(left) + wide(right)).astype(jnp.bfloat16)


def local(
    tokens,
    output_gradient,
    routing,
    router_gate_values,
    gate_weight,
    up_weight,
    down_weight,
    adapter_lower_gate,
    adapter_upper_gate,
    adapter_lower_up,
    adapter_upper_up,
    adapter_lower_down,
    adapter_upper_down,
):
    experts = lax.axis_size("expert")
    me, expert = lax.axis_index("dp"), lax.axis_index("expert")
    tokens_each, feat = tokens.shape
    rank = adapter_lower_gate.shape[1]
    order = jnp.bitwise_xor(jnp.arange(SHARDS, dtype=jnp.int32), me.astype(jnp.int32))
    slab_order = jnp.bitwise_xor(jnp.arange(experts, dtype=jnp.int32), expert.astype(jnp.int32))

    named = routing[:, :, None] == jnp.arange(experts, dtype=jnp.int32)[None, None, :]
    weight_of = jnp.sum(jnp.where(named, router_gate_values[:, :, None], 0.0), axis=1)
    routes = lax.all_gather(weight_of.T, "dp", axis=0, tiled=False)
    route = lax.dynamic_index_in_dim(routes, expert, axis=1, keepdims=False)[order]
    route_blocks = route[:, None, :]
    route_row = route.reshape(1, SHARDS * tokens_each)

    def slabs_first(factor):
        return factor.reshape(factor.shape[0], experts, feat).transpose(1, 0, 2)[slab_order]

    lower_cat = jnp.concatenate([adapter_lower_gate[0], adapter_lower_up[0]], axis=0)
    down_lower = adapter_lower_down[0]

    def place_both(rows, part, swapped, chip, slabs):
        rows.add(part, *((r, 2 * chip) for r in slabs))
        rows.add(swapped, *((r, 2 * chip + 1) for r in slabs))

    def over_experts(block, r):
        return swap(block, r, "expert")

    both = over_experts(jnp.stack([tokens, output_gradient]), 1)
    x_slabs = [both[0]] + [over_experts(tokens, r) for r in range(2, experts)]
    x_near = [tokens] + [swap(tokens, bit) for bit in PLANE[:2]]
    uppers = (adapter_upper_gate[0], adapter_upper_up[0])
    (x_slabs, x_near, dy_near), small = lax.optimization_barrier(
        ((x_slabs, x_near, both[1]), (route_row, adapter_upper_down[0], lower_cat, uppers))
    )
    route_row, down_upper, lower_cat, uppers = small
    lower_slabs, down_upper = slabs_first(lower_cat), slabs_first(down_upper.T)
    ready = (lower_slabs, down_upper, down_lower, down_lower.T, *uppers)

    x_rest = [jnp.stack(x_slabs)]
    x_rest += [swap(x_rest[0], bit) for bit in PLANE[:2]]
    x_near.append(swap(x_near[2], ACROSS))
    dy_late = after(output_gradient, x_rest[0])
    dy_slabs = [output_gradient, dy_near] + [over_experts(dy_late, r) for r in range(2, experts)]

    (x_rest, x_near, dy_slabs), ready = lax.optimization_barrier(
        ((x_rest, x_near, dy_slabs), ready)
    )
    lower_slabs, down_upper, *factors = ready
    uppers = factors[2:]
    half = experts // 2
    x_far = [swap(x_rest[2][: half - 1], ACROSS), swap(x_rest[1][half - 1 :], ALONG)]
    x_near_swapped = swap(jnp.stack(x_near[:2]), CORE)
    x_rest_swapped = [swap(part, CORE) for part in x_rest[:2]]
    dy_all = after(jnp.stack(dy_slabs), x_near_swapped, *x_rest_swapped)
    dy_plane = [swap(dy_all, bit) for bit in PLANE[:2]]

    x_main = Rows(range(4))
    x_main.add(x_near[0], (0, 0))
    x_main.add(x_near[1], (0, 2))
    x_main.add(x_near_swapped, (0, 1), (0, 3))
    for chip in range(2):
        place_both(x_main, x_rest[chip], x_rest_swapped[chip], chip, range(1, experts))

    weights = (gate_weight[0], up_weight[0], down_weight[0])
    saved = [forward_rows(x_main, slab_order, weights, lower_slabs, *uppers)]

    x_far, x_late = after((x_far, (x_near[2:], x_rest[2])), saved[0][0])
    x_pair = jnp.stack(x_late[0])
    x_far = jnp.concatenate(x_far, axis=0)
    x_away = Rows(range(4, SHARDS))
    x_away.add(x_pair, (0, 4), (0, 6))
    x_away.add(swap(x_pair, CORE), (0, 5), (0, 7))
    place_both(x_away, x_late[1], swap(x_late[1], CORE), 2, range(1, experts))
    place_both(x_away, x_far, swap(x_far, CORE), 3, range(1, experts))

    saved.append(forward_rows(x_away, slab_order, weights, lower_slabs, *uppers))

    dy_plane = after(dy_plane, saved[1][0])
    dy_far = [swap(dy_plane[1][:half], ACROSS), swap(dy_plane[0][half:], ALONG)]

    dy_main, dy_away = Rows(range(4)), Rows(range(4, SHARDS))
    for chip, part in enumerate((dy_all, dy_plane[0])):
        place_both(dy_main, part, swap(part, CORE), chip, range(experts))
    split = 4 * tokens_each
    route_halves = (route_row[:, :split], route_row[:, split:])

    def hidden_part(rows, i):
        return hidden_gradients(
            rows, slab_order, route_halves[i], weights[2], down_upper, factors, saved[i][:3]
        )

    grads = [hidden_part(dy_main, 0)]
    place_both(dy_away, dy_plane[1], swap(dy_plane[1], CORE), 2, range(experts))
    for part, slabs in zip(after(dy_far, grads[0][0]), (range(half), range(half, experts))):
        place_both(dy_away, part, swap(part, CORE), 3, slabs)
    grads.append(hidden_part(dy_away, 1))
    d_pair = [grad[0] for grad in grads]
    parts = jnp.concatenate([grad[1] for grad in grads], axis=1)

    def sum_step(total, bit):
        other = swap(total.reshape(SHARDS, 3 * rank, tokens_each), bit)
        shape = (SHARDS // (2 * bit), 2, bit, 3 * rank, tokens_each)
        return total.reshape(shape) + other.reshape(shape)[:, ::-1]

    sums = [parts.reshape(3 * rank, SHARDS, tokens_each).transpose(1, 0, 2)]
    for bit in (CORE, ACROSS, ALONG):
        sums.append(sum_step(sums[-1], bit))

    def send(keep, got):
        chips = [added(keep[i], got[i]) for i in range(SHARDS // 2)]
        return chips, [swap(part, bit) for bit, part in zip(PLANE, chips[1:])]

    def total_rows(chips, moved):
        return sum((wide(part) for part in moved), wide(chips[0]))

    def terms(group, *others):
        here = after(slab_order, *others) if others else slab_order
        keep, away = slab_terms(group, here, d_pair, weights, lower_slabs)
        return keep, swap(away, CORE)

    keep_a, got_a = terms((3, 2), sums[1])
    chips_a, moved_a = send(keep_a, got_a)
    keep_b, got_b = terms((1,), sums[2], *chips_a)
    rows_a = total_rows(chips_a, after(moved_a, keep_b))
    chips_b, moved_b = send(keep_b, got_b)
    keep_c, got_c = terms((0,), sums[3], rows_a, *chips_b)
    rows_b = total_rows(chips_b, after(moved_b, keep_c))
    kept_parts = [(kept[3], grad[2], grad[0], kept[2]) for kept, grad in zip(saved, grads)]
    (low_first, *rest), *others = kept_parts
    kept_parts = [(after(low_first, rows_b), *rest), *others]
    owned, owned_down = owned_gradients(kept_parts, 200 * 1024 * SHARDS * tokens_each * 2 * rank * 4)
    got_c = after(got_c, owned_down)
    chips_c, moved_c = send(keep_c, got_c)

    x, dy = Rows(range(SHARDS)), Rows(range(SHARDS))
    for whole, halves in ((x, (x_main, x_away)), (dy, (dy_main, dy_away))):
        for rows in halves:
            whole.arrays += rows.arrays
            whole.places += rows.places
    total = after(sums[3].reshape(SHARDS, 3 * rank, tokens_each), *chips_c)
    grad_pair, grad_down = shared_gradients(
        x,
        dy,
        order,
        slab_order,
        total[:, : 2 * rank],
        total[:, 2 * rank :] * route_blocks,
    )
    rows_c = total_rows(chips_c, after(moved_c, grad_pair))
    grad_x = rows_c[0]
    for rows, r in ((rows_a[0], 3), (rows_a[1], 2), (rows_b[0], 1)):
        grad_x = grad_x + wide(over_experts(rows.astype(jnp.bfloat16), r))
    grad_x = grad_x.astype(jnp.bfloat16)
    return (
        grad_x,
        grad_pair[None, :rank],
        owned[0].T[None],
        grad_pair[None, rank:],
        owned[1].T[None],
        owned_down[None],
        grad_down.T[None],
    )


def plan(tokens, *others):
    experts, tokens_each, hidden_here = lax.axis_size("expert"), tokens.shape[0], others[3].shape[1]
    planned = (
        lax.axis_size("dp") == SHARDS
        and experts == 4
        and hidden_here % LANES == 0
        and tokens_each % LANES == 0
        and tokens.shape[1] % TILE == 0
    )
    return (local if planned else general_local)(tokens, *others)


def solution(mesh):
    return jax.shard_map(
        plan,
        mesh=mesh,
        in_specs=(
            P("dp", "expert"),
            P("dp", "expert"),
            P("dp", None),
            P("dp", None),
            P("expert", "dp", None),
            P("expert", "dp", None),
            P("expert", "dp", None),
            P("expert", None, None),
            P("expert", "dp", None),
            P("expert", None, None),
            P("expert", "dp", None),
            P("expert", None, "dp"),
            P("expert", None, None),
        ),
        out_specs=(
            P("dp", "expert"),
            P("expert", None, None),
            P("expert", "dp", None),
            P("expert", None, None),
            P("expert", "dp", None),
            P("expert", None, "dp"),
            P("expert", None, None),
        ),
        check_vma=False,
    )
```
